32 devices in a mesh: row: 8 (over y, x, core), col: 4 (over z).
Axes of the slice: x: 2, y: 2, z: 4, core: 2. Of those that a mesh axis runs over, the one named last changes fastest.
Arguments:
- query_field: bfloat16 [128, 64, 1152], P('row', 'col'), may hold values from -136 to 136
- key_field: bfloat16 [128, 64, 1152], P('row', 'col'), may hold values from -8.5 to 8.5
- value_field: bfloat16 [128, 64, 1152], P('row', 'col'), may hold values from -6 to 6
- query_tan: bfloat16 [128, 64, 1152], P('row', 'col'), may hold values from -6 to 6
- key_tan: bfloat16 [128, 64, 1152], P('row', 'col'), may hold values from -6 to 6
- value_tan: bfloat16 [128, 64, 1152], P('row', 'col'), may hold values from -6 to 6
- pool_near: float32 [4, 4], replicated, may hold values from -1.5 to 1.5
- pool_far: float32 [16, 16], replicated, may hold values from -0.375 to 0.375
- level_bias: float32 [2, 16], replicated, may hold values from 0.5 to 2.5
Outputs:
- mixed: bfloat16 [128, 64, 1152], P('row', 'col')
- mixed_tan: bfloat16 [128, 64, 1152], P('row', 'col')
The draws below stay inside these ranges and needn't reach their ends.
All inputs are finite; a program needn't handle non-finite values.
Results may differ from the reference program's by a relative error of at most 0.012.
Values may be sent and summed in bfloat16 or wider, within the bound.
No kernel may reach another device: no remote copies, remote signals or barrier semaphores. Data moves between devices by JAX's collectives and lax.ppermute only.
A program may use at most 128 MiB of HBM per device.

```python
import jax
import jax.numpy as jnp
from jax import lax

D = 1152
HEADS = 16
HEAD_DIM = 72
WIN = 16
RIM = 8
NEAR_POOL = 4
GRID_ROWS = 128
GRID_COLS = 64
N_ROW = 8
N_COL = 4


def query_key_pair(key):
    grid_shape = (GRID_ROWS, GRID_COLS, D)
    queries = 1.4 * jax.random.truncated_normal(jax.random.fold_in(key, 101), -6.0, 6.0, grid_shape, jnp.float32)
    keyset = 1.4 * jax.random.truncated_normal(jax.random.fold_in(key, 102), -6.0, 6.0, grid_shape, jnp.float32)
    return (queries, keyset)


def draw_query_field(key, part):
    return query_key_pair(key)[0].astype(jnp.bfloat16)


def draw_key_field(key, part):
    return query_key_pair(key)[1].astype(jnp.bfloat16)


def level_of(key, extent, split, smallest, top_value):
    level = 1.0
    for position, parts in split:
        draws = jax.random.uniform(jax.random.fold_in(jax.random.fold_in(key, 6), position), (parts,), jnp.float32, smallest / len(split), top_value / len(split))
        level = level * jnp.repeat(jnp.exp(draws), extent[position] // parts).reshape((-1,) + (1,) * (len(extent) - 1 - position))
    return level


def normal_values(stream_key, extent, scale, reach, shards=(), held_as=jnp.bfloat16):
    result = scale * jax.random.normal(stream_key, extent, jnp.float32)
    if shards:
        result = result * level_of(stream_key, extent, shards, -0.22, 0.18)
    return jnp.clip(result, -reach, reach).astype(held_as)


def setup_inputs(seed: int = 0) -> dict:
    key_list = jax.random.split(jax.random.key(seed), 10)
    query_field = draw_query_field(jax.random.fold_in(key_list[9], 71), 0)
    key_field = draw_key_field(jax.random.fold_in(key_list[9], 71), 0)
    value_field = normal_values(key_list[2], (GRID_ROWS, GRID_COLS, D), 1.0, 6.0, ((0, 8), (1, 4)))
    query_tan = normal_values(key_list[3], (GRID_ROWS, GRID_COLS, D), 1.0, 6.0, ((0, 8), (1, 4)))
    key_tan = normal_values(key_list[4], (GRID_ROWS, GRID_COLS, D), 1.0, 6.0, ((0, 8), (1, 4)))
    value_tan = normal_values(key_list[5], (GRID_ROWS, GRID_COLS, D), 1.0, 6.0, ((0, 8), (1, 4)))
    pool_near = normal_values(key_list[6], (NEAR_POOL, NEAR_POOL), (NEAR_POOL * NEAR_POOL) ** -0.5, 1.5, (), jnp.float32)
    pool_far = normal_values(key_list[7], (WIN, WIN), (WIN * WIN) ** -0.5, 0.375, (), jnp.float32)
    level_bias = jnp.clip(jax.random.uniform(key_list[8], (2, HEADS), jnp.float32, 0.5, 2.5), 0.5, 2.5)
    return dict(query_field=query_field, key_field=key_field, value_field=value_field, query_tan=query_tan, key_tan=key_tan, value_tan=value_tan, pool_near=pool_near, pool_far=pool_far, level_bias=level_bias)


def pool_cells(field, weights, size):
    row_count, col_count, width = field.shape
    blocks = field.astype(jnp.float32).reshape(row_count // size, size, col_count // size, size, width)
    pooled = jnp.einsum('apbqd,pq->abd', blocks, weights, precision=lax.Precision.HIGHEST)
    return pooled.astype(jnp.bfloat16)


def attend(queries, queries_tan, key_sets, key_bias):
    count = queries.shape[0]
    score_scale = HEAD_DIM ** -0.5
    query_wide = queries.astype(jnp.float32).reshape(count, HEADS, HEAD_DIM)
    tan_wide = queries_tan.astype(jnp.float32).reshape(count, HEADS, HEAD_DIM)
    keys_wide = key_sets[0].astype(jnp.float32).reshape(-1, HEADS, HEAD_DIM)
    values_wide = key_sets[1].astype(jnp.float32).reshape(-1, HEADS, HEAD_DIM)
    keytan_wide = key_sets[2].astype(jnp.float32).reshape(-1, HEADS, HEAD_DIM)
    valtan_wide = key_sets[3].astype(jnp.float32).reshape(-1, HEADS, HEAD_DIM)
    scores = jnp.einsum('qhd,khd->hqk', query_wide, keys_wide) * score_scale + key_bias[:, None, :]
    tangent = (jnp.einsum('qhd,khd->hqk', tan_wide, keys_wide) + jnp.einsum('qhd,khd->hqk', query_wide, keytan_wide)) * score_scale
    top = jnp.max(scores, axis=-1, keepdims=True)
    expd = jnp.exp(scores - top)
    weights = expd / jnp.sum(expd, axis=-1, keepdims=True)
    weights_low = lax.optimization_barrier(weights.astype(jnp.bfloat16)).astype(jnp.float32)
    product = weights * tangent
    row_total = jnp.sum(product, axis=-1)
    product_low = lax.optimization_barrier(product.astype(jnp.bfloat16)).astype(jnp.float32)
    mix = jnp.einsum('hqk,khd->qhd', weights_low, values_wide)
    mix_tan = jnp.einsum('hqk,khd->qhd', product_low, values_wide) + jnp.einsum('hqk,khd->qhd', weights_low, valtan_wide) - jnp.transpose(row_total)[:, :, None] * mix
    return mix.reshape(count, D).astype(jnp.bfloat16), mix_tan.reshape(count, D).astype(jnp.bfloat16)


def reference(query_field, key_field, value_field, query_tan, key_tan, value_tan, pool_near, pool_far, level_bias):
    fields = (key_field, value_field, key_tan, value_tan)
    padded = jnp.stack([jnp.pad(one_field, ((RIM, RIM), (RIM, RIM), (0, 0))) for one_field in fields])
    near_grid = jnp.stack([pool_cells(one_field, pool_near, NEAR_POOL) for one_field in fields])
    far_keys = jnp.stack([pool_cells(one_field, pool_far, WIN).reshape(-1, D) for one_field in fields])
    span = WIN + 2 * RIM
    near_span = 2 * WIN // NEAR_POOL
    far_count = far_keys.shape[1]

    def one_tile(index):
        tile_row = index // N_COL
        tile_col = index % N_COL
        anchor = jnp.int32(0)
        fine = lax.dynamic_slice(padded, (anchor, tile_row * WIN, tile_col * WIN, anchor), (4, span, span, D)).reshape(4, span * span, D)
        near_block = lax.dynamic_slice(near_grid, (anchor, (tile_row // 2) * near_span, (tile_col // 2) * near_span, anchor), (4, near_span, near_span, D)).reshape(4, near_span * near_span, D)
        key_sets = jnp.concatenate([fine, near_block, far_keys], axis=1)
        row_ids = tile_row * WIN - RIM + jnp.arange(span, dtype=jnp.int32)
        col_ids = tile_col * WIN - RIM + jnp.arange(span, dtype=jnp.int32)
        row_ok = (row_ids >= 0) & (row_ids < GRID_ROWS)
        col_ok = (col_ids >= 0) & (col_ids < GRID_COLS)
        valid = (row_ok[:, None] & col_ok[None, :]).reshape(span * span)
        fine_bias = jnp.where(valid, jnp.float32(0.0), jnp.float32(-jnp.inf))
        key_bias = jnp.concatenate([
            jnp.broadcast_to(fine_bias[None, :], (HEADS, span * span)),
            jnp.broadcast_to(level_bias[0][:, None], (HEADS, near_span * near_span)),
            jnp.broadcast_to(level_bias[1][:, None], (HEADS, far_count))], axis=1)
        queries = lax.dynamic_slice(query_field, (tile_row * WIN, tile_col * WIN, anchor), (WIN, WIN, D)).reshape(WIN * WIN, D)
        queries_tan = lax.dynamic_slice(query_tan, (tile_row * WIN, tile_col * WIN, anchor), (WIN, WIN, D)).reshape(WIN * WIN, D)
        return attend(queries, queries_tan, key_sets, key_bias)

    mixed_tiles, tan_tiles = lax.map(one_tile, jnp.arange(N_ROW * N_COL, dtype=jnp.int32))

    def assemble(tiles):
        return tiles.reshape(N_ROW, N_COL, WIN, WIN, D).transpose(0, 2, 1, 3, 4).reshape(GRID_ROWS, GRID_COLS, D)

    return assemble(mixed_tiles), assemble(tan_tiles)
```

```python
import functools

import jax
import jax.numpy as jnp
from jax import lax
from jax.experimental import pallas as pl
from jax.experimental.pallas import tpu as pltpu
from jax.sharding import PartitionSpec as P

HEADS = 16
RIM = 8
NEAR_POOL = 4
LOG2E = 1.4426950408889634
OFF = -1e30
VMEM_BYTES = 48 * 1024 * 1024
LANES = 128


def split3(weights):
    high = weights.astype(jnp.bfloat16)
    rest = weights - high.astype(jnp.float32)
    mid = rest.astype(jnp.bfloat16)
    low = (rest - mid.astype(jnp.float32)).astype(jnp.bfloat16)
    return jnp.concatenate([high, mid, low], axis=0)


def pack_kernel(parity, pool_near, pool_far, *refs):
    fields = refs[:4]
    col_even, col_odd, row_even, row_odd, near, far = refs[4:]
    cells, width = fields[0].shape
    window = 2 * RIM
    row_is_even = parity[0] == 0
    col_is_even = parity[1] == 0
    near_side = window // NEAR_POOL
    near_count = near_side * near_side
    slot = 2 * near_count
    lane = lax.broadcasted_iota(jnp.int32, (slot, cells), 1)
    line = lax.broadcasted_iota(jnp.int32, (slot, cells), 0)
    row, col = lane // window, lane % window
    kernel_near = jnp.zeros((slot, cells), jnp.float32)
    for p in range(NEAR_POOL):
        for q in range(NEAR_POOL):
            hit = (row % NEAR_POOL == p) & (col % NEAR_POOL == q)
            kernel_near = jnp.where(hit, pool_near[p, q], kernel_near)
    block = (row // NEAR_POOL) * near_side + col // NEAR_POOL
    weights = jnp.where(line == block, kernel_near, 0.0)
    weights = jnp.where(line == near_count, pool_far[...], weights)
    weights = split3(weights)
    half = cells // 4
    for index, field in enumerate(fields):
        block = field[...]
        wide = block.astype(jnp.float32).reshape(window, 2, RIM, width)
        left = wide[:, 0].reshape(cells // 2, width).astype(jnp.bfloat16)
        right = wide[:, 1].reshape(cells // 2, width).astype(jnp.bfloat16)
        col_even[index, : cells // 2] = jnp.where(col_is_even, right, left)
        col_odd[index] = jnp.where(col_is_even, left, right)
        for start, side in ((0, left), (half, right)):
            top, bottom = side[:half], side[half:]
            row_even[index, start : start + half] = jnp.where(row_is_even, bottom, top)
            row_odd[index, start : start + half] = jnp.where(row_is_even, top, bottom)
        pooled = jnp.dot(weights, block, preferred_element_type=jnp.float32)
        pooled = pooled[:slot] + (pooled[slot : 2 * slot] + pooled[2 * slot :])
        pooled = pooled.astype(jnp.bfloat16)
        near[index] = pooled[:near_count]
        col_even[index, cells // 2 :] = pooled[:near_count]
        row_even[index, cells // 2 :] = pooled[:near_count]
        far[index] = pooled[near_count:]


def pack(fields, parity, pool_near, pool_far):
    cells, width = fields[0].shape
    near_count = cells // (NEAR_POOL * NEAR_POOL)
    shape = lambda count: jax.ShapeDtypeStruct((4, count, width), jnp.bfloat16)
    strip = cells // 2
    return pl.pallas_call(
        pack_kernel,
        out_shape=(
            shape(strip + near_count),
            shape(strip),
            shape(strip + near_count),
            shape(strip),
            shape(near_count),
            shape(near_count),
        ),
        in_specs=[pl.BlockSpec(memory_space=pltpu.SMEM)] * 2
        + [pl.BlockSpec(memory_space=pltpu.VMEM)] * 5,
        out_specs=[pl.BlockSpec(memory_space=pltpu.VMEM)] * 6,
        compiler_params=pltpu.CompilerParams(vmem_limit_bytes=VMEM_BYTES),
        name="pack",
    )(parity, pool_near, pool_far.reshape(1, cells), *fields)


def move_kernel(moves, source_count, parity, *refs):
    sources, outs, sems = refs[:source_count], refs[source_count:-1], refs[-1]
    copies = []
    for number, (source, start, out, place, count) in enumerate(moves):
        if not isinstance(start, int):
            start = pl.multiple_of(start(parity), 16)
        copies.append(
            pltpu.make_async_copy(
                sources[source].at[:, pl.ds(start, count)],
                outs[out].at[:, pl.ds(place, count)],
                sems.at[number],
            )
        )
    for copy in copies:
        copy.start()
    for copy in copies:
        copy.wait()


def move(parity, sources, moves, counts, name):
    width = sources[0].shape[2]
    return pl.pallas_call(
        functools.partial(move_kernel, moves, len(sources)),
        out_shape=tuple(jax.ShapeDtypeStruct((4, c, width), jnp.bfloat16) for c in counts),
        in_specs=[pl.BlockSpec(memory_space=pltpu.SMEM)]
        + [pl.BlockSpec(memory_space=pl.ANY)] * len(sources),
        out_specs=[pl.BlockSpec(memory_space=pl.ANY)] * len(counts),
        scratch_shapes=[pltpu.SemaphoreType.DMA((len(moves),))],
        name=name,
    )(parity, *sources)


def attend_kernel(plan, flags, level_bias, query, query_tan, *refs):
    moves, segments, source_count, first, last = plan
    sources, refs = refs[:source_count], refs[source_count:]
    if not first:
        state, refs = refs[:3], refs[3:]
    if last:
        mixed, mixed_tan, keys, sems, mix_acc, tan_acc = refs
    else:
        mix_acc, tan_acc, stats_out, keys, sems = refs
    token_count, width = query.shape
    key_count = keys.shape[1]
    head_dim = width // HEADS
    scale = head_dim**-0.5
    span = 2 * LANES
    copies = []
    for number, (source, field, start, place, count) in enumerate(moves):
        if field is None:
            pair = (sources[source].at[:, pl.ds(start, count)], keys.at[:, pl.ds(place, count)])
        else:
            pair = (sources[source].at[pl.ds(start, count)], keys.at[field, pl.ds(place, count)])
        copies.append(pltpu.make_async_copy(*pair, sems.at[number]))
    for copy in copies:
        copy.start()
    used = segments[-1][1]
    if used < key_count:
        keys[:, used:] = jnp.zeros((4, key_count - used, width), jnp.bfloat16)
    if not first:
        stats_in = state[2]
    if first:
        mix_acc[...] = jnp.zeros(mix_acc.shape, jnp.float32)
        tan_acc[...] = jnp.zeros(tan_acc.shape, jnp.float32)
    else:
        mix_acc[...] = state[0][...]
        tan_acc[...] = state[1][...]
    if not last:
        stats_out[...] = jnp.zeros(stats_out.shape, jnp.float32)
    for copy in copies:
        copy.wait()
    key_lane = lax.broadcasted_iota(jnp.int32, (1, key_count), 1)
    lane = lax.broadcasted_iota(jnp.int32, (1, span), 1)
    stat_lane = lax.broadcasted_iota(jnp.int32, (1, LANES), 1)

    def against(left, right):
        return lax.dot_general(
            left, right, (((1,), (1,)), ((), ())), preferred_element_type=jnp.float32
        )

    def head_step(head, carry):
        tile = jnp.minimum(head * head_dim // LANES, (width - span) // LANES)
        start = pl.multiple_of(tile * LANES, LANES)
        low = head * head_dim - start
        inside = (lane >= low) & (lane < low + head_dim)
        keep = inside.astype(jnp.float32).astype(jnp.bfloat16)
        window = pl.ds(start, span)
        head_query = query[:, window] * keep
        head_qtan = query_tan[:, window] * keep
        key = keys[0, :, window]
        value = keys[1, :, window]
        bias = jnp.full((1, key_count), OFF, jnp.float32)
        for begin, end, kind, number in segments:
            amount = flags[number] if kind == "flag" else level_bias[number, head] * LOG2E
            bias = jnp.where((key_lane >= begin) & (key_lane < end), amount, bias)
        scores = against(head_query, key) * (scale * LOG2E) + bias
        top = jnp.max(scores, axis=1, keepdims=True)
        if not first:
            stats = stats_in[...]
            pick = lambda group: jnp.sum(
                jnp.where(stat_lane == head + group * HEADS, stats, 0.0), axis=1, keepdims=True
            )
            old_top = pick(0)
            top = jnp.maximum(top, old_top)
            fade = jnp.exp2(old_top - top)
        weights = jnp.exp2(scores - top)
        product = weights * (
            against(head_qtan, key) + against(head_query, keys[2, :, window])
        )
        total = jnp.sum(weights, axis=1, keepdims=True)
        row_total = jnp.sum(product, axis=1, keepdims=True) * scale
        weights_low = weights.astype(jnp.bfloat16)
        product_low = product.astype(jnp.bfloat16)
        mix = jnp.dot(weights_low, value, preferred_element_type=jnp.float32)
        extra = scale * jnp.dot(product_low, value, preferred_element_type=jnp.float32)
        extra = extra + jnp.dot(
            weights_low, keys[3, :, window], preferred_element_type=jnp.float32
        )
        if not first:
            total = total + fade * pick(1)
            row_total = row_total + fade * pick(2)
            mix = mix + fade * mix_acc[:, window]
            extra = extra + fade * tan_acc[:, window]
        if last:
            inverse = 1.0 / total
            mix = mix * inverse
            extra = extra * inverse - (row_total * inverse) * mix
        else:
            packed = stats_out[...]
            for group, value_of in enumerate((top, total, row_total)):
                packed = jnp.where(stat_lane == head + group * HEADS, value_of, packed)
            stats_out[...] = packed
        mix_acc[:, window] = jnp.where(inside, mix, mix_acc[:, window])
        tan_acc[:, window] = jnp.where(inside, extra, tan_acc[:, window])
        return carry

    lax.fori_loop(0, HEADS, head_step, 0)
    if last:
        mixed[...] = mix_acc[...].astype(jnp.bfloat16)
        mixed_tan[...] = tan_acc[...].astype(jnp.bfloat16)


def attend(flags, level_bias, query, query_tan, sources, moves, segments, state, last, name):
    token_count, width = query.shape
    key_count = -(-segments[-1][1] // LANES) * LANES
    first = state is None
    vmem = pl.BlockSpec(memory_space=pltpu.VMEM)
    smem = pl.BlockSpec(memory_space=pltpu.SMEM)
    wide = jax.ShapeDtypeStruct((token_count, width), jnp.float32)
    scratch = [
        pltpu.VMEM((4, key_count, width), jnp.bfloat16),
        pltpu.SemaphoreType.DMA((len(moves),)),
    ]
    if last:
        out_shape = (jax.ShapeDtypeStruct((token_count, width), jnp.bfloat16),) * 2
        scratch += [pltpu.VMEM((token_count, width), jnp.float32)] * 2
    else:
        out_shape = (wide, wide, jax.ShapeDtypeStruct((token_count, LANES), jnp.float32))
    plan = (moves, segments, len(sources), first, last)
    state = () if first else state
    return pl.pallas_call(
        functools.partial(attend_kernel, plan),
        out_shape=out_shape,
        in_specs=[smem, smem, vmem, vmem]
        + [pl.BlockSpec(memory_space=pl.ANY)] * len(sources)
        + [vmem] * len(state),
        out_specs=[vmem] * len(out_shape),
        scratch_shapes=scratch,
        compiler_params=pltpu.CompilerParams(vmem_limit_bytes=VMEM_BYTES),
        cost_estimate=pl.CostEstimate(
            flops=12 * token_count * key_count * HEADS * 256,
            bytes_accessed=8 * key_count * width + 20 * token_count * width,
            transcendentals=token_count * key_count * HEADS,
        ),
        name=name,
    )(flags, level_bias, query, query_tan, *sources, *state)


def swap(block, axis, odd):
    count = lax.axis_size(axis)
    route = []
    for low in range(1 if odd else 0, count - 1, 2):
        route += [(low, low + 1), (low + 1, low)]
    return lax.ppermute(block, axis, route)


def body(
    query_field,
    key_field,
    value_field,
    query_tan,
    key_tan,
    value_tan,
    pool_near,
    pool_far,
    level_bias,
):
    window = query_field.shape[0]
    width = query_field.shape[2]
    cells = window * window
    strip = cells // 2
    half = cells // 4
    near_count = cells // (NEAR_POOL * NEAR_POOL)
    far_count = lax.axis_size("row") * lax.axis_size("col")
    flat = lambda field: field.reshape(cells, width)
    fields = tuple(flat(f) for f in (key_field, value_field, key_tan, value_tan))
    query, qtan = flat(query_field), flat(query_tan)
    row, col = lax.axis_index("row"), lax.axis_index("col")
    parity = jnp.stack([row % 2, col % 2]).astype(jnp.int32)
    row_edge = (row == 0) | (row == lax.axis_size("row") - 1)
    col_edge = (col == 0) | (col == lax.axis_size("col") - 1)
    flags = jnp.stack(
        [jnp.bool_(False), row_edge, col_edge, row_edge | col_edge]
    )
    flags = jnp.where(flags, jnp.float32(OFF), jnp.float32(0.0))

    col_even, col_odd, row_even, row_odd, near, far = pack(fields, parity, pool_near, pool_far)
    got_col_even = swap(col_even, "col", False)
    got_col_odd = swap(col_odd, "col", True)
    got_row_odd = swap(row_odd, "row", True)
    got_row_even = swap(row_even, "row", False)
    far_all = lax.all_gather(far[:, :1], ("row", "col"), axis=1, tiled=True)

    state = attend(
        flags,
        level_bias,
        query,
        qtan,
        fields,
        [(i, i, 0, 0, cells) for i in range(4)],
        [(0, cells, "flag", 0)],
        None,
        False,
        "own",
    )
    inner, = move(
        parity,
        (got_col_even, got_col_odd),
        [
            (0, lambda p: (1 - p[0]) * half, 0, 0, half),
            (1, lambda p: (1 - p[0]) * half, 0, half, half),
            (0, strip, 0, strip, near_count),
        ],
        (strip + near_count,),
        "pack_inner",
    )
    got_inner = swap(inner, "row", False)
    outer_even, outer_odd = move(
        parity,
        (got_row_odd,),
        [
            (0, lambda p: (1 - p[1]) * half, 0, 0, half),
            (0, lambda p: p[1] * half, 1, 0, half),
        ],
        (half, half),
        "pack_outer",
    )
    got_outer_even = swap(outer_even, "col", False)
    got_outer_odd = swap(outer_odd, "col", True)

    state = attend(
        flags,
        level_bias,
        query,
        qtan,
        (got_row_even, got_row_odd, got_col_even, got_col_odd),
        [(i, None, 0, i * strip, strip) for i in range(4)],
        [
            (0, strip, "flag", 0),
            (strip, 2 * strip, "flag", 1),
            (2 * strip, 3 * strip, "flag", 0),
            (3 * strip, 4 * strip, "flag", 2),
        ],
        state,
        False,
        "strips",
    )
    far_at = 2 * strip + 4 * near_count
    mixed, mixed_tan = attend(
        flags,
        level_bias,
        query,
        qtan,
        (got_inner, got_outer_even, got_outer_odd, near, got_row_even, got_col_even, far_all),
        [
            (0, None, 0, 0, strip),
            (1, None, 0, strip, half),
            (2, None, 0, strip + half, half),
            (3, None, 0, 2 * strip, near_count),
            (4, None, strip, 2 * strip + near_count, near_count),
            (5, None, strip, 2 * strip + 2 * near_count, near_count),
            (0, None, strip, 2 * strip + 3 * near_count, near_count),
            (6, None, 0, far_at, far_count),
        ],
        [
            (0, half, "flag", 0),
            (half, strip, "flag", 2),
            (strip, strip + half, "flag", 1),
            (strip + half, 2 * strip, "flag", 3),
            (2 * strip, far_at, "level", 0),
            (far_at, far_at + far_count, "level", 1),
        ],
        state,
        True,
        "corners",
    )
    shape = (window, window, width)
    return (mixed.reshape(shape), mixed_tan.reshape(shape))


def solution(mesh):
    field = P("row", "col", None)
    return jax.shard_map(
        body,
        mesh=mesh,
        in_specs=(field,) * 6 + (P(),) * 3,
        out_specs=(field, field),
        check_vma=False,
    )
```

```python
import functools

import jax
import jax.numpy as jnp
from jax import lax
from jax.experimental import pallas as pl
from jax.experimental.pallas import tpu as pltpu
from jax.sharding import PartitionSpec as P

HEADS = 16
RIM = 8
NEAR_POOL = 4
LOG2E = 1.4426950408889634
OFF = -1e30
VMEM_BYTES = 24 * 1024 * 1024
LANES = 128
FIELDS = 4
BF16 = jnp.bfloat16
F32 = jnp.float32


def vmem_spec():
    return pl.BlockSpec(memory_space=pltpu.VMEM)


def smem_spec():
    return pl.BlockSpec(memory_space=pltpu.SMEM)


def any_spec():
    return pl.BlockSpec(memory_space=pl.ANY)


def against(left, right):
    return lax.dot_general(left, right, (((1,), (1,)), ((), ())), preferred_element_type=F32)


def chunk_copies(source, target, sems, first, parts):
    rows = source.shape[0] // parts
    copies = []
    for part in range(parts):
        at = pl.ds(part * rows, rows)
        copies.append(pltpu.make_async_copy(source.at[at], target.at[at], sems.at[first + part]))
    return copies


def split3(weights):
    high = weights.astype(BF16)
    rest = weights - high.astype(F32)
    mid = rest.astype(BF16)
    low = (rest - mid.astype(F32)).astype(BF16)
    return jnp.concatenate([high, mid, low], axis=0)


def pool_weights(pool_near, pool_far, cells, slot):
    window = 2 * RIM
    near_side = window // NEAR_POOL
    lane = lax.broadcasted_iota(jnp.int32, (slot, cells), 1)
    line = lax.broadcasted_iota(jnp.int32, (slot, cells), 0)
    row, col = lane // window, lane % window
    near = jnp.zeros((slot, cells), F32)
    for p in range(NEAR_POOL):
        for q in range(NEAR_POOL):
            hit = (row % NEAR_POOL == p) & (col % NEAR_POOL == q)
            near = jnp.where(hit, pool_near[p, q], near)
    block = (row // NEAR_POOL) * near_side + col // NEAR_POOL
    weights = jnp.where(line == block, near, 0.0)
    weights = jnp.where(line == near_side * near_side, pool_far[...], weights)
    return split3(weights)


def pack_kernel(parity, pool_near, pool_far, *refs):
    sources = refs[:FIELDS]
    col_even, col_odd, row_even, row_odd, small = refs[FIELDS : FIELDS + 5]
    held, sems = refs[FIELDS + 5 :]
    cells, width = sources[0].shape
    window = 2 * RIM
    strip, half = cells // 2, cells // 4
    near_count = cells // (NEAR_POOL * NEAR_POOL)
    copies = []
    for index, source in enumerate(sources):
        copies += chunk_copies(source, held.at[index], sems, 2 * index, 2)
    for copy in copies:
        copy.start()
    row_is_even = parity[0] == 0
    col_is_even = parity[1] == 0
    slot = 2 * near_count
    weights = pool_weights(pool_near, pool_far, cells, slot)
    far_rows = []
    for index in range(FIELDS):
        copies[2 * index].wait()
        copies[2 * index + 1].wait()
        block = held[index]
        wide = block.astype(F32).reshape(window, 2, RIM, width)
        left = wide[:, 0].reshape(strip, width).astype(BF16)
        right = wide[:, 1].reshape(strip, width).astype(BF16)
        col_even[index] = jnp.where(col_is_even, right, left)
        col_odd[index] = jnp.where(col_is_even, left, right)
        for start, side in ((0, left), (half, right)):
            top, bottom = side[:half], side[half:]
            row_even[index, start : start + half] = jnp.where(row_is_even, bottom, top)
            row_odd[index, start : start + half] = jnp.where(row_is_even, top, bottom)
        pooled = jnp.dot(weights, block, preferred_element_type=F32)
        pooled = pooled[:slot] + (pooled[slot : 2 * slot] + pooled[2 * slot :])
        near = pooled[:near_count].astype(BF16)
        row_even[index, strip:] = near
        small[index * near_count : (index + 1) * near_count] = near
        far_rows.append(pooled[near_count : near_count + 1])
    far_rows.append(jnp.zeros((near_count - FIELDS, width), F32))
    small[FIELDS * near_count :] = jnp.concatenate(far_rows, axis=0).astype(BF16)


def pack(fields, parity, pool_near, pool_far):
    cells, width = fields[0].shape
    near_count = cells // (NEAR_POOL * NEAR_POOL)
    strip = cells // 2
    shape = lambda *extent: jax.ShapeDtypeStruct(extent + (width,), BF16)
    return pl.pallas_call(
        pack_kernel,
        out_shape=(
            shape(FIELDS, strip),
            shape(FIELDS, strip),
            shape(FIELDS, strip + near_count),
            shape(FIELDS, strip),
            shape((FIELDS + 1) * near_count),
        ),
        in_specs=[smem_spec(), smem_spec(), vmem_spec()] + [any_spec()] * FIELDS,
        out_specs=[vmem_spec()] * 5,
        scratch_shapes=[
            pltpu.VMEM((FIELDS, cells, width), BF16),
            pltpu.SemaphoreType.DMA((2 * FIELDS,)),
        ],
        compiler_params=pltpu.CompilerParams(vmem_limit_bytes=VMEM_BYTES),
        name="pack",
    )(parity, pool_near, pool_far.reshape(1, cells), *fields)


def inner_kernel(parity, col_even, col_odd, small, far, out):
    strip = col_even.shape[1]
    half = strip // 2
    near_count = (small.shape[0]) // (FIELDS + 1)
    group = strip + near_count
    start = pl.multiple_of((1 - parity[0]) * half, half)
    for index in range(FIELDS):
        at = index * group
        out[at : at + half] = col_even[index, pl.ds(start, half)]
        out[at + half : at + strip] = col_odd[index, pl.ds(start, half)]
        out[at + strip : at + group] = small[index * near_count : (index + 1) * near_count]
    out[FIELDS * group :] = far[...]


def pack_inner(parity, col_even, col_odd, small, far):
    _, strip, width = col_even.shape
    near_count = small.shape[0] // (FIELDS + 1)
    rows = FIELDS * (strip + near_count) + far.shape[0]
    return pl.pallas_call(
        inner_kernel,
        out_shape=jax.ShapeDtypeStruct((rows, width), BF16),
        in_specs=[smem_spec()] + [vmem_spec()] * 4,
        out_specs=vmem_spec(),
        compiler_params=pltpu.CompilerParams(vmem_limit_bytes=VMEM_BYTES),
        name="pack_inner",
    )(parity, col_even, col_odd, small, far)


def outer_kernel(parity, row_odd, outer_even, outer_odd):
    half = row_odd.shape[1] // 2
    to_even = pl.multiple_of((1 - parity[1]) * half, half)
    to_odd = pl.multiple_of(parity[1] * half, half)
    for index in range(FIELDS):
        outer_even[index] = row_odd[index, pl.ds(to_even, half)]
        outer_odd[index] = row_odd[index, pl.ds(to_odd, half)]


def pack_outer(parity, row_odd):
    _, strip, width = row_odd.shape
    shape = jax.ShapeDtypeStruct((FIELDS, strip // 2, width), BF16)
    return pl.pallas_call(
        outer_kernel,
        out_shape=(shape, shape),
        in_specs=[smem_spec(), vmem_spec()],
        out_specs=[vmem_spec()] * 2,
        compiler_params=pltpu.CompilerParams(vmem_limit_bytes=VMEM_BYTES),
        name="pack_outer",
    )(parity, row_odd)


def attend_kernel(segments, first, last, far_count, far_place, flags, level_bias, *refs):
    query, query_tan = refs[:2]
    refs = refs[2:]
    if not first:
        mix_in, tan_in, stats_in = refs[:3]
        refs = refs[3:]
    refs = list(refs)
    sems = refs.pop()
    if last:
        mix_acc, tan_acc, turned_mix, turned_tan = refs[-4:]
        mixed, mixed_tan = refs[-6:-4]
        refs = refs[:-6]
    elif first:
        mix_acc, tan_acc, stats_out, held = refs[-4:]
        refs = refs[:-4]
        copies = []
        for index in range(FIELDS):
            copies += chunk_copies(refs[index], held.at[index], sems, 2 * index, 2)
        for copy in copies:
            copy.start()
        for copy in copies:
            copy.wait()
        refs = [held]
    elif far_count:
        mix_acc, tan_acc, stats_out, far_keys = refs[-4:]
        refs = refs[:-4]
        line = lax.broadcasted_iota(jnp.int32, (far_count, FIELDS * far_count), 0)
        lane = lax.broadcasted_iota(jnp.int32, (far_count, FIELDS * far_count), 1)
        own, other, begin = far_place
        far_rows = jnp.concatenate([refs[own][...], refs[other][begin:]], axis=0)
        for index in range(FIELDS):
            select = (lane == line * FIELDS + index).astype(F32).astype(BF16)
            far_keys[index] = jnp.dot(select, far_rows, preferred_element_type=F32).astype(BF16)
        refs = refs + [far_keys]
    else:
        mix_acc, tan_acc, stats_out = refs[-3:]
        refs = refs[:-3]
    token_count, width = query.shape
    head_dim = width // HEADS
    pad_dim = -(-head_dim // 16) * 16
    scale = head_dim**-0.5
    span = 2 * LANES
    lane = lax.broadcasted_iota(jnp.int32, (1, span), 1)
    pick_line = lax.broadcasted_iota(jnp.int32, (pad_dim, span), 0)
    pick_lane = lax.broadcasted_iota(jnp.int32, (pad_dim, span), 1)

    def head_step(head):
        tile = jnp.minimum(head * head_dim // LANES, (width - span) // LANES)
        start = pl.multiple_of(tile * LANES, LANES)
        low = head * head_dim - start
        window = pl.ds(start, span)
        inside = (lane >= low) & (lane < low + head_dim)
        keep = inside.astype(F32).astype(BF16)
        picked = (pick_lane == pick_line + low) & (pick_line < head_dim)
        pick = picked.astype(F32).astype(BF16)
        head_query = query[:, window] * keep
        head_qtan = query_tan[:, window] * keep
        rows_of = lambda field: jnp.concatenate(
            [reader(refs, field, window) for _, _, _, reader in segments], axis=0
        )
        key, value, key_tan, value_tan = (rows_of(field) for field in range(FIELDS))
        scores = against(key, head_query)
        slopes = against(key, head_qtan) + against(key_tan, head_query)
        turned = jnp.concatenate([against(pick, value), against(pick, value_tan)], axis=0)
        turned = turned.astype(BF16)
        bias = []
        top = None
        at = 0
        for rows, kind, number, _ in segments:
            amount = flags[number] if kind == "flag" else level_bias[number, head] * LOG2E
            bias.append(amount)
            part = jnp.max(scores[at : at + rows], axis=0, keepdims=True) * (scale * LOG2E) + amount
            top = part if top is None else jnp.maximum(top, part)
            at += rows
        if not first:
            old_top = stats_in[head, 0:1]
            top = jnp.maximum(top, old_top)
            fade = jnp.exp2(old_top - top)
        weights_low, product_low = [], []
        total, row_total = 0.0, 0.0
        at = 0
        for (rows, _, _, _), amount in zip(segments, bias):
            weights = jnp.exp2(scores[at : at + rows] * (scale * LOG2E) + (amount - top))
            product = weights * slopes[at : at + rows]
            total = total + jnp.sum(weights, axis=0, keepdims=True)
            row_total = row_total + jnp.sum(product, axis=0, keepdims=True)
            weights_low.append(weights.astype(BF16))
            product_low.append(product.astype(BF16))
            at += rows
        weights_low = jnp.concatenate(weights_low, axis=0)
        product_low = jnp.concatenate(product_low, axis=0)
        both = jnp.dot(turned, weights_low, preferred_element_type=F32)
        extra = jnp.dot(turned[:pad_dim], product_low, preferred_element_type=F32)
        mix = both[:head_dim]
        extra = extra[:head_dim] * scale + both[pad_dim : pad_dim + head_dim]
        row_total = row_total * scale
        if not first:
            total = total + fade * stats_in[head, 1:2]
            row_total = row_total + fade * stats_in[head, 2:3]
            mix = mix + fade * mix_in[head]
            extra = extra + fade * tan_in[head]
        if last:
            inverse = 1.0 / total
            mix = mix * inverse
            extra = extra * inverse - (row_total * inverse) * mix
        return top, total, row_total, mix, extra

    together = 2

    def group_step(group, carry):
        heads = [group * together + i for i in range(together)]
        results = [head_step(head) for head in heads]
        for head, (top, total, row_total, mix, extra) in zip(heads, results):
            mix_acc[head] = mix
            tan_acc[head] = extra
            if not last:
                stats_out[head, 0:1] = top
                stats_out[head, 1:2] = total
                stats_out[head, 2:3] = row_total
        return carry

    lax.fori_loop(0, HEADS // together, group_step, 0)
    if last:
        line = lax.broadcasted_iota(jnp.int32, (token_count, token_count), 0)
        lane = lax.broadcasted_iota(jnp.int32, (token_count, token_count), 1)
        unit = (line == lane).astype(F32).astype(BF16)
        copies = []
        parts = 4
        for number, (acc, turned, out) in enumerate(
            ((mix_acc, turned_mix, mixed), (tan_acc, turned_tan, mixed_tan))
        ):
            flat = acc[...].reshape(width, token_count).astype(BF16)
            turned[...] = against(unit, flat).astype(BF16)
            more = chunk_copies(turned, out, sems, number * parts, parts)
            for copy in more:
                copy.start()
            copies += more
        for copy in copies:
            copy.wait()


def attend(
    flags, level_bias, query, qtan, sources, segments, state, name, far_count=0, far_place=None, last=False
):
    token_count, width = query.shape
    head_dim = width // HEADS
    key_count = sum(segment[0] for segment in segments)
    first = state is None
    wide = jax.ShapeDtypeStruct((HEADS, head_dim, token_count), F32)
    scratch = []
    if last:
        out_shape = (jax.ShapeDtypeStruct((token_count, width), BF16),) * 2
        out_specs = [any_spec()] * 2
        scratch += [pltpu.VMEM(wide.shape, F32)] * 2
        scratch += [pltpu.VMEM((token_count, width), BF16)] * 2
    else:
        out_shape = (wide, wide, jax.ShapeDtypeStruct((HEADS, 8, token_count), F32))
        out_specs = [vmem_spec()] * 3
    if first:
        scratch.append(pltpu.VMEM((FIELDS, token_count, width), BF16))
    if far_count:
        scratch.append(pltpu.VMEM((FIELDS, far_count, width), BF16))
    scratch.append(pltpu.SemaphoreType.DMA((8,)))
    state = () if first else tuple(state)
    return pl.pallas_call(
        functools.partial(attend_kernel, segments, first, last, far_count, far_place),
        out_shape=out_shape,
        in_specs=[smem_spec()] * 2
        + [vmem_spec()] * (2 + len(state))
        + [any_spec() if first else vmem_spec()] * len(sources),
        out_specs=out_specs,
        scratch_shapes=scratch,
        compiler_params=pltpu.CompilerParams(vmem_limit_bytes=VMEM_BYTES),
        cost_estimate=pl.CostEstimate(
            flops=12 * token_count * key_count * HEADS * 256,
            bytes_accessed=8 * key_count * width + 20 * token_count * width,
            transcendentals=token_count * key_count * HEADS,
        ),
        name=name,
    )(flags, level_bias, query, qtan, *state, *sources)


def swap(block, axis, odd):
    count = lax.axis_size(axis)
    route = []
    for low in range(1 if odd else 0, count - 1, 2):
        route += [(low, low + 1), (low + 1, low)]
    return lax.ppermute(block, axis, route)


def join_far(block, axis, bit):
    route = [(i, i ^ (1 << bit)) for i in range(lax.axis_size(axis))]
    return jnp.concatenate([block, lax.ppermute(block, axis, route)], axis=0)


def part(source, begin, rows):
    return lambda refs, field, window: refs[source][field, begin : begin + rows, window]


def flat_part(source, stride, begin, rows):
    def read(refs, field, window):
        at = field * stride + begin
        return refs[source][at : at + rows, window]

    return read


def body(
    query_field,
    key_field,
    value_field,
    query_tan,
    key_tan,
    value_tan,
    pool_near,
    pool_far,
    level_bias,
):
    window = query_field.shape[0]
    width = query_field.shape[2]
    cells = window * window
    strip = cells // 2
    half = cells // 4
    near_count = cells // (NEAR_POOL * NEAR_POOL)
    row_count, col_count = lax.axis_size("row"), lax.axis_size("col")
    far_count = row_count * col_count
    flat = lambda field: field.reshape(cells, width)
    fields = tuple(flat(f) for f in (key_field, value_field, key_tan, value_tan))
    query, qtan = flat(query_field), flat(query_tan)
    row, col = lax.axis_index("row"), lax.axis_index("col")
    parity = jnp.stack([row % 2, col % 2]).astype(jnp.int32)
    row_edge = (row == 0) | (row == row_count - 1)
    col_edge = (col == 0) | (col == col_count - 1)
    flags = jnp.stack([jnp.bool_(False), row_edge, col_edge, row_edge | col_edge])
    flags = jnp.where(flags, F32(OFF), F32(0.0))
    attend_all = functools.partial(attend, flags, level_bias, query, qtan)

    col_even, col_odd, row_even, row_odd, small = pack(fields, parity, pool_near, pool_far)
    got_small = swap(small, "col", False)
    got_col_even = swap(col_even, "col", False)
    got_col_odd = swap(col_odd, "col", True)
    got_row_odd = swap(row_odd, "row", True)
    got_row_even = swap(row_even, "row", False)
    far_at = FIELDS * near_count
    far = jnp.concatenate([small[far_at : far_at + FIELDS], got_small[far_at : far_at + FIELDS]])
    for bit in range(1, col_count.bit_length() - 1):
        far = join_far(far, "col", bit)
    for bit in range(row_count.bit_length() - 2, 0, -1):
        far = join_far(far, "row", bit)

    state = attend_all(
        fields, [(cells, "flag", 0, part(0, 0, cells))], None, "own"
    )
    inner = pack_inner(parity, got_col_even, got_col_odd, got_small, far)
    got_inner = swap(inner, "row", False)
    outer_even, outer_odd = pack_outer(parity, got_row_odd)
    got_outer_even = swap(outer_even, "col", False)
    got_outer_odd = swap(outer_odd, "col", True)

    state = attend_all(
        (got_row_even, got_row_odd, got_col_even, got_col_odd),
        [
            (strip, "flag", 0, part(0, 0, strip)),
            (strip, "flag", 1, part(1, 0, strip)),
            (strip, "flag", 0, part(2, 0, strip)),
            (strip, "flag", 2, part(3, 0, strip)),
        ],
        state,
        "strips",
    )
    group = strip + near_count
    state = attend_all(
        (got_inner, small, got_row_even, got_small, far),
        [
            (half, "flag", 0, flat_part(0, group, 0, half)),
            (half, "flag", 2, flat_part(0, group, half, half)),
            (near_count, "level", 0, flat_part(1, near_count, 0, near_count)),
            (near_count, "level", 0, part(2, strip, near_count)),
            (near_count, "level", 0, flat_part(3, near_count, 0, near_count)),
            (near_count, "level", 0, flat_part(0, group, strip, near_count)),
            (far_count, "level", 1, part(5, 0, far_count)),
        ],
        state,
        "inner",
        far_count,
        (4, 0, FIELDS * group),
    )
    mixed, mixed_tan = attend_all(
        (got_outer_even, got_outer_odd),
        [
            (half, "flag", 1, part(0, 0, half)),
            (half, "flag", 3, part(1, 0, half)),
        ],
        state,
        "outer",
        last=True,
    )
    shape = (window, window, width)
    return (mixed.reshape(shape), mixed_tan.reshape(shape))


def solution(mesh):
    field = P("row", "col", None)
    return jax.shard_map(
        body,
        mesh=mesh,
        in_specs=(field,) * 6 + (P(),) * 3,
        out_specs=(field, field),
        check_vma=False,
    )
```

```python
import functools

import jax
import jax.numpy as jnp
from jax import lax
from jax.experimental import pallas as pl
from jax.experimental.pallas import tpu as pltpu
from jax.sharding import PartitionSpec as P

HEADS = 16
RIM = 8
NEAR_POOL = 4
LOG2E = 1.4426950408889634
OFF = -1e30
VMEM_BYTES = 24 * 1024 * 1024
VMEM_MOST = 58 * 1024 * 1024
LANES = 128
FIELDS = 4
BF16 = jnp.bfloat16
F32 = jnp.float32


def vmem_spec():
    return pl.BlockSpec(memory_space=pltpu.VMEM)


def smem_spec():
    return pl.BlockSpec(memory_space=pltpu.SMEM)


def hbm_spec():
    return pl.BlockSpec(memory_space=pltpu.HBM)


def against(left, right):
    return lax.dot_general(left, right, (((1,), (1,)), ((), ())), preferred_element_type=F32)


def chunk_copies(source, target, sems, first, parts):
    rows = source.shape[0] // parts
    copies = []
    for part in range(parts):
        at = pl.ds(part * rows, rows)
        copies.append(pltpu.make_async_copy(source.at[at], target.at[at], sems.at[first + part]))
    return copies


def split3(weights):
    high = weights.astype(BF16)
    rest = weights - high.astype(F32)
    mid = rest.astype(BF16)
    low = (rest - mid.astype(F32)).astype(BF16)
    return jnp.concatenate([high, mid, low], axis=0)


def pool_weights(pool_near, pool_far, cells, slot):
    window = 2 * RIM
    near_side = window // NEAR_POOL
    lane = lax.broadcasted_iota(jnp.int32, (slot, cells), 1)
    line = lax.broadcasted_iota(jnp.int32, (slot, cells), 0)
    row, col = lane // window, lane % window
    near = jnp.zeros((slot, cells), F32)
    for p in range(NEAR_POOL):
        for q in range(NEAR_POOL):
            hit = (row % NEAR_POOL == p) & (col % NEAR_POOL == q)
            near = jnp.where(hit, pool_near[p, q], near)
    block = (row // NEAR_POOL) * near_side + col // NEAR_POOL
    weights = jnp.where(line == block, near, 0.0)
    weights = jnp.where(line == near_side * near_side, pool_far[...], weights)
    return split3(weights)


def pack_kernel(parity, pool_near, pool_far, *refs):
    sources = refs[:FIELDS]
    col_even, col_odd, row_even, row_odd, far = refs[FIELDS : FIELDS + 5]
    held, sems = refs[FIELDS + 5 :]
    cells, width = sources[0].shape
    window = 2 * RIM
    strip, half = cells // 2, cells // 4
    near_count = cells // (NEAR_POOL * NEAR_POOL)
    copies = []
    for index, source in enumerate(sources):
        copies += chunk_copies(source, held.at[index], sems, 2 * index, 2)
    for copy in copies:
        copy.start()
    row_is_even = parity[0] == 0
    col_is_even = parity[1] == 0
    slot = 2 * near_count
    weights = pool_weights(pool_near, pool_far, cells, slot)
    far_rows = []
    for index in range(FIELDS):
        copies[2 * index].wait()
        copies[2 * index + 1].wait()
        block = held[index]
        wide = block.astype(F32).reshape(window, 2, RIM, width)
        left = wide[:, 0].reshape(strip, width).astype(BF16)
        right = wide[:, 1].reshape(strip, width).astype(BF16)
        col_even[index, :strip] = jnp.where(col_is_even, right, left)
        col_odd[index] = jnp.where(col_is_even, left, right)
        for start, side in ((0, left), (half, right)):
            top, bottom = side[:half], side[half:]
            row_even[index, start : start + half] = jnp.where(row_is_even, bottom, top)
            row_odd[index, start : start + half] = jnp.where(row_is_even, top, bottom)
        pooled = jnp.dot(weights, block, preferred_element_type=F32)
        pooled = pooled[:slot] + (pooled[slot : 2 * slot] + pooled[2 * slot :])
        near = pooled[:near_count].astype(BF16)
        row_even[index, strip:] = near
        col_even[index, strip : strip + near_count] = near
        far_rows.append(pooled[near_count : near_count + 1])
    far_rows.append(jnp.zeros((16 - FIELDS, width), F32))
    far_block = jnp.concatenate(far_rows, axis=0).astype(BF16)
    far[...] = far_block
    for index in range(FIELDS):
        col_even[index, strip + near_count :] = far_block


def pack(fields, parity, pool_near, pool_far):
    cells, width = fields[0].shape
    near_count = cells // (NEAR_POOL * NEAR_POOL)
    strip = cells // 2
    shape = lambda *extent: jax.ShapeDtypeStruct(extent + (width,), BF16)
    return pl.pallas_call(
        pack_kernel,
        out_shape=(
            shape(FIELDS, strip + near_count + 16),
            shape(FIELDS, strip),
            shape(FIELDS, strip + near_count),
            shape(FIELDS, strip),
            shape(16),
        ),
        in_specs=[smem_spec(), smem_spec(), vmem_spec()] + [hbm_spec()] * FIELDS,
        out_specs=[vmem_spec()] * 5,
        scratch_shapes=[
            pltpu.VMEM((FIELDS, cells, width), BF16),
            pltpu.SemaphoreType.DMA((2 * FIELDS,)),
        ],
        compiler_params=pltpu.CompilerParams(vmem_limit_bytes=VMEM_MOST),
        name="pack",
    )(parity, pool_near, pool_far.reshape(1, cells), *fields)


def forward_kernel(parity, *refs):
    col_even, col_odd, row_odd, _ = refs[:4]
    held_even, held_odd, held_row, inner, outer_even, outer_odd, far, sems = refs[4:]
    strip = col_odd.shape[1]
    half = strip // 2
    near_count = col_even.shape[1] - strip - 16
    group = strip + near_count
    copies = []
    for number, (source, target) in enumerate(
        ((row_odd, held_row), (col_even, held_even), (col_odd, held_odd))
    ):
        copies.append(chunk_copies(source, target, sems, FIELDS * number, FIELDS))
    for copy in copies[0] + copies[1] + copies[2]:
        copy.start()
    to_even = pl.multiple_of((1 - parity[1]) * half, half)
    to_odd = pl.multiple_of(parity[1] * half, half)
    start = pl.multiple_of((1 - parity[0]) * half, half)
    for index in range(FIELDS):
        copies[0][index].wait()
        outer_even[index] = held_row[index, pl.ds(to_even, half)]
        outer_odd[index] = held_row[index, pl.ds(to_odd, half)]
    for index in range(FIELDS):
        copies[1][index].wait()
        copies[2][index].wait()
        at = index * group
        inner[at : at + half] = held_even[index, pl.ds(start, half)]
        inner[at + half : at + strip] = held_odd[index, pl.ds(start, half)]
        inner[at + strip : at + group] = held_even[index, strip : strip + near_count]
    far[...] = held_even[0, strip + near_count :]


def forward(parity, col_even, col_odd, row_odd, before):
    _, strip, width = col_odd.shape
    half = strip // 2
    near_count = col_even.shape[1] - strip - 16
    rows = FIELDS * (strip + near_count)
    shape = lambda *extent: jax.ShapeDtypeStruct(extent + (width,), BF16)
    return pl.pallas_call(
        forward_kernel,
        out_shape=(
            shape(FIELDS, col_even.shape[1]),
            shape(FIELDS, strip),
            shape(FIELDS, strip),
            shape(rows),
            shape(FIELDS, half),
            shape(FIELDS, half),
            shape(16),
        ),
        in_specs=[smem_spec()] + [hbm_spec()] * 3 + [vmem_spec()],
        out_specs=[vmem_spec()] * 7,
        scratch_shapes=[pltpu.SemaphoreType.DMA((3 * FIELDS,))],
        compiler_params=pltpu.CompilerParams(vmem_limit_bytes=VMEM_BYTES),
        name="forward",
    )(parity, col_even, col_odd, row_odd, before)


def attend_kernel(plan, flags, level_bias, *refs):
    segments, first, last, staged, held_count, tied, far_count = plan
    refs = list(refs)
    take = lambda count: [refs.pop(0) for _ in range(count)]
    query, query_tan = take(2)
    if not first:
        mix_in, tan_in, stats_in = take(3)
    sources, held = take(staged), take(held_count)
    take(tied)
    if last:
        mixed, mixed_tan = take(2)
    else:
        mix_acc, tan_acc, stats_out = take(3)
    if first:
        query_held, qtan_held = take(2)
    scratch = take(staged)
    if far_count:
        far_keys, = take(1)
    if last:
        mix_acc, tan_acc, turned_mix, turned_tan = take(4)
    sems, = take(1)
    copies = []
    pairs = list(zip(sources, scratch))
    if first:
        pairs += [(query, query_held), (query_tan, qtan_held)]
        query, query_tan = query_held, qtan_held
    for number, (source, target) in enumerate(pairs):
        copies += chunk_copies(source, target, sems, FIELDS * number, FIELDS)
    for copy in copies:
        copy.start()
    if far_count:
        line = lax.broadcasted_iota(jnp.int32, (far_count, FIELDS * far_count), 0)
        lane = lax.broadcasted_iota(jnp.int32, (far_count, FIELDS * far_count), 1)
        for index in range(FIELDS):
            select = (lane == line * FIELDS + index).astype(F32).astype(BF16)
            far_keys[index] = jnp.dot(
                select, held[-1][...], preferred_element_type=F32
            ).astype(BF16)
        held = held + [far_keys]
    for copy in copies:
        copy.wait()
    refs = scratch + held
    token_count, width = query.shape
    head_dim = width // HEADS
    pad_dim = -(-head_dim // 16) * 16
    scale = head_dim**-0.5
    span = 2 * LANES
    lane = lax.broadcasted_iota(jnp.int32, (1, span), 1)
    pick_line = lax.broadcasted_iota(jnp.int32, (pad_dim, span), 0)
    pick_lane = lax.broadcasted_iota(jnp.int32, (pad_dim, span), 1)

    def head_step(head):
        tile = jnp.minimum(head * head_dim // LANES, (width - span) // LANES)
        start = pl.multiple_of(tile * LANES, LANES)
        low = head * head_dim - start
        window = pl.ds(start, span)
        inside = (lane >= low) & (lane < low + head_dim)
        keep = inside.astype(F32).astype(BF16)
        picked = (pick_lane == pick_line + low) & (pick_line < head_dim)
        pick = picked.astype(F32).astype(BF16)
        head_query = query[:, window] * keep
        head_qtan = query_tan[:, window] * keep
        rows_of = lambda field: jnp.concatenate(
            [reader(refs, field, window) for _, _, _, reader in segments], axis=0
        )
        key, value, key_tan, value_tan = (rows_of(field) for field in range(FIELDS))
        scores = against(key, head_query)
        slopes = against(key, head_qtan) + against(key_tan, head_query)
        turned = jnp.concatenate([against(pick, value), against(pick, value_tan)], axis=0)
        turned = turned.astype(BF16)
        bias = []
        top = None
        at = 0
        for rows, kind, number, _ in segments:
            amount = flags[number] if kind == "flag" else level_bias[number, head] * LOG2E
            bias.append(amount)
            part = jnp.max(scores[at : at + rows], axis=0, keepdims=True) * (scale * LOG2E) + amount
            top = part if top is None else jnp.maximum(top, part)
            at += rows
        if not first:
            old_top = stats_in[head, 0:1]
            top = jnp.maximum(top, old_top)
            fade = jnp.exp2(old_top - top)
        weights_low, product_low = [], []
        total, row_total = 0.0, 0.0
        at = 0
        for (rows, _, _, _), amount in zip(segments, bias):
            weights = jnp.exp2(scores[at : at + rows] * (scale * LOG2E) + (amount - top))
            product = weights * slopes[at : at + rows]
            total = total + jnp.sum(weights, axis=0, keepdims=True)
            row_total = row_total + jnp.sum(product, axis=0, keepdims=True)
            weights_low.append(weights.astype(BF16))
            product_low.append(product.astype(BF16))
            at += rows
        weights_low = jnp.concatenate(weights_low, axis=0)
        product_low = jnp.concatenate(product_low, axis=0)
        both = jnp.dot(turned, weights_low, preferred_element_type=F32)
        extra = jnp.dot(turned[:pad_dim], product_low, preferred_element_type=F32)
        mix = both[:head_dim]
        extra = extra[:head_dim] * scale + both[pad_dim : pad_dim + head_dim]
        row_total = row_total * scale
        if not first:
            total = total + fade * stats_in[head, 1:2]
            row_total = row_total + fade * stats_in[head, 2:3]
            mix = mix + fade * mix_in[head]
            extra = extra + fade * tan_in[head]
        if last:
            inverse = 1.0 / total
            mix = mix * inverse
            extra = extra * inverse - (row_total * inverse) * mix
        return top, total, row_total, mix, extra

    together = 4

    def group_step(group, carry):
        heads = [group * together + i for i in range(together)]
        results = [head_step(head) for head in heads]
        for head, (top, total, row_total, mix, extra) in zip(heads, results):
            mix_acc[head] = mix
            tan_acc[head] = extra
            if not last:
                stats_out[head, 0:1] = top
                stats_out[head, 1:2] = total
                stats_out[head, 2:3] = row_total
        return carry

    lax.fori_loop(0, HEADS // together, group_step, 0)
    if last:
        line = lax.broadcasted_iota(jnp.int32, (token_count, token_count), 0)
        lane = lax.broadcasted_iota(jnp.int32, (token_count, token_count), 1)
        unit = (line == lane).astype(F32).astype(BF16)
        copies = []
        for number, (acc, turned, out) in enumerate(
            ((mix_acc, turned_mix, mixed), (tan_acc, turned_tan, mixed_tan))
        ):
            flat = acc[...].reshape(width, token_count).astype(BF16)
            turned[...] = against(unit, flat).astype(BF16)
            more = chunk_copies(turned, out, sems, number * FIELDS, FIELDS)
            for copy in more:
                copy.start()
            copies += more
        for copy in copies:
            copy.wait()


def attend(
    flags, level_bias, query, qtan, state, staged, held, tied, segments, name, far_count=0, last=False
):
    token_count, width = query.shape
    head_dim = width // HEADS
    key_count = sum(segment[0] for segment in segments)
    first = state is None
    wide = jax.ShapeDtypeStruct((HEADS, head_dim, token_count), F32)
    tokens = jax.ShapeDtypeStruct((token_count, width), BF16)
    if last:
        out_shape = (tokens, tokens)
        out_specs = [hbm_spec()] * 2
    else:
        out_shape = (wide, wide, jax.ShapeDtypeStruct((HEADS, 8, token_count), F32))
        if first:
            out_shape += (tokens, tokens)
        out_specs = [vmem_spec()] * len(out_shape)
    scratch = [pltpu.VMEM(source.shape, BF16) for source in staged]
    if far_count:
        scratch.append(pltpu.VMEM((FIELDS, far_count, width), BF16))
    if last:
        scratch += [pltpu.VMEM(wide.shape, F32)] * 2
        scratch += [pltpu.VMEM(tokens.shape, BF16)] * 2
    scratch.append(pltpu.SemaphoreType.DMA((FIELDS * (len(staged) + 2),)))
    state = () if first else tuple(state)
    plan = (segments, first, last, len(staged), len(held), len(tied), far_count)
    return pl.pallas_call(
        functools.partial(attend_kernel, plan),
        out_shape=out_shape,
        in_specs=[smem_spec()] * 2
        + [hbm_spec() if first else vmem_spec()] * 2
        + [vmem_spec()] * len(state)
        + [hbm_spec()] * len(staged)
        + [vmem_spec()] * (len(held) + len(tied)),
        out_specs=out_specs,
        scratch_shapes=scratch,
        compiler_params=pltpu.CompilerParams(vmem_limit_bytes=VMEM_BYTES),
        cost_estimate=pl.CostEstimate(
            flops=token_count * key_count * HEADS,
            bytes_accessed=token_count * width,
            transcendentals=0,
        ),
        name=name,
    )(flags, level_bias, query, qtan, *state, *staged, *held, *tied)


def swap(block, axis, odd):
    count = lax.axis_size(axis)
    route = []
    for low in range(1 if odd else 0, count - 1, 2):
        route += [(low, low + 1), (low + 1, low)]
    return lax.ppermute(block, axis, route)


def part(source, begin, rows):
    return lambda refs, field, window: refs[source][field, begin : begin + rows, window]


def flat_part(source, stride, begin, rows):
    def read(refs, field, window):
        at = field * stride + begin
        return refs[source][at : at + rows, window]

    return read


def body(
    query_field,
    key_field,
    value_field,
    query_tan,
    key_tan,
    value_tan,
    pool_near,
    pool_far,
    level_bias,
):
    window = query_field.shape[0]
    width = query_field.shape[2]
    cells = window * window
    strip = cells // 2
    half = cells // 4
    near_count = cells // (NEAR_POOL * NEAR_POOL)
    row_count, col_count = lax.axis_size("row"), lax.axis_size("col")
    far_count = row_count * col_count
    flat = lambda field: field.reshape(cells, width)
    fields = tuple(flat(f) for f in (key_field, value_field, key_tan, value_tan))
    query, qtan = flat(query_field), flat(query_tan)
    row, col = lax.axis_index("row"), lax.axis_index("col")
    parity = jnp.stack([row % 2, col % 2]).astype(jnp.int32)
    row_edge = (row == 0) | (row == row_count - 1)
    col_edge = (col == 0) | (col == col_count - 1)
    flags = jnp.stack([jnp.bool_(False), row_edge, col_edge, row_edge | col_edge])
    flags = jnp.where(flags, F32(OFF), F32(0.0))
    attend_all = functools.partial(attend, flags, level_bias)

    col_even, col_odd, row_even, row_odd, own_far = pack(fields, parity, pool_near, pool_far)
    got_row_odd = swap(row_odd, "row", True)
    got_col_even = swap(col_even, "col", False)
    got_col_odd = swap(col_odd, "col", True)
    got_row_even = swap(row_even, "row", False)

    far = jnp.zeros((far_count * FIELDS, width), BF16)
    place = (row * col_count + col) * FIELDS
    far = lax.dynamic_update_slice_in_dim(far, own_far[:FIELDS], place, 0)
    far = lax.psum(far, ("row", "col"))

    group = strip + near_count
    own_near = row_even[:, strip:]
    *state, query, qtan = attend_all(
        query,
        qtan,
        None,
        fields + (got_row_even,),
        (),
        (),
        [
            (cells, "flag", 0, lambda refs, field, window: refs[field][:, window]),
            (strip, "flag", 0, part(4, 0, strip)),
            (near_count, "level", 0, part(4, strip, near_count)),
        ],
        "own",
    )
    held_even, held_odd, held_row, inner, outer_even, outer_odd, _ = forward(
        parity, got_col_even, got_col_odd, got_row_odd, state[2]
    )
    got_outer_even = swap(outer_even, "col", False)
    got_outer_odd = swap(outer_odd, "col", True)
    got_inner = swap(inner, "row", False)

    state = attend_all(
        query,
        qtan,
        state,
        (),
        (held_row, held_even, held_odd),
        (),
        [
            (strip, "flag", 1, part(0, 0, strip)),
            (strip, "flag", 0, part(1, 0, strip)),
            (strip, "flag", 2, part(2, 0, strip)),
        ],
        "strips",
    )
    state = attend_all(
        query,
        qtan,
        state,
        (),
        (got_inner, own_near, held_even),
        (),
        [
            (half, "flag", 0, flat_part(0, group, 0, half)),
            (half, "flag", 2, flat_part(0, group, half, half)),
            (near_count, "level", 0, part(1, 0, near_count)),
            (near_count, "level", 0, part(2, strip, near_count)),
            (near_count, "level", 0, flat_part(0, group, strip, near_count)),
        ],
        "inner",
    )
    mixed, mixed_tan = attend_all(
        query,
        qtan,
        state,
        (),
        (got_outer_even, got_outer_odd, far),
        (),
        [
            (half, "flag", 1, part(0, 0, half)),
            (half, "flag", 3, part(1, 0, half)),
            (far_count, "level", 1, part(3, 0, far_count)),
        ],
        "outer",
        far_count,
        last=True,
    )
    shape = (window, window, width)
    return (mixed.reshape(shape), mixed_tan.reshape(shape))


def solution(mesh):
    field = P("row", "col", None)
    return jax.shard_map(
        body,
        mesh=mesh,
        in_specs=(field,) * 6 + (P(),) * 3,
        out_specs=(field, field),
        check_vma=False,
    )
```

```python
import functools

import jax
import jax.numpy as jnp
from jax import lax
from jax.experimental import pallas as pl
from jax.experimental.pallas import tpu as pltpu
from jax.sharding import PartitionSpec as P

HEADS = 16
RIM = 8
NEAR_POOL = 4
LOG2E = 1.4426950408889634
OFF = -1e30
PACK_BYTES = 60 * 1024 * 1024
VMEM_BYTES = 28 * 1024 * 1024
LANES = 128
FIELDS = 4
BF16 = jnp.bfloat16
F32 = jnp.float32


def vmem_spec():
    return pl.BlockSpec(memory_space=pltpu.VMEM)


def smem_spec():
    return pl.BlockSpec(memory_space=pltpu.SMEM)


def hbm_spec():
    return pl.BlockSpec(memory_space=pltpu.HBM)


def any_spec():
    return pl.BlockSpec(memory_space=pl.ANY)


def against(left, right):
    return lax.dot_general(left, right, (((1,), (1,)), ((), ())), preferred_element_type=F32)


def chunk_copies(source, target, sems, first, parts):
    rows = source.shape[0]
    step = -(-rows // parts)
    if len(source.shape) == 2:
        step = -(-step // 16) * 16
    copies = []
    for number, begin in enumerate(range(0, rows, step)):
        at = pl.ds(begin, min(step, rows - begin))
        copies.append(pltpu.make_async_copy(source.at[at], target.at[at], sems.at[first + number]))
    return copies


def split3(weights):
    high = weights.astype(BF16)
    rest = weights - high.astype(F32)
    mid = rest.astype(BF16)
    low = (rest - mid.astype(F32)).astype(BF16)
    return jnp.concatenate([high, mid, low], axis=0)


def pool_weights(pool_near, pool_far, cells):
    window = 2 * RIM
    near_side = window // NEAR_POOL
    near_count = near_side * near_side
    lane = lax.broadcasted_iota(jnp.int32, (near_count, cells), 1)
    line = lax.broadcasted_iota(jnp.int32, (near_count, cells), 0)
    row, col = lane // window, lane % window
    near = jnp.zeros((near_count, cells), F32)
    for p in range(NEAR_POOL):
        for q in range(NEAR_POOL):
            hit = (row % NEAR_POOL == p) & (col % NEAR_POOL == q)
            near = jnp.where(hit, pool_near[p, q], near)
    block = (row // NEAR_POOL) * near_side + col // NEAR_POOL
    near = split3(jnp.where(line == block, near, 0.0))
    spread = (line == col).astype(F32).astype(BF16)
    far = jnp.dot(split3(pool_far), spread, preferred_element_type=F32)
    far_line = lax.broadcasted_iota(jnp.int32, far.shape, 0) % window
    far_lane = lax.broadcasted_iota(jnp.int32, far.shape, 1) // window
    far = jnp.where(far_line == far_lane, far, 0.0)
    rows = [
        jnp.sum(far[i * window : (i + 1) * window], axis=0, keepdims=True) for i in range(3)
    ]
    rows.append(jnp.zeros((near_count - 3, cells), F32))
    return jnp.concatenate([near, jnp.concatenate(rows, axis=0).astype(BF16)], axis=0)


def halves(block, width):
    cells = block.shape[0]
    wide = block.astype(F32).reshape(cells // (2 * RIM), 2, RIM, width)
    left = wide[:, 0].reshape(cells // 2, width).astype(BF16)
    right = wide[:, 1].reshape(cells // 2, width).astype(BF16)
    return left, right


def pack_kernel(pool_near, pool_far, *refs):
    sources, outs = refs[:FIELDS], refs[FIELDS : FIELDS + 5]
    held = refs[FIELDS + 5]
    kept, sems, out_sems = refs[FIELDS + 6 : -2], refs[-2], refs[-1]
    cells, width = sources[0].shape
    strip, half = cells // 2, cells // 4
    near_count = cells // (NEAR_POOL * NEAR_POOL)
    row_is_even = lax.axis_index("row") % 2 == 0
    col_is_even = lax.axis_index("col") % 2 == 0
    copies = []
    for index, source in enumerate(sources):
        copies += chunk_copies(source, held.at[index], sems, 2 * index, 2)
    for copy in copies:
        copy.start()
    weights = pool_weights(pool_near, pool_far[...], cells)
    far_rows = []
    sent = []
    for index in range(FIELDS):
        copies[2 * index].wait()
        copies[2 * index + 1].wait()
        block = held[index]
        left, right = halves(block, width)
        even = jnp.where(col_is_even, right, left)
        odd = jnp.where(col_is_even, left, right)
        outer = lambda side: jnp.where(row_is_even, side[:half], side[half:])
        pooled = jnp.dot(weights, block, preferred_element_type=F32)
        near = pooled[:near_count] + (
            pooled[near_count : 2 * near_count] + pooled[2 * near_count : 3 * near_count]
        )
        near = near.astype(BF16)
        far = pooled[3 * near_count :]
        far_rows.append(far[0:1] + (far[1:2] + far[2:3]))
        kept[0][index, :half] = outer(even)
        kept[0][index, half:] = outer(odd)
        kept[1][index, :strip] = even
        kept[1][index, strip:] = near
        kept[2][index] = odd
        kept[3][index, :strip] = jnp.where(row_is_even, block[strip:], block[:strip])
        kept[3][index, strip : strip + near_count] = near
        for number in range(3):
            copy = pltpu.make_async_copy(
                kept[number].at[index], outs[number].at[index], out_sems.at[3 * index + number]
            )
            copy.start()
            sent.append(copy)
    far_rows.append(jnp.zeros((16 - FIELDS, width), F32))
    kept[4][...] = jnp.concatenate(far_rows, axis=0).astype(BF16)
    for index in range(FIELDS):
        kept[3][index, strip + near_count :] = kept[4][...]
    for number in (3, 4):
        copy = pltpu.make_async_copy(
            kept[number], outs[number], out_sems.at[3 * FIELDS + number - 3]
        )
        copy.start()
        sent.append(copy)
    for copy in sent:
        copy.wait()


def pack(fields, pool_near, pool_far):
    cells, width = fields[0].shape
    strip = cells // 2
    near_count = cells // (NEAR_POOL * NEAR_POOL)
    shapes = [
        (FIELDS, strip, width),
        (FIELDS, strip + near_count, width),
        (FIELDS, strip, width),
        (FIELDS, strip + near_count + 16, width),
        (16, width),
    ]
    return pl.pallas_call(
        pack_kernel,
        out_shape=tuple(jax.ShapeDtypeStruct(s, BF16) for s in shapes),
        in_specs=[smem_spec(), vmem_spec()] + [hbm_spec()] * FIELDS,
        out_specs=[hbm_spec()] * len(shapes),
        scratch_shapes=[pltpu.VMEM((FIELDS, cells, width), BF16)]
        + [pltpu.VMEM(s, BF16) for s in shapes]
        + [pltpu.SemaphoreType.DMA((2 * FIELDS,)), pltpu.SemaphoreType.DMA((3 * FIELDS + 2,))],
        compiler_params=pltpu.CompilerParams(vmem_limit_bytes=PACK_BYTES),
        name="pack",
    )(pool_near, pool_far, *fields)


TOGETHER = 4
GROUPS = HEADS // TOGETHER


def group_copy(source, target, sem, group):
    at = pl.ds(group * TOGETHER, TOGETHER)
    return pltpu.make_async_copy(source.at[at], target.at[at], sem.at[group])


def attend_kernel(plan, level_bias, *refs):
    segments, first, last, staged, tied, far_count, far_blocks = plan
    refs = list(refs)
    take = lambda count: [refs.pop(0) for _ in range(count)]
    query_in, qtan_in = take(2)
    state_in = [] if first else take(3)
    sources = take(staged)
    take(tied)
    if last:
        outs = take(2)
    else:
        outs = take(5 if first else 3)
    query, query_tan = take(2)
    state = [] if first else take(3)
    scratch = take(staged)
    acc = take(3)
    far_keys = take(1) if far_count else []
    if last:
        turned = take(2)
    if first:
        raw = take(2)
    sems, state_sems, out_sems = take(3)
    width, token_count = query.shape
    head_dim = width // HEADS
    pad_dim = -(-head_dim // 16) * 16
    scale = head_dim**-0.5
    span = 2 * LANES
    copies = []
    pairs = list(zip((query_in, qtan_in), raw if first else (query, query_tan)))
    pairs += list(zip(sources, scratch))
    for number, (source, target) in enumerate(pairs):
        copies += chunk_copies(source, target, sems, FIELDS * number, FIELDS)
    for copy in copies:
        copy.start()
    for number, (source, target) in enumerate(zip(state_in, state)):
        for group in range(GROUPS):
            group_copy(source, target, state_sems.at[number], group).start()
    if first:
        line = lax.broadcasted_iota(jnp.int32, (LANES, LANES), 0)
        lane = lax.broadcasted_iota(jnp.int32, (LANES, LANES), 1)
        unit = (line == lane).astype(F32).astype(BF16)
        for copy in copies[: 2 * FIELDS]:
            copy.wait()
        for source, target in zip(raw, (query, query_tan)):
            for at in range(0, width, LANES):
                target[at : at + LANES] = against(unit, source[:, at : at + LANES]).astype(BF16)
        kept = chunk_copies(query, outs[3], sems, 0, FIELDS)
        kept += chunk_copies(query_tan, outs[4], sems, FIELDS, FIELDS)
        for copy in kept:
            copy.start()
        for copy in copies[2 * FIELDS :]:
            copy.wait()
    else:
        for copy in copies:
            copy.wait()
    if far_count:
        line = lax.broadcasted_iota(jnp.int32, (far_count, FIELDS * far_count), 0)
        lane = lax.broadcasted_iota(jnp.int32, (far_count, FIELDS * far_count), 1)
        far_rows = jnp.concatenate([scratch[i][begin:] for i, begin in far_blocks], axis=0)
        for index in range(FIELDS):
            select = (lane == line * FIELDS + index).astype(F32).astype(BF16)
            far_keys[0][index] = jnp.dot(
                select, far_rows, preferred_element_type=F32
            ).astype(BF16)
    refs = scratch + far_keys
    row, col = lax.axis_index("row"), lax.axis_index("col")
    row_edge = (row == 0) | (row == lax.axis_size("row") - 1)
    col_edge = (col == 0) | (col == lax.axis_size("col") - 1)
    off = lambda edge: jnp.where(edge, F32(OFF), F32(0.0))
    flags = (F32(0.0), off(row_edge), off(col_edge), off(row_edge | col_edge))
    channel = lax.broadcasted_iota(jnp.int32, (span, token_count), 0)
    pick_line = lax.broadcasted_iota(jnp.int32, (pad_dim, span), 0)
    pick_lane = lax.broadcasted_iota(jnp.int32, (pad_dim, span), 1)

    def head_step(head):
        tile = jnp.minimum(head * head_dim // LANES, (width - span) // LANES)
        start = pl.multiple_of(tile * LANES, LANES)
        low = head * head_dim - start
        window = pl.ds(start, span)
        inside = (channel >= low) & (channel < low + head_dim)
        keep = inside.astype(F32).astype(BF16)
        picked = (pick_lane == pick_line + low) & (pick_line < head_dim)
        pick = picked.astype(F32).astype(BF16)
        head_query = query[window] * keep
        head_qtan = query_tan[window] * keep
        rows_of = lambda field: jnp.concatenate(
            [reader(refs, field, window) for _, _, _, reader in segments], axis=0
        )
        key, value, key_tan, value_tan = (rows_of(field) for field in range(FIELDS))
        scores = jnp.dot(key, head_query, preferred_element_type=F32)
        slopes = jnp.dot(key, head_qtan, preferred_element_type=F32)
        slopes = slopes + jnp.dot(key_tan, head_query, preferred_element_type=F32)
        turned = jnp.concatenate([against(pick, value), against(pick, value_tan)], axis=0)
        turned = turned.astype(BF16)
        bias = []
        top = None
        at = 0
        for rows, kind, number, _ in segments:
            amount = flags[number] if kind == "flag" else level_bias[number, head] * LOG2E
            bias.append(amount)
            part = jnp.max(scores[at : at + rows], axis=0, keepdims=True) * (scale * LOG2E) + amount
            top = part if top is None else jnp.maximum(top, part)
            at += rows
        if not first:
            old_top = state[2][head, 0:1]
            top = jnp.maximum(top, old_top)
            fade = jnp.exp2(old_top - top)
        weights_low, product_low = [], []
        total, row_total = 0.0, 0.0
        at = 0
        for (rows, _, _, _), amount in zip(segments, bias):
            weights = jnp.exp2(scores[at : at + rows] * (scale * LOG2E) + (amount - top))
            product = weights * slopes[at : at + rows]
            total = total + jnp.sum(weights, axis=0, keepdims=True)
            row_total = row_total + jnp.sum(product, axis=0, keepdims=True)
            weights_low.append(weights.astype(BF16))
            product_low.append(product.astype(BF16))
            at += rows
        weights_low = jnp.concatenate(weights_low, axis=0)
        product_low = jnp.concatenate(product_low, axis=0)
        both = jnp.dot(turned, weights_low, preferred_element_type=F32)
        extra = jnp.dot(turned[:pad_dim], product_low, preferred_element_type=F32)
        mix = both[:head_dim]
        extra = extra[:head_dim] * scale + both[pad_dim : pad_dim + head_dim]
        row_total = row_total * scale
        if not first:
            total = total + fade * state[2][head, 1:2]
            row_total = row_total + fade * state[2][head, 2:3]
            mix = mix + fade * state[0][head]
            extra = extra + fade * state[1][head]
        if last:
            inverse = 1.0 / total
            mix = mix * inverse
            extra = extra * inverse - (row_total * inverse) * mix
        return top, total, row_total, mix, extra

    def group_step(group, carry):
        for number, (source, target) in enumerate(zip(state_in, state)):
            group_copy(source, target, state_sems.at[number], group).wait()
        heads = [group * TOGETHER + i for i in range(TOGETHER)]
        results = [head_step(head) for head in heads]
        for head, (top, total, row_total, mix, extra) in zip(heads, results):
            acc[0][head] = mix
            acc[1][head] = extra
            if not last:
                acc[2][head, 0:1] = top
                acc[2][head, 1:2] = total
                acc[2][head, 2:3] = row_total
        if not last:
            for number in range(3):
                group_copy(acc[number], outs[number], out_sems.at[number], group).start()
        return carry

    if not last:
        acc[2][...] = jnp.zeros(acc[2].shape, F32)
    lax.fori_loop(0, GROUPS, group_step, 0)
    if last:
        line = lax.broadcasted_iota(jnp.int32, (token_count, token_count), 0)
        lane = lax.broadcasted_iota(jnp.int32, (token_count, token_count), 1)
        unit = (line == lane).astype(F32).astype(BF16)
        sent = []
        for number in range(2):
            flat = acc[number][...].reshape(width, token_count).astype(BF16)
            turned[number][...] = against(unit, flat).astype(BF16)
            more = chunk_copies(turned[number], outs[number], sems, number * FIELDS, FIELDS)
            for copy in more:
                copy.start()
            sent += more
        for copy in sent:
            copy.wait()
    else:
        for number in range(3):
            for group in range(GROUPS):
                group_copy(acc[number], outs[number], out_sems.at[number], group).wait()
        if first:
            for copy in kept:
                copy.wait()


def attend(level_bias, query, qtan, state, staged, tied, segments, name, far=(0, ()), last=False):
    first = state is None
    if first:
        token_count, width = query.shape
    else:
        width, token_count = query.shape
    head_dim = width // HEADS
    key_count = sum(segment[0] for segment in segments)
    wide = (HEADS, head_dim, token_count)
    states = (wide, wide, (HEADS, 8, token_count))
    vmem = lambda shape, kind: pltpu.VMEM(shape, kind)
    tokens = jax.ShapeDtypeStruct((token_count, width), BF16)
    turned = jax.ShapeDtypeStruct((width, token_count), BF16)
    if last:
        out_shape = (tokens, tokens)
    else:
        out_shape = tuple(jax.ShapeDtypeStruct(s, F32) for s in states)
        if first:
            out_shape += (turned, turned)
    scratch = [vmem(turned.shape, BF16)] * 2
    if not first:
        scratch += [vmem(s, F32) for s in states]
    scratch += [vmem(source.shape, BF16) for source in staged]
    scratch += [vmem(s, F32) for s in states]
    if far[0]:
        scratch.append(vmem((FIELDS, far[0], width), BF16))
    if last or first:
        scratch += [vmem(tokens.shape, BF16)] * 2
    scratch.append(pltpu.SemaphoreType.DMA((FIELDS * (len(staged) + 2),)))
    scratch += [pltpu.SemaphoreType.DMA((3, GROUPS))] * 2
    state = () if first else tuple(state)
    operands = (query, qtan, *state, *staged, *tied)
    plan = (segments, first, last, len(staged), len(tied), far[0], far[1])
    return pl.pallas_call(
        functools.partial(attend_kernel, plan),
        out_shape=out_shape,
        in_specs=[smem_spec()]
        + [hbm_spec()] * (2 + len(state))
        + [hbm_spec() if first and i < FIELDS else any_spec() for i in range(len(staged))]
        + [any_spec()] * len(tied),
        out_specs=[hbm_spec()] * len(out_shape),
        scratch_shapes=scratch,
        compiler_params=pltpu.CompilerParams(vmem_limit_bytes=VMEM_BYTES),
        cost_estimate=pl.CostEstimate(
            flops=token_count * key_count * HEADS,
            bytes_accessed=token_count * width,
            transcendentals=0,
        ),
        name=name,
    )(level_bias, *operands)


def swap(block, axis, odd):
    count = lax.axis_size(axis)
    route = []
    for low in range(1 if odd else 0, count - 1, 2):
        route += [(low, low + 1), (low + 1, low)]
    return lax.ppermute(block, axis, route)


def part(source, begin, rows):
    return lambda refs, field, window: refs[source][field, begin : begin + rows, window]


def flat_part(source, stride, begin, rows):
    def read(refs, field, window):
        at = field * stride + begin
        return refs[source][at : at + rows, window]

    return read


def toward_mate(source, half):
    def read(refs, field, window):
        start = pl.multiple_of((lax.axis_index("row") % 2) * half, half)
        return refs[source][field, pl.ds(start, half), window]

    return read


def send_to(block, axis, mask):
    return lax.ppermute(block, axis, [(i, i ^ mask) for i in range(lax.axis_size(axis))])


def gather_far(far):
    for bit in range(lax.axis_size("row").bit_length() - 2, 0, -1):
        far = jnp.concatenate([far, send_to(far, "row", 1 << bit)])
    for bit in range(lax.axis_size("col").bit_length() - 2, 0, -1):
        far = jnp.concatenate([far, send_to(far, "col", 1 << bit)])
    return far


def body(
    query_field,
    key_field,
    value_field,
    query_tan,
    key_tan,
    value_tan,
    pool_near,
    pool_far,
    level_bias,
):
    window = query_field.shape[0]
    width = query_field.shape[2]
    cells = window * window
    strip, half = cells // 2, cells // 4
    near_count = cells // (NEAR_POOL * NEAR_POOL)
    row_count, col_count = lax.axis_size("row"), lax.axis_size("col")
    far_count = row_count * col_count
    flat = lambda field: field.reshape(cells, width)
    fields = tuple(flat(f) for f in (key_field, value_field, key_tan, value_tan))

    row_odd, col_even, col_odd, row_even, far = pack(fields, pool_near, pool_far)
    got_row_odd = swap(row_odd, "row", True)
    got_col_even = swap(col_even, "col", False)
    got_col_odd = swap(col_odd, "col", True)
    got_row_even = swap(row_even, "row", False)

    *state, query, qtan = attend(
        level_bias,
        flat(query_field),
        flat(query_tan),
        None,
        fields + (got_row_even,),
        (),
        [
            (cells, "flag", 0, lambda refs, field, window: refs[field][:, window]),
            (strip, "flag", 0, part(4, 0, strip)),
            (near_count, "level", 0, part(4, strip, near_count)),
        ],
        "own",
    )
    attend_more = functools.partial(attend, level_bias, query, qtan)
    mate_far = got_row_even[0, strip + near_count : strip + near_count + FIELDS]
    far = jnp.concatenate([far[:FIELDS], mate_far])
    far, stats = lax.optimization_barrier((far, state[2]))
    state = (state[0], state[1], stats)
    far_shape = jax.ShapeDtypeStruct((FIELDS * far_count // 2, width), BF16)
    far = lax.cond(
        lax.axis_index("row") < row_count,
        gather_far,
        lambda block: jnp.zeros(far_shape.shape, far_shape.dtype),
        far,
    )
    got_col_even, got_col_odd, far = lax.optimization_barrier((got_col_even, got_col_odd, far))
    corner = got_row_odd[:, :half].reshape(FIELDS * half, width)
    got_outer_even = swap(jnp.concatenate([corner, far]), "col", False)
    got_outer_odd = swap(got_row_odd[:, half:], "col", True)
    got_inner_even = swap(got_col_even, "row", False)
    got_inner_odd = swap(got_col_odd, "row", False)

    state = attend_more(
        state,
        (got_row_odd, got_col_even, got_col_odd),
        (),
        [
            (strip, "flag", 1, part(0, 0, strip)),
            (strip, "flag", 0, part(1, 0, strip)),
            (strip, "flag", 2, part(2, 0, strip)),
        ],
        "strips",
    )
    state = attend_more(
        state,
        (got_inner_even, got_inner_odd, got_col_even, row_even),
        (),
        [
            (half, "flag", 0, toward_mate(0, half)),
            (half, "flag", 2, toward_mate(1, half)),
            (near_count, "level", 0, part(0, strip, near_count)),
            (near_count, "level", 0, part(2, strip, near_count)),
            (near_count, "level", 0, part(3, strip, near_count)),
        ],
        "inner",
    )
    mixed, mixed_tan = attend_more(
        state,
        (got_outer_even, got_outer_odd, far),
        (),
        [
            (half, "flag", 1, flat_part(0, half, 0, half)),
            (half, "flag", 3, part(1, 0, half)),
            (far_count, "level", 1, part(3, 0, far_count)),
        ],
        "outer",
        far=(far_count, ((0, FIELDS * half), (2, 0))),
        last=True,
    )
    shape = (window, window, width)
    return (mixed.reshape(shape), mixed_tan.reshape(shape))


def solution(mesh):
    field = P("row", "col", None)
    return jax.shard_map(
        body,
        mesh=mesh,
        in_specs=(field,) * 6 + (P(),) * 3,
        out_specs=(field, field),
        check_vma=False,
    )
```

```python
import functools

import jax
import jax.numpy as jnp
from jax import lax
from jax.experimental import pallas as pl
from jax.experimental.pallas import tpu as pltpu
from jax.sharding import PartitionSpec as P

HEADS = 16
RIM = 8
NEAR_POOL = 4
LOG2E = 1.4426950408889634
OFF = -1e30
PACK_BYTES = 60 * 1024 * 1024
VMEM_BYTES = 28 * 1024 * 1024
LANES = 128
FIELDS = 4
BF16 = jnp.bfloat16
F32 = jnp.float32


def vmem_spec():
    return pl.BlockSpec(memory_space=pltpu.VMEM)


def smem_spec():
    return pl.BlockSpec(memory_space=pltpu.SMEM)


def hbm_spec():
    return pl.BlockSpec(memory_space=pltpu.HBM)


def any_spec():
    return pl.BlockSpec(memory_space=pl.ANY)


def against(left, right):
    return lax.dot_general(left, right, (((1,), (1,)), ((), ())), preferred_element_type=F32)


def chunk_copies(source, target, sems, first, parts):
    rows = source.shape[0]
    step = -(-rows // parts)
    if len(source.shape) == 2:
        step = -(-step // 16) * 16
    copies = []
    for number, begin in enumerate(range(0, rows, step)):
        at = pl.ds(begin, min(step, rows - begin))
        copies.append(pltpu.make_async_copy(source.at[at], target.at[at], sems.at[first + number]))
    return copies


def split3(weights):
    high = weights.astype(BF16)
    rest = weights - high.astype(F32)
    mid = rest.astype(BF16)
    low = (rest - mid.astype(F32)).astype(BF16)
    return jnp.concatenate([high, mid, low], axis=0)


def pool_weights(pool_near, pool_far, cells):
    window = 2 * RIM
    near_side = window // NEAR_POOL
    near_count = near_side * near_side
    lane = lax.broadcasted_iota(jnp.int32, (near_count, cells), 1)
    line = lax.broadcasted_iota(jnp.int32, (near_count, cells), 0)
    row, col = lane // window, lane % window
    near = jnp.zeros((near_count, cells), F32)
    for p in range(NEAR_POOL):
        for q in range(NEAR_POOL):
            hit = (row % NEAR_POOL == p) & (col % NEAR_POOL == q)
            near = jnp.where(hit, pool_near[p, q], near)
    block = (row // NEAR_POOL) * near_side + col // NEAR_POOL
    near = split3(jnp.where(line == block, near, 0.0))
    spread = (line == col).astype(F32).astype(BF16)
    far = jnp.dot(split3(pool_far), spread, preferred_element_type=F32)
    far_line = lax.broadcasted_iota(jnp.int32, far.shape, 0) % window
    far_lane = lax.broadcasted_iota(jnp.int32, far.shape, 1) // window
    far = jnp.where(far_line == far_lane, far, 0.0)
    rows = [
        jnp.sum(far[i * window : (i + 1) * window], axis=0, keepdims=True) for i in range(3)
    ]
    rows.append(jnp.zeros((near_count - 3, cells), F32))
    return jnp.concatenate([near, jnp.concatenate(rows, axis=0).astype(BF16)], axis=0)


def halves(block, width):
    cells = block.shape[0]
    wide = block.astype(F32).reshape(cells // (2 * RIM), 2, RIM, width)
    left = wide[:, 0].reshape(cells // 2, width).astype(BF16)
    right = wide[:, 1].reshape(cells // 2, width).astype(BF16)
    return left, right


def pack_kernel(pool_near, pool_far, *refs):
    sources, outs = refs[:FIELDS], refs[FIELDS : FIELDS + 5]
    held = refs[FIELDS + 5]
    kept, sems, out_sems = refs[FIELDS + 6 : -2], refs[-2], refs[-1]
    cells, width = sources[0].shape
    strip, half = cells // 2, cells // 4
    near_count = cells // (NEAR_POOL * NEAR_POOL)
    row_is_even = lax.axis_index("row") % 2 == 0
    col_is_even = lax.axis_index("col") % 2 == 0
    copies = []
    for index, source in enumerate(sources):
        copies += chunk_copies(source, held.at[index], sems, 2 * index, 2)
    for copy in copies:
        copy.start()
    weights = pool_weights(pool_near, pool_far[...], cells)
    far_rows = []
    sent = []
    for index in range(FIELDS):
        copies[2 * index].wait()
        copies[2 * index + 1].wait()
        block = held[index]
        left, right = halves(block, width)
        even = jnp.where(col_is_even, right, left)
        odd = jnp.where(col_is_even, left, right)
        outer = lambda side: jnp.where(row_is_even, side[:half], side[half:])
        pooled = jnp.dot(weights, block, preferred_element_type=F32)
        near = pooled[:near_count] + (
            pooled[near_count : 2 * near_count] + pooled[2 * near_count : 3 * near_count]
        )
        near = near.astype(BF16)
        far = pooled[3 * near_count :]
        far_rows.append(far[0:1] + (far[1:2] + far[2:3]))
        kept[0][index, :half] = outer(even)
        kept[0][index, half:] = outer(odd)
        kept[1][index, :strip] = even
        kept[1][index, strip:] = near
        kept[2][index] = odd
        kept[3][index, :strip] = jnp.where(row_is_even, block[strip:], block[:strip])
        kept[3][index, strip : strip + near_count] = near
        for number in range(3):
            copy = pltpu.make_async_copy(
                kept[number].at[index], outs[number].at[index], out_sems.at[3 * index + number]
            )
            copy.start()
            sent.append(copy)
    far_rows.append(jnp.zeros((16 - FIELDS, width), F32))
    kept[4][...] = jnp.concatenate(far_rows, axis=0).astype(BF16)
    for index in range(FIELDS):
        kept[3][index, strip + near_count :] = kept[4][...]
    for number in (3, 4):
        copy = pltpu.make_async_copy(
            kept[number], outs[number], out_sems.at[3 * FIELDS + number - 3]
        )
        copy.start()
        sent.append(copy)
    for copy in sent:
        copy.wait()


def pack(fields, pool_near, pool_far):
    cells, width = fields[0].shape
    strip = cells // 2
    near_count = cells // (NEAR_POOL * NEAR_POOL)
    shapes = [
        (FIELDS, strip, width),
        (FIELDS, strip + near_count, width),
        (FIELDS, strip, width),
        (FIELDS, strip + near_count + 16, width),
        (16, width),
    ]
    return pl.pallas_call(
        pack_kernel,
        out_shape=tuple(jax.ShapeDtypeStruct(s, BF16) for s in shapes),
        in_specs=[smem_spec(), vmem_spec()] + [hbm_spec()] * FIELDS,
        out_specs=[hbm_spec()] * len(shapes),
        scratch_shapes=[pltpu.VMEM((FIELDS, cells, width), BF16)]
        + [pltpu.VMEM(s, BF16) for s in shapes]
        + [pltpu.SemaphoreType.DMA((2 * FIELDS,)), pltpu.SemaphoreType.DMA((3 * FIELDS + 2,))],
        compiler_params=pltpu.CompilerParams(vmem_limit_bytes=PACK_BYTES),
        name="pack",
    )(pool_near, pool_far, *fields)


TOGETHER = 4
GROUPS = HEADS // TOGETHER


def group_copy(source, target, sem, group):
    at = pl.ds(group * TOGETHER, TOGETHER)
    return pltpu.make_async_copy(source.at[at], target.at[at], sem.at[group])


def window_of(head, head_dim, width):
    span = 2 * LANES
    tile = jnp.minimum(head * head_dim // LANES, (width - span) // LANES)
    start = pl.multiple_of(tile * LANES, LANES)
    return pl.ds(start, span), head * head_dim - start


def turn_queries(raw, turned, masked):
    width = raw.shape[1]
    head_dim = width // HEADS
    span = 2 * LANES
    line = lax.broadcasted_iota(jnp.int32, (LANES, LANES), 0)
    lane = lax.broadcasted_iota(jnp.int32, (LANES, LANES), 1)
    unit = (line == lane).astype(F32).astype(BF16)
    for at in range(0, width, LANES):
        turned[at : at + LANES] = against(unit, raw[:, at : at + LANES]).astype(BF16)
    channel = lax.broadcasted_iota(jnp.int32, (span, raw.shape[0]), 0)
    for head in range(HEADS):
        start = min(head * head_dim // LANES, (width - span) // LANES) * LANES
        low = head * head_dim - start
        keep = ((channel >= low) & (channel < low + head_dim)).astype(F32).astype(BF16)
        masked[head] = turned[start : start + span] * keep


def device_flags():
    row, col = lax.axis_index("row"), lax.axis_index("col")
    row_edge = (row == 0) | (row == lax.axis_size("row") - 1)
    col_edge = (col == 0) | (col == lax.axis_size("col") - 1)
    off = lambda edge: jnp.where(edge, F32(OFF), F32(0.0))
    return (F32(0.0), off(row_edge), off(col_edge), off(row_edge | col_edge))


def attend_group(segments, refs, queries, level_bias, heads, width, old):
    head_dim = width // HEADS
    pad_dim = -(-head_dim // 16) * 16
    scale = head_dim**-0.5
    span = 2 * LANES
    flags = device_flags()
    pick_line = lax.broadcasted_iota(jnp.int32, (pad_dim, span), 0)
    pick_lane = lax.broadcasted_iota(jnp.int32, (pad_dim, span), 1)
    products = []
    for head in heads:
        window, low = window_of(head, head_dim, width)
        rows_of = lambda field: jnp.concatenate(
            [reader(refs, field, window) for _, _, _, reader in segments], axis=0
        )
        key, value, key_tan, value_tan = (rows_of(field) for field in range(FIELDS))
        scores = jnp.dot(key, queries[0][head], preferred_element_type=F32)
        slopes = jnp.dot(key, queries[1][head], preferred_element_type=F32)
        slopes = slopes + jnp.dot(key_tan, queries[0][head], preferred_element_type=F32)
        picked = (pick_lane == pick_line + low) & (pick_line < head_dim)
        pick = picked.astype(F32).astype(BF16)
        turned = jnp.concatenate([against(pick, value), against(pick, value_tan)], axis=0)
        products.append((scores, slopes, turned.astype(BF16)))
    weighted = []
    for head, (scores, slopes, turned) in zip(heads, products):
        bias = []
        top = None
        at = 0
        for rows, kind, number, _ in segments:
            amount = flags[number] if kind == "flag" else level_bias[number, head] * LOG2E
            bias.append(amount)
            part = jnp.max(scores[at : at + rows], axis=0, keepdims=True) * (scale * LOG2E) + amount
            top = part if top is None else jnp.maximum(top, part)
            at += rows
        fade = None
        if old is not None:
            old_top = old[2][head, 0:1]
            top = jnp.maximum(top, old_top)
            fade = jnp.exp2(old_top - top)
        weights_low, product_low = [], []
        total, row_total = 0.0, 0.0
        at = 0
        for (rows, _, _, _), amount in zip(segments, bias):
            weights = jnp.exp2(scores[at : at + rows] * (scale * LOG2E) + (amount - top))
            product = weights * slopes[at : at + rows]
            total = total + jnp.sum(weights, axis=0, keepdims=True)
            row_total = row_total + jnp.sum(product, axis=0, keepdims=True)
            weights_low.append(weights.astype(BF16))
            product_low.append(product.astype(BF16))
            at += rows
        weights_low = jnp.concatenate(weights_low, axis=0)
        product_low = jnp.concatenate(product_low, axis=0)
        weighted.append((top, fade, total, row_total * scale, weights_low, product_low))
    results = []
    for (_, _, turned), (_, _, _, _, weights_low, product_low) in zip(products, weighted):
        both = jnp.dot(turned, weights_low, preferred_element_type=F32)
        extra = jnp.dot(turned[:pad_dim], product_low, preferred_element_type=F32)
        mix = both[:head_dim]
        results.append((mix, extra[:head_dim] * scale + both[pad_dim : pad_dim + head_dim]))
    out = []
    for head, (top, fade, total, row_total, _, _), (mix, extra) in zip(heads, weighted, results):
        if old is not None:
            total = total + fade * old[2][head, 1:2]
            row_total = row_total + fade * old[2][head, 2:3]
            mix = mix + fade * old[0][head]
            extra = extra + fade * old[1][head]
        out.append((top, total, row_total, mix, extra))
    return out


def keep_state(state, heads, results):
    for head, (top, total, row_total, mix, extra) in zip(heads, results):
        state[0][head] = mix
        state[1][head] = extra
        state[2][head, 0:1] = top
        state[2][head, 1:2] = total
        state[2][head, 2:3] = row_total


def own_kernel(segments, level_bias, *refs):
    query_in, qtan_in = refs[:2]
    sources = refs[2 : 3 + FIELDS]
    outs = refs[3 + FIELDS : 8 + FIELDS]
    raw, turned, masked = refs[8 + FIELDS : 10 + FIELDS], refs[10 + FIELDS], refs[11 + FIELDS : 13 + FIELDS]
    held = refs[13 + FIELDS : 14 + 2 * FIELDS]
    state = refs[14 + 2 * FIELDS : 17 + 2 * FIELDS]
    sems, out_sems = refs[17 + 2 * FIELDS :]
    width = query_in.shape[1]
    copies = []
    for number, (source, target) in enumerate(
        list(zip((query_in, qtan_in), raw)) + list(zip(sources, held))
    ):
        copies += chunk_copies(source, target, sems, FIELDS * number, FIELDS)
    for copy in copies:
        copy.start()
    state[2][...] = jnp.zeros(state[2].shape, F32)
    sent = []
    for number in range(2):
        for copy in copies[FIELDS * number : FIELDS * (number + 1)]:
            copy.wait()
        turn_queries(raw[number], turned, masked[number])
        for group in range(GROUPS):
            sent.append(
                group_copy(masked[number], outs[3 + number], out_sems.at[3 + number], group)
            )
            sent[-1].start()
    for copy in copies[2 * FIELDS :]:
        copy.wait()

    def group_step(group, carry):
        heads = [group * TOGETHER + i for i in range(TOGETHER)]
        results = attend_group(segments, held, masked, level_bias, heads, width, None)
        keep_state(state, heads, results)
        for number in range(3):
            group_copy(state[number], outs[number], out_sems.at[number], group).start()
        return carry

    lax.fori_loop(0, GROUPS, group_step, 0)
    for number in range(3):
        for group in range(GROUPS):
            group_copy(state[number], outs[number], out_sems.at[number], group).wait()
    for copy in sent:
        copy.wait()


def state_shapes(token_count, width):
    wide = (HEADS, width // HEADS, token_count)
    return (wide, wide, (HEADS, 8, token_count))


def own_cost(token_count, width, key_count):
    return pl.CostEstimate(
        flops=token_count * key_count * HEADS,
        bytes_accessed=token_count * width,
        transcendentals=0,
    )


def attend_own(level_bias, query, qtan, fields, mate, segments):
    token_count, width = query.shape
    states = state_shapes(token_count, width)
    masked = (HEADS, 2 * LANES, token_count)
    operands = (query, qtan, *fields, mate)
    return pl.pallas_call(
        functools.partial(own_kernel, segments),
        out_shape=tuple(jax.ShapeDtypeStruct(s, F32) for s in states)
        + (jax.ShapeDtypeStruct(masked, BF16),) * 2,
        in_specs=[smem_spec()] + [hbm_spec()] * len(operands),
        out_specs=[hbm_spec()] * 5,
        scratch_shapes=[pltpu.VMEM(query.shape, BF16)] * 2
        + [pltpu.VMEM((width, token_count), BF16)]
        + [pltpu.VMEM(masked, BF16)] * 2
        + [pltpu.VMEM(source.shape, BF16) for source in operands[2:]]
        + [pltpu.VMEM(s, F32) for s in states]
        + [
            pltpu.SemaphoreType.DMA((FIELDS * len(operands),)),
            pltpu.SemaphoreType.DMA((5, GROUPS)),
        ],
        compiler_params=pltpu.CompilerParams(vmem_limit_bytes=PACK_BYTES),
        cost_estimate=own_cost(token_count, width, sum(s[0] for s in segments)),
        name="own",
    )(level_bias, *operands)


def more_kernel(segments, count, level_bias, *refs):
    queries, old, sources, state = refs[:2], refs[2:5], refs[5 : 5 + count], refs[5 + count :]
    width = old[0].shape[0] * old[0].shape[1]
    state[2][...] = jnp.zeros(state[2].shape, F32)

    def group_step(group, carry):
        heads = [group * TOGETHER + i for i in range(TOGETHER)]
        results = attend_group(segments, sources, queries, level_bias, heads, width, old)
        keep_state(state, heads, results)
        return carry

    lax.fori_loop(0, GROUPS, group_step, 0)


def attend_more(level_bias, queries, state, sources, segments, name):
    token_count = queries[0].shape[2]
    width = state[0].shape[0] * state[0].shape[1]
    operands = (*queries, *state, *sources)
    return pl.pallas_call(
        functools.partial(more_kernel, segments, len(sources)),
        out_shape=tuple(jax.ShapeDtypeStruct(s, F32) for s in state_shapes(token_count, width)),
        in_specs=[smem_spec()] + [vmem_spec()] * len(operands),
        out_specs=[vmem_spec()] * 3,
        compiler_params=pltpu.CompilerParams(vmem_limit_bytes=VMEM_BYTES),
        cost_estimate=own_cost(token_count, width, sum(s[0] for s in segments)),
        name=name,
    )(level_bias, *operands)


def last_kernel(segments, count, far_count, far_blocks, level_bias, *refs):
    queries, old, sources = refs[:2], refs[2:5], refs[5 : 5 + count]
    outs = refs[5 + count : 7 + count]
    far_keys, mix_acc, tan_acc, turned, sems = refs[7 + count :]
    width, token_count = old[0].shape[0] * old[0].shape[1], old[0].shape[2]
    line = lax.broadcasted_iota(jnp.int32, (far_count, FIELDS * far_count), 0)
    lane = lax.broadcasted_iota(jnp.int32, (far_count, FIELDS * far_count), 1)
    far_rows = jnp.concatenate([sources[i][begin:] for i, begin in far_blocks], axis=0)
    for index in range(FIELDS):
        select = (lane == line * FIELDS + index).astype(F32).astype(BF16)
        far_keys[index] = jnp.dot(select, far_rows, preferred_element_type=F32).astype(BF16)
    sources = sources + (far_keys,)

    def group_step(group, carry):
        heads = [group * TOGETHER + i for i in range(TOGETHER)]
        results = attend_group(segments, sources, queries, level_bias, heads, width, old)
        for head, (_, total, row_total, mix, extra) in zip(heads, results):
            inverse = 1.0 / total
            mix = mix * inverse
            mix_acc[head] = mix
            tan_acc[head] = extra * inverse - (row_total * inverse) * mix
        return carry

    lax.fori_loop(0, GROUPS, group_step, 0)
    line = lax.broadcasted_iota(jnp.int32, (token_count, token_count), 0)
    lane = lax.broadcasted_iota(jnp.int32, (token_count, token_count), 1)
    unit = (line == lane).astype(F32).astype(BF16)
    sent = []
    for number, acc in enumerate((mix_acc, tan_acc)):
        flat = acc[...].reshape(width, token_count).astype(BF16)
        turned[number] = against(unit, flat).astype(BF16)
        more = chunk_copies(turned.at[number], outs[number], sems, number * FIELDS, FIELDS)
        for copy in more:
            copy.start()
        sent += more
    for copy in sent:
        copy.wait()


def attend_last(level_bias, queries, state, sources, segments, far_count, far_blocks):
    token_count = queries[0].shape[2]
    width = state[0].shape[0] * state[0].shape[1]
    states = state_shapes(token_count, width)
    operands = (*queries, *state, *sources)
    return pl.pallas_call(
        functools.partial(last_kernel, segments, len(sources), far_count, far_blocks),
        out_shape=(jax.ShapeDtypeStruct((token_count, width), BF16),) * 2,
        in_specs=[smem_spec()] + [vmem_spec()] * len(operands),
        out_specs=[hbm_spec()] * 2,
        scratch_shapes=[
            pltpu.VMEM((FIELDS, far_count, width), BF16),
            pltpu.VMEM(states[0], F32),
            pltpu.VMEM(states[1], F32),
            pltpu.VMEM((2, token_count, width), BF16),
            pltpu.SemaphoreType.DMA((2 * FIELDS,)),
        ],
        compiler_params=pltpu.CompilerParams(vmem_limit_bytes=VMEM_BYTES),
        cost_estimate=own_cost(token_count, width, sum(s[0] for s in segments)),
        name="outer",
    )(level_bias, *operands)


def swap(block, axis, odd):
    count = lax.axis_size(axis)
    route = []
    for low in range(1 if odd else 0, count - 1, 2):
        route += [(low, low + 1), (low + 1, low)]
    return lax.ppermute(block, axis, route)


def part(source, begin, rows):
    return lambda refs, field, window: refs[source][field, begin : begin + rows, window]


def flat_part(source, stride, begin, rows):
    def read(refs, field, window):
        at = field * stride + begin
        return refs[source][at : at + rows, window]

    return read


def toward_mate(source, half):
    def read(refs, field, window):
        start = pl.multiple_of((lax.axis_index("row") % 2) * half, half)
        return refs[source][field, pl.ds(start, half), window]

    return read


def send_to(block, axis, mask):
    return lax.ppermute(block, axis, [(i, i ^ mask) for i in range(lax.axis_size(axis))])


def gather_far(far):
    for bit in range(lax.axis_size("row").bit_length() - 2, 0, -1):
        far = jnp.concatenate([far, send_to(far, "row", 1 << bit)])
    for bit in range(lax.axis_size("col").bit_length() - 2, 0, -1):
        far = jnp.concatenate([far, send_to(far, "col", 1 << bit)])
    return far


def body(
    query_field,
    key_field,
    value_field,
    query_tan,
    key_tan,
    value_tan,
    pool_near,
    pool_far,
    level_bias,
):
    window = query_field.shape[0]
    width = query_field.shape[2]
    cells = window * window
    strip, half = cells // 2, cells // 4
    near_count = cells // (NEAR_POOL * NEAR_POOL)
    row_count, col_count = lax.axis_size("row"), lax.axis_size("col")
    far_count = row_count * col_count
    flat = lambda field: field.reshape(cells, width)
    fields = tuple(flat(f) for f in (key_field, value_field, key_tan, value_tan))

    row_odd, col_even, col_odd, row_even, far = pack(fields, pool_near, pool_far)
    got_row_odd = swap(row_odd, "row", True)
    got_col_even = swap(col_even, "col", False)
    got_col_odd = swap(col_odd, "col", True)
    got_row_even = swap(row_even, "row", False)

    *state, query, qtan = attend_own(
        level_bias,
        flat(query_field),
        flat(query_tan),
        fields,
        got_row_even,
        [
            (cells, "flag", 0, lambda refs, field, window: refs[field][:, window]),
            (strip, "flag", 0, part(4, 0, strip)),
            (near_count, "level", 0, part(4, strip, near_count)),
        ],
    )
    queries = (query, qtan)
    mate_far = got_row_even[0, strip + near_count : strip + near_count + FIELDS]
    far = jnp.concatenate([far[:FIELDS], mate_far])
    far, stats = lax.optimization_barrier((far, state[2]))
    state = (state[0], state[1], stats)
    far_shape = jax.ShapeDtypeStruct((FIELDS * far_count // 2, width), BF16)
    far = lax.cond(
        lax.axis_index("row") < row_count,
        gather_far,
        lambda block: jnp.zeros(far_shape.shape, far_shape.dtype),
        far,
    )
    got_col_even, got_col_odd, far = lax.optimization_barrier((got_col_even, got_col_odd, far))
    corner = got_row_odd[:, :half].reshape(FIELDS * half, width)
    got_outer_even = swap(jnp.concatenate([corner, far]), "col", False)
    got_outer_odd = swap(got_row_odd[:, half:], "col", True)
    got_inner_even = swap(got_col_even, "row", False)
    got_inner_odd = swap(got_col_odd, "row", False)

    state = attend_more(
        level_bias,
        queries,
        state,
        (got_row_odd, got_col_even, got_col_odd),
        [
            (strip, "flag", 1, part(0, 0, strip)),
            (strip, "flag", 0, part(1, 0, strip)),
            (strip, "flag", 2, part(2, 0, strip)),
        ],
        "strips",
    )
    state = attend_more(
        level_bias,
        queries,
        state,
        (got_inner_even, got_inner_odd, got_col_even, row_even),
        [
            (half, "flag", 0, toward_mate(0, half)),
            (half, "flag", 2, toward_mate(1, half)),
            (near_count, "level", 0, part(0, strip, near_count)),
            (near_count, "level", 0, part(2, strip, near_count)),
            (near_count, "level", 0, part(3, strip, near_count)),
        ],
        "inner",
    )
    mixed, mixed_tan = attend_last(
        level_bias,
        queries,
        state,
        (got_outer_even, got_outer_odd, far),
        [
            (half, "flag", 1, flat_part(0, half, 0, half)),
            (half, "flag", 3, part(1, 0, half)),
            (far_count, "level", 1, part(3, 0, far_count)),
        ],
        far_count,
        ((0, FIELDS * half), (2, 0)),
    )
    shape = (window, window, width)
    return (mixed.reshape(shape), mixed_tan.reshape(shape))


def solution(mesh):
    field = P("row", "col", None)
    return jax.shard_map(
        body,
        mesh=mesh,
        in_specs=(field,) * 6 + (P(),) * 3,
        out_specs=(field, field),
        check_vma=False,
    )
```

```python
import functools

import jax
import jax.numpy as jnp
from jax import lax
from jax.experimental import pallas as pl
from jax.experimental.pallas import tpu as pltpu
from jax.sharding import PartitionSpec as P

HEADS = 16
RIM = 8
NEAR_POOL = 4
LOG2E = 1.4426950408889634
OFF = -1e30
PACK_BYTES = 60 * 1024 * 1024
VMEM_BYTES = 28 * 1024 * 1024
LANES = 128
FIELDS = 4
BF16 = jnp.bfloat16
F32 = jnp.float32


def vmem_spec():
    return pl.BlockSpec(memory_space=pltpu.VMEM)


def smem_spec():
    return pl.BlockSpec(memory_space=pltpu.SMEM)


def hbm_spec():
    return pl.BlockSpec(memory_space=pltpu.HBM)


def any_spec():
    return pl.BlockSpec(memory_space=pl.ANY)


def against(left, right):
    return lax.dot_general(left, right, (((1,), (1,)), ((), ())), preferred_element_type=F32)


def chunk_copies(source, target, sems, first, parts):
    rows = source.shape[0]
    step = -(-rows // parts)
    if len(source.shape) == 2:
        step = -(-step // 16) * 16
    copies = []
    for number, begin in enumerate(range(0, rows, step)):
        at = pl.ds(begin, min(step, rows - begin))
        copies.append(pltpu.make_async_copy(source.at[at], target.at[at], sems.at[first + number]))
    return copies


def split3(weights):
    high = weights.astype(BF16)
    rest = weights - high.astype(F32)
    mid = rest.astype(BF16)
    low = (rest - mid.astype(F32)).astype(BF16)
    return jnp.concatenate([high, mid, low], axis=0)


def pool_weights(pool_near, pool_far, cells):
    window = 2 * RIM
    near_side = window // NEAR_POOL
    near_count = near_side * near_side
    lane = lax.broadcasted_iota(jnp.int32, (near_count, cells), 1)
    line = lax.broadcasted_iota(jnp.int32, (near_count, cells), 0)
    row, col = lane // window, lane % window
    near = jnp.zeros((near_count, cells), F32)
    for p in range(NEAR_POOL):
        for q in range(NEAR_POOL):
            hit = (row % NEAR_POOL == p) & (col % NEAR_POOL == q)
            near = jnp.where(hit, pool_near[p, q], near)
    block = (row // NEAR_POOL) * near_side + col // NEAR_POOL
    near = split3(jnp.where(line == block, near, 0.0))
    spread = (line == col).astype(F32).astype(BF16)
    far = jnp.dot(split3(pool_far), spread, preferred_element_type=F32)
    far_line = lax.broadcasted_iota(jnp.int32, far.shape, 0) % window
    far_lane = lax.broadcasted_iota(jnp.int32, far.shape, 1) // window
    far = jnp.where(far_line == far_lane, far, 0.0)
    rows = [
        jnp.sum(far[i * window : (i + 1) * window], axis=0, keepdims=True) for i in range(3)
    ]
    rows.append(jnp.zeros((near_count - 3, cells), F32))
    return jnp.concatenate([near, jnp.concatenate(rows, axis=0).astype(BF16)], axis=0)


def halves(block, width):
    cells = block.shape[0]
    wide = block.astype(F32).reshape(cells // (2 * RIM), 2, RIM, width)
    left = wide[:, 0].reshape(cells // 2, width).astype(BF16)
    right = wide[:, 1].reshape(cells // 2, width).astype(BF16)
    return left, right


def pack_kernel(pool_near, pool_far, *refs):
    sources, outs = refs[:FIELDS], refs[FIELDS : FIELDS + 5]
    held = refs[FIELDS + 5]
    kept, sems, out_sems = refs[FIELDS + 6 : -2], refs[-2], refs[-1]
    cells, width = sources[0].shape
    strip, half = cells // 2, cells // 4
    near_count = cells // (NEAR_POOL * NEAR_POOL)
    row_is_even = lax.axis_index("row") % 2 == 0
    col_is_even = lax.axis_index("col") % 2 == 0
    copies = []
    for index, source in enumerate(sources):
        copies += chunk_copies(source, held.at[index], sems, 2 * index, 2)
    for copy in copies:
        copy.start()
    weights = pool_weights(pool_near, pool_far[...], cells)
    far_rows = []
    sent = []
    for index in range(FIELDS):
        copies[2 * index].wait()
        copies[2 * index + 1].wait()
        block = held[index]
        left, right = halves(block, width)
        even = jnp.where(col_is_even, right, left)
        odd = jnp.where(col_is_even, left, right)
        outer = lambda side: jnp.where(row_is_even, side[:half], side[half:])
        pooled = jnp.dot(weights, block, preferred_element_type=F32)
        near = pooled[:near_count] + (
            pooled[near_count : 2 * near_count] + pooled[2 * near_count : 3 * near_count]
        )
        near = near.astype(BF16)
        far = pooled[3 * near_count :]
        far_rows.append(far[0:1] + (far[1:2] + far[2:3]))
        kept[0][index, :half] = outer(even)
        kept[0][index, half:] = outer(odd)
        kept[1][index, :strip] = even
        kept[1][index, strip:] = near
        kept[2][index] = odd
        kept[3][index, :strip] = jnp.where(row_is_even, block[strip:], block[:strip])
        kept[3][index, strip : strip + near_count] = near
        for number in range(3):
            copy = pltpu.make_async_copy(
                kept[number].at[index], outs[number].at[index], out_sems.at[3 * index + number]
            )
            copy.start()
            sent.append(copy)
    far_rows.append(jnp.zeros((16 - FIELDS, width), F32))
    kept[4][...] = jnp.concatenate(far_rows, axis=0).astype(BF16)
    for index in range(FIELDS):
        kept[3][index, strip + near_count :] = kept[4][...]
    for number in (3, 4):
        copy = pltpu.make_async_copy(
            kept[number], outs[number], out_sems.at[3 * FIELDS + number - 3]
        )
        copy.start()
        sent.append(copy)
    for copy in sent:
        copy.wait()


def pack(fields, pool_near, pool_far):
    cells, width = fields[0].shape
    strip = cells // 2
    near_count = cells // (NEAR_POOL * NEAR_POOL)
    shapes = [
        (FIELDS, strip, width),
        (FIELDS, strip + near_count, width),
        (FIELDS, strip, width),
        (FIELDS, strip + near_count + 16, width),
        (16, width),
    ]
    return pl.pallas_call(
        pack_kernel,
        out_shape=tuple(jax.ShapeDtypeStruct(s, BF16) for s in shapes),
        in_specs=[smem_spec(), vmem_spec()] + [hbm_spec()] * FIELDS,
        out_specs=[hbm_spec()] * len(shapes),
        scratch_shapes=[pltpu.VMEM((FIELDS, cells, width), BF16)]
        + [pltpu.VMEM(s, BF16) for s in shapes]
        + [pltpu.SemaphoreType.DMA((2 * FIELDS,)), pltpu.SemaphoreType.DMA((3 * FIELDS + 2,))],
        compiler_params=pltpu.CompilerParams(vmem_limit_bytes=PACK_BYTES),
        name="pack",
    )(pool_near, pool_far, *fields)


TOGETHER = 2
GROUPS = HEADS // TOGETHER


def group_copy(source, target, sem, group):
    at = pl.ds(group * TOGETHER, TOGETHER)
    return pltpu.make_async_copy(source.at[at], target.at[at], sem.at[group])


def masked_start(head, head_dim, width):
    return min(head * head_dim // LANES, (width - 2 * LANES) // LANES) * LANES


def turn_queries(raw, turned, masked):
    width = raw.shape[1]
    head_dim = width // HEADS
    span = 2 * LANES
    line = lax.broadcasted_iota(jnp.int32, (LANES, LANES), 0)
    lane = lax.broadcasted_iota(jnp.int32, (LANES, LANES), 1)
    unit = (line == lane).astype(F32).astype(BF16)
    for at in range(0, width, LANES):
        turned[at : at + LANES] = against(unit, raw[:, at : at + LANES]).astype(BF16)
    channel = lax.broadcasted_iota(jnp.int32, (span, raw.shape[0]), 0)
    for head in range(HEADS):
        start = masked_start(head, head_dim, width)
        low = head * head_dim - start
        keep = ((channel >= low) & (channel < low + head_dim)).astype(F32).astype(BF16)
        masked[head] = turned[start : start + span] * keep


def device_flags():
    row, col = lax.axis_index("row"), lax.axis_index("col")
    row_edge = (row == 0) | (row == lax.axis_size("row") - 1)
    col_edge = (col == 0) | (col == lax.axis_size("col") - 1)
    off = lambda edge: jnp.where(edge, F32(OFF), F32(0.0))
    return (F32(0.0), off(row_edge), off(col_edge), off(row_edge | col_edge))


def head_products(head, segments, refs, queries, width):
    head_dim = width // HEADS
    start = head * head_dim // LANES * LANES
    low = head * head_dim - start
    one_tile = low + head_dim <= LANES
    span = LANES if one_tile else 2 * LANES
    window = slice(start, start + span)
    at = start - masked_start(head, head_dim, width)
    rows_of = lambda field: jnp.concatenate(
        [reader(refs, field, window) for _, _, _, reader in segments], axis=0
    )
    key, value, key_tan, value_tan = (rows_of(field) for field in range(FIELDS))
    query, query_tan = (ref[head, at : at + span] for ref in queries)
    scores = jnp.dot(key, query, preferred_element_type=F32)
    if one_tile:
        slopes = jnp.dot(
            jnp.concatenate([key, key_tan], axis=1),
            jnp.concatenate([query_tan, query], axis=0),
            preferred_element_type=F32,
        )
    else:
        slopes = jnp.dot(key, query_tan, preferred_element_type=F32)
        slopes = slopes + jnp.dot(key_tan, query, preferred_element_type=F32)
    line = lax.broadcasted_iota(jnp.int32, (head_dim + 8, span), 0)
    lane = lax.broadcasted_iota(jnp.int32, (head_dim + 8, span), 1)
    pick = ((lane == line + low) & (line < head_dim)).astype(F32).astype(BF16)
    ones_line = lax.broadcasted_iota(jnp.int32, (8, value.shape[0]), 0)
    turned = jnp.concatenate(
        [
            against(pick, value)[:head_dim],
            (ones_line == 0).astype(F32),
            against(pick, value_tan),
        ],
        axis=0,
    )
    return scores, slopes, turned.astype(BF16)


def head_result(head, segments, level_bias, flags, products, olds, width):
    scores, slopes, turned = products
    head_dim = width // HEADS
    pad_dim = head_dim + 8
    scale = head_dim**-0.5
    bias = []
    top = None
    at = 0
    for rows, kind, number, _ in segments:
        amount = flags[number] if kind == "flag" else level_bias[number, head] * LOG2E
        bias.append(amount)
        part = jnp.max(scores[at : at + rows], axis=0, keepdims=True) * (scale * LOG2E) + amount
        top = part if top is None else jnp.maximum(top, part)
        at += rows
    for old in olds:
        top = jnp.maximum(top, old[2][head, 0:1])
    weights_low, product_low = [], []
    at = 0
    for (rows, _, _, _), amount in zip(segments, bias):
        weights = jnp.exp2(scores[at : at + rows] * (scale * LOG2E) + (amount - top))
        weights_low.append(weights.astype(BF16))
        product_low.append((weights * slopes[at : at + rows]).astype(BF16))
        at += rows
    both = jnp.dot(turned, jnp.concatenate(weights_low, axis=0), preferred_element_type=F32)
    extra = jnp.dot(
        turned[:pad_dim], jnp.concatenate(product_low, axis=0), preferred_element_type=F32
    )
    mix = both[:head_dim]
    total = both[head_dim : head_dim + 1]
    row_total = extra[head_dim : head_dim + 1] * scale
    extra = extra[:head_dim] * scale + both[pad_dim : pad_dim + head_dim]
    for old in olds:
        fade = jnp.exp2(old[2][head, 0:1] - top)
        total = total + fade * old[2][head, 1:2]
        row_total = row_total + fade * old[2][head, 2:3]
        mix = mix + fade * old[0][head]
        extra = extra + fade * old[1][head]
    return top, total, row_total, mix, extra


def attend_heads(segments, refs, queries, level_bias, width, olds, keep):
    flags = device_flags()
    stages = [range(first, first + TOGETHER) for first in range(0, HEADS, TOGETHER)]
    make = lambda heads: [head_products(head, segments, refs, queries, width) for head in heads]
    ready = make(stages[0])
    for number, heads in enumerate(stages):
        coming = make(stages[number + 1]) if number + 1 < len(stages) else None
        for head, products in zip(heads, ready):
            keep(head, *head_result(head, segments, level_bias, flags, products, olds, width))
        ready = coming


def keeper(state):
    def keep(head, top, total, row_total, mix, extra):
        state[0][head] = mix
        state[1][head] = extra
        state[2][head, 0:1] = top
        state[2][head, 1:2] = total
        state[2][head, 2:3] = row_total

    return keep


def own_kernel(segments, level_bias, *refs):
    query_in, qtan_in = refs[:2]
    sources = refs[2 : 3 + FIELDS]
    outs = refs[3 + FIELDS : 8 + FIELDS]
    raw, turned, masked = refs[8 + FIELDS : 10 + FIELDS], refs[10 + FIELDS], refs[11 + FIELDS : 13 + FIELDS]
    held = refs[13 + FIELDS : 14 + 2 * FIELDS]
    state = refs[14 + 2 * FIELDS : 17 + 2 * FIELDS]
    sems, out_sems = refs[17 + 2 * FIELDS :]
    width = query_in.shape[1]
    copies = []
    for number, (source, target) in enumerate(
        list(zip((query_in, qtan_in), raw)) + list(zip(sources, held))
    ):
        copies += chunk_copies(source, target, sems, FIELDS * number, FIELDS)
    for copy in copies:
        copy.start()
    state[2][...] = jnp.zeros(state[2].shape, F32)
    sent = []
    for number in range(2):
        for copy in copies[FIELDS * number : FIELDS * (number + 1)]:
            copy.wait()
        turn_queries(raw[number], turned, masked[number])
        for group in range(GROUPS):
            sent.append(
                group_copy(masked[number], outs[3 + number], out_sems.at[3 + number], group)
            )
            sent[-1].start()
    for copy in copies[2 * FIELDS :]:
        copy.wait()

    attend_heads(segments, held, masked, level_bias, width, [], keeper(state))
    for number in range(3):
        for group in range(GROUPS):
            group_copy(state[number], outs[number], out_sems.at[number], group).start()
    for number in range(3):
        for group in range(GROUPS):
            group_copy(state[number], outs[number], out_sems.at[number], group).wait()
    for copy in sent:
        copy.wait()


def state_shapes(token_count, width):
    wide = (HEADS, width // HEADS, token_count)
    return (wide, wide, (HEADS, 8, token_count))


def own_cost(token_count, width, key_count):
    return pl.CostEstimate(
        flops=token_count * key_count * HEADS,
        bytes_accessed=token_count * width,
        transcendentals=0,
    )


def attend_own(level_bias, query, qtan, fields, mate, segments):
    token_count, width = query.shape
    states = state_shapes(token_count, width)
    masked = (HEADS, 2 * LANES, token_count)
    operands = (query, qtan, *fields, mate)
    return pl.pallas_call(
        functools.partial(own_kernel, segments),
        out_shape=tuple(jax.ShapeDtypeStruct(s, F32) for s in states)
        + (jax.ShapeDtypeStruct(masked, BF16),) * 2,
        in_specs=[smem_spec()] + [hbm_spec()] * len(operands),
        out_specs=[hbm_spec()] * 5,
        scratch_shapes=[pltpu.VMEM(query.shape, BF16)] * 2
        + [pltpu.VMEM((width, token_count), BF16)]
        + [pltpu.VMEM(masked, BF16)] * 2
        + [pltpu.VMEM(source.shape, BF16) for source in operands[2:]]
        + [pltpu.VMEM(s, F32) for s in states]
        + [
            pltpu.SemaphoreType.DMA((FIELDS * len(operands),)),
            pltpu.SemaphoreType.DMA((5, GROUPS)),
        ],
        compiler_params=pltpu.CompilerParams(vmem_limit_bytes=PACK_BYTES),
        cost_estimate=own_cost(token_count, width, sum(s[0] for s in segments)),
        name="own",
    )(level_bias, *operands)


def more_kernel(segments, old_count, count, level_bias, *refs):
    queries, refs = refs[:2], refs[2:]
    olds = [refs[3 * i : 3 * i + 3] for i in range(old_count)]
    refs = refs[3 * old_count :]
    sources, state = refs[:count], refs[count:]
    width = state[0].shape[0] * state[0].shape[1]
    state[2][...] = jnp.zeros(state[2].shape, F32)
    attend_heads(segments, sources, queries, level_bias, width, olds, keeper(state))


def attend_more(level_bias, queries, olds, sources, segments, name):
    token_count = queries[0].shape[2]
    width = sources[0].shape[-1]
    operands = (*queries, *[array for old in olds for array in old], *sources)
    return pl.pallas_call(
        functools.partial(more_kernel, segments, len(olds), len(sources)),
        out_shape=tuple(jax.ShapeDtypeStruct(s, F32) for s in state_shapes(token_count, width)),
        in_specs=[smem_spec()] + [vmem_spec()] * len(operands),
        out_specs=[vmem_spec()] * 3,
        compiler_params=pltpu.CompilerParams(vmem_limit_bytes=VMEM_BYTES),
        cost_estimate=own_cost(token_count, width, sum(s[0] for s in segments)),
        name=name,
    )(level_bias, *operands)


def last_kernel(segments, old_count, count, far_count, far_blocks, level_bias, *refs):
    queries, refs = refs[:2], refs[2:]
    olds = [refs[3 * i : 3 * i + 3] for i in range(old_count)]
    refs = refs[3 * old_count :]
    sources, outs = refs[:count], refs[count : count + 2]
    far_keys, mix_acc, tan_acc, turned, sems = refs[count + 2 :]
    width, token_count = outs[0].shape[1], outs[0].shape[0]
    line = lax.broadcasted_iota(jnp.int32, (far_count, FIELDS * far_count), 0)
    lane = lax.broadcasted_iota(jnp.int32, (far_count, FIELDS * far_count), 1)
    far_rows = jnp.concatenate([sources[i][begin:] for i, begin in far_blocks], axis=0)
    for index in range(FIELDS):
        select = (lane == line * FIELDS + index).astype(F32).astype(BF16)
        far_keys[index] = jnp.dot(select, far_rows, preferred_element_type=F32).astype(BF16)
    sources = sources + (far_keys,)

    def keep(head, top, total, row_total, mix, extra):
        inverse = 1.0 / total
        mix = mix * inverse
        mix_acc[head] = mix
        tan_acc[head] = extra * inverse - (row_total * inverse) * mix

    attend_heads(segments, sources, queries, level_bias, width, olds, keep)
    line = lax.broadcasted_iota(jnp.int32, (token_count, token_count), 0)
    lane = lax.broadcasted_iota(jnp.int32, (token_count, token_count), 1)
    unit = (line == lane).astype(F32).astype(BF16)
    sent = []
    for number, acc in enumerate((mix_acc, tan_acc)):
        flat = acc[...].reshape(width, token_count).astype(BF16)
        turned[number] = against(unit, flat).astype(BF16)
        more = chunk_copies(turned.at[number], outs[number], sems, number * FIELDS, FIELDS)
        for copy in more:
            copy.start()
        sent += more
    for copy in sent:
        copy.wait()


def attend_last(level_bias, queries, olds, sources, segments, far_count, far_blocks):
    token_count = queries[0].shape[2]
    width = sources[0].shape[-1]
    states = state_shapes(token_count, width)
    operands = (*queries, *[array for old in olds for array in old], *sources)
    return pl.pallas_call(
        functools.partial(
            last_kernel, segments, len(olds), len(sources), far_count, far_blocks
        ),
        out_shape=(jax.ShapeDtypeStruct((token_count, width), BF16),) * 2,
        in_specs=[smem_spec()] + [vmem_spec()] * len(operands),
        out_specs=[hbm_spec()] * 2,
        scratch_shapes=[
            pltpu.VMEM((FIELDS, far_count, width), BF16),
            pltpu.VMEM(states[0], F32),
            pltpu.VMEM(states[1], F32),
            pltpu.VMEM((2, token_count, width), BF16),
            pltpu.SemaphoreType.DMA((2 * FIELDS,)),
        ],
        compiler_params=pltpu.CompilerParams(vmem_limit_bytes=VMEM_BYTES),
        cost_estimate=own_cost(token_count, width, sum(s[0] for s in segments)),
        name="outer",
    )(level_bias, *operands)


def swap(block, axis, odd):
    count = lax.axis_size(axis)
    route = []
    for low in range(1 if odd else 0, count - 1, 2):
        route += [(low, low + 1), (low + 1, low)]
    return lax.ppermute(block, axis, route)


def part(source, begin, rows):
    return lambda refs, field, window: refs[source][field, begin : begin + rows, window]


def flat_part(source, stride, begin, rows):
    def read(refs, field, window):
        at = field * stride + begin
        return refs[source][at : at + rows, window]

    return read


def toward_mate(source, half):
    def read(refs, field, window):
        start = pl.multiple_of((lax.axis_index("row") % 2) * half, half)
        return refs[source][field, pl.ds(start, half), window]

    return read


def send_to(block, axis, mask):
    return lax.ppermute(block, axis, [(i, i ^ mask) for i in range(lax.axis_size(axis))])


def gather_far(far):
    for bit in range(lax.axis_size("row").bit_length() - 2, 0, -1):
        far = jnp.concatenate([far, send_to(far, "row", 1 << bit)])
    for bit in range(lax.axis_size("col").bit_length() - 2, 0, -1):
        far = jnp.concatenate([far, send_to(far, "col", 1 << bit)])
    return far


def body(
    query_field,
    key_field,
    value_field,
    query_tan,
    key_tan,
    value_tan,
    pool_near,
    pool_far,
    level_bias,
):
    window = query_field.shape[0]
    width = query_field.shape[2]
    cells = window * window
    strip, half = cells // 2, cells // 4
    near_count = cells // (NEAR_POOL * NEAR_POOL)
    row_count, col_count = lax.axis_size("row"), lax.axis_size("col")
    far_count = row_count * col_count
    flat = lambda field: field.reshape(cells, width)
    fields = tuple(flat(f) for f in (key_field, value_field, key_tan, value_tan))

    row_odd, col_even, col_odd, row_even, far = pack(fields, pool_near, pool_far)
    got_row_odd = swap(row_odd, "row", True)
    got_col_even = swap(col_even, "col", False)
    got_col_odd = swap(col_odd, "col", True)
    got_row_even = swap(row_even, "row", False)

    *own_state, query, qtan = attend_own(
        level_bias,
        flat(query_field),
        flat(query_tan),
        fields,
        got_row_even,
        [
            (cells, "flag", 0, lambda refs, field, window: refs[field][:, window]),
            (strip, "flag", 0, part(4, 0, strip)),
            (near_count, "level", 0, part(4, strip, near_count)),
        ],
    )
    queries = (query, qtan)
    mate_far = got_row_even[0, strip + near_count : strip + near_count + FIELDS]
    far = jnp.concatenate([far[:FIELDS], mate_far])
    far, stats = lax.optimization_barrier((far, own_state[2]))
    own_state = (own_state[0], own_state[1], stats)
    far = lax.cond(
        lax.axis_index("row") < row_count,
        gather_far,
        lambda block: jnp.zeros((FIELDS * far_count // 2, width), BF16),
        far,
    )
    got_row_odd, far = lax.optimization_barrier((got_row_odd, far))
    to_even = jnp.concatenate([got_row_odd[:, :half].reshape(FIELDS * half, width), far])
    to_odd = got_row_odd[:, half:]
    got_col_even, got_col_odd, to_even, to_odd = lax.optimization_barrier(
        (got_col_even, got_col_odd, to_even, to_odd)
    )
    got_outer_even = swap(to_even, "col", False)
    got_outer_odd = swap(to_odd, "col", True)
    got_inner_even = swap(got_col_even, "row", False)
    got_inner_odd = swap(got_col_odd, "row", False)

    state = attend_more(
        level_bias,
        queries,
        [],
        (got_row_odd, got_col_even, got_col_odd),
        [
            (strip, "flag", 0, part(1, 0, strip)),
            (strip, "flag", 1, part(0, 0, strip)),
            (strip, "flag", 2, part(2, 0, strip)),
        ],
        "strips",
    )
    state = attend_more(
        level_bias,
        queries,
        [state],
        (got_inner_even, got_inner_odd, got_col_even, row_even),
        [
            (half, "flag", 0, toward_mate(0, half)),
            (half, "flag", 2, toward_mate(1, half)),
            (near_count, "level", 0, part(0, strip, near_count)),
            (near_count, "level", 0, part(2, strip, near_count)),
            (near_count, "level", 0, part(3, strip, near_count)),
        ],
        "inner",
    )
    mixed, mixed_tan = attend_last(
        level_bias,
        queries,
        [state, own_state],
        (got_outer_even, got_outer_odd, far),
        [
            (half, "flag", 1, flat_part(0, half, 0, half)),
            (half, "flag", 3, part(1, 0, half)),
            (far_count, "level", 1, part(3, 0, far_count)),
        ],
        far_count,
        ((0, FIELDS * half), (2, 0)),
    )
    shape = (window, window, width)
    return (mixed.reshape(shape), mixed_tan.reshape(shape))


def solution(mesh):
    field = P("row", "col", None)
    return jax.shard_map(
        body,
        mesh=mesh,
        in_specs=(field,) * 6 + (P(),) * 3,
        out_specs=(field, field),
        check_vma=False,
    )
```

```python
import functools

import jax
import jax.numpy as jnp
from jax import lax
from jax.experimental import pallas as pl
from jax.experimental.pallas import tpu as pltpu
from jax.sharding import PartitionSpec as P

HEADS = 16
RIM = 8
NEAR_POOL = 4
LOG2E = 1.4426950408889634
OFF = -1e30
PACK_BYTES = 60 * 1024 * 1024
VMEM_BYTES = 28 * 1024 * 1024
LANES = 128
FIELDS = 4
BF16 = jnp.bfloat16
F32 = jnp.float32


def vmem_spec():
    return pl.BlockSpec(memory_space=pltpu.VMEM)


def smem_spec():
    return pl.BlockSpec(memory_space=pltpu.SMEM)


def hbm_spec():
    return pl.BlockSpec(memory_space=pltpu.HBM)


def any_spec():
    return pl.BlockSpec(memory_space=pl.ANY)


def against(left, right):
    return lax.dot_general(left, right, (((1,), (1,)), ((), ())), preferred_element_type=F32)


def chunk_copies(source, target, sems, first, parts):
    rows = source.shape[0]
    step = -(-rows // parts)
    if len(source.shape) == 2:
        step = -(-step // 16) * 16
    copies = []
    for number, begin in enumerate(range(0, rows, step)):
        at = pl.ds(begin, min(step, rows - begin))
        copies.append(pltpu.make_async_copy(source.at[at], target.at[at], sems.at[first + number]))
    return copies


def split3(weights):
    high = weights.astype(BF16)
    rest = weights - high.astype(F32)
    mid = rest.astype(BF16)
    low = (rest - mid.astype(F32)).astype(BF16)
    return jnp.concatenate([high, mid, low], axis=0)


def pool_weights(pool_near, pool_far, cells):
    window = 2 * RIM
    near_side = window // NEAR_POOL
    near_count = near_side * near_side
    lane = lax.broadcasted_iota(jnp.int32, (near_count, cells), 1)
    line = lax.broadcasted_iota(jnp.int32, (near_count, cells), 0)
    row, col = lane // window, lane % window
    near = jnp.zeros((near_count, cells), F32)
    for p in range(NEAR_POOL):
        for q in range(NEAR_POOL):
            hit = (row % NEAR_POOL == p) & (col % NEAR_POOL == q)
            near = jnp.where(hit, pool_near[p, q], near)
    block = (row // NEAR_POOL) * near_side + col // NEAR_POOL
    near = split3(jnp.where(line == block, near, 0.0))
    spread = (line == col).astype(F32).astype(BF16)
    far = jnp.dot(split3(pool_far), spread, preferred_element_type=F32)
    far_line = lax.broadcasted_iota(jnp.int32, far.shape, 0) % window
    far_lane = lax.broadcasted_iota(jnp.int32, far.shape, 1) // window
    far = jnp.where(far_line == far_lane, far, 0.0)
    rows = [
        jnp.sum(far[i * window : (i + 1) * window], axis=0, keepdims=True) for i in range(3)
    ]
    rows.append(jnp.zeros((near_count - 3, cells), F32))
    return jnp.concatenate([near, jnp.concatenate(rows, axis=0).astype(BF16)], axis=0)


def halves(block, width):
    cells = block.shape[0]
    wide = block.astype(F32).reshape(cells // (2 * RIM), 2, RIM, width)
    left = wide[:, 0].reshape(cells // 2, width).astype(BF16)
    right = wide[:, 1].reshape(cells // 2, width).astype(BF16)
    return left, right


def pack_kernel(pool_near, pool_far, *refs):
    sources, outs = refs[:FIELDS], refs[FIELDS : FIELDS + 6]
    held = refs[FIELDS + 6]
    kept, sems, out_sems = refs[FIELDS + 7 : -2], refs[-2], refs[-1]
    cells, width = sources[0].shape
    strip, half = cells // 2, cells // 4
    near_count = cells // (NEAR_POOL * NEAR_POOL)
    row_is_even = lax.axis_index("row") % 2 == 0
    col_is_even = lax.axis_index("col") % 2 == 0
    copies = []
    for index, source in enumerate(sources):
        copies += chunk_copies(source, held.at[index], sems, 2 * index, 2)
    for copy in copies:
        copy.start()
    weights = pool_weights(pool_near, pool_far[...], cells)
    far_rows = []
    sent = []
    for index in range(FIELDS):
        copies[2 * index].wait()
        copies[2 * index + 1].wait()
        block = held[index]
        left, right = halves(block, width)
        even = jnp.where(col_is_even, right, left)
        odd = jnp.where(col_is_even, left, right)
        outer = lambda side: jnp.where(row_is_even, side[:half], side[half:])
        pooled = jnp.dot(weights, block, preferred_element_type=F32)
        near = pooled[:near_count] + (
            pooled[near_count : 2 * near_count] + pooled[2 * near_count : 3 * near_count]
        )
        near = near.astype(BF16)
        far = pooled[3 * near_count :]
        far_rows.append(far[0:1] + (far[1:2] + far[2:3]))
        kept[0][index] = outer(even)
        kept[1][index] = outer(odd)
        kept[2][index, :strip] = even
        kept[2][index, strip:] = near
        kept[3][index] = odd
        kept[4][index, :strip] = jnp.where(row_is_even, block[strip:], block[:strip])
        kept[4][index, strip : strip + near_count] = near
        for number in range(4):
            copy = pltpu.make_async_copy(
                kept[number].at[index], outs[number].at[index], out_sems.at[4 * index + number]
            )
            copy.start()
            sent.append(copy)
    far_rows.append(jnp.zeros((16 - FIELDS, width), F32))
    kept[5][...] = jnp.concatenate(far_rows, axis=0).astype(BF16)
    for index in range(FIELDS):
        kept[4][index, strip + near_count :] = kept[5][...]
    for number in (4, 5):
        copy = pltpu.make_async_copy(
            kept[number], outs[number], out_sems.at[4 * FIELDS + number - 4]
        )
        copy.start()
        sent.append(copy)
    for copy in sent:
        copy.wait()


def pack(fields, pool_near, pool_far):
    cells, width = fields[0].shape
    strip = cells // 2
    near_count = cells // (NEAR_POOL * NEAR_POOL)
    shapes = [
        (FIELDS, strip // 2, width),
        (FIELDS, strip // 2, width),
        (FIELDS, strip + near_count, width),
        (FIELDS, strip, width),
        (FIELDS, strip + near_count + 16, width),
        (16, width),
    ]
    return pl.pallas_call(
        pack_kernel,
        out_shape=tuple(jax.ShapeDtypeStruct(s, BF16) for s in shapes),
        in_specs=[smem_spec(), vmem_spec()] + [hbm_spec()] * FIELDS,
        out_specs=[hbm_spec()] * len(shapes),
        scratch_shapes=[pltpu.VMEM((FIELDS, cells, width), BF16)]
        + [pltpu.VMEM(s, BF16) for s in shapes]
        + [pltpu.SemaphoreType.DMA((2 * FIELDS,)), pltpu.SemaphoreType.DMA((4 * FIELDS + 2,))],
        compiler_params=pltpu.CompilerParams(vmem_limit_bytes=PACK_BYTES),
        name="pack",
    )(pool_near, pool_far, *fields)


TOGETHER = 2
GROUPS = HEADS // TOGETHER


def group_copy(source, target, sem, group):
    at = pl.ds(group * TOGETHER, TOGETHER)
    return pltpu.make_async_copy(source.at[at], target.at[at], sem.at[group])


def masked_start(head, head_dim, width):
    return min(head * head_dim // LANES, (width - 2 * LANES) // LANES) * LANES


def turn_queries(raw, turned, masked):
    width = raw.shape[1]
    head_dim = width // HEADS
    span = 2 * LANES
    line = lax.broadcasted_iota(jnp.int32, (LANES, LANES), 0)
    lane = lax.broadcasted_iota(jnp.int32, (LANES, LANES), 1)
    unit = (line == lane).astype(F32).astype(BF16)
    for at in range(0, width, LANES):
        turned[at : at + LANES] = against(unit, raw[:, at : at + LANES]).astype(BF16)
    channel = lax.broadcasted_iota(jnp.int32, (span, raw.shape[0]), 0)
    for head in range(HEADS):
        start = masked_start(head, head_dim, width)
        low = head * head_dim - start
        keep = ((channel >= low) & (channel < low + head_dim)).astype(F32).astype(BF16)
        masked[head] = turned[start : start + span] * keep


def device_flags():
    row, col = lax.axis_index("row"), lax.axis_index("col")
    row_edge = (row == 0) | (row == lax.axis_size("row") - 1)
    col_edge = (col == 0) | (col == lax.axis_size("col") - 1)
    off = lambda edge: jnp.where(edge, F32(OFF), F32(0.0))
    return (F32(0.0), off(row_edge), off(col_edge), off(row_edge | col_edge))


def head_products(head, segments, refs, queries, width):
    head_dim = width // HEADS
    start = head * head_dim // LANES * LANES
    low = head * head_dim - start
    one_tile = low + head_dim <= LANES
    span = LANES if one_tile else 2 * LANES
    window = slice(start, start + span)
    at = start - masked_start(head, head_dim, width)
    rows_of = lambda field: jnp.concatenate(
        [reader(refs, field, window) for _, _, _, reader in segments], axis=0
    )
    key, value, key_tan, value_tan = (rows_of(field) for field in range(FIELDS))
    query, query_tan = (ref[head, at : at + span] for ref in queries)
    scores = jnp.dot(key, query, preferred_element_type=F32)
    if one_tile:
        slopes = jnp.dot(
            jnp.concatenate([key, key_tan], axis=1),
            jnp.concatenate([query_tan, query], axis=0),
            preferred_element_type=F32,
        )
    else:
        slopes = jnp.dot(key, query_tan, preferred_element_type=F32)
        slopes = slopes + jnp.dot(key_tan, query, preferred_element_type=F32)
    line = lax.broadcasted_iota(jnp.int32, (head_dim + 8, span), 0)
    lane = lax.broadcasted_iota(jnp.int32, (head_dim + 8, span), 1)
    pick = ((lane == line + low) & (line < head_dim)).astype(F32).astype(BF16)
    ones_line = lax.broadcasted_iota(jnp.int32, (8, value.shape[0]), 0)
    turned = jnp.concatenate(
        [
            against(pick, value)[:head_dim],
            (ones_line == 0).astype(F32),
            against(pick, value_tan),
        ],
        axis=0,
    )
    return scores, slopes, turned.astype(BF16)


def head_result(head, segments, level_bias, flags, products, olds, width):
    scores, slopes, turned = products
    head_dim = width // HEADS
    pad_dim = head_dim + 8
    scale = head_dim**-0.5
    bias = []
    top = None
    at = 0
    for rows, kind, number, _ in segments:
        amount = flags[number] if kind == "flag" else level_bias[number, head] * LOG2E
        bias.append(amount)
        part = jnp.max(scores[at : at + rows], axis=0, keepdims=True) * (scale * LOG2E) + amount
        top = part if top is None else jnp.maximum(top, part)
        at += rows
    for old in olds:
        top = jnp.maximum(top, old[2][head, 0:1])
    weights_low, product_low = [], []
    at = 0
    for (rows, _, _, _), amount in zip(segments, bias):
        weights = jnp.exp2(scores[at : at + rows] * (scale * LOG2E) + (amount - top))
        weights_low.append(weights.astype(BF16))
        product_low.append((weights * slopes[at : at + rows]).astype(BF16))
        at += rows
    both = jnp.dot(turned, jnp.concatenate(weights_low, axis=0), preferred_element_type=F32)
    extra = jnp.dot(
        turned[:pad_dim], jnp.concatenate(product_low, axis=0), preferred_element_type=F32
    )
    mix = both[:head_dim]
    total = both[head_dim : head_dim + 1]
    row_total = extra[head_dim : head_dim + 1] * scale
    extra = extra[:head_dim] * scale + both[pad_dim : pad_dim + head_dim]
    for old in olds:
        fade = jnp.exp2(old[2][head, 0:1] - top)
        total = total + fade * old[2][head, 1:2]
        row_total = row_total + fade * old[2][head, 2:3]
        mix = mix + fade * old[0][head]
        extra = extra + fade * old[1][head]
    return top, total, row_total, mix, extra


def attend_heads(segments, refs, queries, level_bias, width, olds, keep):
    flags = device_flags()
    stages = [range(first, first + TOGETHER) for first in range(0, HEADS, TOGETHER)]
    make = lambda heads: [head_products(head, segments, refs, queries, width) for head in heads]
    ready = make(stages[0])
    for number, heads in enumerate(stages):
        coming = make(stages[number + 1]) if number + 1 < len(stages) else None
        for head, products in zip(heads, ready):
            keep(head, *head_result(head, segments, level_bias, flags, products, olds, width))
        ready = coming


def keeper(state):
    def keep(head, top, total, row_total, mix, extra):
        state[0][head] = mix
        state[1][head] = extra
        state[2][head, 0:1] = top
        state[2][head, 1:2] = total
        state[2][head, 2:3] = row_total

    return keep


def own_kernel(segments, level_bias, *refs):
    query_in, qtan_in = refs[:2]
    sources = refs[2 : 3 + FIELDS]
    outs = refs[3 + FIELDS : 8 + FIELDS]
    raw, turned, masked = refs[8 + FIELDS : 10 + FIELDS], refs[10 + FIELDS], refs[11 + FIELDS : 13 + FIELDS]
    held = refs[13 + FIELDS : 14 + 2 * FIELDS]
    state = refs[14 + 2 * FIELDS : 17 + 2 * FIELDS]
    sems, out_sems = refs[17 + 2 * FIELDS :]
    width = query_in.shape[1]
    copies = []
    for number, (source, target) in enumerate(
        list(zip((query_in, qtan_in), raw)) + list(zip(sources, held))
    ):
        copies += chunk_copies(source, target, sems, FIELDS * number, FIELDS)
    for copy in copies:
        copy.start()
    state[2][...] = jnp.zeros(state[2].shape, F32)
    sent = []
    for number in range(2):
        for copy in copies[FIELDS * number : FIELDS * (number + 1)]:
            copy.wait()
        turn_queries(raw[number], turned, masked[number])
        for group in range(GROUPS):
            sent.append(
                group_copy(masked[number], outs[3 + number], out_sems.at[3 + number], group)
            )
            sent[-1].start()
    for copy in copies[2 * FIELDS :]:
        copy.wait()

    attend_heads(segments, held, masked, level_bias, width, [], keeper(state))
    for number in range(3):
        for group in range(GROUPS):
            group_copy(state[number], outs[number], out_sems.at[number], group).start()
    for number in range(3):
        for group in range(GROUPS):
            group_copy(state[number], outs[number], out_sems.at[number], group).wait()
    for copy in sent:
        copy.wait()


def state_shapes(token_count, width):
    wide = (HEADS, width // HEADS, token_count)
    return (wide, wide, (HEADS, 8, token_count))


def own_cost(token_count, width, key_count):
    return pl.CostEstimate(
        flops=token_count * key_count * HEADS,
        bytes_accessed=token_count * width,
        transcendentals=0,
    )


def attend_own(level_bias, query, qtan, fields, mate, segments):
    token_count, width = query.shape
    states = state_shapes(token_count, width)
    masked = (HEADS, 2 * LANES, token_count)
    operands = (query, qtan, *fields, mate)
    return pl.pallas_call(
        functools.partial(own_kernel, segments),
        out_shape=tuple(jax.ShapeDtypeStruct(s, F32) for s in states)
        + (jax.ShapeDtypeStruct(masked, BF16),) * 2,
        in_specs=[smem_spec()] + [hbm_spec()] * len(operands),
        out_specs=[hbm_spec()] * 5,
        scratch_shapes=[pltpu.VMEM(query.shape, BF16)] * 2
        + [pltpu.VMEM((width, token_count), BF16)]
        + [pltpu.VMEM(masked, BF16)] * 2
        + [pltpu.VMEM(source.shape, BF16) for source in operands[2:]]
        + [pltpu.VMEM(s, F32) for s in states]
        + [
            pltpu.SemaphoreType.DMA((FIELDS * len(operands),)),
            pltpu.SemaphoreType.DMA((5, GROUPS)),
        ],
        compiler_params=pltpu.CompilerParams(vmem_limit_bytes=PACK_BYTES),
        cost_estimate=own_cost(token_count, width, sum(s[0] for s in segments)),
        name="own",
    )(level_bias, *operands)


def more_kernel(segments, old_count, count, level_bias, *refs):
    queries, refs = refs[:2], refs[2:]
    olds = [refs[3 * i : 3 * i + 3] for i in range(old_count)]
    refs = refs[3 * old_count :]
    sources, state = refs[:count], refs[count:]
    width = state[0].shape[0] * state[0].shape[1]
    state[2][...] = jnp.zeros(state[2].shape, F32)
    attend_heads(segments, sources, queries, level_bias, width, olds, keeper(state))


def attend_more(level_bias, queries, olds, sources, segments, name):
    token_count = queries[0].shape[2]
    width = sources[0].shape[-1]
    operands = (*queries, *[array for old in olds for array in old], *sources)
    return pl.pallas_call(
        functools.partial(more_kernel, segments, len(olds), len(sources)),
        out_shape=tuple(jax.ShapeDtypeStruct(s, F32) for s in state_shapes(token_count, width)),
        in_specs=[smem_spec()] + [vmem_spec()] * len(operands),
        out_specs=[vmem_spec()] * 3,
        compiler_params=pltpu.CompilerParams(vmem_limit_bytes=VMEM_BYTES),
        cost_estimate=own_cost(token_count, width, sum(s[0] for s in segments)),
        name=name,
    )(level_bias, *operands)


def last_kernel(segments, old_count, count, far_count, far_blocks, level_bias, *refs):
    queries, refs = refs[:2], refs[2:]
    olds = [refs[3 * i : 3 * i + 3] for i in range(old_count)]
    refs = refs[3 * old_count :]
    sources, outs = refs[:count], refs[count : count + 2]
    far_keys, mix_acc, tan_acc, turned, sems = refs[count + 2 :]
    width, token_count = outs[0].shape[1], outs[0].shape[0]
    line = lax.broadcasted_iota(jnp.int32, (far_count, FIELDS * far_count), 0)
    lane = lax.broadcasted_iota(jnp.int32, (far_count, FIELDS * far_count), 1)
    far_rows = jnp.concatenate([sources[i][begin:] for i, begin in far_blocks], axis=0)
    for index in range(FIELDS):
        select = (lane == line * FIELDS + index).astype(F32).astype(BF16)
        far_keys[index] = jnp.dot(select, far_rows, preferred_element_type=F32).astype(BF16)
    sources = sources + (far_keys,)

    def keep(head, top, total, row_total, mix, extra):
        inverse = 1.0 / total
        mix = mix * inverse
        mix_acc[head] = mix
        tan_acc[head] = extra * inverse - (row_total * inverse) * mix

    attend_heads(segments, sources, queries, level_bias, width, olds, keep)
    line = lax.broadcasted_iota(jnp.int32, (token_count, token_count), 0)
    lane = lax.broadcasted_iota(jnp.int32, (token_count, token_count), 1)
    unit = (line == lane).astype(F32).astype(BF16)
    sent = []
    for number, acc in enumerate((mix_acc, tan_acc)):
        flat = acc[...].reshape(width, token_count).astype(BF16)
        turned[number] = against(unit, flat).astype(BF16)
        more = chunk_copies(turned.at[number], outs[number], sems, number * FIELDS, FIELDS)
        for copy in more:
            copy.start()
        sent += more
    for copy in sent:
        copy.wait()


def attend_last(level_bias, queries, olds, sources, segments, far_count, far_blocks):
    token_count = queries[0].shape[2]
    width = sources[0].shape[-1]
    states = state_shapes(token_count, width)
    operands = (*queries, *[array for old in olds for array in old], *sources)
    return pl.pallas_call(
        functools.partial(
            last_kernel, segments, len(olds), len(sources), far_count, far_blocks
        ),
        out_shape=(jax.ShapeDtypeStruct((token_count, width), BF16),) * 2,
        in_specs=[smem_spec()] + [vmem_spec()] * len(operands),
        out_specs=[hbm_spec()] * 2,
        scratch_shapes=[
            pltpu.VMEM((FIELDS, far_count, width), BF16),
            pltpu.VMEM(states[0], F32),
            pltpu.VMEM(states[1], F32),
            pltpu.VMEM((2, token_count, width), BF16),
            pltpu.SemaphoreType.DMA((2 * FIELDS,)),
        ],
        compiler_params=pltpu.CompilerParams(vmem_limit_bytes=VMEM_BYTES),
        cost_estimate=own_cost(token_count, width, sum(s[0] for s in segments)),
        name="outer",
    )(level_bias, *operands)


def swap(block, axis, odd):
    count = lax.axis_size(axis)
    route = []
    for low in range(1 if odd else 0, count - 1, 2):
        route += [(low, low + 1), (low + 1, low)]
    return lax.ppermute(block, axis, route)


def part(source, begin, rows):
    return lambda refs, field, window: refs[source][field, begin : begin + rows, window]


def flat_part(source, stride, begin, rows):
    def read(refs, field, window):
        at = field * stride + begin
        return refs[source][at : at + rows, window]

    return read


def toward_mate(source, half):
    def read(refs, field, window):
        start = pl.multiple_of((lax.axis_index("row") % 2) * half, half)
        return refs[source][field, pl.ds(start, half), window]

    return read


def send_to(block, axis, mask):
    return lax.ppermute(block, axis, [(i, i ^ mask) for i in range(lax.axis_size(axis))])


def gather_rows(far):
    for bit in range(lax.axis_size("row").bit_length() - 2, 0, -1):
        far = jnp.concatenate([far, send_to(far, "row", 1 << bit)])
    return far


def body(
    query_field,
    key_field,
    value_field,
    query_tan,
    key_tan,
    value_tan,
    pool_near,
    pool_far,
    level_bias,
):
    window = query_field.shape[0]
    width = query_field.shape[2]
    cells = window * window
    strip, half = cells // 2, cells // 4
    near_count = cells // (NEAR_POOL * NEAR_POOL)
    row_count, col_count = lax.axis_size("row"), lax.axis_size("col")
    far_count = row_count * col_count
    flat = lambda field: field.reshape(cells, width)
    fields = tuple(flat(f) for f in (key_field, value_field, key_tan, value_tan))

    row_odd_even, row_odd_odd, col_even, col_odd, row_even, far = pack(
        fields, pool_near, pool_far
    )
    got_col_even = swap(col_even, "col", False)
    got_col_odd = swap(col_odd, "col", True)
    got_row_odd_even = swap(row_odd_even, "row", True)
    got_row_even = swap(row_even, "row", False)
    mate_far = got_row_even[0, strip + near_count : strip + near_count + FIELDS]
    far, got_row_odd_even = lax.optimization_barrier(
        (jnp.concatenate([far[:FIELDS], mate_far]), got_row_odd_even)
    )
    far = lax.cond(
        lax.axis_index("row") < row_count,
        gather_rows,
        lambda block: jnp.zeros((FIELDS * row_count, width), BF16),
        far,
    )
    row_odd_odd, got_row_even, far = lax.optimization_barrier((row_odd_odd, got_row_even, far))
    got_row_odd_odd = swap(row_odd_odd, "row", True)

    *own_state, query, qtan = attend_own(
        level_bias,
        flat(query_field),
        flat(query_tan),
        fields,
        got_row_even,
        [
            (cells, "flag", 0, lambda refs, field, window: refs[field][:, window]),
            (strip, "flag", 0, part(4, 0, strip)),
            (near_count, "level", 0, part(4, strip, near_count)),
        ],
    )
    queries = (query, qtan)
    far, stats = lax.optimization_barrier((far, own_state[2]))
    own_state = (own_state[0], own_state[1], stats)
    for bit in range(col_count.bit_length() - 2, 0, -1):
        far = jnp.concatenate([far, send_to(far, "col", 1 << bit)])
    got_col_even, got_col_odd, got_row_odd_odd, far = lax.optimization_barrier(
        (got_col_even, got_col_odd, got_row_odd_odd, far)
    )
    corner = got_row_odd_even.reshape(FIELDS * half, width)
    got_outer_even = swap(jnp.concatenate([corner, far]), "col", False)
    got_outer_odd = swap(got_row_odd_odd, "col", True)
    got_inner_even = swap(got_col_even, "row", False)
    got_inner_odd = swap(got_col_odd, "row", False)

    state = attend_more(
        level_bias,
        queries,
        [],
        (got_row_odd_even, got_row_odd_odd, got_col_even, got_col_odd),
        [
            (half, "flag", 1, part(0, 0, half)),
            (half, "flag", 1, part(1, 0, half)),
            (strip, "flag", 0, part(2, 0, strip)),
            (strip, "flag", 2, part(3, 0, strip)),
        ],
        "strips",
    )
    state = attend_more(
        level_bias,
        queries,
        [state],
        (got_inner_even, got_inner_odd, got_col_even, row_even),
        [
            (half, "flag", 0, toward_mate(0, half)),
            (half, "flag", 2, toward_mate(1, half)),
            (near_count, "level", 0, part(0, strip, near_count)),
            (near_count, "level", 0, part(2, strip, near_count)),
            (near_count, "level", 0, part(3, strip, near_count)),
        ],
        "inner",
    )
    mixed, mixed_tan = attend_last(
        level_bias,
        queries,
        [state, own_state],
        (got_outer_even, got_outer_odd, far),
        [
            (half, "flag", 1, flat_part(0, half, 0, half)),
            (half, "flag", 3, part(1, 0, half)),
            (far_count, "level", 1, part(3, 0, far_count)),
        ],
        far_count,
        ((0, FIELDS * half), (2, 0)),
    )
    shape = (window, window, width)
    return (mixed.reshape(shape), mixed_tan.reshape(shape))


def solution(mesh):
    field = P("row", "col", None)
    return jax.shard_map(
        body,
        mesh=mesh,
        in_specs=(field,) * 6 + (P(),) * 3,
        out_specs=(field, field),
        check_vma=False,
    )
```

```python
import functools

import jax
import jax.numpy as jnp
from jax import lax
from jax.experimental import pallas as pl
from jax.experimental.pallas import tpu as pltpu
from jax.sharding import PartitionSpec as P

HEADS = 16
RIM = 8
NEAR_POOL = 4
LOG2E = 1.4426950408889634
OFF = -1e30
PACK_BYTES = 60 * 1024 * 1024
VMEM_BYTES = 28 * 1024 * 1024
LANES = 128
FIELDS = 4
BF16 = jnp.bfloat16
F32 = jnp.float32


def vmem_spec():
    return pl.BlockSpec(memory_space=pltpu.VMEM)


def smem_spec():
    return pl.BlockSpec(memory_space=pltpu.SMEM)


def hbm_spec():
    return pl.BlockSpec(memory_space=pltpu.HBM)


def any_spec():
    return pl.BlockSpec(memory_space=pl.ANY)


def against(left, right):
    return lax.dot_general(left, right, (((1,), (1,)), ((), ())), preferred_element_type=F32)


def chunk_copies(source, target, sems, first, parts):
    rows = source.shape[0]
    step = -(-rows // parts)
    if len(source.shape) == 2:
        step = -(-step // 16) * 16
    copies = []
    for number, begin in enumerate(range(0, rows, step)):
        at = pl.ds(begin, min(step, rows - begin))
        copies.append(pltpu.make_async_copy(source.at[at], target.at[at], sems.at[first + number]))
    return copies


def split3(weights):
    high = weights.astype(BF16)
    rest = weights - high.astype(F32)
    mid = rest.astype(BF16)
    low = (rest - mid.astype(F32)).astype(BF16)
    return jnp.concatenate([high, mid, low], axis=0)


def pool_weights(pool_near, pool_far, cells):
    window = 2 * RIM
    near_side = window // NEAR_POOL
    near_count = near_side * near_side
    lane = lax.broadcasted_iota(jnp.int32, (near_count, cells), 1)
    line = lax.broadcasted_iota(jnp.int32, (near_count, cells), 0)
    row, col = lane // window, lane % window
    near = jnp.zeros((near_count, cells), F32)
    for p in range(NEAR_POOL):
        for q in range(NEAR_POOL):
            hit = (row % NEAR_POOL == p) & (col % NEAR_POOL == q)
            near = jnp.where(hit, pool_near[p, q], near)
    block = (row // NEAR_POOL) * near_side + col // NEAR_POOL
    near = split3(jnp.where(line == block, near, 0.0))
    spread = (line == col).astype(F32).astype(BF16)
    far = jnp.dot(split3(pool_far), spread, preferred_element_type=F32)
    far_line = lax.broadcasted_iota(jnp.int32, far.shape, 0) % window
    far_lane = lax.broadcasted_iota(jnp.int32, far.shape, 1) // window
    far = jnp.where(far_line == far_lane, far, 0.0)
    rows = [
        jnp.sum(far[i * window : (i + 1) * window], axis=0, keepdims=True) for i in range(3)
    ]
    rows.append(jnp.zeros((near_count - 3, cells), F32))
    return jnp.concatenate([near, jnp.concatenate(rows, axis=0).astype(BF16)], axis=0)


def halves(block, width):
    cells = block.shape[0]
    wide = block.astype(F32).reshape(cells // (2 * RIM), 2, RIM, width)
    left = wide[:, 0].reshape(cells // 2, width).astype(BF16)
    right = wide[:, 1].reshape(cells // 2, width).astype(BF16)
    return left, right


def pack_kernel(pool_near, pool_far, *refs):
    sources, outs = refs[:FIELDS], refs[FIELDS : FIELDS + 5]
    held = refs[FIELDS + 5]
    kept, sems, out_sems = refs[FIELDS + 6 : -2], refs[-2], refs[-1]
    cells, width = sources[0].shape
    strip, half = cells // 2, cells // 4
    near_count = cells // (NEAR_POOL * NEAR_POOL)
    row_is_even = lax.axis_index("row") % 2 == 0
    col_is_even = lax.axis_index("col") % 2 == 0
    copies = []
    for index, source in enumerate(sources):
        copies += chunk_copies(source, held.at[index], sems, 2 * index, 2)
    for copy in copies:
        copy.start()
    weights = pool_weights(pool_near, pool_far[...], cells)
    far_rows = []
    sent = []
    for index in range(FIELDS):
        copies[2 * index].wait()
        copies[2 * index + 1].wait()
        block = held[index]
        left, right = halves(block, width)
        even = jnp.where(col_is_even, right, left)
        odd = jnp.where(col_is_even, left, right)
        outer = lambda side: jnp.where(row_is_even, side[:half], side[half:])
        pooled = jnp.dot(weights, block, preferred_element_type=F32)
        near = pooled[:near_count] + (
            pooled[near_count : 2 * near_count] + pooled[2 * near_count : 3 * near_count]
        )
        near = near.astype(BF16)
        far = pooled[3 * near_count :]
        far_rows.append(far[0:1] + (far[1:2] + far[2:3]))
        kept[0][index, :half] = outer(even)
        kept[0][index, half:] = outer(odd)
        kept[1][index, :strip] = even
        kept[1][index, strip:] = near
        kept[2][index] = odd
        kept[3][index, :strip] = jnp.where(row_is_even, block[strip:], block[:strip])
        kept[3][index, strip : strip + near_count] = near
        for number in range(3):
            copy = pltpu.make_async_copy(
                kept[number].at[index], outs[number].at[index], out_sems.at[3 * index + number]
            )
            copy.start()
            sent.append(copy)
    far_rows.append(jnp.zeros((16 - FIELDS, width), F32))
    kept[4][...] = jnp.concatenate(far_rows, axis=0).astype(BF16)
    for index in range(FIELDS):
        kept[3][index, strip + near_count :] = kept[4][...]
    for number in (3, 4):
        copy = pltpu.make_async_copy(
            kept[number], outs[number], out_sems.at[3 * FIELDS + number - 3]
        )
        copy.start()
        sent.append(copy)
    for copy in sent:
        copy.wait()


def pack(fields, pool_near, pool_far):
    cells, width = fields[0].shape
    strip = cells // 2
    near_count = cells // (NEAR_POOL * NEAR_POOL)
    shapes = [
        (FIELDS, strip, width),
        (FIELDS, strip + near_count, width),
        (FIELDS, strip, width),
        (FIELDS, strip + near_count + 16, width),
        (16, width),
    ]
    return pl.pallas_call(
        pack_kernel,
        out_shape=tuple(jax.ShapeDtypeStruct(s, BF16) for s in shapes),
        in_specs=[smem_spec(), vmem_spec()] + [hbm_spec()] * FIELDS,
        out_specs=[hbm_spec()] * len(shapes),
        scratch_shapes=[pltpu.VMEM((FIELDS, cells, width), BF16)]
        + [pltpu.VMEM(s, BF16) for s in shapes]
        + [pltpu.SemaphoreType.DMA((2 * FIELDS,)), pltpu.SemaphoreType.DMA((3 * FIELDS + 2,))],
        compiler_params=pltpu.CompilerParams(vmem_limit_bytes=PACK_BYTES),
        name="pack",
    )(pool_near, pool_far, *fields)


TOGETHER = 2
GROUPS = HEADS // TOGETHER


def group_copy(source, target, sem, group):
    at = pl.ds(group * TOGETHER, TOGETHER)
    return pltpu.make_async_copy(source.at[at], target.at[at], sem.at[group])


def masked_start(head, head_dim, width):
    return min(head * head_dim // LANES, (width - 2 * LANES) // LANES) * LANES


def turn_queries(raw, turned, masked):
    width = raw.shape[1]
    head_dim = width // HEADS
    span = 2 * LANES
    line = lax.broadcasted_iota(jnp.int32, (LANES, LANES), 0)
    lane = lax.broadcasted_iota(jnp.int32, (LANES, LANES), 1)
    unit = (line == lane).astype(F32).astype(BF16)
    for at in range(0, width, LANES):
        turned[at : at + LANES] = against(unit, raw[:, at : at + LANES]).astype(BF16)
    channel = lax.broadcasted_iota(jnp.int32, (span, raw.shape[0]), 0)
    for head in range(HEADS):
        start = masked_start(head, head_dim, width)
        low = head * head_dim - start
        keep = ((channel >= low) & (channel < low + head_dim)).astype(F32).astype(BF16)
        masked[head] = turned[start : start + span] * keep


def device_flags():
    row, col = lax.axis_index("row"), lax.axis_index("col")
    row_edge = (row == 0) | (row == lax.axis_size("row") - 1)
    col_edge = (col == 0) | (col == lax.axis_size("col") - 1)
    off = lambda edge: jnp.where(edge, F32(OFF), F32(0.0))
    return (F32(0.0), off(row_edge), off(col_edge), off(row_edge | col_edge))


def head_products(head, segments, refs, queries, width):
    head_dim = width // HEADS
    start = head * head_dim // LANES * LANES
    low = head * head_dim - start
    one_tile = low + head_dim <= LANES
    span = LANES if one_tile else 2 * LANES
    window = slice(start, start + span)
    at = start - masked_start(head, head_dim, width)
    rows_of = lambda field: jnp.concatenate(
        [reader(refs, field, window) for _, _, _, reader in segments], axis=0
    )
    key, value, key_tan, value_tan = (rows_of(field) for field in range(FIELDS))
    query, query_tan = (ref[head, at : at + span] for ref in queries)
    scores = jnp.dot(key, query, preferred_element_type=F32)
    if one_tile:
        slopes = jnp.dot(
            jnp.concatenate([key, key_tan], axis=1),
            jnp.concatenate([query_tan, query], axis=0),
            preferred_element_type=F32,
        )
    else:
        slopes = jnp.dot(key, query_tan, preferred_element_type=F32)
        slopes = slopes + jnp.dot(key_tan, query, preferred_element_type=F32)
    line = lax.broadcasted_iota(jnp.int32, (head_dim + 8, span), 0)
    lane = lax.broadcasted_iota(jnp.int32, (head_dim + 8, span), 1)
    pick = ((lane == line + low) & (line < head_dim)).astype(F32).astype(BF16)
    ones_line = lax.broadcasted_iota(jnp.int32, (8, value.shape[0]), 0)
    turned = jnp.concatenate(
        [
            against(pick, value)[:head_dim],
            (ones_line == 0).astype(F32),
            against(pick, value_tan),
        ],
        axis=0,
    )
    return scores, slopes, turned.astype(BF16)


def head_result(head, segments, level_bias, flags, products, olds, width):
    scores, slopes, turned = products
    head_dim = width // HEADS
    pad_dim = head_dim + 8
    scale = head_dim**-0.5
    bias = []
    top = None
    at = 0
    for rows, kind, number, _ in segments:
        amount = flags[number] if kind == "flag" else level_bias[number, head] * LOG2E
        bias.append(amount)
        part = jnp.max(scores[at : at + rows], axis=0, keepdims=True) * (scale * LOG2E) + amount
        top = part if top is None else jnp.maximum(top, part)
        at += rows
    for old in olds:
        top = jnp.maximum(top, old[2][head, 0:1])
    weights_low, product_low = [], []
    at = 0
    for (rows, _, _, _), amount in zip(segments, bias):
        weights = jnp.exp2(scores[at : at + rows] * (scale * LOG2E) + (amount - top))
        weights_low.append(weights.astype(BF16))
        product_low.append((weights * slopes[at : at + rows]).astype(BF16))
        at += rows
    both = jnp.dot(turned, jnp.concatenate(weights_low, axis=0), preferred_element_type=F32)
    extra = jnp.dot(
        turned[:pad_dim], jnp.concatenate(product_low, axis=0), preferred_element_type=F32
    )
    mix = both[:head_dim]
    total = both[head_dim : head_dim + 1]
    row_total = extra[head_dim : head_dim + 1] * scale
    extra = extra[:head_dim] * scale + both[pad_dim : pad_dim + head_dim]
    for old in olds:
        fade = jnp.exp2(old[2][head, 0:1] - top)
        total = total + fade * old[2][head, 1:2]
        row_total = row_total + fade * old[2][head, 2:3]
        mix = mix + fade * old[0][head]
        extra = extra + fade * old[1][head]
    return top, total, row_total, mix, extra


def attend_heads(segments, refs, queries, level_bias, width, olds, keep):
    flags = device_flags()
    stages = [range(first, first + TOGETHER) for first in range(0, HEADS, TOGETHER)]
    make = lambda heads: [head_products(head, segments, refs, queries, width) for head in heads]
    ready = make(stages[0])
    for number, heads in enumerate(stages):
        coming = make(stages[number + 1]) if number + 1 < len(stages) else None
        for head, products in zip(heads, ready):
            keep(head, *head_result(head, segments, level_bias, flags, products, olds, width))
        ready = coming


def keeper(state):
    def keep(head, top, total, row_total, mix, extra):
        state[0][head] = mix
        state[1][head] = extra
        state[2][head, 0:1] = top
        state[2][head, 1:2] = total
        state[2][head, 2:3] = row_total

    return keep


def own_kernel(segments, level_bias, *refs):
    query_in, qtan_in = refs[:2]
    sources = refs[2 : 3 + FIELDS]
    outs = refs[3 + FIELDS : 8 + FIELDS]
    raw, turned, masked = refs[8 + FIELDS : 10 + FIELDS], refs[10 + FIELDS], refs[11 + FIELDS : 13 + FIELDS]
    held = refs[13 + FIELDS : 14 + 2 * FIELDS]
    state = refs[14 + 2 * FIELDS : 17 + 2 * FIELDS]
    sems, out_sems = refs[17 + 2 * FIELDS :]
    width = query_in.shape[1]
    copies = []
    for number, (source, target) in enumerate(
        list(zip((query_in, qtan_in), raw)) + list(zip(sources, held))
    ):
        copies += chunk_copies(source, target, sems, FIELDS * number, FIELDS)
    for copy in copies:
        copy.start()
    state[2][...] = jnp.zeros(state[2].shape, F32)
    sent = []
    for number in range(2):
        for copy in copies[FIELDS * number : FIELDS * (number + 1)]:
            copy.wait()
        turn_queries(raw[number], turned, masked[number])
        for group in range(GROUPS):
            sent.append(
                group_copy(masked[number], outs[3 + number], out_sems.at[3 + number], group)
            )
            sent[-1].start()
    for copy in copies[2 * FIELDS :]:
        copy.wait()

    attend_heads(segments, held, masked, level_bias, width, [], keeper(state))
    for number in range(3):
        for group in range(GROUPS):
            group_copy(state[number], outs[number], out_sems.at[number], group).start()
    for number in range(3):
        for group in range(GROUPS):
            group_copy(state[number], outs[number], out_sems.at[number], group).wait()
    for copy in sent:
        copy.wait()


def state_shapes(token_count, width):
    wide = (HEADS, width // HEADS, token_count)
    return (wide, wide, (HEADS, 8, token_count))


def own_cost(token_count, width, key_count):
    return pl.CostEstimate(
        flops=token_count * key_count * HEADS,
        bytes_accessed=token_count * width,
        transcendentals=0,
    )


def attend_own(level_bias, query, qtan, fields, mate, segments):
    token_count, width = query.shape
    states = state_shapes(token_count, width)
    masked = (HEADS, 2 * LANES, token_count)
    operands = (query, qtan, *fields, mate)
    return pl.pallas_call(
        functools.partial(own_kernel, segments),
        out_shape=tuple(jax.ShapeDtypeStruct(s, F32) for s in states)
        + (jax.ShapeDtypeStruct(masked, BF16),) * 2,
        in_specs=[smem_spec()] + [hbm_spec()] * len(operands),
        out_specs=[hbm_spec()] * 5,
        scratch_shapes=[pltpu.VMEM(query.shape, BF16)] * 2
        + [pltpu.VMEM((width, token_count), BF16)]
        + [pltpu.VMEM(masked, BF16)] * 2
        + [pltpu.VMEM(source.shape, BF16) for source in operands[2:]]
        + [pltpu.VMEM(s, F32) for s in states]
        + [
            pltpu.SemaphoreType.DMA((FIELDS * len(operands),)),
            pltpu.SemaphoreType.DMA((5, GROUPS)),
        ],
        compiler_params=pltpu.CompilerParams(vmem_limit_bytes=PACK_BYTES),
        cost_estimate=own_cost(token_count, width, sum(s[0] for s in segments)),
        name="own",
    )(level_bias, *operands)


def more_kernel(segments, old_count, count, level_bias, *refs):
    queries, refs = refs[:2], refs[2:]
    olds = [refs[3 * i : 3 * i + 3] for i in range(old_count)]
    refs = refs[3 * old_count :]
    sources, state = refs[:count], refs[count:]
    width = state[0].shape[0] * state[0].shape[1]
    state[2][...] = jnp.zeros(state[2].shape, F32)
    attend_heads(segments, sources, queries, level_bias, width, olds, keeper(state))


def attend_more(level_bias, queries, olds, sources, segments, name):
    token_count = queries[0].shape[2]
    width = sources[0].shape[-1]
    operands = (*queries, *[array for old in olds for array in old], *sources)
    return pl.pallas_call(
        functools.partial(more_kernel, segments, len(olds), len(sources)),
        out_shape=tuple(jax.ShapeDtypeStruct(s, F32) for s in state_shapes(token_count, width)),
        in_specs=[smem_spec()] + [vmem_spec()] * len(operands),
        out_specs=[vmem_spec()] * 3,
        compiler_params=pltpu.CompilerParams(vmem_limit_bytes=VMEM_BYTES),
        cost_estimate=own_cost(token_count, width, sum(s[0] for s in segments)),
        name=name,
    )(level_bias, *operands)


def last_kernel(segments, old_count, count, far_count, far_blocks, level_bias, *refs):
    queries, refs = refs[:2], refs[2:]
    olds = [refs[3 * i : 3 * i + 3] for i in range(old_count)]
    refs = refs[3 * old_count :]
    sources, outs = refs[:count], refs[count : count + 2]
    far_keys, mix_acc, tan_acc, turned, sems = refs[count + 2 :]
    width, token_count = outs[0].shape[1], outs[0].shape[0]
    line = lax.broadcasted_iota(jnp.int32, (far_count, FIELDS * far_count), 0)
    lane = lax.broadcasted_iota(jnp.int32, (far_count, FIELDS * far_count), 1)
    far_rows = jnp.concatenate([sources[i][begin:] for i, begin in far_blocks], axis=0)
    for index in range(FIELDS):
        select = (lane == line * FIELDS + index).astype(F32).astype(BF16)
        far_keys[index] = jnp.dot(select, far_rows, preferred_element_type=F32).astype(BF16)
    sources = sources + (far_keys,)

    def keep(head, top, total, row_total, mix, extra):
        inverse = 1.0 / total
        mix = mix * inverse
        mix_acc[head] = mix
        tan_acc[head] = extra * inverse - (row_total * inverse) * mix

    attend_heads(segments, sources, queries, level_bias, width, olds, keep)
    line = lax.broadcasted_iota(jnp.int32, (token_count, token_count), 0)
    lane = lax.broadcasted_iota(jnp.int32, (token_count, token_count), 1)
    unit = (line == lane).astype(F32).astype(BF16)
    sent = []
    for number, acc in enumerate((mix_acc, tan_acc)):
        flat = acc[...].reshape(width, token_count).astype(BF16)
        turned[number] = against(unit, flat).astype(BF16)
        more = chunk_copies(turned.at[number], outs[number], sems, number * FIELDS, FIELDS)
        for copy in more:
            copy.start()
        sent += more
    for copy in sent:
        copy.wait()


def attend_last(level_bias, queries, olds, sources, segments, far_count, far_blocks):
    token_count = queries[0].shape[2]
    width = sources[0].shape[-1]
    states = state_shapes(token_count, width)
    operands = (*queries, *[array for old in olds for array in old], *sources)
    return pl.pallas_call(
        functools.partial(
            last_kernel, segments, len(olds), len(sources), far_count, far_blocks
        ),
        out_shape=(jax.ShapeDtypeStruct((token_count, width), BF16),) * 2,
        in_specs=[smem_spec()] + [vmem_spec()] * len(operands),
        out_specs=[hbm_spec()] * 2,
        scratch_shapes=[
            pltpu.VMEM((FIELDS, far_count, width), BF16),
            pltpu.VMEM(states[0], F32),
            pltpu.VMEM(states[1], F32),
            pltpu.VMEM((2, token_count, width), BF16),
            pltpu.SemaphoreType.DMA((2 * FIELDS,)),
        ],
        compiler_params=pltpu.CompilerParams(vmem_limit_bytes=VMEM_BYTES),
        cost_estimate=own_cost(token_count, width, sum(s[0] for s in segments)),
        name="outer",
    )(level_bias, *operands)


def swap(block, axis, odd):
    count = lax.axis_size(axis)
    route = []
    for low in range(1 if odd else 0, count - 1, 2):
        route += [(low, low + 1), (low + 1, low)]
    return lax.ppermute(block, axis, route)


def part(source, begin, rows):
    return lambda refs, field, window: refs[source][field, begin : begin + rows, window]


def flat_part(source, stride, begin, rows):
    def read(refs, field, window):
        at = field * stride + begin
        return refs[source][at : at + rows, window]

    return read


def toward_mate(source, half):
    def read(refs, field, window):
        start = pl.multiple_of((lax.axis_index("row") % 2) * half, half)
        return refs[source][field, pl.ds(start, half), window]

    return read


def send_to(block, axis, mask):
    return lax.ppermute(block, axis, [(i, i ^ mask) for i in range(lax.axis_size(axis))])


def gather_far(far):
    for bit in range(lax.axis_size("row").bit_length() - 2, 0, -1):
        far = jnp.concatenate([far, send_to(far, "row", 1 << bit)])
    for bit in range(lax.axis_size("col").bit_length() - 2, 0, -1):
        far = jnp.concatenate([far, send_to(far, "col", 1 << bit)])
    return far


def body(
    query_field,
    key_field,
    value_field,
    query_tan,
    key_tan,
    value_tan,
    pool_near,
    pool_far,
    level_bias,
):
    window = query_field.shape[0]
    width = query_field.shape[2]
    cells = window * window
    strip, half = cells // 2, cells // 4
    near_count = cells // (NEAR_POOL * NEAR_POOL)
    row_count, col_count = lax.axis_size("row"), lax.axis_size("col")
    far_count = row_count * col_count
    flat = lambda field: field.reshape(cells, width)
    fields = tuple(flat(f) for f in (key_field, value_field, key_tan, value_tan))

    row_odd, col_even, col_odd, row_even, far = pack(fields, pool_near, pool_far)
    got_row_odd = swap(row_odd, "row", True)
    got_col_even = swap(col_even, "col", False)
    got_col_odd = swap(col_odd, "col", True)
    got_row_even = swap(row_even, "row", False)

    *own_state, query, qtan = attend_own(
        level_bias,
        flat(query_field),
        flat(query_tan),
        fields,
        got_row_even,
        [
            (cells, "flag", 0, lambda refs, field, window: refs[field][:, window]),
            (strip, "flag", 0, part(4, 0, strip)),
            (near_count, "level", 0, part(4, strip, near_count)),
        ],
    )
    queries = (query, qtan)
    mate_far = got_row_even[0, strip + near_count : strip + near_count + FIELDS]
    far = jnp.concatenate([far[:FIELDS], mate_far])
    far, stats = lax.optimization_barrier((far, own_state[2]))
    own_state = (own_state[0], own_state[1], stats)
    far = lax.cond(
        lax.axis_index("row") < row_count,
        gather_far,
        lambda block: jnp.zeros((FIELDS * far_count // 2, width), BF16),
        far,
    )
    got_row_odd, got_col_even, far = lax.optimization_barrier((got_row_odd, got_col_even, far))
    to_even = jnp.concatenate([got_row_odd[:, :half].reshape(FIELDS * half, width), far])
    to_odd = got_row_odd[:, half:]
    got_col_even, got_col_odd, to_even, to_odd = lax.optimization_barrier(
        (got_col_even, got_col_odd, to_even, to_odd)
    )
    got_outer_even = swap(to_even, "col", False)
    got_outer_odd = swap(to_odd, "col", True)
    got_inner_even = swap(got_col_even, "row", False)
    got_inner_odd = swap(got_col_odd, "row", False)

    state = attend_more(
        level_bias,
        queries,
        [],
        (got_row_odd, got_col_even, got_col_odd),
        [
            (strip, "flag", 0, part(1, 0, strip)),
            (strip, "flag", 1, part(0, 0, strip)),
            (strip, "flag", 2, part(2, 0, strip)),
        ],
        "strips",
    )
    state = attend_more(
        level_bias,
        queries,
        [state],
        (got_inner_even, got_inner_odd, got_col_even, row_even),
        [
            (half, "flag", 0, toward_mate(0, half)),
            (half, "flag", 2, toward_mate(1, half)),
            (near_count, "level", 0, part(0, strip, near_count)),
            (near_count, "level", 0, part(2, strip, near_count)),
            (near_count, "level", 0, part(3, strip, near_count)),
        ],
        "inner",
    )
    mixed, mixed_tan = attend_last(
        level_bias,
        queries,
        [state, own_state],
        (got_outer_even, got_outer_odd, far),
        [
            (half, "flag", 1, flat_part(0, half, 0, half)),
            (half, "flag", 3, part(1, 0, half)),
            (far_count, "level", 1, part(3, 0, far_count)),
        ],
        far_count,
        ((0, FIELDS * half), (2, 0)),
    )
    shape = (window, window, width)
    return (mixed.reshape(shape), mixed_tan.reshape(shape))


def solution(mesh):
    field = P("row", "col", None)
    return jax.shard_map(
        body,
        mesh=mesh,
        in_specs=(field,) * 6 + (P(),) * 3,
        out_specs=(field, field),
        check_vma=False,
    )
```

```python
import functools

import jax
import jax.numpy as jnp
from jax import lax
from jax.experimental import pallas as pl
from jax.experimental.pallas import tpu as pltpu
from jax.sharding import PartitionSpec as P

HEADS = 16
RIM = 8
NEAR_POOL = 4
LOG2E = 1.4426950408889634
OFF = -1e30
PACK_BYTES = 60 * 1024 * 1024
VMEM_BYTES = 28 * 1024 * 1024
LANES = 128
FIELDS = 4
BF16 = jnp.bfloat16
F32 = jnp.float32


def vmem_spec():
    return pl.BlockSpec(memory_space=pltpu.VMEM)


def smem_spec():
    return pl.BlockSpec(memory_space=pltpu.SMEM)


def hbm_spec():
    return pl.BlockSpec(memory_space=pltpu.HBM)


def any_spec():
    return pl.BlockSpec(memory_space=pl.ANY)


def against(left, right):
    return lax.dot_general(left, right, (((1,), (1,)), ((), ())), preferred_element_type=F32)


def chunk_copies(source, target, sems, first, parts):
    rows = source.shape[0]
    step = -(-rows // parts)
    if len(source.shape) == 2:
        step = -(-step // 16) * 16
    copies = []
    for number, begin in enumerate(range(0, rows, step)):
        at = pl.ds(begin, min(step, rows - begin))
        copies.append(pltpu.make_async_copy(source.at[at], target.at[at], sems.at[first + number]))
    return copies


def split3(weights):
    high = weights.astype(BF16)
    rest = weights - high.astype(F32)
    mid = rest.astype(BF16)
    low = (rest - mid.astype(F32)).astype(BF16)
    return jnp.concatenate([high, mid, low], axis=0)


def pool_weights(pool_near, pool_far, cells):
    window = 2 * RIM
    near_side = window // NEAR_POOL
    near_count = near_side * near_side
    lane = lax.broadcasted_iota(jnp.int32, (near_count, cells), 1)
    line = lax.broadcasted_iota(jnp.int32, (near_count, cells), 0)
    row, col = lane // window, lane % window
    near = jnp.zeros((near_count, cells), F32)
    for p in range(NEAR_POOL):
        for q in range(NEAR_POOL):
            hit = (row % NEAR_POOL == p) & (col % NEAR_POOL == q)
            near = jnp.where(hit, pool_near[p, q], near)
    block = (row // NEAR_POOL) * near_side + col // NEAR_POOL
    near = split3(jnp.where(line == block, near, 0.0))
    spread = (line == col).astype(F32).astype(BF16)
    far = jnp.dot(split3(pool_far), spread, preferred_element_type=F32)
    far_line = lax.broadcasted_iota(jnp.int32, far.shape, 0) % window
    far_lane = lax.broadcasted_iota(jnp.int32, far.shape, 1) // window
    far = jnp.where(far_line == far_lane, far, 0.0)
    rows = [
        jnp.sum(far[i * window : (i + 1) * window], axis=0, keepdims=True) for i in range(3)
    ]
    rows.append(jnp.zeros((near_count - 3, cells), F32))
    return jnp.concatenate([near, jnp.concatenate(rows, axis=0).astype(BF16)], axis=0)


def halves(block, width):
    cells = block.shape[0]
    wide = block.astype(F32).reshape(cells // (2 * RIM), 2, RIM, width)
    left = wide[:, 0].reshape(cells // 2, width).astype(BF16)
    right = wide[:, 1].reshape(cells // 2, width).astype(BF16)
    return left, right


def pack_kernel(pool_near, pool_far, *refs):
    sources, outs = refs[:FIELDS], refs[FIELDS : FIELDS + 5]
    held = refs[FIELDS + 5]
    kept, sems, out_sems = refs[FIELDS + 6 : -2], refs[-2], refs[-1]
    cells, width = sources[0].shape
    strip, half = cells // 2, cells // 4
    near_count = cells // (NEAR_POOL * NEAR_POOL)
    row_is_even = lax.axis_index("row") % 2 == 0
    col_is_even = lax.axis_index("col") % 2 == 0
    copies = []
    for index, source in enumerate(sources):
        copies += chunk_copies(source, held.at[index], sems, 2 * index, 2)
    for copy in copies:
        copy.start()
    weights = pool_weights(pool_near, pool_far[...], cells)
    far_rows = []
    sent = []
    for index in range(FIELDS):
        copies[2 * index].wait()
        copies[2 * index + 1].wait()
        block = held[index]
        left, right = halves(block, width)
        even = jnp.where(col_is_even, right, left)
        odd = jnp.where(col_is_even, left, right)
        outer = lambda side: jnp.where(row_is_even, side[:half], side[half:])
        pooled = jnp.dot(weights, block, preferred_element_type=F32)
        near = pooled[:near_count] + (
            pooled[near_count : 2 * near_count] + pooled[2 * near_count : 3 * near_count]
        )
        near = near.astype(BF16)
        far = pooled[3 * near_count :]
        far_rows.append(far[0:1] + (far[1:2] + far[2:3]))
        kept[0][index, :half] = outer(even)
        kept[0][index, half:] = outer(odd)
        kept[1][index, :strip] = even
        kept[1][index, strip:] = near
        kept[2][index] = odd
        kept[3][index, :strip] = jnp.where(row_is_even, block[strip:], block[:strip])
        kept[3][index, strip:] = near
        for number in range(4):
            copy = pltpu.make_async_copy(
                kept[number].at[index], outs[number].at[index], out_sems.at[4 * index + number]
            )
            copy.start()
            sent.append(copy)
    far_rows.append(jnp.zeros((16 - FIELDS, width), F32))
    kept[4][...] = jnp.concatenate(far_rows, axis=0).astype(BF16)
    copy = pltpu.make_async_copy(kept[4], outs[4], out_sems.at[4 * FIELDS])
    copy.start()
    sent.append(copy)
    for copy in sent:
        copy.wait()


def pack(fields, pool_near, pool_far):
    cells, width = fields[0].shape
    strip = cells // 2
    near_count = cells // (NEAR_POOL * NEAR_POOL)
    shapes = [
        (FIELDS, strip, width),
        (FIELDS, strip + near_count, width),
        (FIELDS, strip, width),
        (FIELDS, strip + near_count, width),
        (16, width),
    ]
    return pl.pallas_call(
        pack_kernel,
        out_shape=tuple(jax.ShapeDtypeStruct(s, BF16) for s in shapes),
        in_specs=[smem_spec(), vmem_spec()] + [hbm_spec()] * FIELDS,
        out_specs=[hbm_spec()] * len(shapes),
        scratch_shapes=[pltpu.VMEM((FIELDS, cells, width), BF16)]
        + [pltpu.VMEM(s, BF16) for s in shapes]
        + [pltpu.SemaphoreType.DMA((2 * FIELDS,)), pltpu.SemaphoreType.DMA((4 * FIELDS + 1,))],
        compiler_params=pltpu.CompilerParams(vmem_limit_bytes=PACK_BYTES),
        name="pack",
    )(pool_near, pool_far, *fields)


TOGETHER = 2
GROUPS = HEADS // TOGETHER


def group_copy(source, target, sem, group):
    at = pl.ds(group * TOGETHER, TOGETHER)
    return pltpu.make_async_copy(source.at[at], target.at[at], sem.at[group])


def masked_start(head, head_dim, width):
    return min(head * head_dim // LANES, (width - 2 * LANES) // LANES) * LANES


def turn_queries(raw, turned, masked):
    width = raw.shape[1]
    head_dim = width // HEADS
    span = 2 * LANES
    line = lax.broadcasted_iota(jnp.int32, (LANES, LANES), 0)
    lane = lax.broadcasted_iota(jnp.int32, (LANES, LANES), 1)
    unit = (line == lane).astype(F32).astype(BF16)
    for at in range(0, width, LANES):
        turned[at : at + LANES] = against(unit, raw[:, at : at + LANES]).astype(BF16)
    channel = lax.broadcasted_iota(jnp.int32, (span, raw.shape[0]), 0)
    for head in range(HEADS):
        start = masked_start(head, head_dim, width)
        low = head * head_dim - start
        keep = ((channel >= low) & (channel < low + head_dim)).astype(F32).astype(BF16)
        masked[head] = turned[start : start + span] * keep


def device_flags():
    row, col = lax.axis_index("row"), lax.axis_index("col")
    row_edge = (row == 0) | (row == lax.axis_size("row") - 1)
    col_edge = (col == 0) | (col == lax.axis_size("col") - 1)
    off = lambda edge: jnp.where(edge, F32(OFF), F32(0.0))
    return (F32(0.0), off(row_edge), off(col_edge), off(row_edge | col_edge))


def head_products(head, segments, refs, queries, width):
    head_dim = width // HEADS
    start = head * head_dim // LANES * LANES
    low = head * head_dim - start
    one_tile = low + head_dim <= LANES
    span = LANES if one_tile else 2 * LANES
    window = slice(start, start + span)
    at = start - masked_start(head, head_dim, width)
    rows_of = lambda field: jnp.concatenate(
        [reader(refs, field, window) for _, _, _, reader in segments], axis=0
    )
    key, value, key_tan, value_tan = (rows_of(field) for field in range(FIELDS))
    query, query_tan = (ref[head, at : at + span] for ref in queries)
    scores = jnp.dot(key, query, preferred_element_type=F32)
    if one_tile:
        slopes = jnp.dot(
            jnp.concatenate([key, key_tan], axis=1),
            jnp.concatenate([query_tan, query], axis=0),
            preferred_element_type=F32,
        )
    else:
        slopes = jnp.dot(key, query_tan, preferred_element_type=F32)
        slopes = slopes + jnp.dot(key_tan, query, preferred_element_type=F32)
    line = lax.broadcasted_iota(jnp.int32, (head_dim + 8, span), 0)
    lane = lax.broadcasted_iota(jnp.int32, (head_dim + 8, span), 1)
    pick = ((lane == line + low) & (line < head_dim)).astype(F32).astype(BF16)
    ones_line = lax.broadcasted_iota(jnp.int32, (8, value.shape[0]), 0)
    turned = jnp.concatenate(
        [
            against(pick, value)[:head_dim],
            (ones_line == 0).astype(F32),
            against(pick, value_tan),
        ],
        axis=0,
    )
    return scores, slopes, turned.astype(BF16)


def head_result(head, segments, level_bias, flags, products, olds, width):
    scores, slopes, turned = products
    head_dim = width // HEADS
    pad_dim = head_dim + 8
    scale = head_dim**-0.5
    bias = []
    top = None
    at = 0
    for rows, kind, number, _ in segments:
        amount = flags[number] if kind == "flag" else level_bias[number, head] * LOG2E
        bias.append(amount)
        part = jnp.max(scores[at : at + rows], axis=0, keepdims=True) * (scale * LOG2E) + amount
        top = part if top is None else jnp.maximum(top, part)
        at += rows
    for old in olds:
        top = jnp.maximum(top, old[2][head, 0:1])
    weights_low, product_low = [], []
    at = 0
    for (rows, _, _, _), amount in zip(segments, bias):
        weights = jnp.exp2(scores[at : at + rows] * (scale * LOG2E) + (amount - top))
        weights_low.append(weights.astype(BF16))
        product_low.append((weights * slopes[at : at + rows]).astype(BF16))
        at += rows
    both = jnp.dot(turned, jnp.concatenate(weights_low, axis=0), preferred_element_type=F32)
    extra = jnp.dot(
        turned[:pad_dim], jnp.concatenate(product_low, axis=0), preferred_element_type=F32
    )
    mix = both[:head_dim]
    total = both[head_dim : head_dim + 1]
    row_total = extra[head_dim : head_dim + 1] * scale
    extra = extra[:head_dim] * scale + both[pad_dim : pad_dim + head_dim]
    for old in olds:
        fade = jnp.exp2(old[2][head, 0:1] - top)
        total = total + fade * old[2][head, 1:2]
        row_total = row_total + fade * old[2][head, 2:3]
        mix = mix + fade * old[0][head]
        extra = extra + fade * old[1][head]
    return top, total, row_total, mix, extra


def attend_heads(segments, refs, queries, level_bias, width, olds, keep):
    flags = device_flags()
    stages = [range(first, first + TOGETHER) for first in range(0, HEADS, TOGETHER)]
    make = lambda heads: [head_products(head, segments, refs, queries, width) for head in heads]
    ready = make(stages[0])
    for number, heads in enumerate(stages):
        coming = make(stages[number + 1]) if number + 1 < len(stages) else None
        for head, products in zip(heads, ready):
            keep(head, *head_result(head, segments, level_bias, flags, products, olds, width))
        ready = coming


def keeper(state):
    def keep(head, top, total, row_total, mix, extra):
        state[0][head] = mix
        state[1][head] = extra
        state[2][head, 0:1] = top
        state[2][head, 1:2] = total
        state[2][head, 2:3] = row_total

    return keep


def own_kernel(segments, level_bias, *refs):
    query_in, qtan_in = refs[:2]
    sources = refs[2 : 3 + FIELDS]
    outs = refs[3 + FIELDS : 8 + FIELDS]
    raw, turned, masked = refs[8 + FIELDS : 10 + FIELDS], refs[10 + FIELDS], refs[11 + FIELDS : 13 + FIELDS]
    held = refs[13 + FIELDS : 14 + 2 * FIELDS]
    state = refs[14 + 2 * FIELDS : 17 + 2 * FIELDS]
    sems, out_sems = refs[17 + 2 * FIELDS :]
    width = query_in.shape[1]
    copies = []
    for number, (source, target) in enumerate(
        list(zip((query_in, qtan_in), raw)) + list(zip(sources, held))
    ):
        copies += chunk_copies(source, target, sems, FIELDS * number, FIELDS)
    for copy in copies:
        copy.start()
    state[2][...] = jnp.zeros(state[2].shape, F32)
    sent = []
    for number in range(2):
        for copy in copies[FIELDS * number : FIELDS * (number + 1)]:
            copy.wait()
        turn_queries(raw[number], turned, masked[number])
        for group in range(GROUPS):
            sent.append(
                group_copy(masked[number], outs[3 + number], out_sems.at[3 + number], group)
            )
            sent[-1].start()
    for copy in copies[2 * FIELDS :]:
        copy.wait()

    attend_heads(segments, held, masked, level_bias, width, [], keeper(state))
    for number in range(3):
        for group in range(GROUPS):
            group_copy(state[number], outs[number], out_sems.at[number], group).start()
    for number in range(3):
        for group in range(GROUPS):
            group_copy(state[number], outs[number], out_sems.at[number], group).wait()
    for copy in sent:
        copy.wait()


def state_shapes(token_count, width):
    wide = (HEADS, width // HEADS, token_count)
    return (wide, wide, (HEADS, 8, token_count))


def own_cost(token_count, width, key_count):
    return pl.CostEstimate(
        flops=token_count * key_count * HEADS,
        bytes_accessed=token_count * width,
        transcendentals=0,
    )


def attend_own(level_bias, query, qtan, fields, mate, segments):
    token_count, width = query.shape
    states = state_shapes(token_count, width)
    masked = (HEADS, 2 * LANES, token_count)
    operands = (query, qtan, *fields, mate)
    return pl.pallas_call(
        functools.partial(own_kernel, segments),
        out_shape=tuple(jax.ShapeDtypeStruct(s, F32) for s in states)
        + (jax.ShapeDtypeStruct(masked, BF16),) * 2,
        in_specs=[smem_spec()] + [hbm_spec()] * len(operands),
        out_specs=[hbm_spec()] * 5,
        scratch_shapes=[pltpu.VMEM(query.shape, BF16)] * 2
        + [pltpu.VMEM((width, token_count), BF16)]
        + [pltpu.VMEM(masked, BF16)] * 2
        + [pltpu.VMEM(source.shape, BF16) for source in operands[2:]]
        + [pltpu.VMEM(s, F32) for s in states]
        + [
            pltpu.SemaphoreType.DMA((FIELDS * len(operands),)),
            pltpu.SemaphoreType.DMA((5, GROUPS)),
        ],
        compiler_params=pltpu.CompilerParams(vmem_limit_bytes=PACK_BYTES),
        cost_estimate=own_cost(token_count, width, sum(s[0] for s in segments)),
        name="own",
    )(level_bias, *operands)


def more_kernel(segments, old_count, count, level_bias, *refs):
    queries, refs = refs[:2], refs[2:]
    olds = [refs[3 * i : 3 * i + 3] for i in range(old_count)]
    refs = refs[3 * old_count :]
    sources, state = refs[:count], refs[count:]
    width = state[0].shape[0] * state[0].shape[1]
    state[2][...] = jnp.zeros(state[2].shape, F32)
    attend_heads(segments, sources, queries, level_bias, width, olds, keeper(state))


def attend_more(level_bias, queries, olds, sources, segments, name):
    token_count = queries[0].shape[2]
    width = sources[0].shape[-1]
    operands = (*queries, *[array for old in olds for array in old], *sources)
    return pl.pallas_call(
        functools.partial(more_kernel, segments, len(olds), len(sources)),
        out_shape=tuple(jax.ShapeDtypeStruct(s, F32) for s in state_shapes(token_count, width)),
        in_specs=[smem_spec()] + [vmem_spec()] * len(operands),
        out_specs=[vmem_spec()] * 3,
        compiler_params=pltpu.CompilerParams(vmem_limit_bytes=VMEM_BYTES),
        cost_estimate=own_cost(token_count, width, sum(s[0] for s in segments)),
        name=name,
    )(level_bias, *operands)


def last_kernel(segments, old_count, count, far_count, far_blocks, level_bias, *refs):
    queries, refs = refs[:2], refs[2:]
    olds = [refs[3 * i : 3 * i + 3] for i in range(old_count)]
    refs = refs[3 * old_count :]
    sources, outs = refs[:count], refs[count : count + 2]
    far_keys, mix_acc, tan_acc, turned, sems = refs[count + 2 :]
    width, token_count = outs[0].shape[1], outs[0].shape[0]
    line = lax.broadcasted_iota(jnp.int32, (far_count, FIELDS * far_count), 0)
    lane = lax.broadcasted_iota(jnp.int32, (far_count, FIELDS * far_count), 1)
    far_rows = jnp.concatenate([sources[i][begin:] for i, begin in far_blocks], axis=0)
    for index in range(FIELDS):
        select = (lane == line * FIELDS + index).astype(F32).astype(BF16)
        far_keys[index] = jnp.dot(select, far_rows, preferred_element_type=F32).astype(BF16)
    sources = sources + (far_keys,)

    def keep(head, top, total, row_total, mix, extra):
        inverse = 1.0 / total
        mix = mix * inverse
        mix_acc[head] = mix
        tan_acc[head] = extra * inverse - (row_total * inverse) * mix

    attend_heads(segments, sources, queries, level_bias, width, olds, keep)
    line = lax.broadcasted_iota(jnp.int32, (token_count, token_count), 0)
    lane = lax.broadcasted_iota(jnp.int32, (token_count, token_count), 1)
    unit = (line == lane).astype(F32).astype(BF16)
    sent = []
    for number, acc in enumerate((mix_acc, tan_acc)):
        flat = acc[...].reshape(width, token_count).astype(BF16)
        turned[number] = against(unit, flat).astype(BF16)
        more = chunk_copies(turned.at[number], outs[number], sems, number * FIELDS, FIELDS)
        for copy in more:
            copy.start()
        sent += more
    for copy in sent:
        copy.wait()


def attend_last(level_bias, queries, olds, sources, segments, far_count, far_blocks):
    token_count = queries[0].shape[2]
    width = sources[0].shape[-1]
    states = state_shapes(token_count, width)
    operands = (*queries, *[array for old in olds for array in old], *sources)
    return pl.pallas_call(
        functools.partial(
            last_kernel, segments, len(olds), len(sources), far_count, far_blocks
        ),
        out_shape=(jax.ShapeDtypeStruct((token_count, width), BF16),) * 2,
        in_specs=[smem_spec()] + [vmem_spec()] * len(operands),
        out_specs=[hbm_spec()] * 2,
        scratch_shapes=[
            pltpu.VMEM((FIELDS, far_count, width), BF16),
            pltpu.VMEM(states[0], F32),
            pltpu.VMEM(states[1], F32),
            pltpu.VMEM((2, token_count, width), BF16),
            pltpu.SemaphoreType.DMA((2 * FIELDS,)),
        ],
        compiler_params=pltpu.CompilerParams(vmem_limit_bytes=VMEM_BYTES),
        cost_estimate=own_cost(token_count, width, sum(s[0] for s in segments)),
        name="outer",
    )(level_bias, *operands)


def swap(block, axis, odd):
    count = lax.axis_size(axis)
    route = []
    for low in range(1 if odd else 0, count - 1, 2):
        route += [(low, low + 1), (low + 1, low)]
    return lax.ppermute(block, axis, route)


def part(source, begin, rows):
    return lambda refs, field, window: refs[source][field, begin : begin + rows, window]


def flat_part(source, stride, begin, rows):
    def read(refs, field, window):
        at = field * stride + begin
        return refs[source][at : at + rows, window]

    return read


def toward_mate(source, half):
    def read(refs, field, window):
        start = pl.multiple_of((lax.axis_index("row") % 2) * half, half)
        return refs[source][field, pl.ds(start, half), window]

    return read


def send_to(block, axis, mask):
    return lax.ppermute(block, axis, [(i, i ^ mask) for i in range(lax.axis_size(axis))])


def gather_cols(far):
    count = lax.axis_size("col")
    if count <= 4:
        return jnp.concatenate([far] + [send_to(far, "col", mask) for mask in range(1, count)])
    for bit in range(count.bit_length() - 1):
        far = jnp.concatenate([far, send_to(far, "col", 1 << bit)])
    return far


def gather_rows(far):
    bits = range(lax.axis_size("row").bit_length() - 1)
    for bit in sorted(bits, key=lambda bit: bit == 1):
        far = jnp.concatenate([far, send_to(far, "row", 1 << bit)])
    return far


def on_all(gather, far, growth):
    shape = (far.shape[0] * growth,) + far.shape[1:]
    taken = lax.axis_index("row") < lax.axis_size("row")
    return lax.cond(taken, gather, lambda block: jnp.zeros(shape, block.dtype), far)


def body(
    query_field,
    key_field,
    value_field,
    query_tan,
    key_tan,
    value_tan,
    pool_near,
    pool_far,
    level_bias,
):
    window = query_field.shape[0]
    width = query_field.shape[2]
    cells = window * window
    strip, half = cells // 2, cells // 4
    near_count = cells // (NEAR_POOL * NEAR_POOL)
    row_count, col_count = lax.axis_size("row"), lax.axis_size("col")
    far_count = row_count * col_count
    flat = lambda field: field.reshape(cells, width)
    fields = tuple(flat(f) for f in (key_field, value_field, key_tan, value_tan))

    row_odd, col_even, col_odd, row_even, far = pack(fields, pool_near, pool_far)
    far = on_all(gather_cols, far[:FIELDS], col_count)
    col_even, col_odd, far = lax.optimization_barrier((col_even, col_odd, far))
    got_row_odd = swap(row_odd, "row", True)
    got_col_even = swap(col_even, "col", False)
    got_col_odd = swap(col_odd, "col", True)
    got_row_even = swap(row_even, "row", False)

    *own_state, query, qtan = attend_own(
        level_bias,
        flat(query_field),
        flat(query_tan),
        fields,
        got_row_even,
        [
            (cells, "flag", 0, lambda refs, field, window: refs[field][:, window]),
            (strip, "flag", 0, part(4, 0, strip)),
            (near_count, "level", 0, part(4, strip, near_count)),
        ],
    )
    queries = (query, qtan)
    far, stats = lax.optimization_barrier((far, own_state[2]))
    own_state = (own_state[0], own_state[1], stats)
    far = on_all(gather_rows, far, row_count)
    got_row_odd, far = lax.optimization_barrier((got_row_odd, far))
    to_even, to_odd = got_row_odd[:, :half], got_row_odd[:, half:]
    got_col_even, got_col_odd, to_even, to_odd = lax.optimization_barrier(
        (got_col_even, got_col_odd, to_even, to_odd)
    )
    got_outer_even = swap(to_even, "col", False)
    got_outer_odd = swap(to_odd, "col", True)
    got_inner_even = swap(got_col_even, "row", False)
    got_inner_odd = swap(got_col_odd, "row", False)

    state = attend_more(
        level_bias,
        queries,
        [],
        (got_row_odd, got_col_even, got_col_odd),
        [
            (strip, "flag", 0, part(1, 0, strip)),
            (strip, "flag", 1, part(0, 0, strip)),
            (strip, "flag", 2, part(2, 0, strip)),
        ],
        "strips",
    )
    state = attend_more(
        level_bias,
        queries,
        [state],
        (got_inner_even, got_inner_odd, got_col_even, row_even),
        [
            (half, "flag", 0, toward_mate(0, half)),
            (half, "flag", 2, toward_mate(1, half)),
            (near_count, "level", 0, part(0, strip, near_count)),
            (near_count, "level", 0, part(2, strip, near_count)),
            (near_count, "level", 0, part(3, strip, near_count)),
        ],
        "inner",
    )
    mixed, mixed_tan = attend_last(
        level_bias,
        queries,
        [state, own_state],
        (got_outer_even, got_outer_odd, far),
        [
            (half, "flag", 1, part(0, 0, half)),
            (half, "flag", 3, part(1, 0, half)),
            (far_count, "level", 1, part(3, 0, far_count)),
        ],
        far_count,
        ((2, 0),),
    )
    shape = (window, window, width)
    return (mixed.reshape(shape), mixed_tan.reshape(shape))


def solution(mesh):
    field = P("row", "col", None)
    return jax.shard_map(
        body,
        mesh=mesh,
        in_specs=(field,) * 6 + (P(),) * 3,
        out_specs=(field, field),
        check_vma=False,
    )
```

```python
import functools

import jax
import jax.numpy as jnp
from jax import lax
from jax.experimental import pallas as pl
from jax.experimental.pallas import tpu as pltpu
from jax.sharding import PartitionSpec as P

HEADS = 16
RIM = 8
NEAR_POOL = 4
LOG2E = 1.4426950408889634
OFF = -1e30
PACK_BYTES = 60 * 1024 * 1024
VMEM_BYTES = 28 * 1024 * 1024
LANES = 128
FIELDS = 4
BF16 = jnp.bfloat16
F32 = jnp.float32


def vmem_spec():
    return pl.BlockSpec(memory_space=pltpu.VMEM)


def smem_spec():
    return pl.BlockSpec(memory_space=pltpu.SMEM)


def hbm_spec():
    return pl.BlockSpec(memory_space=pltpu.HBM)


def any_spec():
    return pl.BlockSpec(memory_space=pl.ANY)


def against(left, right):
    return lax.dot_general(left, right, (((1,), (1,)), ((), ())), preferred_element_type=F32)


def chunk_copies(source, target, sems, first, parts):
    rows = source.shape[0]
    step = -(-rows // parts)
    if len(source.shape) == 2:
        step = -(-step // 16) * 16
    copies = []
    for number, begin in enumerate(range(0, rows, step)):
        at = pl.ds(begin, min(step, rows - begin))
        copies.append(pltpu.make_async_copy(source.at[at], target.at[at], sems.at[first + number]))
    return copies


def split3(weights):
    high = weights.astype(BF16)
    rest = weights - high.astype(F32)
    mid = rest.astype(BF16)
    low = (rest - mid.astype(F32)).astype(BF16)
    return jnp.concatenate([high, mid, low], axis=0)


def pool_weights(pool_near, pool_far, cells):
    window = 2 * RIM
    near_side = window // NEAR_POOL
    near_count = near_side * near_side
    lane = lax.broadcasted_iota(jnp.int32, (near_count, cells), 1)
    line = lax.broadcasted_iota(jnp.int32, (near_count, cells), 0)
    row, col = lane // window, lane % window
    near = jnp.zeros((near_count, cells), F32)
    for p in range(NEAR_POOL):
        for q in range(NEAR_POOL):
            hit = (row % NEAR_POOL == p) & (col % NEAR_POOL == q)
            near = jnp.where(hit, pool_near[p, q], near)
    block = (row // NEAR_POOL) * near_side + col // NEAR_POOL
    near = split3(jnp.where(line == block, near, 0.0))
    spread = (line == col).astype(F32).astype(BF16)
    far = jnp.dot(split3(pool_far), spread, preferred_element_type=F32)
    far_line = lax.broadcasted_iota(jnp.int32, far.shape, 0) % window
    far_lane = lax.broadcasted_iota(jnp.int32, far.shape, 1) // window
    far = jnp.where(far_line == far_lane, far, 0.0)
    rows = [
        jnp.sum(far[i * window : (i + 1) * window], axis=0, keepdims=True) for i in range(3)
    ]
    rows.append(jnp.zeros((near_count - 3, cells), F32))
    return jnp.concatenate([near, jnp.concatenate(rows, axis=0).astype(BF16)], axis=0)


def halves(block, width):
    cells = block.shape[0]
    wide = block.astype(F32).reshape(cells // (2 * RIM), 2, RIM, width)
    left = wide[:, 0].reshape(cells // 2, width).astype(BF16)
    right = wide[:, 1].reshape(cells // 2, width).astype(BF16)
    return left, right


def pack_kernel(pool_near, pool_far, *refs):
    sources, outs = refs[:FIELDS], refs[FIELDS : FIELDS + 5]
    held = refs[FIELDS + 5]
    kept, sems, out_sems = refs[FIELDS + 6 : -2], refs[-2], refs[-1]
    cells, width = sources[0].shape
    strip, half = cells // 2, cells // 4
    near_count = cells // (NEAR_POOL * NEAR_POOL)
    row_is_even = lax.axis_index("row") % 2 == 0
    col_is_even = lax.axis_index("col") % 2 == 0
    copies = []
    for index, source in enumerate(sources):
        copies += chunk_copies(source, held.at[index], sems, 2 * index, 2)
    for copy in copies:
        copy.start()
    weights = pool_weights(pool_near, pool_far[...], cells)
    far_rows = []
    sent = []
    for index in range(FIELDS):
        copies[2 * index].wait()
        copies[2 * index + 1].wait()
        block = held[index]
        left, right = halves(block, width)
        even = jnp.where(col_is_even, right, left)
        odd = jnp.where(col_is_even, left, right)
        outer = lambda side: jnp.where(row_is_even, side[:half], side[half:])
        pooled = jnp.dot(weights, block, preferred_element_type=F32)
        near = pooled[:near_count] + (
            pooled[near_count : 2 * near_count] + pooled[2 * near_count : 3 * near_count]
        )
        near = near.astype(BF16)
        far = pooled[3 * near_count :]
        far_rows.append(far[0:1] + (far[1:2] + far[2:3]))
        kept[0][index, :half] = outer(even)
        kept[0][index, half:] = outer(odd)
        at = index * (strip + near_count)
        kept[1][at : at + strip] = even
        kept[1][at + strip : at + strip + near_count] = near
        kept[2][index] = odd
        kept[3][index, :strip] = jnp.where(row_is_even, block[strip:], block[:strip])
        kept[3][index, strip:] = near
        for number in (0, 2, 3):
            copy = pltpu.make_async_copy(
                kept[number].at[index], outs[number].at[index], out_sems.at[4 * index + number]
            )
            copy.start()
            sent.append(copy)
    far_rows.append(jnp.zeros((16 - FIELDS, width), F32))
    kept[4][...] = jnp.concatenate(far_rows, axis=0).astype(BF16)
    kept[1][FIELDS * (strip + near_count) :] = kept[4][...]
    for number, source in ((1, 1), (4 * FIELDS, 4)):
        copy = pltpu.make_async_copy(kept[source], outs[source], out_sems.at[number])
        copy.start()
        sent.append(copy)
    for copy in sent:
        copy.wait()


def pack(fields, pool_near, pool_far):
    cells, width = fields[0].shape
    strip = cells // 2
    near_count = cells // (NEAR_POOL * NEAR_POOL)
    shapes = [
        (FIELDS, strip, width),
        (FIELDS * (strip + near_count) + 16, width),
        (FIELDS, strip, width),
        (FIELDS, strip + near_count, width),
        (16, width),
    ]
    return pl.pallas_call(
        pack_kernel,
        out_shape=tuple(jax.ShapeDtypeStruct(s, BF16) for s in shapes),
        in_specs=[smem_spec(), vmem_spec()] + [hbm_spec()] * FIELDS,
        out_specs=[hbm_spec()] * len(shapes),
        scratch_shapes=[pltpu.VMEM((FIELDS, cells, width), BF16)]
        + [pltpu.VMEM(s, BF16) for s in shapes]
        + [pltpu.SemaphoreType.DMA((2 * FIELDS,)), pltpu.SemaphoreType.DMA((4 * FIELDS + 1,))],
        compiler_params=pltpu.CompilerParams(vmem_limit_bytes=PACK_BYTES),
        name="pack",
    )(pool_near, pool_far, *fields)


TOGETHER = 2
GROUPS = HEADS // TOGETHER


def group_copy(source, target, sem, group):
    at = pl.ds(group * TOGETHER, TOGETHER)
    return pltpu.make_async_copy(source.at[at], target.at[at], sem.at[group])


def masked_start(head, head_dim, width):
    return min(head * head_dim // LANES, (width - 2 * LANES) // LANES) * LANES


def turn_queries(raw, turned, masked):
    width = raw.shape[1]
    head_dim = width // HEADS
    span = 2 * LANES
    line = lax.broadcasted_iota(jnp.int32, (LANES, LANES), 0)
    lane = lax.broadcasted_iota(jnp.int32, (LANES, LANES), 1)
    unit = (line == lane).astype(F32).astype(BF16)
    for at in range(0, width, LANES):
        turned[at : at + LANES] = against(unit, raw[:, at : at + LANES]).astype(BF16)
    channel = lax.broadcasted_iota(jnp.int32, (span, raw.shape[0]), 0)
    for head in range(HEADS):
        start = masked_start(head, head_dim, width)
        low = head * head_dim - start
        keep = ((channel >= low) & (channel < low + head_dim)).astype(F32).astype(BF16)
        masked[head] = turned[start : start + span] * keep


def device_flags():
    row, col = lax.axis_index("row"), lax.axis_index("col")
    row_edge = (row == 0) | (row == lax.axis_size("row") - 1)
    col_edge = (col == 0) | (col == lax.axis_size("col") - 1)
    off = lambda edge: jnp.where(edge, F32(OFF), F32(0.0))
    return (F32(0.0), off(row_edge), off(col_edge), off(row_edge | col_edge))


def head_products(head, segments, refs, queries, width):
    head_dim = width // HEADS
    start = head * head_dim // LANES * LANES
    low = head * head_dim - start
    one_tile = low + head_dim <= LANES
    span = LANES if one_tile else 2 * LANES
    window = slice(start, start + span)
    at = start - masked_start(head, head_dim, width)
    rows_of = lambda field: jnp.concatenate(
        [reader(refs, field, window) for _, _, _, reader in segments], axis=0
    )
    key, value, key_tan, value_tan = (rows_of(field) for field in range(FIELDS))
    query, query_tan = (ref[head, at : at + span] for ref in queries)
    scores = jnp.dot(key, query, preferred_element_type=F32)
    if one_tile:
        slopes = jnp.dot(
            jnp.concatenate([key, key_tan], axis=1),
            jnp.concatenate([query_tan, query], axis=0),
            preferred_element_type=F32,
        )
    else:
        slopes = jnp.dot(key, query_tan, preferred_element_type=F32)
        slopes = slopes + jnp.dot(key_tan, query, preferred_element_type=F32)
    line = lax.broadcasted_iota(jnp.int32, (head_dim + 8, span), 0)
    lane = lax.broadcasted_iota(jnp.int32, (head_dim + 8, span), 1)
    pick = ((lane == line + low) & (line < head_dim)).astype(F32).astype(BF16)
    ones_line = lax.broadcasted_iota(jnp.int32, (8, value.shape[0]), 0)
    turned = jnp.concatenate(
        [
            against(pick, value)[:head_dim],
            (ones_line == 0).astype(F32),
            against(pick, value_tan),
        ],
        axis=0,
    )
    return scores, slopes, turned.astype(BF16)


def head_result(head, segments, level_bias, flags, products, olds, width):
    scores, slopes, turned = products
    head_dim = width // HEADS
    pad_dim = head_dim + 8
    scale = head_dim**-0.5
    bias = []
    top = None
    at = 0
    for rows, kind, number, _ in segments:
        amount = flags[number] if kind == "flag" else level_bias[number, head] * LOG2E
        bias.append(amount)
        part = jnp.max(scores[at : at + rows], axis=0, keepdims=True) * (scale * LOG2E) + amount
        top = part if top is None else jnp.maximum(top, part)
        at += rows
    for old in olds:
        top = jnp.maximum(top, old[2][head, 0:1])
    weights_low, product_low = [], []
    at = 0
    for (rows, _, _, _), amount in zip(segments, bias):
        weights = jnp.exp2(scores[at : at + rows] * (scale * LOG2E) + (amount - top))
        weights_low.append(weights.astype(BF16))
        product_low.append((weights * slopes[at : at + rows]).astype(BF16))
        at += rows
    both = jnp.dot(turned, jnp.concatenate(weights_low, axis=0), preferred_element_type=F32)
    extra = jnp.dot(
        turned[:pad_dim], jnp.concatenate(product_low, axis=0), preferred_element_type=F32
    )
    mix = both[:head_dim]
    total = both[head_dim : head_dim + 1]
    row_total = extra[head_dim : head_dim + 1] * scale
    extra = extra[:head_dim] * scale + both[pad_dim : pad_dim + head_dim]
    for old in olds:
        fade = jnp.exp2(old[2][head, 0:1] - top)
        total = total + fade * old[2][head, 1:2]
        row_total = row_total + fade * old[2][head, 2:3]
        mix = mix + fade * old[0][head]
        extra = extra + fade * old[1][head]
    return top, total, row_total, mix, extra


def attend_heads(segments, refs, queries, level_bias, width, olds, keep):
    flags = device_flags()
    stages = [range(first, first + TOGETHER) for first in range(0, HEADS, TOGETHER)]
    make = lambda heads: [head_products(head, segments, refs, queries, width) for head in heads]
    ready = make(stages[0])
    for number, heads in enumerate(stages):
        coming = make(stages[number + 1]) if number + 1 < len(stages) else None
        for head, products in zip(heads, ready):
            keep(head, *head_result(head, segments, level_bias, flags, products, olds, width))
        ready = coming


def keeper(state):
    def keep(head, top, total, row_total, mix, extra):
        state[0][head] = mix
        state[1][head] = extra
        state[2][head, 0:1] = top
        state[2][head, 1:2] = total
        state[2][head, 2:3] = row_total

    return keep


def own_kernel(segments, level_bias, *refs):
    query_in, qtan_in = refs[:2]
    sources = refs[2 : 3 + FIELDS]
    outs = refs[3 + FIELDS : 8 + FIELDS]
    raw, turned, masked = refs[8 + FIELDS : 10 + FIELDS], refs[10 + FIELDS], refs[11 + FIELDS : 13 + FIELDS]
    held = refs[13 + FIELDS : 14 + 2 * FIELDS]
    state = refs[14 + 2 * FIELDS : 17 + 2 * FIELDS]
    sems, out_sems = refs[17 + 2 * FIELDS :]
    width = query_in.shape[1]
    copies = []
    for number, (source, target) in enumerate(
        list(zip((query_in, qtan_in), raw)) + list(zip(sources, held))
    ):
        copies += chunk_copies(source, target, sems, FIELDS * number, FIELDS)
    for copy in copies:
        copy.start()
    state[2][...] = jnp.zeros(state[2].shape, F32)
    sent = []
    for number in range(2):
        for copy in copies[FIELDS * number : FIELDS * (number + 1)]:
            copy.wait()
        turn_queries(raw[number], turned, masked[number])
        for group in range(GROUPS):
            sent.append(
                group_copy(masked[number], outs[3 + number], out_sems.at[3 + number], group)
            )
            sent[-1].start()
    for copy in copies[2 * FIELDS :]:
        copy.wait()

    attend_heads(segments, held, masked, level_bias, width, [], keeper(state))
    for number in range(3):
        for group in range(GROUPS):
            group_copy(state[number], outs[number], out_sems.at[number], group).start()
    for number in range(3):
        for group in range(GROUPS):
            group_copy(state[number], outs[number], out_sems.at[number], group).wait()
    for copy in sent:
        copy.wait()


def state_shapes(token_count, width):
    wide = (HEADS, width // HEADS, token_count)
    return (wide, wide, (HEADS, 8, token_count))


def own_cost(token_count, width, key_count):
    return pl.CostEstimate(
        flops=token_count * key_count * HEADS,
        bytes_accessed=token_count * width,
        transcendentals=0,
    )


def attend_own(level_bias, query, qtan, fields, mate, segments):
    token_count, width = query.shape
    states = state_shapes(token_count, width)
    masked = (HEADS, 2 * LANES, token_count)
    operands = (query, qtan, *fields, mate)
    return pl.pallas_call(
        functools.partial(own_kernel, segments),
        out_shape=tuple(jax.ShapeDtypeStruct(s, F32) for s in states)
        + (jax.ShapeDtypeStruct(masked, BF16),) * 2,
        in_specs=[smem_spec()] + [hbm_spec()] * len(operands),
        out_specs=[hbm_spec()] * 5,
        scratch_shapes=[pltpu.VMEM(query.shape, BF16)] * 2
        + [pltpu.VMEM((width, token_count), BF16)]
        + [pltpu.VMEM(masked, BF16)] * 2
        + [pltpu.VMEM(source.shape, BF16) for source in operands[2:]]
        + [pltpu.VMEM(s, F32) for s in states]
        + [
            pltpu.SemaphoreType.DMA((FIELDS * len(operands),)),
            pltpu.SemaphoreType.DMA((5, GROUPS)),
        ],
        compiler_params=pltpu.CompilerParams(vmem_limit_bytes=PACK_BYTES),
        cost_estimate=own_cost(token_count, width, sum(s[0] for s in segments)),
        name="own",
    )(level_bias, *operands)


def more_kernel(segments, old_count, count, level_bias, *refs):
    queries, refs = refs[:2], refs[2:]
    olds = [refs[3 * i : 3 * i + 3] for i in range(old_count)]
    refs = refs[3 * old_count :]
    sources, state = refs[:count], refs[count:]
    width = state[0].shape[0] * state[0].shape[1]
    state[2][...] = jnp.zeros(state[2].shape, F32)
    attend_heads(segments, sources, queries, level_bias, width, olds, keeper(state))


def attend_more(level_bias, queries, olds, sources, segments, name):
    token_count = queries[0].shape[2]
    width = sources[0].shape[-1]
    operands = (*queries, *[array for old in olds for array in old], *sources)
    return pl.pallas_call(
        functools.partial(more_kernel, segments, len(olds), len(sources)),
        out_shape=tuple(jax.ShapeDtypeStruct(s, F32) for s in state_shapes(token_count, width)),
        in_specs=[smem_spec()] + [vmem_spec()] * len(operands),
        out_specs=[vmem_spec()] * 3,
        compiler_params=pltpu.CompilerParams(vmem_limit_bytes=VMEM_BYTES),
        cost_estimate=own_cost(token_count, width, sum(s[0] for s in segments)),
        name=name,
    )(level_bias, *operands)


def last_kernel(segments, old_count, count, far_count, far_blocks, level_bias, *refs):
    queries, refs = refs[:2], refs[2:]
    olds = [refs[3 * i : 3 * i + 3] for i in range(old_count)]
    refs = refs[3 * old_count :]
    sources, outs = refs[:count], refs[count : count + 2]
    far_keys, mix_acc, tan_acc, turned, sems = refs[count + 2 :]
    width, token_count = outs[0].shape[1], outs[0].shape[0]
    line = lax.broadcasted_iota(jnp.int32, (far_count, FIELDS * far_count), 0)
    lane = lax.broadcasted_iota(jnp.int32, (far_count, FIELDS * far_count), 1)
    far_rows = jnp.concatenate([sources[i][begin:] for i, begin in far_blocks], axis=0)
    for index in range(FIELDS):
        select = (lane == line * FIELDS + index).astype(F32).astype(BF16)
        far_keys[index] = jnp.dot(select, far_rows, preferred_element_type=F32).astype(BF16)
    sources = sources + (far_keys,)

    def keep(head, top, total, row_total, mix, extra):
        inverse = 1.0 / total
        mix = mix * inverse
        mix_acc[head] = mix
        tan_acc[head] = extra * inverse - (row_total * inverse) * mix

    attend_heads(segments, sources, queries, level_bias, width, olds, keep)
    line = lax.broadcasted_iota(jnp.int32, (token_count, token_count), 0)
    lane = lax.broadcasted_iota(jnp.int32, (token_count, token_count), 1)
    unit = (line == lane).astype(F32).astype(BF16)
    sent = []
    for number, acc in enumerate((mix_acc, tan_acc)):
        flat = acc[...].reshape(width, token_count).astype(BF16)
        turned[number] = against(unit, flat).astype(BF16)
        more = chunk_copies(turned.at[number], outs[number], sems, number * FIELDS, FIELDS)
        for copy in more:
            copy.start()
        sent += more
    for copy in sent:
        copy.wait()


def attend_last(level_bias, queries, olds, sources, segments, far_count, far_blocks):
    token_count = queries[0].shape[2]
    width = sources[0].shape[-1]
    states = state_shapes(token_count, width)
    operands = (*queries, *[array for old in olds for array in old], *sources)
    return pl.pallas_call(
        functools.partial(
            last_kernel, segments, len(olds), len(sources), far_count, far_blocks
        ),
        out_shape=(jax.ShapeDtypeStruct((token_count, width), BF16),) * 2,
        in_specs=[smem_spec()] + [vmem_spec()] * len(operands),
        out_specs=[hbm_spec()] * 2,
        scratch_shapes=[
            pltpu.VMEM((FIELDS, far_count, width), BF16),
            pltpu.VMEM(states[0], F32),
            pltpu.VMEM(states[1], F32),
            pltpu.VMEM((2, token_count, width), BF16),
            pltpu.SemaphoreType.DMA((2 * FIELDS,)),
        ],
        compiler_params=pltpu.CompilerParams(vmem_limit_bytes=VMEM_BYTES),
        cost_estimate=own_cost(token_count, width, sum(s[0] for s in segments)),
        name="outer",
    )(level_bias, *operands)


def swap(block, axis, odd):
    count = lax.axis_size(axis)
    route = []
    for low in range(1 if odd else 0, count - 1, 2):
        route += [(low, low + 1), (low + 1, low)]
    return lax.ppermute(block, axis, route)


def part(source, begin, rows):
    return lambda refs, field, window: refs[source][field, begin : begin + rows, window]


def flat_part(source, stride, begin, rows):
    def read(refs, field, window):
        at = field * stride + begin
        return refs[source][at : at + rows, window]

    return read


def flat_toward_mate(source, stride, half):
    def read(refs, field, window):
        start = pl.multiple_of(field * stride + (lax.axis_index("row") % 2) * half, 16)
        return refs[source][pl.ds(start, half), window]

    return read


def toward_mate(source, half):
    def read(refs, field, window):
        start = pl.multiple_of((lax.axis_index("row") % 2) * half, half)
        return refs[source][field, pl.ds(start, half), window]

    return read


def send_to(block, axis, mask):
    return lax.ppermute(block, axis, [(i, i ^ mask) for i in range(lax.axis_size(axis))])


def gather_rows(far):
    for bit in range(lax.axis_size("row").bit_length() - 1):
        if bit != 1:
            far = jnp.concatenate([far, send_to(far, "row", 1 << bit)])
    return far


def on_all(gather, far, growth):
    shape = (far.shape[0] * growth,) + far.shape[1:]
    taken = lax.axis_index("row") < lax.axis_size("row")
    return lax.cond(taken, gather, lambda block: jnp.zeros(shape, block.dtype), far)


def body(
    query_field,
    key_field,
    value_field,
    query_tan,
    key_tan,
    value_tan,
    pool_near,
    pool_far,
    level_bias,
):
    window = query_field.shape[0]
    width = query_field.shape[2]
    cells = window * window
    strip, half = cells // 2, cells // 4
    near_count = cells // (NEAR_POOL * NEAR_POOL)
    row_count, col_count = lax.axis_size("row"), lax.axis_size("col")
    far_count = row_count * col_count
    flat = lambda field: field.reshape(cells, width)
    fields = tuple(flat(f) for f in (key_field, value_field, key_tan, value_tan))

    row_odd, col_even, col_odd, row_even, far = pack(fields, pool_near, pool_far)
    group = strip + near_count
    far = far[:FIELDS]
    got_col_even = swap(col_even, "col", False)
    got_row_odd = swap(row_odd, "row", True)
    got_col_odd = swap(col_odd, "col", True)
    got_row_even = swap(row_even, "row", False)

    *own_state, query, qtan = attend_own(
        level_bias,
        flat(query_field),
        flat(query_tan),
        fields,
        got_row_even,
        [
            (cells, "flag", 0, lambda refs, field, window: refs[field][:, window]),
            (strip, "flag", 0, part(4, 0, strip)),
            (near_count, "level", 0, part(4, strip, near_count)),
        ],
    )
    queries = (query, qtan)
    far_from = [send_to(far, "col", mask) for mask in range(2, min(col_count, 4))]
    mate_far = got_col_even[FIELDS * group : FIELDS * group + FIELDS]
    row_state = attend_more(
        level_bias,
        queries,
        [own_state],
        (got_row_odd,),
        [(strip, "flag", 1, part(0, 0, strip))],
        "row_strip",
    )
    got_row_odd, stats = lax.optimization_barrier((got_row_odd, row_state[2]))
    row_state = (row_state[0], row_state[1], stats)
    to_even, to_odd = got_row_odd[:, :half], got_row_odd[:, half:]
    got_col_even, got_col_odd, to_even, to_odd, far_from = lax.optimization_barrier(
        (got_col_even, got_col_odd, to_even, to_odd, far_from)
    )
    got_outer_even = swap(to_even, "col", False)
    got_outer_odd = swap(to_odd, "col", True)
    got_inner_even = swap(got_col_even, "row", False)
    got_inner_odd = swap(got_col_odd, "row", False)
    far = jnp.concatenate([far, mate_far, *far_from])
    for bit in range(2, col_count.bit_length() - 1):
        far = jnp.concatenate([far, send_to(far, "col", 1 << bit)])
    far = on_all(gather_rows, far, row_count // 2)
    more_far = send_to(far, "row", 2)

    state = attend_more(
        level_bias,
        queries,
        [row_state],
        (got_col_even, got_col_odd),
        [
            (strip, "flag", 0, flat_part(0, group, 0, strip)),
            (strip, "flag", 2, part(1, 0, strip)),
        ],
        "strips",
    )
    state = attend_more(
        level_bias,
        queries,
        [state],
        (got_inner_even, got_inner_odd, got_col_even, row_even),
        [
            (half, "flag", 0, flat_toward_mate(0, group, half)),
            (half, "flag", 2, toward_mate(1, half)),
            (near_count, "level", 0, flat_part(0, group, strip, near_count)),
            (near_count, "level", 0, flat_part(2, group, strip, near_count)),
            (near_count, "level", 0, part(3, strip, near_count)),
        ],
        "inner",
    )
    mixed, mixed_tan = attend_last(
        level_bias,
        queries,
        [state],
        (got_outer_even, got_outer_odd, far, more_far),
        [
            (half, "flag", 1, part(0, 0, half)),
            (half, "flag", 3, part(1, 0, half)),
            (far_count, "level", 1, part(4, 0, far_count)),
        ],
        far_count,
        ((2, 0), (3, 0)),
    )
    shape = (window, window, width)
    return (mixed.reshape(shape), mixed_tan.reshape(shape))


def solution(mesh):
    field = P("row", "col", None)
    return jax.shard_map(
        body,
        mesh=mesh,
        in_specs=(field,) * 6 + (P(),) * 3,
        out_specs=(field, field),
        check_vma=False,
    )
```

```python
import functools

import jax
import jax.numpy as jnp
from jax import lax
from jax.experimental import pallas as pl
from jax.experimental.pallas import tpu as pltpu
from jax.sharding import PartitionSpec as P

HEADS = 16
RIM = 8
NEAR_POOL = 4
LOG2E = 1.4426950408889634
OFF = -1e30
PACK_BYTES = 60 * 1024 * 1024
VMEM_BYTES = 28 * 1024 * 1024
LANES = 128
FIELDS = 4
BF16 = jnp.bfloat16
F32 = jnp.float32


def vmem_spec():
    return pl.BlockSpec(memory_space=pltpu.VMEM)


def smem_spec():
    return pl.BlockSpec(memory_space=pltpu.SMEM)


def hbm_spec():
    return pl.BlockSpec(memory_space=pltpu.HBM)


def any_spec():
    return pl.BlockSpec(memory_space=pl.ANY)


def against(left, right):
    return lax.dot_general(left, right, (((1,), (1,)), ((), ())), preferred_element_type=F32)


def chunk_copies(source, target, sems, first, parts):
    rows = source.shape[0]
    step = -(-rows // parts)
    if len(source.shape) == 2:
        step = -(-step // 16) * 16
    copies = []
    for number, begin in enumerate(range(0, rows, step)):
        at = pl.ds(begin, min(step, rows - begin))
        copies.append(pltpu.make_async_copy(source.at[at], target.at[at], sems.at[first + number]))
    return copies


def split3(weights):
    high = weights.astype(BF16)
    rest = weights - high.astype(F32)
    mid = rest.astype(BF16)
    low = (rest - mid.astype(F32)).astype(BF16)
    return jnp.concatenate([high, mid, low], axis=0)


def pool_weights(pool_near, pool_far, cells):
    window = 2 * RIM
    near_side = window // NEAR_POOL
    near_count = near_side * near_side
    lane = lax.broadcasted_iota(jnp.int32, (near_count, cells), 1)
    line = lax.broadcasted_iota(jnp.int32, (near_count, cells), 0)
    row, col = lane // window, lane % window
    near = jnp.zeros((near_count, cells), F32)
    for p in range(NEAR_POOL):
        for q in range(NEAR_POOL):
            hit = (row % NEAR_POOL == p) & (col % NEAR_POOL == q)
            near = jnp.where(hit, pool_near[p, q], near)
    block = (row // NEAR_POOL) * near_side + col // NEAR_POOL
    near = split3(jnp.where(line == block, near, 0.0))
    spread = (line == col).astype(F32).astype(BF16)
    far = jnp.dot(split3(pool_far), spread, preferred_element_type=F32)
    far_line = lax.broadcasted_iota(jnp.int32, far.shape, 0) % window
    far_lane = lax.broadcasted_iota(jnp.int32, far.shape, 1) // window
    far = jnp.where(far_line == far_lane, far, 0.0)
    rows = [
        jnp.sum(far[i * window : (i + 1) * window], axis=0, keepdims=True) for i in range(3)
    ]
    rows.append(jnp.zeros((near_count - 3, cells), F32))
    return jnp.concatenate([near, jnp.concatenate(rows, axis=0).astype(BF16)], axis=0)


def halves(block, width):
    cells = block.shape[0]
    wide = block.astype(F32).reshape(cells // (2 * RIM), 2, RIM, width)
    left = wide[:, 0].reshape(cells // 2, width).astype(BF16)
    right = wide[:, 1].reshape(cells // 2, width).astype(BF16)
    return left, right


def pack_kernel(pool_near, pool_far, *refs):
    sources, outs = refs[:FIELDS], refs[FIELDS : FIELDS + 5]
    held = refs[FIELDS + 5]
    kept, sems, out_sems = refs[FIELDS + 6 : -2], refs[-2], refs[-1]
    cells, width = sources[0].shape
    strip, half = cells // 2, cells // 4
    near_count = cells // (NEAR_POOL * NEAR_POOL)
    row_is_even = lax.axis_index("row") % 2 == 0
    col_is_even = lax.axis_index("col") % 2 == 0
    copies = []
    for index, source in enumerate(sources):
        copies += chunk_copies(source, held.at[index], sems, 2 * index, 2)
    for copy in copies:
        copy.start()
    weights = pool_weights(pool_near, pool_far[...], cells)
    far_rows = []
    sent = []
    for index in range(FIELDS):
        copies[2 * index].wait()
        copies[2 * index + 1].wait()
        block = held[index]
        left, right = halves(block, width)
        even = jnp.where(col_is_even, right, left)
        odd = jnp.where(col_is_even, left, right)
        outer = lambda side: jnp.where(row_is_even, side[:half], side[half:])
        pooled = jnp.dot(weights, block, preferred_element_type=F32)
        near = pooled[:near_count] + (
            pooled[near_count : 2 * near_count] + pooled[2 * near_count : 3 * near_count]
        )
        near = near.astype(BF16)
        far = pooled[3 * near_count :]
        far_rows.append(far[0:1] + (far[1:2] + far[2:3]))
        kept[0][index, :half] = outer(even)
        kept[0][index, half:] = outer(odd)
        at = index * (strip + near_count)
        kept[1][at : at + strip] = even
        kept[1][at + strip : at + strip + near_count] = near
        kept[2][index] = odd
        kept[3][index, :strip] = jnp.where(row_is_even, block[strip:], block[:strip])
        kept[3][index, strip:] = near
        for number in (0, 2, 3):
            copy = pltpu.make_async_copy(
                kept[number].at[index], outs[number].at[index], out_sems.at[4 * index + number]
            )
            copy.start()
            sent.append(copy)
    far_rows.append(jnp.zeros((16 - FIELDS, width), F32))
    kept[4][...] = jnp.concatenate(far_rows, axis=0).astype(BF16)
    kept[1][FIELDS * (strip + near_count) :] = kept[4][...]
    for number, source in ((1, 1), (4 * FIELDS, 4)):
        copy = pltpu.make_async_copy(kept[source], outs[source], out_sems.at[number])
        copy.start()
        sent.append(copy)
    for copy in sent:
        copy.wait()


def pack(fields, pool_near, pool_far):
    cells, width = fields[0].shape
    strip = cells // 2
    near_count = cells // (NEAR_POOL * NEAR_POOL)
    shapes = [
        (FIELDS, strip, width),
        (FIELDS * (strip + near_count) + 16, width),
        (FIELDS, strip, width),
        (FIELDS, strip + near_count, width),
        (16, width),
    ]
    return pl.pallas_call(
        pack_kernel,
        out_shape=tuple(jax.ShapeDtypeStruct(s, BF16) for s in shapes),
        in_specs=[smem_spec(), vmem_spec()] + [hbm_spec()] * FIELDS,
        out_specs=[hbm_spec()] * len(shapes),
        scratch_shapes=[pltpu.VMEM((FIELDS, cells, width), BF16)]
        + [pltpu.VMEM(s, BF16) for s in shapes]
        + [pltpu.SemaphoreType.DMA((2 * FIELDS,)), pltpu.SemaphoreType.DMA((4 * FIELDS + 1,))],
        compiler_params=pltpu.CompilerParams(vmem_limit_bytes=PACK_BYTES),
        name="pack",
    )(pool_near, pool_far, *fields)


TOGETHER = 2


def masked_start(head, head_dim, width):
    return min(head * head_dim // LANES, (width - 2 * LANES) // LANES) * LANES


def turn_queries(raw, turned, masked):
    width = raw.shape[1]
    head_dim = width // HEADS
    span = 2 * LANES
    line = lax.broadcasted_iota(jnp.int32, (LANES, LANES), 0)
    lane = lax.broadcasted_iota(jnp.int32, (LANES, LANES), 1)
    unit = (line == lane).astype(F32).astype(BF16)
    for at in range(0, width, LANES):
        turned[at : at + LANES] = against(unit, raw[:, at : at + LANES]).astype(BF16)
    channel = lax.broadcasted_iota(jnp.int32, (span, raw.shape[0]), 0)
    for head in range(HEADS):
        start = masked_start(head, head_dim, width)
        low = head * head_dim - start
        keep = ((channel >= low) & (channel < low + head_dim)).astype(F32).astype(BF16)
        masked[head] = turned[start : start + span] * keep


def device_flags():
    row, col = lax.axis_index("row"), lax.axis_index("col")
    row_edge = (row == 0) | (row == lax.axis_size("row") - 1)
    col_edge = (col == 0) | (col == lax.axis_size("col") - 1)
    off = lambda edge: jnp.where(edge, F32(OFF), F32(0.0))
    return (F32(0.0), off(row_edge), off(col_edge), off(row_edge | col_edge))


def head_products(head, segments, refs, queries, width):
    head_dim = width // HEADS
    start = head * head_dim // LANES * LANES
    low = head * head_dim - start
    one_tile = low + head_dim <= LANES
    span = LANES if one_tile else 2 * LANES
    window = slice(start, start + span)
    at = start - masked_start(head, head_dim, width)
    rows_of = lambda field: jnp.concatenate(
        [reader(refs, field, window) for _, _, _, reader in segments], axis=0
    )
    key, value, key_tan, value_tan = (rows_of(field) for field in range(FIELDS))
    query, query_tan = (ref[head, at : at + span] for ref in queries)
    scores = jnp.dot(key, query, preferred_element_type=F32)
    if one_tile:
        slopes = jnp.dot(
            jnp.concatenate([key, key_tan], axis=1),
            jnp.concatenate([query_tan, query], axis=0),
            preferred_element_type=F32,
        )
    else:
        slopes = jnp.dot(key, query_tan, preferred_element_type=F32)
        slopes = slopes + jnp.dot(key_tan, query, preferred_element_type=F32)
    line = lax.broadcasted_iota(jnp.int32, (head_dim + 8, span), 0)
    lane = lax.broadcasted_iota(jnp.int32, (head_dim + 8, span), 1)
    pick = ((lane == line + low) & (line < head_dim)).astype(F32).astype(BF16)
    ones_line = lax.broadcasted_iota(jnp.int32, (8, value.shape[0]), 0)
    turned = jnp.concatenate(
        [
            against(pick, value)[:head_dim],
            (ones_line == 0).astype(F32),
            against(pick, value_tan),
        ],
        axis=0,
    )
    return scores, slopes, turned.astype(BF16)


def head_result(head, segments, level_bias, flags, products, olds, width):
    scores, slopes, turned = products
    head_dim = width // HEADS
    pad_dim = head_dim + 8
    scale = head_dim**-0.5
    bias = []
    top = None
    at = 0
    for rows, kind, number, _ in segments:
        amount = flags[number] if kind == "flag" else level_bias[number, head] * LOG2E
        bias.append(amount)
        part = jnp.max(scores[at : at + rows], axis=0, keepdims=True) * (scale * LOG2E) + amount
        top = part if top is None else jnp.maximum(top, part)
        at += rows
    for old in olds:
        top = jnp.maximum(top, old[2][head, 0:1])
    weights_low, product_low = [], []
    at = 0
    for (rows, _, _, _), amount in zip(segments, bias):
        weights = jnp.exp2(scores[at : at + rows] * (scale * LOG2E) + (amount - top))
        weights_low.append(weights.astype(BF16))
        product_low.append((weights * slopes[at : at + rows]).astype(BF16))
        at += rows
    both = jnp.dot(turned, jnp.concatenate(weights_low, axis=0), preferred_element_type=F32)
    extra = jnp.dot(
        turned[:pad_dim], jnp.concatenate(product_low, axis=0), preferred_element_type=F32
    )
    mix = both[:head_dim]
    total = both[head_dim : head_dim + 1]
    row_total = extra[head_dim : head_dim + 1] * scale
    extra = extra[:head_dim] * scale + both[pad_dim : pad_dim + head_dim]
    for old in olds:
        fade = jnp.exp2(old[2][head, 0:1] - top)
        total = total + fade * old[2][head, 1:2]
        row_total = row_total + fade * old[2][head, 2:3]
        mix = mix + fade * old[0][head]
        extra = extra + fade * old[1][head]
    return top, total, row_total, mix, extra


def attend_heads(segments, refs, queries, level_bias, width, olds, keep):
    flags = device_flags()
    stages = [range(first, first + TOGETHER) for first in range(0, HEADS, TOGETHER)]
    make = lambda heads: [head_products(head, segments, refs, queries, width) for head in heads]
    ready = make(stages[0])
    for number, heads in enumerate(stages):
        coming = make(stages[number + 1]) if number + 1 < len(stages) else None
        for head, products in zip(heads, ready):
            keep(head, *head_result(head, segments, level_bias, flags, products, olds, width))
        ready = coming


def keeper(state):
    def keep(head, top, total, row_total, mix, extra):
        state[0][head] = mix
        state[1][head] = extra
        state[2][head, 0:1] = top
        state[2][head, 1:2] = total
        state[2][head, 2:3] = row_total

    return keep


def own_kernel(segments, level_bias, query, qtan, *refs):
    sources, state = refs[: FIELDS + 1], refs[FIELDS + 1 : FIELDS + 4]
    masked, turned = refs[FIELDS + 4 : FIELDS + 6], refs[FIELDS + 6]
    state[2][...] = jnp.zeros(state[2].shape, F32)
    for raw, target in zip((query, qtan), masked):
        turn_queries(raw, turned, target)
    attend_heads(segments, sources, masked, level_bias, query.shape[1], [], keeper(state))


def state_shapes(token_count, width):
    wide = (HEADS, width // HEADS, token_count)
    return (wide, wide, (HEADS, 8, token_count))


def own_cost(token_count, width, key_count):
    return pl.CostEstimate(
        flops=token_count * key_count * HEADS,
        bytes_accessed=token_count * width,
        transcendentals=0,
    )


def attend_own(level_bias, query, qtan, fields, mate, segments):
    token_count, width = query.shape
    states = state_shapes(token_count, width)
    masked = (HEADS, 2 * LANES, token_count)
    operands = (query, qtan, *fields, mate)
    return pl.pallas_call(
        functools.partial(own_kernel, segments),
        out_shape=tuple(jax.ShapeDtypeStruct(s, F32) for s in states)
        + (jax.ShapeDtypeStruct(masked, BF16),) * 2,
        in_specs=[smem_spec()] + [vmem_spec()] * len(operands),
        out_specs=[vmem_spec()] * 5,
        scratch_shapes=[pltpu.VMEM((width, token_count), BF16)],
        compiler_params=pltpu.CompilerParams(vmem_limit_bytes=VMEM_BYTES),
        cost_estimate=own_cost(token_count, width, sum(s[0] for s in segments)),
        name="own",
    )(level_bias, *operands)


def more_kernel(segments, old_count, count, level_bias, *refs):
    queries, refs = refs[:2], refs[2:]
    olds = [refs[3 * i : 3 * i + 3] for i in range(old_count)]
    refs = refs[3 * old_count :]
    sources, state = refs[:count], refs[count:]
    width = state[0].shape[0] * state[0].shape[1]
    state[2][...] = jnp.zeros(state[2].shape, F32)
    attend_heads(segments, sources, queries, level_bias, width, olds, keeper(state))


def attend_more(level_bias, queries, olds, sources, segments, name):
    token_count = queries[0].shape[2]
    width = sources[0].shape[-1]
    operands = (*queries, *[array for old in olds for array in old], *sources)
    return pl.pallas_call(
        functools.partial(more_kernel, segments, len(olds), len(sources)),
        out_shape=tuple(jax.ShapeDtypeStruct(s, F32) for s in state_shapes(token_count, width)),
        in_specs=[smem_spec()] + [vmem_spec()] * len(operands),
        out_specs=[vmem_spec()] * 3,
        compiler_params=pltpu.CompilerParams(vmem_limit_bytes=VMEM_BYTES),
        cost_estimate=own_cost(token_count, width, sum(s[0] for s in segments)),
        name=name,
    )(level_bias, *operands)


def last_kernel(segments, old_count, count, far_count, far_blocks, level_bias, *refs):
    queries, refs = refs[:2], refs[2:]
    olds = [refs[3 * i : 3 * i + 3] for i in range(old_count)]
    refs = refs[3 * old_count :]
    sources, outs = refs[:count], refs[count : count + 2]
    far_keys, mix_acc, tan_acc, turned, sems = refs[count + 2 :]
    width, token_count = outs[0].shape[1], outs[0].shape[0]
    line = lax.broadcasted_iota(jnp.int32, (far_count, FIELDS * far_count), 0)
    lane = lax.broadcasted_iota(jnp.int32, (far_count, FIELDS * far_count), 1)
    far_rows = jnp.concatenate([sources[i][begin:] for i, begin in far_blocks], axis=0)
    for index in range(FIELDS):
        select = (lane == line * FIELDS + index).astype(F32).astype(BF16)
        far_keys[index] = jnp.dot(select, far_rows, preferred_element_type=F32).astype(BF16)
    sources = sources + (far_keys,)

    def keep(head, top, total, row_total, mix, extra):
        inverse = 1.0 / total
        mix = mix * inverse
        mix_acc[head] = mix
        tan_acc[head] = extra * inverse - (row_total * inverse) * mix

    attend_heads(segments, sources, queries, level_bias, width, olds, keep)
    line = lax.broadcasted_iota(jnp.int32, (token_count, token_count), 0)
    lane = lax.broadcasted_iota(jnp.int32, (token_count, token_count), 1)
    unit = (line == lane).astype(F32).astype(BF16)
    sent = []
    for number, acc in enumerate((mix_acc, tan_acc)):
        flat = acc[...].reshape(width, token_count).astype(BF16)
        turned[number] = against(unit, flat).astype(BF16)
        more = chunk_copies(turned.at[number], outs[number], sems, number * FIELDS, FIELDS)
        for copy in more:
            copy.start()
        sent += more
    for copy in sent:
        copy.wait()


def attend_last(level_bias, queries, olds, sources, segments, far_count, far_blocks):
    token_count = queries[0].shape[2]
    width = sources[0].shape[-1]
    states = state_shapes(token_count, width)
    operands = (*queries, *[array for old in olds for array in old], *sources)
    return pl.pallas_call(
        functools.partial(
            last_kernel, segments, len(olds), len(sources), far_count, far_blocks
        ),
        out_shape=(jax.ShapeDtypeStruct((token_count, width), BF16),) * 2,
        in_specs=[smem_spec()] + [vmem_spec()] * len(operands),
        out_specs=[hbm_spec()] * 2,
        scratch_shapes=[
            pltpu.VMEM((FIELDS, far_count, width), BF16),
            pltpu.VMEM(states[0], F32),
            pltpu.VMEM(states[1], F32),
            pltpu.VMEM((2, token_count, width), BF16),
            pltpu.SemaphoreType.DMA((2 * FIELDS,)),
        ],
        compiler_params=pltpu.CompilerParams(vmem_limit_bytes=VMEM_BYTES),
        cost_estimate=own_cost(token_count, width, sum(s[0] for s in segments)),
        name="outer",
    )(level_bias, *operands)


def swap(block, axis, odd):
    count = lax.axis_size(axis)
    route = []
    for low in range(1 if odd else 0, count - 1, 2):
        route += [(low, low + 1), (low + 1, low)]
    return lax.ppermute(block, axis, route)


def part(source, begin, rows):
    return lambda refs, field, window: refs[source][field, begin : begin + rows, window]


def flat_part(source, stride, begin, rows):
    def read(refs, field, window):
        at = field * stride + begin
        return refs[source][at : at + rows, window]

    return read


def flat_toward_mate(source, stride, half):
    def read(refs, field, window):
        start = pl.multiple_of(field * stride + (lax.axis_index("row") % 2) * half, 16)
        return refs[source][pl.ds(start, half), window]

    return read


def toward_mate(source, half):
    def read(refs, field, window):
        start = pl.multiple_of((lax.axis_index("row") % 2) * half, half)
        return refs[source][field, pl.ds(start, half), window]

    return read


def send_to(block, axis, mask):
    return lax.ppermute(block, axis, [(i, i ^ mask) for i in range(lax.axis_size(axis))])


def gather_rows(far):
    count = lax.axis_size("row")
    if count <= 8:
        return [far] + [send_to(far, "row", mask) for mask in range(2, count, 2)]
    for bit in range(1, count.bit_length() - 1):
        far = jnp.concatenate([far, send_to(far, "row", 1 << bit)])
    return [far]


def body(
    query_field,
    key_field,
    value_field,
    query_tan,
    key_tan,
    value_tan,
    pool_near,
    pool_far,
    level_bias,
):
    window = query_field.shape[0]
    width = query_field.shape[2]
    cells = window * window
    strip, half = cells // 2, cells // 4
    near_count = cells // (NEAR_POOL * NEAR_POOL)
    row_count, col_count = lax.axis_size("row"), lax.axis_size("col")
    far_count = row_count * col_count
    flat = lambda field: field.reshape(cells, width)
    fields = tuple(flat(f) for f in (key_field, value_field, key_tan, value_tan))

    row_odd, col_even, col_odd, row_even, far = pack(fields, pool_near, pool_far)
    group = strip + near_count
    far = far[:FIELDS]
    got_col_even = swap(col_even, "col", False)
    got_row_odd = swap(row_odd, "row", True)
    got_col_odd = swap(col_odd, "col", True)
    got_row_even = swap(row_even, "row", False)

    *own_state, query, qtan = attend_own(
        level_bias,
        flat(query_field),
        flat(query_tan),
        fields,
        got_row_even,
        [
            (cells, "flag", 0, lambda refs, field, window: refs[field][:, window]),
            (strip, "flag", 0, part(4, 0, strip)),
            (near_count, "level", 0, part(4, strip, near_count)),
        ],
    )
    queries = (query, qtan)
    far_from = [send_to(far, "col", mask) for mask in range(2, min(col_count, 4))]
    mate_far = got_col_even[FIELDS * group : FIELDS * group + FIELDS]
    row_state = attend_more(
        level_bias,
        queries,
        [],
        (got_row_odd,),
        [(strip, "flag", 1, part(0, 0, strip))],
        "row_strip",
    )
    got_row_odd, stats = lax.optimization_barrier((got_row_odd, row_state[2]))
    row_state = (row_state[0], row_state[1], stats)
    to_even, to_odd = got_row_odd[:, :half], got_row_odd[:, half:]
    got_col_even, got_col_odd, to_even, to_odd, far_from = lax.optimization_barrier(
        (got_col_even, got_col_odd, to_even, to_odd, far_from)
    )
    got_outer_even = swap(to_even, "col", False)
    got_outer_odd = swap(to_odd, "col", True)
    got_inner_even = swap(got_col_even, "row", False)
    got_inner_odd = swap(got_col_odd, "row", False)
    far = jnp.concatenate([far, mate_far, *far_from])
    for bit in range(2, col_count.bit_length() - 1):
        far = jnp.concatenate([far, send_to(far, "col", 1 << bit)])
    far = jnp.concatenate([far, send_to(far, "row", 1)])

    state = attend_more(
        level_bias,
        queries,
        [row_state],
        (got_col_even, got_col_odd),
        [
            (strip, "flag", 0, flat_part(0, group, 0, strip)),
            (strip, "flag", 2, part(1, 0, strip)),
        ],
        "strips",
    )
    far, stats = lax.optimization_barrier((far, state[2]))
    state = (state[0], state[1], stats)
    far_blocks = gather_rows(far)
    state = attend_more(
        level_bias,
        queries,
        [state],
        (got_inner_even, got_inner_odd, got_col_even, row_even),
        [
            (half, "flag", 0, flat_toward_mate(0, group, half)),
            (half, "flag", 2, toward_mate(1, half)),
            (near_count, "level", 0, flat_part(0, group, strip, near_count)),
            (near_count, "level", 0, flat_part(2, group, strip, near_count)),
            (near_count, "level", 0, part(3, strip, near_count)),
        ],
        "inner",
    )
    mixed, mixed_tan = attend_last(
        level_bias,
        queries,
        [state, own_state],
        (got_outer_even, got_outer_odd, *far_blocks),
        [
            (half, "flag", 1, part(0, 0, half)),
            (half, "flag", 3, part(1, 0, half)),
            (far_count, "level", 1, part(2 + len(far_blocks), 0, far_count)),
        ],
        far_count,
        tuple((2 + number, 0) for number in range(len(far_blocks))),
    )
    shape = (window, window, width)
    return (mixed.reshape(shape), mixed_tan.reshape(shape))


def solution(mesh):
    field = P("row", "col", None)
    return jax.shard_map(
        body,
        mesh=mesh,
        in_specs=(field,) * 6 + (P(),) * 3,
        out_specs=(field, field),
        check_vma=False,
    )
```

```python
import functools

import jax
import jax.numpy as jnp
from jax import lax
from jax.experimental import pallas as pl
from jax.experimental.pallas import tpu as pltpu
from jax.sharding import PartitionSpec as P

HEADS = 16
RIM = 8
NEAR_POOL = 4
LOG2E = 1.4426950408889634
OFF = -1e30
PACK_BYTES = 60 * 1024 * 1024
VMEM_BYTES = 28 * 1024 * 1024
LANES = 128
FIELDS = 4
BF16 = jnp.bfloat16
F32 = jnp.float32


def vmem_spec():
    return pl.BlockSpec(memory_space=pltpu.VMEM)


def smem_spec():
    return pl.BlockSpec(memory_space=pltpu.SMEM)


def hbm_spec():
    return pl.BlockSpec(memory_space=pltpu.HBM)


def any_spec():
    return pl.BlockSpec(memory_space=pl.ANY)


def against(left, right):
    return lax.dot_general(left, right, (((1,), (1,)), ((), ())), preferred_element_type=F32)


def chunk_copies(source, target, sems, first, parts):
    rows = source.shape[0]
    step = -(-rows // parts)
    if len(source.shape) == 2:
        step = -(-step // 16) * 16
    copies = []
    for number, begin in enumerate(range(0, rows, step)):
        at = pl.ds(begin, min(step, rows - begin))
        copies.append(pltpu.make_async_copy(source.at[at], target.at[at], sems.at[first + number]))
    return copies


def split3(weights):
    high = weights.astype(BF16)
    rest = weights - high.astype(F32)
    mid = rest.astype(BF16)
    low = (rest - mid.astype(F32)).astype(BF16)
    return jnp.concatenate([high, mid, low], axis=0)


def pool_weights(pool_near, pool_far, cells):
    window = 2 * RIM
    near_side = window // NEAR_POOL
    near_count = near_side * near_side
    lane = lax.broadcasted_iota(jnp.int32, (near_count, cells), 1)
    line = lax.broadcasted_iota(jnp.int32, (near_count, cells), 0)
    row, col = lane // window, lane % window
    near = jnp.zeros((near_count, cells), F32)
    for p in range(NEAR_POOL):
        for q in range(NEAR_POOL):
            hit = (row % NEAR_POOL == p) & (col % NEAR_POOL == q)
            near = jnp.where(hit, pool_near[p, q], near)
    block = (row // NEAR_POOL) * near_side + col // NEAR_POOL
    near = split3(jnp.where(line == block, near, 0.0))
    spread = (line == col).astype(F32).astype(BF16)
    far = jnp.dot(split3(pool_far), spread, preferred_element_type=F32)
    far_line = lax.broadcasted_iota(jnp.int32, far.shape, 0) % window
    far_lane = lax.broadcasted_iota(jnp.int32, far.shape, 1) // window
    far = jnp.where(far_line == far_lane, far, 0.0)
    rows = [
        jnp.sum(far[i * window : (i + 1) * window], axis=0, keepdims=True) for i in range(3)
    ]
    rows.append(jnp.zeros((near_count - 3, cells), F32))
    return jnp.concatenate([near, jnp.concatenate(rows, axis=0).astype(BF16)], axis=0)


def halves(block, width):
    cells = block.shape[0]
    wide = block.astype(F32).reshape(cells // (2 * RIM), 2, RIM, width)
    left = wide[:, 0].reshape(cells // 2, width).astype(BF16)
    right = wide[:, 1].reshape(cells // 2, width).astype(BF16)
    return left, right


def pack_kernel(pool_near, pool_far, *refs):
    sources, outs = refs[:FIELDS], refs[FIELDS : FIELDS + 5]
    held = refs[FIELDS + 5]
    kept, sems, out_sems = refs[FIELDS + 6 : -2], refs[-2], refs[-1]
    cells, width = sources[0].shape
    strip, half = cells // 2, cells // 4
    near_count = cells // (NEAR_POOL * NEAR_POOL)
    row_is_even = lax.axis_index("row") % 2 == 0
    col_is_even = lax.axis_index("col") % 2 == 0
    copies = []
    for index, source in enumerate(sources):
        copies += chunk_copies(source, held.at[index], sems, 2 * index, 2)
    for copy in copies:
        copy.start()
    weights = pool_weights(pool_near, pool_far[...], cells)
    far_rows = []
    sent = []
    for index in range(FIELDS):
        copies[2 * index].wait()
        copies[2 * index + 1].wait()
        block = held[index]
        left, right = halves(block, width)
        even = jnp.where(col_is_even, right, left)
        odd = jnp.where(col_is_even, left, right)
        outer = lambda side: jnp.where(row_is_even, side[:half], side[half:])
        pooled = jnp.dot(weights, block, preferred_element_type=F32)
        near = pooled[:near_count] + (
            pooled[near_count : 2 * near_count] + pooled[2 * near_count : 3 * near_count]
        )
        near = near.astype(BF16)
        far = pooled[3 * near_count :]
        far_rows.append(far[0:1] + (far[1:2] + far[2:3]))
        kept[0][index, :half] = outer(even)
        kept[0][index, half:] = outer(odd)
        at = index * (strip + near_count)
        kept[1][at : at + strip] = even
        kept[1][at + strip : at + strip + near_count] = near
        kept[2][index] = odd
        kept[3][index, :strip] = jnp.where(row_is_even, block[strip:], block[:strip])
        kept[3][index, strip:] = near
        for number in (0, 2, 3):
            copy = pltpu.make_async_copy(
                kept[number].at[index], outs[number].at[index], out_sems.at[4 * index + number]
            )
            copy.start()
            sent.append(copy)
    far_rows.append(jnp.zeros((16 - FIELDS, width), F32))
    kept[4][...] = jnp.concatenate(far_rows, axis=0).astype(BF16)
    kept[1][FIELDS * (strip + near_count) :] = kept[4][...]
    for number, source in ((1, 1), (4 * FIELDS, 4)):
        copy = pltpu.make_async_copy(kept[source], outs[source], out_sems.at[number])
        copy.start()
        sent.append(copy)
    for copy in sent:
        copy.wait()


def pack(fields, pool_near, pool_far):
    cells, width = fields[0].shape
    strip = cells // 2
    near_count = cells // (NEAR_POOL * NEAR_POOL)
    shapes = [
        (FIELDS, strip, width),
        (FIELDS * (strip + near_count) + 16, width),
        (FIELDS, strip, width),
        (FIELDS, strip + near_count, width),
        (16, width),
    ]
    return pl.pallas_call(
        pack_kernel,
        out_shape=tuple(jax.ShapeDtypeStruct(s, BF16) for s in shapes),
        in_specs=[smem_spec(), vmem_spec()] + [hbm_spec()] * FIELDS,
        out_specs=[hbm_spec()] * len(shapes),
        scratch_shapes=[pltpu.VMEM((FIELDS, cells, width), BF16)]
        + [pltpu.VMEM(s, BF16) for s in shapes]
        + [pltpu.SemaphoreType.DMA((2 * FIELDS,)), pltpu.SemaphoreType.DMA((4 * FIELDS + 1,))],
        compiler_params=pltpu.CompilerParams(vmem_limit_bytes=PACK_BYTES),
        name="pack",
    )(pool_near, pool_far, *fields)


TOGETHER = 2


def masked_start(head, head_dim, width):
    return min(head * head_dim // LANES, (width - 2 * LANES) // LANES) * LANES


def turn_queries(raw, turned, masked):
    width = raw.shape[1]
    head_dim = width // HEADS
    span = 2 * LANES
    line = lax.broadcasted_iota(jnp.int32, (LANES, LANES), 0)
    lane = lax.broadcasted_iota(jnp.int32, (LANES, LANES), 1)
    unit = (line == lane).astype(F32).astype(BF16)
    for at in range(0, width, LANES):
        turned[at : at + LANES] = against(unit, raw[:, at : at + LANES]).astype(BF16)
    channel = lax.broadcasted_iota(jnp.int32, (span, raw.shape[0]), 0)
    for head in range(HEADS):
        start = masked_start(head, head_dim, width)
        low = head * head_dim - start
        keep = ((channel >= low) & (channel < low + head_dim)).astype(F32).astype(BF16)
        masked[head] = turned[start : start + span] * keep


def device_flags():
    row, col = lax.axis_index("row"), lax.axis_index("col")
    row_edge = (row == 0) | (row == lax.axis_size("row") - 1)
    col_edge = (col == 0) | (col == lax.axis_size("col") - 1)
    off = lambda edge: jnp.where(edge, F32(OFF), F32(0.0))
    return (F32(0.0), off(row_edge), off(col_edge), off(row_edge | col_edge))


def head_products(head, segments, refs, queries, width):
    head_dim = width // HEADS
    start = head * head_dim // LANES * LANES
    low = head * head_dim - start
    one_tile = low + head_dim <= LANES
    span = LANES if one_tile else 2 * LANES
    window = slice(start, start + span)
    at = start - masked_start(head, head_dim, width)
    rows_of = lambda field: jnp.concatenate(
        [reader(refs, field, window) for _, _, _, reader in segments], axis=0
    )
    key, value, key_tan, value_tan = (rows_of(field) for field in range(FIELDS))
    query, query_tan = (ref[head, at : at + span] for ref in queries)
    scores = jnp.dot(key, query, preferred_element_type=F32)
    if one_tile:
        slopes = jnp.dot(
            jnp.concatenate([key, key_tan], axis=1),
            jnp.concatenate([query_tan, query], axis=0),
            preferred_element_type=F32,
        )
    else:
        slopes = jnp.dot(key, query_tan, preferred_element_type=F32)
        slopes = slopes + jnp.dot(key_tan, query, preferred_element_type=F32)
    line = lax.broadcasted_iota(jnp.int32, (head_dim + 8, span), 0)
    lane = lax.broadcasted_iota(jnp.int32, (head_dim + 8, span), 1)
    pick = ((lane == line + low) & (line < head_dim)).astype(F32).astype(BF16)
    ones_line = lax.broadcasted_iota(jnp.int32, (8, value.shape[0]), 0)
    turned = jnp.concatenate(
        [
            against(pick, value)[:head_dim],
            (ones_line == 0).astype(F32),
            against(pick, value_tan),
        ],
        axis=0,
    )
    return scores, slopes, turned.astype(BF16)


def head_result(head, segments, level_bias, flags, products, olds, width):
    scores, slopes, turned = products
    head_dim = width // HEADS
    pad_dim = head_dim + 8
    scale = head_dim**-0.5
    bias = []
    top = None
    at = 0
    for rows, kind, number, _ in segments:
        amount = flags[number] if kind == "flag" else level_bias[number, head] * LOG2E
        bias.append(amount)
        part = jnp.max(scores[at : at + rows], axis=0, keepdims=True) * (scale * LOG2E) + amount
        top = part if top is None else jnp.maximum(top, part)
        at += rows
    for old in olds:
        top = jnp.maximum(top, old[2][head, 0:1])
    weights_low, product_low = [], []
    at = 0
    for (rows, _, _, _), amount in zip(segments, bias):
        weights = jnp.exp2(scores[at : at + rows] * (scale * LOG2E) + (amount - top))
        weights_low.append(weights.astype(BF16))
        product_low.append((weights * slopes[at : at + rows]).astype(BF16))
        at += rows
    both = jnp.dot(turned, jnp.concatenate(weights_low, axis=0), preferred_element_type=F32)
    extra = jnp.dot(
        turned[:pad_dim], jnp.concatenate(product_low, axis=0), preferred_element_type=F32
    )
    mix = both[:head_dim]
    total = both[head_dim : head_dim + 1]
    row_total = extra[head_dim : head_dim + 1] * scale
    extra = extra[:head_dim] * scale + both[pad_dim : pad_dim + head_dim]
    for old in olds:
        fade = jnp.exp2(old[2][head, 0:1] - top)
        total = total + fade * old[2][head, 1:2]
        row_total = row_total + fade * old[2][head, 2:3]
        mix = mix + fade * old[0][head]
        extra = extra + fade * old[1][head]
    return top, total, row_total, mix, extra


def attend_heads(segments, refs, queries, level_bias, width, olds, keep):
    flags = device_flags()
    stages = [range(first, first + TOGETHER) for first in range(0, HEADS, TOGETHER)]
    make = lambda heads: [head_products(head, segments, refs, queries, width) for head in heads]
    ready = make(stages[0])
    for number, heads in enumerate(stages):
        coming = make(stages[number + 1]) if number + 1 < len(stages) else None
        for head, products in zip(heads, ready):
            keep(head, *head_result(head, segments, level_bias, flags, products, olds, width))
        ready = coming


def keeper(state):
    def keep(head, top, total, row_total, mix, extra):
        state[0][head] = mix
        state[1][head] = extra
        state[2][head, 0:1] = top
        state[2][head, 1:2] = total
        state[2][head, 2:3] = row_total

    return keep


def own_kernel(segments, level_bias, query, qtan, *refs):
    sources, state = refs[: FIELDS + 1], refs[FIELDS + 1 : FIELDS + 4]
    masked, turned = refs[FIELDS + 4 : FIELDS + 6], refs[FIELDS + 6]
    state[2][...] = jnp.zeros(state[2].shape, F32)
    for raw, target in zip((query, qtan), masked):
        turn_queries(raw, turned, target)
    attend_heads(segments, sources, masked, level_bias, query.shape[1], [], keeper(state))


def state_shapes(token_count, width):
    wide = (HEADS, width // HEADS, token_count)
    return (wide, wide, (HEADS, 8, token_count))


def own_cost(token_count, width, key_count):
    return pl.CostEstimate(
        flops=token_count * key_count * HEADS,
        bytes_accessed=token_count * width,
        transcendentals=0,
    )


def attend_own(level_bias, query, qtan, fields, mate, segments):
    token_count, width = query.shape
    states = state_shapes(token_count, width)
    masked = (HEADS, 2 * LANES, token_count)
    operands = (query, qtan, *fields, mate)
    return pl.pallas_call(
        functools.partial(own_kernel, segments),
        out_shape=tuple(jax.ShapeDtypeStruct(s, F32) for s in states)
        + (jax.ShapeDtypeStruct(masked, BF16),) * 2,
        in_specs=[smem_spec()] + [vmem_spec()] * len(operands),
        out_specs=[vmem_spec()] * 5,
        scratch_shapes=[pltpu.VMEM((width, token_count), BF16)],
        compiler_params=pltpu.CompilerParams(vmem_limit_bytes=VMEM_BYTES),
        cost_estimate=own_cost(token_count, width, sum(s[0] for s in segments)),
        name="own",
    )(level_bias, *operands)


def more_kernel(segments, old_count, count, level_bias, *refs):
    queries, refs = refs[:2], refs[2:]
    olds = [refs[3 * i : 3 * i + 3] for i in range(old_count)]
    refs = refs[3 * old_count :]
    sources, state = refs[:count], refs[count:]
    width = state[0].shape[0] * state[0].shape[1]
    state[2][...] = jnp.zeros(state[2].shape, F32)
    attend_heads(segments, sources, queries, level_bias, width, olds, keeper(state))


def attend_more(level_bias, queries, olds, sources, segments, name):
    token_count = queries[0].shape[2]
    width = sources[0].shape[-1]
    operands = (*queries, *[array for old in olds for array in old], *sources)
    return pl.pallas_call(
        functools.partial(more_kernel, segments, len(olds), len(sources)),
        out_shape=tuple(jax.ShapeDtypeStruct(s, F32) for s in state_shapes(token_count, width)),
        in_specs=[smem_spec()] + [vmem_spec()] * len(operands),
        out_specs=[vmem_spec()] * 3,
        compiler_params=pltpu.CompilerParams(vmem_limit_bytes=VMEM_BYTES),
        cost_estimate=own_cost(token_count, width, sum(s[0] for s in segments)),
        name=name,
    )(level_bias, *operands)


def last_kernel(segments, old_count, count, far_count, far_blocks, level_bias, *refs):
    queries, refs = refs[:2], refs[2:]
    olds = [refs[3 * i : 3 * i + 3] for i in range(old_count)]
    refs = refs[3 * old_count :]
    sources, outs = refs[:count], refs[count : count + 2]
    far_keys, mix_acc, tan_acc, turned, sems = refs[count + 2 :]
    width, token_count = outs[0].shape[1], outs[0].shape[0]
    line = lax.broadcasted_iota(jnp.int32, (far_count, FIELDS * far_count), 0)
    lane = lax.broadcasted_iota(jnp.int32, (far_count, FIELDS * far_count), 1)
    far_rows = jnp.concatenate([sources[i][begin:] for i, begin in far_blocks], axis=0)
    for index in range(FIELDS):
        select = (lane == line * FIELDS + index).astype(F32).astype(BF16)
        far_keys[index] = jnp.dot(select, far_rows, preferred_element_type=F32).astype(BF16)
    sources = sources + (far_keys,)

    def keep(head, top, total, row_total, mix, extra):
        inverse = 1.0 / total
        mix = mix * inverse
        mix_acc[head] = mix
        tan_acc[head] = extra * inverse - (row_total * inverse) * mix

    attend_heads(segments, sources, queries, level_bias, width, olds, keep)
    line = lax.broadcasted_iota(jnp.int32, (token_count, token_count), 0)
    lane = lax.broadcasted_iota(jnp.int32, (token_count, token_count), 1)
    unit = (line == lane).astype(F32).astype(BF16)
    sent = []
    for number, acc in enumerate((mix_acc, tan_acc)):
        flat = acc[...].reshape(width, token_count).astype(BF16)
        turned[number] = against(unit, flat).astype(BF16)
        more = chunk_copies(turned.at[number], outs[number], sems, number * FIELDS, FIELDS)
        for copy in more:
            copy.start()
        sent += more
    for copy in sent:
        copy.wait()


def attend_last(level_bias, queries, olds, sources, segments, far_count, far_blocks):
    token_count = queries[0].shape[2]
    width = sources[0].shape[-1]
    states = state_shapes(token_count, width)
    operands = (*queries, *[array for old in olds for array in old], *sources)
    return pl.pallas_call(
        functools.partial(
            last_kernel, segments, len(olds), len(sources), far_count, far_blocks
        ),
        out_shape=(jax.ShapeDtypeStruct((token_count, width), BF16),) * 2,
        in_specs=[smem_spec()] + [vmem_spec()] * len(operands),
        out_specs=[hbm_spec()] * 2,
        scratch_shapes=[
            pltpu.VMEM((FIELDS, far_count, width), BF16),
            pltpu.VMEM(states[0], F32),
            pltpu.VMEM(states[1], F32),
            pltpu.VMEM((2, token_count, width), BF16),
            pltpu.SemaphoreType.DMA((2 * FIELDS,)),
        ],
        compiler_params=pltpu.CompilerParams(vmem_limit_bytes=VMEM_BYTES),
        cost_estimate=own_cost(token_count, width, sum(s[0] for s in segments)),
        name="outer",
    )(level_bias, *operands)


def swap(block, axis, odd):
    count = lax.axis_size(axis)
    route = []
    for low in range(1 if odd else 0, count - 1, 2):
        route += [(low, low + 1), (low + 1, low)]
    return lax.ppermute(block, axis, route)


def part(source, begin, rows):
    return lambda refs, field, window: refs[source][field, begin : begin + rows, window]


def flat_part(source, stride, begin, rows):
    def read(refs, field, window):
        at = field * stride + begin
        return refs[source][at : at + rows, window]

    return read


def flat_toward_mate(source, stride, half):
    def read(refs, field, window):
        start = pl.multiple_of(field * stride + (lax.axis_index("row") % 2) * half, 16)
        return refs[source][pl.ds(start, half), window]

    return read


def toward_mate(source, half):
    def read(refs, field, window):
        start = pl.multiple_of((lax.axis_index("row") % 2) * half, half)
        return refs[source][field, pl.ds(start, half), window]

    return read


def send_to(block, axis, mask):
    return lax.ppermute(block, axis, [(i, i ^ mask) for i in range(lax.axis_size(axis))])


def join(blocks):
    rows = sum(block.shape[0] for block in blocks)
    total, at = None, 0
    for block in blocks:
        count = block.shape[0]
        padded = jnp.pad(block, ((at, rows - at - count), (0, 0)))
        total = padded if total is None else total + padded
        at += count
    return total


def gather_rows(far):
    count = lax.axis_size("row")
    if count <= 8:
        return [far] + [send_to(far, "row", mask) for mask in range(2, count, 2)]
    for bit in range(1, count.bit_length() - 1):
        far = join([far, send_to(far, "row", 1 << bit)])
    return [far]


def body(
    query_field,
    key_field,
    value_field,
    query_tan,
    key_tan,
    value_tan,
    pool_near,
    pool_far,
    level_bias,
):
    window = query_field.shape[0]
    width = query_field.shape[2]
    cells = window * window
    strip, half = cells // 2, cells // 4
    near_count = cells // (NEAR_POOL * NEAR_POOL)
    row_count, col_count = lax.axis_size("row"), lax.axis_size("col")
    far_count = row_count * col_count
    flat = lambda field: field.reshape(cells, width)
    fields = tuple(flat(f) for f in (key_field, value_field, key_tan, value_tan))

    row_odd, col_even, col_odd, row_even, far = pack(fields, pool_near, pool_far)
    group = strip + near_count
    far = far[:FIELDS]
    got_col_even = swap(col_even, "col", False)
    got_row_odd = swap(row_odd, "row", True)
    got_col_odd = swap(col_odd, "col", True)
    got_row_even = swap(row_even, "row", False)

    *own_state, query, qtan = attend_own(
        level_bias,
        flat(query_field),
        flat(query_tan),
        fields,
        got_row_even,
        [
            (cells, "flag", 0, lambda refs, field, window: refs[field][:, window]),
            (strip, "flag", 0, part(4, 0, strip)),
            (near_count, "level", 0, part(4, strip, near_count)),
        ],
    )
    queries = (query, qtan)
    far_from = [send_to(far, "col", mask) for mask in range(2, min(col_count, 4))]
    mate_far = got_col_even[FIELDS * group : FIELDS * group + FIELDS]
    row_state = attend_more(
        level_bias,
        queries,
        [],
        (got_row_odd,),
        [(strip, "flag", 1, part(0, 0, strip))],
        "row_strip",
    )
    got_row_odd, stats = lax.optimization_barrier((got_row_odd, row_state[2]))
    row_state = (row_state[0], row_state[1], stats)
    to_even, to_odd = got_row_odd[:, :half], got_row_odd[:, half:]
    got_col_even, got_col_odd, to_even, to_odd, far_from = lax.optimization_barrier(
        (got_col_even, got_col_odd, to_even, to_odd, far_from)
    )
    got_outer_even = swap(to_even, "col", False)
    got_outer_odd = swap(to_odd, "col", True)
    got_inner_even = swap(got_col_even, "row", False)
    got_inner_odd = swap(got_col_odd, "row", False)
    far = join([far, mate_far, *far_from])
    for bit in range(2, col_count.bit_length() - 1):
        far = join([far, send_to(far, "col", 1 << bit)])
    far = join([far, send_to(far, "row", 1)])

    state = attend_more(
        level_bias,
        queries,
        [row_state],
        (got_col_even, got_col_odd),
        [
            (strip, "flag", 0, flat_part(0, group, 0, strip)),
            (strip, "flag", 2, part(1, 0, strip)),
        ],
        "strips",
    )
    far, stats = lax.optimization_barrier((far, state[2]))
    state = (state[0], state[1], stats)
    far_blocks = gather_rows(far)
    state = attend_more(
        level_bias,
        queries,
        [state],
        (got_inner_even, got_inner_odd, got_col_even, row_even),
        [
            (half, "flag", 0, flat_toward_mate(0, group, half)),
            (half, "flag", 2, toward_mate(1, half)),
            (near_count, "level", 0, flat_part(0, group, strip, near_count)),
            (near_count, "level", 0, flat_part(2, group, strip, near_count)),
            (near_count, "level", 0, part(3, strip, near_count)),
        ],
        "inner",
    )
    mixed, mixed_tan = attend_last(
        level_bias,
        queries,
        [state, own_state],
        (got_outer_even, got_outer_odd, *far_blocks),
        [
            (half, "flag", 1, part(0, 0, half)),
            (half, "flag", 3, part(1, 0, half)),
            (far_count, "level", 1, part(2 + len(far_blocks), 0, far_count)),
        ],
        far_count,
        tuple((2 + number, 0) for number in range(len(far_blocks))),
    )
    shape = (window, window, width)
    return (mixed.reshape(shape), mixed_tan.reshape(shape))


def solution(mesh):
    field = P("row", "col", None)
    return jax.shard_map(
        body,
        mesh=mesh,
        in_specs=(field,) * 6 + (P(),) * 3,
        out_specs=(field, field),
        check_vma=False,
    )
```

```python
import functools

import jax
import jax.numpy as jnp
from jax import lax
from jax.experimental import pallas as pl
from jax.experimental.pallas import tpu as pltpu
from jax.sharding import PartitionSpec as P

HEADS = 16
RIM = 8
NEAR_POOL = 4
LOG2E = 1.4426950408889634
OFF = -1e30
PACK_BYTES = 60 * 1024 * 1024
VMEM_BYTES = 28 * 1024 * 1024
LANES = 128
FIELDS = 4
BF16 = jnp.bfloat16
F32 = jnp.float32


def vmem_spec():
    return pl.BlockSpec(memory_space=pltpu.VMEM)


def smem_spec():
    return pl.BlockSpec(memory_space=pltpu.SMEM)


def hbm_spec():
    return pl.BlockSpec(memory_space=pltpu.HBM)


def any_spec():
    return pl.BlockSpec(memory_space=pl.ANY)


def against(left, right):
    return lax.dot_general(left, right, (((1,), (1,)), ((), ())), preferred_element_type=F32)


def chunk_copies(source, target, sems, first, parts):
    rows = source.shape[0]
    step = -(-rows // parts)
    if len(source.shape) == 2:
        step = -(-step // 16) * 16
    copies = []
    for number, begin in enumerate(range(0, rows, step)):
        at = pl.ds(begin, min(step, rows - begin))
        copies.append(pltpu.make_async_copy(source.at[at], target.at[at], sems.at[first + number]))
    return copies


def split3(weights):
    high = weights.astype(BF16)
    rest = weights - high.astype(F32)
    mid = rest.astype(BF16)
    low = (rest - mid.astype(F32)).astype(BF16)
    return jnp.concatenate([high, mid, low], axis=0)


def pool_weights(pool_near, pool_far, cells):
    window = 2 * RIM
    near_side = window // NEAR_POOL
    near_count = near_side * near_side
    lane = lax.broadcasted_iota(jnp.int32, (near_count, cells), 1)
    line = lax.broadcasted_iota(jnp.int32, (near_count, cells), 0)
    row, col = lane // window, lane % window
    near = jnp.zeros((near_count, cells), F32)
    for p in range(NEAR_POOL):
        for q in range(NEAR_POOL):
            hit = (row % NEAR_POOL == p) & (col % NEAR_POOL == q)
            near = jnp.where(hit, pool_near[p, q], near)
    block = (row // NEAR_POOL) * near_side + col // NEAR_POOL
    near = split3(jnp.where(line == block, near, 0.0))
    spread = (line == col).astype(F32).astype(BF16)
    far = jnp.dot(split3(pool_far), spread, preferred_element_type=F32)
    far_line = lax.broadcasted_iota(jnp.int32, far.shape, 0) % window
    far_lane = lax.broadcasted_iota(jnp.int32, far.shape, 1) // window
    far = jnp.where(far_line == far_lane, far, 0.0)
    rows = [
        jnp.sum(far[i * window : (i + 1) * window], axis=0, keepdims=True) for i in range(3)
    ]
    rows.append(jnp.zeros((near_count - 3, cells), F32))
    return jnp.concatenate([near, jnp.concatenate(rows, axis=0).astype(BF16)], axis=0)


def halves(block, width):
    cells = block.shape[0]
    wide = block.astype(F32).reshape(cells // (2 * RIM), 2, RIM, width)
    left = wide[:, 0].reshape(cells // 2, width).astype(BF16)
    right = wide[:, 1].reshape(cells // 2, width).astype(BF16)
    return left, right


def pack_kernel(pool_near, pool_far, *refs):
    sources, outs = refs[:FIELDS], refs[FIELDS : FIELDS + 5]
    held = refs[FIELDS + 5]
    kept, sems, out_sems = refs[FIELDS + 6 : -2], refs[-2], refs[-1]
    cells, width = sources[0].shape
    strip, half = cells // 2, cells // 4
    near_count = cells // (NEAR_POOL * NEAR_POOL)
    row_is_even = lax.axis_index("row") % 2 == 0
    col_is_even = lax.axis_index("col") % 2 == 0
    copies = []
    for index, source in enumerate(sources):
        copies += chunk_copies(source, held.at[index], sems, 2 * index, 2)
    for copy in copies:
        copy.start()
    weights = pool_weights(pool_near, pool_far[...], cells)
    far_rows = []
    sent = []
    for index in range(FIELDS):
        copies[2 * index].wait()
        copies[2 * index + 1].wait()
        block = held[index]
        left, right = halves(block, width)
        even = jnp.where(col_is_even, right, left)
        odd = jnp.where(col_is_even, left, right)
        outer = lambda side: jnp.where(row_is_even, side[:half], side[half:])
        pooled = jnp.dot(weights, block, preferred_element_type=F32)
        near = pooled[:near_count] + (
            pooled[near_count : 2 * near_count] + pooled[2 * near_count : 3 * near_count]
        )
        near = near.astype(BF16)
        far = pooled[3 * near_count :]
        far_rows.append(far[0:1] + (far[1:2] + far[2:3]))
        kept[0][index, :half] = outer(even)
        kept[0][index, half:] = outer(odd)
        at = index * (strip + near_count)
        kept[1][at : at + strip] = even
        kept[1][at + strip : at + strip + near_count] = near
        kept[2][index] = odd
        kept[3][index, :strip] = jnp.where(row_is_even, block[strip:], block[:strip])
        kept[3][index, strip:] = near
        for number in (0, 2, 3):
            copy = pltpu.make_async_copy(
                kept[number].at[index], outs[number].at[index], out_sems.at[4 * index + number]
            )
            copy.start()
            sent.append(copy)
    far_rows.append(jnp.zeros((16 - FIELDS, width), F32))
    kept[4][...] = jnp.concatenate(far_rows, axis=0).astype(BF16)
    kept[1][FIELDS * (strip + near_count) :] = kept[4][...]
    for number, source in ((1, 1), (4 * FIELDS, 4)):
        copy = pltpu.make_async_copy(kept[source], outs[source], out_sems.at[number])
        copy.start()
        sent.append(copy)
    for copy in sent:
        copy.wait()


def pack(fields, pool_near, pool_far):
    cells, width = fields[0].shape
    strip = cells // 2
    near_count = cells // (NEAR_POOL * NEAR_POOL)
    shapes = [
        (FIELDS, strip, width),
        (FIELDS * (strip + near_count) + 16, width),
        (FIELDS, strip, width),
        (FIELDS, strip + near_count, width),
        (16, width),
    ]
    return pl.pallas_call(
        pack_kernel,
        out_shape=tuple(jax.ShapeDtypeStruct(s, BF16) for s in shapes),
        in_specs=[smem_spec(), vmem_spec()] + [hbm_spec()] * FIELDS,
        out_specs=[hbm_spec()] * len(shapes),
        scratch_shapes=[pltpu.VMEM((FIELDS, cells, width), BF16)]
        + [pltpu.VMEM(s, BF16) for s in shapes]
        + [pltpu.SemaphoreType.DMA((2 * FIELDS,)), pltpu.SemaphoreType.DMA((4 * FIELDS + 1,))],
        compiler_params=pltpu.CompilerParams(vmem_limit_bytes=PACK_BYTES),
        name="pack",
    )(pool_near, pool_far, *fields)


def forward_kernel(col_even, col_odd, first, second, third):
    strip = col_odd.shape[1]
    half = strip // 2
    near_count = (col_even.shape[0] - 16) // FIELDS - strip
    group = strip + near_count
    start = (1 - lax.axis_index("row") % 2) * half
    even = lambda index: col_even[pl.ds(pl.multiple_of(index * group + start, 16), half)]
    odd = lambda index: col_odd[index, pl.ds(pl.multiple_of(start, half), half)]
    for index in range(FIELDS - 1):
        first[index * half : (index + 1) * half] = even(index)
        second[index * half : (index + 1) * half] = odd(index)
    third[:half] = even(FIELDS - 1)
    third[half:strip] = odd(FIELDS - 1)
    for index in range(FIELDS):
        at = strip + index * near_count
        third[at : at + near_count] = col_even[index * group + strip : (index + 1) * group]


def forward(col_even, col_odd):
    _, strip, width = col_odd.shape
    shape = jax.ShapeDtypeStruct(((FIELDS - 1) * strip // 2, width), BF16)
    return pl.pallas_call(
        forward_kernel,
        out_shape=(shape,) * 3,
        in_specs=[vmem_spec()] * 2,
        out_specs=[vmem_spec()] * 3,
        compiler_params=pltpu.CompilerParams(vmem_limit_bytes=VMEM_BYTES),
        name="forward",
    )(col_even, col_odd)


TOGETHER = 2


def masked_start(head, head_dim, width):
    return min(head * head_dim // LANES, (width - 2 * LANES) // LANES) * LANES


def turn_queries(raw, turned, masked):
    width = raw.shape[1]
    head_dim = width // HEADS
    span = 2 * LANES
    line = lax.broadcasted_iota(jnp.int32, (LANES, LANES), 0)
    lane = lax.broadcasted_iota(jnp.int32, (LANES, LANES), 1)
    unit = (line == lane).astype(F32).astype(BF16)
    for at in range(0, width, LANES):
        turned[at : at + LANES] = against(unit, raw[:, at : at + LANES]).astype(BF16)
    channel = lax.broadcasted_iota(jnp.int32, (span, raw.shape[0]), 0)
    for head in range(HEADS):
        start = masked_start(head, head_dim, width)
        low = head * head_dim - start
        keep = ((channel >= low) & (channel < low + head_dim)).astype(F32).astype(BF16)
        masked[head] = turned[start : start + span] * keep


def device_flags():
    row, col = lax.axis_index("row"), lax.axis_index("col")
    row_edge = (row == 0) | (row == lax.axis_size("row") - 1)
    col_edge = (col == 0) | (col == lax.axis_size("col") - 1)
    off = lambda edge: jnp.where(edge, F32(OFF), F32(0.0))
    return (F32(0.0), off(row_edge), off(col_edge), off(row_edge | col_edge))


def head_products(head, segments, refs, queries, width):
    head_dim = width // HEADS
    start = head * head_dim // LANES * LANES
    low = head * head_dim - start
    one_tile = low + head_dim <= LANES
    span = LANES if one_tile else 2 * LANES
    window = slice(start, start + span)
    at = start - masked_start(head, head_dim, width)
    rows_of = lambda field: jnp.concatenate(
        [reader(refs, field, window) for _, _, _, reader in segments], axis=0
    )
    key, value, key_tan, value_tan = (rows_of(field) for field in range(FIELDS))
    query, query_tan = (ref[head, at : at + span] for ref in queries)
    scores = jnp.dot(key, query, preferred_element_type=F32)
    if one_tile:
        slopes = jnp.dot(
            jnp.concatenate([key, key_tan], axis=1),
            jnp.concatenate([query_tan, query], axis=0),
            preferred_element_type=F32,
        )
    else:
        slopes = jnp.dot(key, query_tan, preferred_element_type=F32)
        slopes = slopes + jnp.dot(key_tan, query, preferred_element_type=F32)
    line = lax.broadcasted_iota(jnp.int32, (head_dim + 8, span), 0)
    lane = lax.broadcasted_iota(jnp.int32, (head_dim + 8, span), 1)
    pick = ((lane == line + low) & (line < head_dim)).astype(F32).astype(BF16)
    ones_line = lax.broadcasted_iota(jnp.int32, (8, value.shape[0]), 0)
    turned = jnp.concatenate(
        [
            against(pick, value)[:head_dim],
            (ones_line == 0).astype(F32),
            against(pick, value_tan),
        ],
        axis=0,
    )
    return scores, slopes, turned.astype(BF16)


def head_result(head, segments, level_bias, flags, products, olds, width):
    scores, slopes, turned = products
    head_dim = width // HEADS
    pad_dim = head_dim + 8
    scale = head_dim**-0.5
    bias = []
    top = None
    at = 0
    for rows, kind, number, _ in segments:
        amount = flags[number] if kind == "flag" else level_bias[number, head] * LOG2E
        bias.append(amount)
        part = jnp.max(scores[at : at + rows], axis=0, keepdims=True) * (scale * LOG2E) + amount
        top = part if top is None else jnp.maximum(top, part)
        at += rows
    for old in olds:
        top = jnp.maximum(top, old[2][head, 0:1])
    weights_low, product_low = [], []
    at = 0
    for (rows, _, _, _), amount in zip(segments, bias):
        weights = jnp.exp2(scores[at : at + rows] * (scale * LOG2E) + (amount - top))
        weights_low.append(weights.astype(BF16))
        product_low.append((weights * slopes[at : at + rows]).astype(BF16))
        at += rows
    both = jnp.dot(turned, jnp.concatenate(weights_low, axis=0), preferred_element_type=F32)
    extra = jnp.dot(
        turned[:pad_dim], jnp.concatenate(product_low, axis=0), preferred_element_type=F32
    )
    mix = both[:head_dim]
    total = both[head_dim : head_dim + 1]
    row_total = extra[head_dim : head_dim + 1] * scale
    extra = extra[:head_dim] * scale + both[pad_dim : pad_dim + head_dim]
    for old in olds:
        fade = jnp.exp2(old[2][head, 0:1] - top)
        total = total + fade * old[2][head, 1:2]
        row_total = row_total + fade * old[2][head, 2:3]
        mix = mix + fade * old[0][head]
        extra = extra + fade * old[1][head]
    return top, total, row_total, mix, extra


def attend_heads(segments, refs, queries, level_bias, width, olds, keep):
    flags = device_flags()
    stages = [range(first, first + TOGETHER) for first in range(0, HEADS, TOGETHER)]
    make = lambda heads: [head_products(head, segments, refs, queries, width) for head in heads]
    ready = make(stages[0])
    for number, heads in enumerate(stages):
        coming = make(stages[number + 1]) if number + 1 < len(stages) else None
        for head, products in zip(heads, ready):
            keep(head, *head_result(head, segments, level_bias, flags, products, olds, width))
        ready = coming


def keeper(state):
    def keep(head, top, total, row_total, mix, extra):
        state[0][head] = mix
        state[1][head] = extra
        state[2][head, 0:1] = top
        state[2][head, 1:2] = total
        state[2][head, 2:3] = row_total

    return keep


def own_kernel(segments, level_bias, query, qtan, *refs):
    sources, state = refs[: FIELDS + 1], refs[FIELDS + 1 : FIELDS + 4]
    masked, turned = refs[FIELDS + 4 : FIELDS + 6], refs[FIELDS + 6]
    state[2][...] = jnp.zeros(state[2].shape, F32)
    for raw, target in zip((query, qtan), masked):
        turn_queries(raw, turned, target)
    attend_heads(segments, sources, masked, level_bias, query.shape[1], [], keeper(state))


def state_shapes(token_count, width):
    wide = (HEADS, width // HEADS, token_count)
    return (wide, wide, (HEADS, 8, token_count))


def own_cost(token_count, width, key_count):
    return pl.CostEstimate(
        flops=token_count * key_count * HEADS,
        bytes_accessed=token_count * width,
        transcendentals=0,
    )


def attend_own(level_bias, query, qtan, fields, mate, segments):
    token_count, width = query.shape
    states = state_shapes(token_count, width)
    masked = (HEADS, 2 * LANES, token_count)
    operands = (query, qtan, *fields, mate)
    return pl.pallas_call(
        functools.partial(own_kernel, segments),
        out_shape=tuple(jax.ShapeDtypeStruct(s, F32) for s in states)
        + (jax.ShapeDtypeStruct(masked, BF16),) * 2,
        in_specs=[smem_spec()] + [vmem_spec()] * len(operands),
        out_specs=[vmem_spec()] * 5,
        scratch_shapes=[pltpu.VMEM((width, token_count), BF16)],
        compiler_params=pltpu.CompilerParams(vmem_limit_bytes=VMEM_BYTES),
        cost_estimate=own_cost(token_count, width, sum(s[0] for s in segments)),
        name="own",
    )(level_bias, *operands)


def more_kernel(segments, old_count, count, level_bias, *refs):
    queries, refs = refs[:2], refs[2:]
    olds = [refs[3 * i : 3 * i + 3] for i in range(old_count)]
    refs = refs[3 * old_count :]
    sources, state = refs[:count], refs[count:]
    width = state[0].shape[0] * state[0].shape[1]
    state[2][...] = jnp.zeros(state[2].shape, F32)
    attend_heads(segments, sources, queries, level_bias, width, olds, keeper(state))


def attend_more(level_bias, queries, olds, sources, segments, name):
    token_count = queries[0].shape[2]
    width = sources[0].shape[-1]
    operands = (*queries, *[array for old in olds for array in old], *sources)
    return pl.pallas_call(
        functools.partial(more_kernel, segments, len(olds), len(sources)),
        out_shape=tuple(jax.ShapeDtypeStruct(s, F32) for s in state_shapes(token_count, width)),
        in_specs=[smem_spec()] + [vmem_spec()] * len(operands),
        out_specs=[vmem_spec()] * 3,
        compiler_params=pltpu.CompilerParams(vmem_limit_bytes=VMEM_BYTES),
        cost_estimate=own_cost(token_count, width, sum(s[0] for s in segments)),
        name=name,
    )(level_bias, *operands)


def last_kernel(segments, old_count, count, far_count, far_blocks, level_bias, *refs):
    queries, refs = refs[:2], refs[2:]
    olds = [refs[3 * i : 3 * i + 3] for i in range(old_count)]
    refs = refs[3 * old_count :]
    sources, outs = refs[:count], refs[count : count + 2]
    far_keys, mix_acc, tan_acc, turned, sems = refs[count + 2 :]
    width, token_count = outs[0].shape[1], outs[0].shape[0]
    line = lax.broadcasted_iota(jnp.int32, (far_count, FIELDS * far_count), 0)
    lane = lax.broadcasted_iota(jnp.int32, (far_count, FIELDS * far_count), 1)
    far_rows = jnp.concatenate([sources[i][begin:] for i, begin in far_blocks], axis=0)
    for index in range(FIELDS):
        select = (lane == line * FIELDS + index).astype(F32).astype(BF16)
        far_keys[index] = jnp.dot(select, far_rows, preferred_element_type=F32).astype(BF16)
    sources = sources + (far_keys,)

    def keep(head, top, total, row_total, mix, extra):
        inverse = 1.0 / total
        mix = mix * inverse
        mix_acc[head] = mix
        tan_acc[head] = extra * inverse - (row_total * inverse) * mix

    attend_heads(segments, sources, queries, level_bias, width, olds, keep)
    line = lax.broadcasted_iota(jnp.int32, (token_count, token_count), 0)
    lane = lax.broadcasted_iota(jnp.int32, (token_count, token_count), 1)
    unit = (line == lane).astype(F32).astype(BF16)
    sent = []
    for number, acc in enumerate((mix_acc, tan_acc)):
        flat = acc[...].reshape(width, token_count).astype(BF16)
        turned[number] = against(unit, flat).astype(BF16)
        more = chunk_copies(turned.at[number], outs[number], sems, number * FIELDS, FIELDS)
        for copy in more:
            copy.start()
        sent += more
    for copy in sent:
        copy.wait()


def attend_last(level_bias, queries, olds, sources, segments, far_count, far_blocks):
    token_count = queries[0].shape[2]
    width = sources[0].shape[-1]
    states = state_shapes(token_count, width)
    operands = (*queries, *[array for old in olds for array in old], *sources)
    return pl.pallas_call(
        functools.partial(
            last_kernel, segments, len(olds), len(sources), far_count, far_blocks
        ),
        out_shape=(jax.ShapeDtypeStruct((token_count, width), BF16),) * 2,
        in_specs=[smem_spec()] + [vmem_spec()] * len(operands),
        out_specs=[hbm_spec()] * 2,
        scratch_shapes=[
            pltpu.VMEM((FIELDS, far_count, width), BF16),
            pltpu.VMEM(states[0], F32),
            pltpu.VMEM(states[1], F32),
            pltpu.VMEM((2, token_count, width), BF16),
            pltpu.SemaphoreType.DMA((2 * FIELDS,)),
        ],
        compiler_params=pltpu.CompilerParams(vmem_limit_bytes=VMEM_BYTES),
        cost_estimate=own_cost(token_count, width, sum(s[0] for s in segments)),
        name="outer",
    )(level_bias, *operands)


def swap(block, axis, odd):
    count = lax.axis_size(axis)
    route = []
    for low in range(1 if odd else 0, count - 1, 2):
        route += [(low, low + 1), (low + 1, low)]
    return lax.ppermute(block, axis, route)


def part(source, begin, rows):
    return lambda refs, field, window: refs[source][field, begin : begin + rows, window]


def flat_part(source, stride, begin, rows):
    def read(refs, field, window):
        at = field * stride + begin
        return refs[source][at : at + rows, window]

    return read


def forwarded(source, rest, half):
    def read(refs, field, window):
        if field < FIELDS - 1:
            return refs[source][field * half : (field + 1) * half, window]
        return refs[2][rest : rest + half, window]

    return read


def send_to(block, axis, mask):
    return lax.ppermute(block, axis, [(i, i ^ mask) for i in range(lax.axis_size(axis))])


def join(blocks):
    rows = sum(block.shape[0] for block in blocks)
    total, at = None, 0
    for block in blocks:
        count = block.shape[0]
        padded = jnp.pad(block, ((at, rows - at - count), (0, 0)))
        total = padded if total is None else total + padded
        at += count
    return total


def gather_rows(far):
    count = lax.axis_size("row")
    if count <= 8:
        return [far] + [send_to(far, "row", mask) for mask in range(2, count, 2)]
    for bit in range(1, count.bit_length() - 1):
        far = join([far, send_to(far, "row", 1 << bit)])
    return [far]


def body(
    query_field,
    key_field,
    value_field,
    query_tan,
    key_tan,
    value_tan,
    pool_near,
    pool_far,
    level_bias,
):
    window = query_field.shape[0]
    width = query_field.shape[2]
    cells = window * window
    strip, half = cells // 2, cells // 4
    near_count = cells // (NEAR_POOL * NEAR_POOL)
    row_count, col_count = lax.axis_size("row"), lax.axis_size("col")
    far_count = row_count * col_count
    flat = lambda field: field.reshape(cells, width)
    fields = tuple(flat(f) for f in (key_field, value_field, key_tan, value_tan))

    row_odd, col_even, col_odd, row_even, far = pack(fields, pool_near, pool_far)
    group = strip + near_count
    far = far[:FIELDS]
    got_col_even = swap(col_even, "col", False)
    got_row_odd = swap(row_odd, "row", True)
    got_col_odd = swap(col_odd, "col", True)
    got_row_even = swap(row_even, "row", False)

    *own_state, query, qtan = attend_own(
        level_bias,
        flat(query_field),
        flat(query_tan),
        fields,
        got_row_even,
        [
            (cells, "flag", 0, lambda refs, field, window: refs[field][:, window]),
            (strip, "flag", 0, part(4, 0, strip)),
            (near_count, "level", 0, part(4, strip, near_count)),
        ],
    )
    queries = (query, qtan)
    far_from = [send_to(far, "col", mask) for mask in range(2, min(col_count, 4))]
    mate_far = got_col_even[FIELDS * group : FIELDS * group + FIELDS]
    row_state = attend_more(
        level_bias,
        queries,
        [],
        (got_row_odd,),
        [(strip, "flag", 1, part(0, 0, strip))],
        "row_strip",
    )
    got_row_odd, stats = lax.optimization_barrier((got_row_odd, row_state[2]))
    row_state = (row_state[0], row_state[1], stats)
    to_even, to_odd = got_row_odd[:, :half], got_row_odd[:, half:]
    got_outer_even = swap(to_even, "col", False)
    got_outer_odd = swap(to_odd, "col", True)
    got_inner = [swap(block, "row", False) for block in forward(got_col_even, got_col_odd)]
    far = join([far, mate_far, *far_from])
    for bit in range(2, col_count.bit_length() - 1):
        far = join([far, send_to(far, "col", 1 << bit)])
    far = join([far, send_to(far, "row", 1)])

    state = attend_more(
        level_bias,
        queries,
        [row_state],
        (got_col_even, got_col_odd),
        [
            (strip, "flag", 0, flat_part(0, group, 0, strip)),
            (strip, "flag", 2, part(1, 0, strip)),
        ],
        "strips",
    )
    far, stats = lax.optimization_barrier((far, state[2]))
    state = (state[0], state[1], stats)
    far_blocks = gather_rows(far)
    state = attend_more(
        level_bias,
        queries,
        [state],
        (*got_inner, got_col_even, row_even),
        [
            (half, "flag", 0, forwarded(0, 0, half)),
            (half, "flag", 2, forwarded(1, half, half)),
            (near_count, "level", 0, flat_part(2, near_count, strip, near_count)),
            (near_count, "level", 0, flat_part(3, group, strip, near_count)),
            (near_count, "level", 0, part(4, strip, near_count)),
        ],
        "inner",
    )
    mixed, mixed_tan = attend_last(
        level_bias,
        queries,
        [state, own_state],
        (got_outer_even, got_outer_odd, *far_blocks),
        [
            (half, "flag", 1, part(0, 0, half)),
            (half, "flag", 3, part(1, 0, half)),
            (far_count, "level", 1, part(2 + len(far_blocks), 0, far_count)),
        ],
        far_count,
        tuple((2 + number, 0) for number in range(len(far_blocks))),
    )
    shape = (window, window, width)
    return (mixed.reshape(shape), mixed_tan.reshape(shape))


def solution(mesh):
    field = P("row", "col", None)
    return jax.shard_map(
        body,
        mesh=mesh,
        in_specs=(field,) * 6 + (P(),) * 3,
        out_specs=(field, field),
        check_vma=False,
    )
```

```python
import functools

import jax
import jax.numpy as jnp
from jax import lax
from jax.experimental import pallas as pl
from jax.experimental.pallas import tpu as pltpu
from jax.sharding import PartitionSpec as P

HEADS = 16
RIM = 8
NEAR_POOL = 4
LOG2E = 1.4426950408889634
OFF = -1e30
PACK_BYTES = 60 * 1024 * 1024
VMEM_BYTES = 28 * 1024 * 1024
LANES = 128
FIELDS = 4
BF16 = jnp.bfloat16
F32 = jnp.float32


def vmem_spec():
    return pl.BlockSpec(memory_space=pltpu.VMEM)


def smem_spec():
    return pl.BlockSpec(memory_space=pltpu.SMEM)


def hbm_spec():
    return pl.BlockSpec(memory_space=pltpu.HBM)


def any_spec():
    return pl.BlockSpec(memory_space=pl.ANY)


def against(left, right):
    return lax.dot_general(left, right, (((1,), (1,)), ((), ())), preferred_element_type=F32)


def chunk_copies(source, target, sems, first, parts):
    rows = source.shape[0]
    step = -(-rows // parts)
    if len(source.shape) == 2:
        step = -(-step // 16) * 16
    copies = []
    for number, begin in enumerate(range(0, rows, step)):
        at = pl.ds(begin, min(step, rows - begin))
        copies.append(pltpu.make_async_copy(source.at[at], target.at[at], sems.at[first + number]))
    return copies


def split3(weights):
    high = weights.astype(BF16)
    rest = weights - high.astype(F32)
    mid = rest.astype(BF16)
    low = (rest - mid.astype(F32)).astype(BF16)
    return jnp.concatenate([high, mid, low], axis=0)


def pool_weights(pool_near, pool_far, cells):
    window = 2 * RIM
    near_side = window // NEAR_POOL
    near_count = near_side * near_side
    lane = lax.broadcasted_iota(jnp.int32, (near_count, cells), 1)
    line = lax.broadcasted_iota(jnp.int32, (near_count, cells), 0)
    row, col = lane // window, lane % window
    near = jnp.zeros((near_count, cells), F32)
    for p in range(NEAR_POOL):
        for q in range(NEAR_POOL):
            hit = (row % NEAR_POOL == p) & (col % NEAR_POOL == q)
            near = jnp.where(hit, pool_near[p, q], near)
    block = (row // NEAR_POOL) * near_side + col // NEAR_POOL
    near = split3(jnp.where(line == block, near, 0.0))
    spread = (line == col).astype(F32).astype(BF16)
    far = jnp.dot(split3(pool_far), spread, preferred_element_type=F32)
    far_line = lax.broadcasted_iota(jnp.int32, far.shape, 0) % window
    far_lane = lax.broadcasted_iota(jnp.int32, far.shape, 1) // window
    far = jnp.where(far_line == far_lane, far, 0.0)
    rows = [
        jnp.sum(far[i * window : (i + 1) * window], axis=0, keepdims=True) for i in range(3)
    ]
    rows.append(jnp.zeros((near_count - 3, cells), F32))
    return jnp.concatenate([near, jnp.concatenate(rows, axis=0).astype(BF16)], axis=0)


def halves(block, width):
    cells = block.shape[0]
    wide = block.astype(F32).reshape(cells // (2 * RIM), 2, RIM, width)
    left = wide[:, 0].reshape(cells // 2, width).astype(BF16)
    right = wide[:, 1].reshape(cells // 2, width).astype(BF16)
    return left, right


def pack_kernel(pool_near, pool_far, *refs):
    sources, outs = refs[:FIELDS], refs[FIELDS : FIELDS + 5]
    held = refs[FIELDS + 5]
    kept, sems, out_sems = refs[FIELDS + 6 : -2], refs[-2], refs[-1]
    cells, width = sources[0].shape
    strip, half = cells // 2, cells // 4
    near_count = cells // (NEAR_POOL * NEAR_POOL)
    row_is_even = lax.axis_index("row") % 2 == 0
    col_is_even = lax.axis_index("col") % 2 == 0
    copies = []
    for index, source in enumerate(sources):
        copies += chunk_copies(source, held.at[index], sems, 2 * index, 2)
    for copy in copies:
        copy.start()
    weights = pool_weights(pool_near, pool_far[...], cells)
    far_rows = []
    sent = []
    for index in range(FIELDS):
        copies[2 * index].wait()
        copies[2 * index + 1].wait()
        block = held[index]
        left, right = halves(block, width)
        even = jnp.where(col_is_even, right, left)
        odd = jnp.where(col_is_even, left, right)
        outer = lambda side: jnp.where(row_is_even, side[:half], side[half:])
        pooled = jnp.dot(weights, block, preferred_element_type=F32)
        near = pooled[:near_count] + (
            pooled[near_count : 2 * near_count] + pooled[2 * near_count : 3 * near_count]
        )
        near = near.astype(BF16)
        far = pooled[3 * near_count :]
        far_rows.append(far[0:1] + (far[1:2] + far[2:3]))
        kept[0][index, :half] = outer(even)
        kept[0][index, half:] = outer(odd)
        at = index * (strip + near_count)
        kept[1][at : at + strip] = even
        kept[1][at + strip : at + strip + near_count] = near
        kept[2][index] = odd
        kept[3][index, :strip] = jnp.where(row_is_even, block[strip:], block[:strip])
        kept[3][index, strip:] = near
        for number in (0, 2, 3):
            copy = pltpu.make_async_copy(
                kept[number].at[index], outs[number].at[index], out_sems.at[4 * index + number]
            )
            copy.start()
            sent.append(copy)
    far_rows.append(jnp.zeros((16 - FIELDS, width), F32))
    kept[4][...] = jnp.concatenate(far_rows, axis=0).astype(BF16)
    kept[1][FIELDS * (strip + near_count) :] = kept[4][...]
    for number, source in ((1, 1), (4 * FIELDS, 4)):
        copy = pltpu.make_async_copy(kept[source], outs[source], out_sems.at[number])
        copy.start()
        sent.append(copy)
    for copy in sent:
        copy.wait()


def pack(fields, pool_near, pool_far):
    cells, width = fields[0].shape
    strip = cells // 2
    near_count = cells // (NEAR_POOL * NEAR_POOL)
    shapes = [
        (FIELDS, strip, width),
        (FIELDS * (strip + near_count) + 16, width),
        (FIELDS, strip, width),
        (FIELDS, strip + near_count, width),
        (16, width),
    ]
    return pl.pallas_call(
        pack_kernel,
        out_shape=tuple(jax.ShapeDtypeStruct(s, BF16) for s in shapes),
        in_specs=[smem_spec(), vmem_spec()] + [hbm_spec()] * FIELDS,
        out_specs=[hbm_spec()] * len(shapes),
        scratch_shapes=[pltpu.VMEM((FIELDS, cells, width), BF16)]
        + [pltpu.VMEM(s, BF16) for s in shapes]
        + [pltpu.SemaphoreType.DMA((2 * FIELDS,)), pltpu.SemaphoreType.DMA((4 * FIELDS + 1,))],
        compiler_params=pltpu.CompilerParams(vmem_limit_bytes=PACK_BYTES),
        name="pack",
    )(pool_near, pool_far, *fields)


def forward_kernel(col_even, col_odd, first, second, third):
    strip = col_odd.shape[1]
    half = strip // 2
    near_count = (col_even.shape[0] - 16) // FIELDS - strip
    group = strip + near_count
    start = (1 - lax.axis_index("row") % 2) * half
    even = lambda index: col_even[pl.ds(pl.multiple_of(index * group + start, 16), half)]
    odd = lambda index: col_odd[index, pl.ds(pl.multiple_of(start, half), half)]
    for index in range(FIELDS - 1):
        first[index * half : (index + 1) * half] = even(index)
        second[index * half : (index + 1) * half] = odd(index)
    third[:half] = even(FIELDS - 1)
    third[half:strip] = odd(FIELDS - 1)
    for index in range(FIELDS):
        at = strip + index * near_count
        third[at : at + near_count] = col_even[index * group + strip : (index + 1) * group]


def forward(col_even, col_odd):
    _, strip, width = col_odd.shape
    shape = jax.ShapeDtypeStruct(((FIELDS - 1) * strip // 2, width), BF16)
    return pl.pallas_call(
        forward_kernel,
        out_shape=(shape,) * 3,
        in_specs=[vmem_spec()] * 2,
        out_specs=[vmem_spec()] * 3,
        compiler_params=pltpu.CompilerParams(vmem_limit_bytes=VMEM_BYTES),
        name="forward",
    )(col_even, col_odd)


TOGETHER = 2


def masked_start(head, head_dim, width):
    return min(head * head_dim // LANES, (width - 2 * LANES) // LANES) * LANES


def turn_queries(raw, turned, masked):
    width = raw.shape[1]
    head_dim = width // HEADS
    span = 2 * LANES
    line = lax.broadcasted_iota(jnp.int32, (LANES, LANES), 0)
    lane = lax.broadcasted_iota(jnp.int32, (LANES, LANES), 1)
    unit = (line == lane).astype(F32).astype(BF16)
    for at in range(0, width, LANES):
        turned[at : at + LANES] = against(unit, raw[:, at : at + LANES]).astype(BF16)
    channel = lax.broadcasted_iota(jnp.int32, (span, raw.shape[0]), 0)
    for head in range(HEADS):
        start = masked_start(head, head_dim, width)
        low = head * head_dim - start
        keep = ((channel >= low) & (channel < low + head_dim)).astype(F32).astype(BF16)
        masked[head] = turned[start : start + span] * keep


def device_flags():
    row, col = lax.axis_index("row"), lax.axis_index("col")
    row_edge = (row == 0) | (row == lax.axis_size("row") - 1)
    col_edge = (col == 0) | (col == lax.axis_size("col") - 1)
    off = lambda edge: jnp.where(edge, F32(OFF), F32(0.0))
    return (F32(0.0), off(row_edge), off(col_edge), off(row_edge | col_edge))


def head_products(head, segments, refs, queries, width):
    head_dim = width // HEADS
    start = head * head_dim // LANES * LANES
    low = head * head_dim - start
    one_tile = low + head_dim <= LANES
    span = LANES if one_tile else 2 * LANES
    window = slice(start, start + span)
    at = start - masked_start(head, head_dim, width)
    rows_of = lambda field: jnp.concatenate(
        [reader(refs, field, window) for _, _, _, reader in segments], axis=0
    )
    key, value, key_tan, value_tan = (rows_of(field) for field in range(FIELDS))
    query, query_tan = (ref[head, at : at + span] for ref in queries)
    if one_tile:
        scores = jnp.dot(key, query, preferred_element_type=F32)
        slopes = jnp.dot(
            jnp.concatenate([key, key_tan], axis=1),
            jnp.concatenate([query_tan, query], axis=0),
            preferred_element_type=F32,
        )
    else:
        count = key.shape[0]
        both = jnp.dot(
            jnp.concatenate([key, key_tan], axis=0), query, preferred_element_type=F32
        )
        scores = both[:count]
        slopes = jnp.dot(key, query_tan, preferred_element_type=F32) + both[count:]
    line = lax.broadcasted_iota(jnp.int32, (head_dim + 8, span), 0)
    lane = lax.broadcasted_iota(jnp.int32, (head_dim + 8, span), 1)
    pick = ((lane == line + low) & (line < head_dim)).astype(F32).astype(BF16)
    ones_line = lax.broadcasted_iota(jnp.int32, (8, value.shape[0]), 0)
    turned = jnp.concatenate(
        [
            against(pick, value)[:head_dim],
            (ones_line == 0).astype(F32),
            against(pick, value_tan),
        ],
        axis=0,
    )
    return scores, slopes, turned.astype(BF16)


def head_result(head, segments, level_bias, flags, products, olds, width):
    scores, slopes, turned = products
    head_dim = width // HEADS
    pad_dim = head_dim + 8
    scale = head_dim**-0.5
    bias = []
    top = None
    at = 0
    for rows, kind, number, _ in segments:
        amount = flags[number] if kind == "flag" else level_bias[number, head] * LOG2E
        bias.append(amount)
        part = jnp.max(scores[at : at + rows], axis=0, keepdims=True) * (scale * LOG2E) + amount
        top = part if top is None else jnp.maximum(top, part)
        at += rows
    for old in olds:
        top = jnp.maximum(top, old[2][head, 0:1])
    weights_low, product_low = [], []
    at = 0
    for (rows, _, _, _), amount in zip(segments, bias):
        weights = jnp.exp2(scores[at : at + rows] * (scale * LOG2E) + (amount - top))
        weights_low.append(weights.astype(BF16))
        product_low.append((weights * slopes[at : at + rows]).astype(BF16))
        at += rows
    both = jnp.dot(turned, jnp.concatenate(weights_low, axis=0), preferred_element_type=F32)
    extra = jnp.dot(
        turned[:pad_dim], jnp.concatenate(product_low, axis=0), preferred_element_type=F32
    )
    mix = both[:head_dim]
    total = both[head_dim : head_dim + 1]
    row_total = extra[head_dim : head_dim + 1] * scale
    extra = extra[:head_dim] * scale + both[pad_dim : pad_dim + head_dim]
    for old in olds:
        fade = jnp.exp2(old[2][head, 0:1] - top)
        total = total + fade * old[2][head, 1:2]
        row_total = row_total + fade * old[2][head, 2:3]
        mix = mix + fade * old[0][head]
        extra = extra + fade * old[1][head]
    return top, total, row_total, mix, extra


def attend_heads(segments, refs, queries, level_bias, width, olds, keep):
    flags = device_flags()
    stages = [range(first, first + TOGETHER) for first in range(0, HEADS, TOGETHER)]
    make = lambda heads: [head_products(head, segments, refs, queries, width) for head in heads]
    ready = make(stages[0])
    for number, heads in enumerate(stages):
        coming = make(stages[number + 1]) if number + 1 < len(stages) else None
        for head, products in zip(heads, ready):
            keep(head, *head_result(head, segments, level_bias, flags, products, olds, width))
        ready = coming


def keeper(state):
    def keep(head, top, total, row_total, mix, extra):
        state[0][head] = mix
        state[1][head] = extra
        state[2][head, 0:1] = top
        state[2][head, 1:2] = total
        state[2][head, 2:3] = row_total

    return keep


def own_kernel(segments, level_bias, query, qtan, *refs):
    sources, state = refs[: FIELDS + 1], refs[FIELDS + 1 : FIELDS + 4]
    masked, turned = refs[FIELDS + 4 : FIELDS + 6], refs[FIELDS + 6]
    state[2][...] = jnp.zeros(state[2].shape, F32)
    for raw, target in zip((query, qtan), masked):
        turn_queries(raw, turned, target)
    attend_heads(segments, sources, masked, level_bias, query.shape[1], [], keeper(state))


def state_shapes(token_count, width):
    wide = (HEADS, width // HEADS, token_count)
    return (wide, wide, (HEADS, 8, token_count))


def own_cost(token_count, width, key_count):
    return pl.CostEstimate(
        flops=token_count * key_count * HEADS,
        bytes_accessed=token_count * width,
        transcendentals=0,
    )


def attend_own(level_bias, query, qtan, fields, mate, segments):
    token_count, width = query.shape
    states = state_shapes(token_count, width)
    masked = (HEADS, 2 * LANES, token_count)
    operands = (query, qtan, *fields, mate)
    return pl.pallas_call(
        functools.partial(own_kernel, segments),
        out_shape=tuple(jax.ShapeDtypeStruct(s, F32) for s in states)
        + (jax.ShapeDtypeStruct(masked, BF16),) * 2,
        in_specs=[smem_spec()] + [vmem_spec()] * len(operands),
        out_specs=[vmem_spec()] * 5,
        scratch_shapes=[pltpu.VMEM((width, token_count), BF16)],
        compiler_params=pltpu.CompilerParams(vmem_limit_bytes=VMEM_BYTES),
        cost_estimate=own_cost(token_count, width, sum(s[0] for s in segments)),
        name="own",
    )(level_bias, *operands)


def more_kernel(segments, old_count, count, level_bias, *refs):
    queries, refs = refs[:2], refs[2:]
    olds = [refs[3 * i : 3 * i + 3] for i in range(old_count)]
    refs = refs[3 * old_count :]
    sources, state = refs[:count], refs[count:]
    width = state[0].shape[0] * state[0].shape[1]
    state[2][...] = jnp.zeros(state[2].shape, F32)
    attend_heads(segments, sources, queries, level_bias, width, olds, keeper(state))


def attend_more(level_bias, queries, olds, sources, segments, name):
    token_count = queries[0].shape[2]
    width = sources[0].shape[-1]
    operands = (*queries, *[array for old in olds for array in old], *sources)
    return pl.pallas_call(
        functools.partial(more_kernel, segments, len(olds), len(sources)),
        out_shape=tuple(jax.ShapeDtypeStruct(s, F32) for s in state_shapes(token_count, width)),
        in_specs=[smem_spec()] + [vmem_spec()] * len(operands),
        out_specs=[vmem_spec()] * 3,
        compiler_params=pltpu.CompilerParams(vmem_limit_bytes=VMEM_BYTES),
        cost_estimate=own_cost(token_count, width, sum(s[0] for s in segments)),
        name=name,
    )(level_bias, *operands)


def last_kernel(segments, old_count, count, far_count, far_blocks, level_bias, *refs):
    queries, refs = refs[:2], refs[2:]
    olds = [refs[3 * i : 3 * i + 3] for i in range(old_count)]
    refs = refs[3 * old_count :]
    sources, outs = refs[:count], refs[count : count + 2]
    far_keys, mix_acc, tan_acc, turned, sems = refs[count + 2 :]
    width, token_count = outs[0].shape[1], outs[0].shape[0]
    line = lax.broadcasted_iota(jnp.int32, (far_count, FIELDS * far_count), 0)
    lane = lax.broadcasted_iota(jnp.int32, (far_count, FIELDS * far_count), 1)
    far_rows = jnp.concatenate([sources[i][begin:] for i, begin in far_blocks], axis=0)
    for index in range(FIELDS):
        select = (lane == line * FIELDS + index).astype(F32).astype(BF16)
        far_keys[index] = jnp.dot(select, far_rows, preferred_element_type=F32).astype(BF16)
    sources = sources + (far_keys,)

    line = lax.broadcasted_iota(jnp.int32, (token_count, token_count), 0)
    lane = lax.broadcasted_iota(jnp.int32, (token_count, token_count), 1)
    unit = (line == lane).astype(F32).astype(BF16)
    head_dim = width // HEADS
    tiles = width // LANES
    sent = []

    def keep(head, top, total, row_total, mix, extra):
        inverse = 1.0 / total
        mix = mix * inverse
        rows = slice(head * head_dim, (head + 1) * head_dim)
        mix_acc[rows] = mix
        tan_acc[rows] = extra * inverse - (row_total * inverse) * mix
        for tile in range(len(sent) // 2, (head + 1) * head_dim // LANES):
            at = slice(tile * LANES, (tile + 1) * LANES)
            for number, acc in enumerate((mix_acc, tan_acc)):
                turned[number, :, at] = against(unit, acc[at].astype(BF16)).astype(BF16)
                copy = pltpu.make_async_copy(
                    turned.at[number, :, at],
                    outs[number].at[:, at],
                    sems.at[number * tiles + tile],
                )
                copy.start()
                sent.append(copy)

    attend_heads(segments, sources, queries, level_bias, width, olds, keep)
    for copy in sent:
        copy.wait()


def attend_last(level_bias, queries, olds, sources, segments, far_count, far_blocks):
    token_count = queries[0].shape[2]
    width = sources[0].shape[-1]
    operands = (*queries, *[array for old in olds for array in old], *sources)
    return pl.pallas_call(
        functools.partial(
            last_kernel, segments, len(olds), len(sources), far_count, far_blocks
        ),
        out_shape=(jax.ShapeDtypeStruct((token_count, width), BF16),) * 2,
        in_specs=[smem_spec()] + [vmem_spec()] * len(operands),
        out_specs=[hbm_spec()] * 2,
        scratch_shapes=[
            pltpu.VMEM((FIELDS, far_count, width), BF16),
            pltpu.VMEM((width, token_count), F32),
            pltpu.VMEM((width, token_count), F32),
            pltpu.VMEM((2, token_count, width), BF16),
            pltpu.SemaphoreType.DMA((2 * width // LANES,)),
        ],
        compiler_params=pltpu.CompilerParams(vmem_limit_bytes=VMEM_BYTES),
        cost_estimate=own_cost(token_count, width, sum(s[0] for s in segments)),
        name="outer",
    )(level_bias, *operands)


def swap(block, axis, odd):
    count = lax.axis_size(axis)
    route = []
    for low in range(1 if odd else 0, count - 1, 2):
        route += [(low, low + 1), (low + 1, low)]
    return lax.ppermute(block, axis, route)


def part(source, begin, rows):
    return lambda refs, field, window: refs[source][field, begin : begin + rows, window]


def flat_part(source, stride, begin, rows):
    def read(refs, field, window):
        at = field * stride + begin
        return refs[source][at : at + rows, window]

    return read


def forwarded(source, rest, half):
    def read(refs, field, window):
        if field < FIELDS - 1:
            return refs[source][field * half : (field + 1) * half, window]
        return refs[2][rest : rest + half, window]

    return read


def send_to(block, axis, mask):
    return lax.ppermute(block, axis, [(i, i ^ mask) for i in range(lax.axis_size(axis))])


def join(blocks):
    rows = sum(block.shape[0] for block in blocks)
    total, at = None, 0
    for block in blocks:
        count = block.shape[0]
        padded = jnp.pad(block, ((at, rows - at - count), (0, 0)))
        total = padded if total is None else total + padded
        at += count
    return total


def gather_rows(far):
    count = lax.axis_size("row")
    if count <= 8:
        return [far] + [send_to(far, "row", mask) for mask in range(2, count, 2)]
    for bit in range(1, count.bit_length() - 1):
        far = join([far, send_to(far, "row", 1 << bit)])
    return [far]


def body(
    query_field,
    key_field,
    value_field,
    query_tan,
    key_tan,
    value_tan,
    pool_near,
    pool_far,
    level_bias,
):
    window = query_field.shape[0]
    width = query_field.shape[2]
    cells = window * window
    strip, half = cells // 2, cells // 4
    near_count = cells // (NEAR_POOL * NEAR_POOL)
    row_count, col_count = lax.axis_size("row"), lax.axis_size("col")
    far_count = row_count * col_count
    flat = lambda field: field.reshape(cells, width)
    fields = tuple(flat(f) for f in (key_field, value_field, key_tan, value_tan))

    row_odd, col_even, col_odd, row_even, far = pack(fields, pool_near, pool_far)
    group = strip + near_count
    far = far[:FIELDS]
    got_col_even = swap(col_even, "col", False)
    got_row_odd = swap(row_odd, "row", True)
    got_col_odd = swap(col_odd, "col", True)
    got_row_even = swap(row_even, "row", False)

    *own_state, query, qtan = attend_own(
        level_bias,
        flat(query_field),
        flat(query_tan),
        fields,
        got_row_even,
        [
            (cells, "flag", 0, lambda refs, field, window: refs[field][:, window]),
            (strip, "flag", 0, part(4, 0, strip)),
            (near_count, "level", 0, part(4, strip, near_count)),
        ],
    )
    queries = (query, qtan)
    far_from = [send_to(far, "col", mask) for mask in range(2, min(col_count, 4))]
    mate_far = got_col_even[FIELDS * group : FIELDS * group + FIELDS]
    row_state = attend_more(
        level_bias,
        queries,
        [],
        (got_row_odd,),
        [(strip, "flag", 1, part(0, 0, strip))],
        "row_strip",
    )
    got_row_odd, stats = lax.optimization_barrier((got_row_odd, row_state[2]))
    row_state = (row_state[0], row_state[1], stats)
    to_even, to_odd = got_row_odd[:, :half], got_row_odd[:, half:]
    got_outer_even = swap(to_even, "col", False)
    got_outer_odd = swap(to_odd, "col", True)
    got_inner = [swap(block, "row", False) for block in forward(got_col_even, got_col_odd)]
    far = join([far, mate_far, *far_from])
    for bit in range(2, col_count.bit_length() - 1):
        far = join([far, send_to(far, "col", 1 << bit)])
    far = join([far, send_to(far, "row", 1)])

    state = attend_more(
        level_bias,
        queries,
        [row_state],
        (got_col_even, got_col_odd),
        [
            (strip, "flag", 0, flat_part(0, group, 0, strip)),
            (strip, "flag", 2, part(1, 0, strip)),
        ],
        "strips",
    )
    far, stats = lax.optimization_barrier((far, state[2]))
    state = (state[0], state[1], stats)
    far_blocks = gather_rows(far)
    state = attend_more(
        level_bias,
        queries,
        [state],
        (*got_inner, got_col_even, row_even),
        [
            (half, "flag", 0, forwarded(0, 0, half)),
            (half, "flag", 2, forwarded(1, half, half)),
            (near_count, "level", 0, flat_part(2, near_count, strip, near_count)),
            (near_count, "level", 0, flat_part(3, group, strip, near_count)),
            (near_count, "level", 0, part(4, strip, near_count)),
        ],
        "inner",
    )
    mixed, mixed_tan = attend_last(
        level_bias,
        queries,
        [state, own_state],
        (got_outer_even, got_outer_odd, *far_blocks),
        [
            (half, "flag", 1, part(0, 0, half)),
            (half, "flag", 3, part(1, 0, half)),
            (far_count, "level", 1, part(2 + len(far_blocks), 0, far_count)),
        ],
        far_count,
        tuple((2 + number, 0) for number in range(len(far_blocks))),
    )
    shape = (window, window, width)
    return (mixed.reshape(shape), mixed_tan.reshape(shape))


def solution(mesh):
    field = P("row", "col", None)
    return jax.shard_map(
        body,
        mesh=mesh,
        in_specs=(field,) * 6 + (P(),) * 3,
        out_specs=(field, field),
        check_vma=False,
    )
```

```python
import functools

import jax
import jax.numpy as jnp
from jax import lax
from jax.experimental import pallas as pl
from jax.experimental.pallas import tpu as pltpu
from jax.sharding import PartitionSpec as P

HEADS = 16
RIM = 8
NEAR_POOL = 4
LOG2E = 1.4426950408889634
OFF = -1e30
PACK_BYTES = 60 * 1024 * 1024
VMEM_BYTES = 28 * 1024 * 1024
LANES = 128
FIELDS = 4
BF16 = jnp.bfloat16
F32 = jnp.float32


def vmem_spec():
    return pl.BlockSpec(memory_space=pltpu.VMEM)


def smem_spec():
    return pl.BlockSpec(memory_space=pltpu.SMEM)


def hbm_spec():
    return pl.BlockSpec(memory_space=pltpu.HBM)


def any_spec():
    return pl.BlockSpec(memory_space=pl.ANY)


def against(left, right):
    return lax.dot_general(left, right, (((1,), (1,)), ((), ())), preferred_element_type=F32)


def chunk_copies(source, target, sems, first, parts):
    rows = source.shape[0]
    step = -(-rows // parts)
    if len(source.shape) == 2:
        step = -(-step // 16) * 16
    copies = []
    for number, begin in enumerate(range(0, rows, step)):
        at = pl.ds(begin, min(step, rows - begin))
        copies.append(pltpu.make_async_copy(source.at[at], target.at[at], sems.at[first + number]))
    return copies


def split3(weights):
    high = weights.astype(BF16)
    rest = weights - high.astype(F32)
    mid = rest.astype(BF16)
    low = (rest - mid.astype(F32)).astype(BF16)
    return jnp.concatenate([high, mid, low], axis=0)


def pool_weights(pool_near, pool_far, cells):
    window = 2 * RIM
    near_side = window // NEAR_POOL
    near_count = near_side * near_side
    lane = lax.broadcasted_iota(jnp.int32, (near_count, cells), 1)
    line = lax.broadcasted_iota(jnp.int32, (near_count, cells), 0)
    row, col = lane // window, lane % window
    near = jnp.zeros((near_count, cells), F32)
    for p in range(NEAR_POOL):
        for q in range(NEAR_POOL):
            hit = (row % NEAR_POOL == p) & (col % NEAR_POOL == q)
            near = jnp.where(hit, pool_near[p, q], near)
    block = (row // NEAR_POOL) * near_side + col // NEAR_POOL
    near = split3(jnp.where(line == block, near, 0.0))
    spread = (line == col).astype(F32).astype(BF16)
    far = jnp.dot(split3(pool_far), spread, preferred_element_type=F32)
    far_line = lax.broadcasted_iota(jnp.int32, far.shape, 0) % window
    far_lane = lax.broadcasted_iota(jnp.int32, far.shape, 1) // window
    far = jnp.where(far_line == far_lane, far, 0.0)
    rows = [
        jnp.sum(far[i * window : (i + 1) * window], axis=0, keepdims=True) for i in range(3)
    ]
    rows.append(jnp.zeros((near_count - 3, cells), F32))
    return jnp.concatenate([near, jnp.concatenate(rows, axis=0).astype(BF16)], axis=0)


def halves(block, width):
    cells = block.shape[0]
    wide = block.astype(F32).reshape(cells // (2 * RIM), 2, RIM, width)
    left = wide[:, 0].reshape(cells // 2, width).astype(BF16)
    right = wide[:, 1].reshape(cells // 2, width).astype(BF16)
    return left, right


def pack_kernel(pool_near, pool_far, *refs):
    sources, outs = refs[:FIELDS], refs[FIELDS : FIELDS + 5]
    held = refs[FIELDS + 5]
    kept, sems, out_sems = refs[FIELDS + 6 : -2], refs[-2], refs[-1]
    cells, width = sources[0].shape
    strip, half = cells // 2, cells // 4
    near_count = cells // (NEAR_POOL * NEAR_POOL)
    row_is_even = lax.axis_index("row") % 2 == 0
    col_is_even = lax.axis_index("col") % 2 == 0
    copies = []
    for index, source in enumerate(sources):
        copies += chunk_copies(source, held.at[index], sems, 2 * index, 2)
    for copy in copies:
        copy.start()
    weights = pool_weights(pool_near, pool_far[...], cells)
    far_rows = []
    sent = []
    for index in range(FIELDS):
        copies[2 * index].wait()
        copies[2 * index + 1].wait()
        block = held[index]
        left, right = halves(block, width)
        even = jnp.where(col_is_even, right, left)
        odd = jnp.where(col_is_even, left, right)
        outer = lambda side: jnp.where(row_is_even, side[:half], side[half:])
        pooled = jnp.dot(weights, block, preferred_element_type=F32)
        near = pooled[:near_count] + (
            pooled[near_count : 2 * near_count] + pooled[2 * near_count : 3 * near_count]
        )
        near = near.astype(BF16)
        far = pooled[3 * near_count :]
        far_rows.append(far[0:1] + (far[1:2] + far[2:3]))
        kept[0][index, :half] = outer(even)
        kept[0][index, half:] = outer(odd)
        at = index * (strip + near_count)
        kept[1][at : at + strip] = even
        kept[1][at + strip : at + strip + near_count] = near
        kept[2][index] = odd
        kept[3][at : at + strip] = jnp.where(row_is_even, block[strip:], block[:strip])
        kept[3][at + strip : at + strip + near_count] = near
        for number in (0, 2):
            copy = pltpu.make_async_copy(
                kept[number].at[index], outs[number].at[index], out_sems.at[4 * index + number]
            )
            copy.start()
            sent.append(copy)
    far_rows.append(jnp.zeros((16 - FIELDS, width), F32))
    kept[4][...] = jnp.concatenate(far_rows, axis=0).astype(BF16)
    for source in (1, 3):
        kept[source][FIELDS * (strip + near_count) :] = kept[4][...]
    for number, source in ((1, 1), (3, 3), (4 * FIELDS, 4)):
        copy = pltpu.make_async_copy(kept[source], outs[source], out_sems.at[number])
        copy.start()
        sent.append(copy)
    for copy in sent:
        copy.wait()


def pack(fields, pool_near, pool_far):
    cells, width = fields[0].shape
    strip = cells // 2
    near_count = cells // (NEAR_POOL * NEAR_POOL)
    shapes = [
        (FIELDS, strip, width),
        (FIELDS * (strip + near_count) + 16, width),
        (FIELDS, strip, width),
        (FIELDS * (strip + near_count) + 16, width),
        (16, width),
    ]
    return pl.pallas_call(
        pack_kernel,
        out_shape=tuple(jax.ShapeDtypeStruct(s, BF16) for s in shapes),
        in_specs=[smem_spec(), vmem_spec()] + [hbm_spec()] * FIELDS,
        out_specs=[hbm_spec()] * len(shapes),
        scratch_shapes=[pltpu.VMEM((FIELDS, cells, width), BF16)]
        + [pltpu.VMEM(s, BF16) for s in shapes]
        + [pltpu.SemaphoreType.DMA((2 * FIELDS,)), pltpu.SemaphoreType.DMA((4 * FIELDS + 1,))],
        compiler_params=pltpu.CompilerParams(vmem_limit_bytes=PACK_BYTES),
        name="pack",
    )(pool_near, pool_far, *fields)


def forward_kernel(col_even, col_odd, first, second, third):
    strip = col_odd.shape[1]
    half = strip // 2
    near_count = (col_even.shape[0] - 16) // FIELDS - strip
    group = strip + near_count
    start = (1 - lax.axis_index("row") % 2) * half
    even = lambda index: col_even[pl.ds(pl.multiple_of(index * group + start, 16), half)]
    odd = lambda index: col_odd[index, pl.ds(pl.multiple_of(start, half), half)]
    for index in range(FIELDS - 1):
        first[index * half : (index + 1) * half] = even(index)
        second[index * half : (index + 1) * half] = odd(index)
    third[:half] = even(FIELDS - 1)
    third[half:strip] = odd(FIELDS - 1)
    for index in range(FIELDS):
        at = strip + index * near_count
        third[at : at + near_count] = col_even[index * group + strip : (index + 1) * group]


def forward(col_even, col_odd):
    _, strip, width = col_odd.shape
    shape = jax.ShapeDtypeStruct(((FIELDS - 1) * strip // 2, width), BF16)
    return pl.pallas_call(
        forward_kernel,
        out_shape=(shape,) * 3,
        in_specs=[vmem_spec()] * 2,
        out_specs=[vmem_spec()] * 3,
        compiler_params=pltpu.CompilerParams(vmem_limit_bytes=VMEM_BYTES),
        name="forward",
    )(col_even, col_odd)


TOGETHER = 2


def masked_start(head, head_dim, width):
    return min(head * head_dim // LANES, (width - 2 * LANES) // LANES) * LANES


def turn_queries(raw, turned, masked):
    width = raw.shape[1]
    head_dim = width // HEADS
    span = 2 * LANES
    line = lax.broadcasted_iota(jnp.int32, (LANES, LANES), 0)
    lane = lax.broadcasted_iota(jnp.int32, (LANES, LANES), 1)
    unit = (line == lane).astype(F32).astype(BF16)
    for at in range(0, width, LANES):
        turned[at : at + LANES] = against(unit, raw[:, at : at + LANES]).astype(BF16)
    channel = lax.broadcasted_iota(jnp.int32, (span, raw.shape[0]), 0)
    for head in range(HEADS):
        start = masked_start(head, head_dim, width)
        low = head * head_dim - start
        keep = ((channel >= low) & (channel < low + head_dim)).astype(F32).astype(BF16)
        masked[head] = turned[start : start + span] * keep


def device_flags():
    row, col = lax.axis_index("row"), lax.axis_index("col")
    row_edge = (row == 0) | (row == lax.axis_size("row") - 1)
    col_edge = (col == 0) | (col == lax.axis_size("col") - 1)
    off = lambda edge: jnp.where(edge, F32(OFF), F32(0.0))
    return (F32(0.0), off(row_edge), off(col_edge), off(row_edge | col_edge))


def head_products(head, segments, refs, queries, width):
    head_dim = width // HEADS
    start = head * head_dim // LANES * LANES
    low = head * head_dim - start
    one_tile = low + head_dim <= LANES
    span = LANES if one_tile else 2 * LANES
    window = slice(start, start + span)
    at = start - masked_start(head, head_dim, width)
    rows_of = lambda field: jnp.concatenate(
        [reader(refs, field, window) for _, _, _, reader in segments], axis=0
    )
    key, value, key_tan, value_tan = (rows_of(field) for field in range(FIELDS))
    query, query_tan = (ref[head, at : at + span] for ref in queries)
    if one_tile:
        scores = jnp.dot(key, query, preferred_element_type=F32)
        slopes = jnp.dot(
            jnp.concatenate([key, key_tan], axis=1),
            jnp.concatenate([query_tan, query], axis=0),
            preferred_element_type=F32,
        )
    else:
        count = key.shape[0]
        both = jnp.dot(
            jnp.concatenate([key, key_tan], axis=0), query, preferred_element_type=F32
        )
        scores = both[:count]
        slopes = jnp.dot(key, query_tan, preferred_element_type=F32) + both[count:]
    line = lax.broadcasted_iota(jnp.int32, (head_dim + 8, span), 0)
    lane = lax.broadcasted_iota(jnp.int32, (head_dim + 8, span), 1)
    pick = ((lane == line + low) & (line < head_dim)).astype(F32).astype(BF16)
    ones_line = lax.broadcasted_iota(jnp.int32, (8, value.shape[0]), 0)
    turned = jnp.concatenate(
        [
            against(pick, value)[:head_dim],
            (ones_line == 0).astype(F32),
            against(pick, value_tan),
        ],
        axis=0,
    )
    return scores, slopes, turned.astype(BF16)


def head_result(head, segments, level_bias, flags, products, olds, width):
    scores, slopes, turned = products
    head_dim = width // HEADS
    pad_dim = head_dim + 8
    scale = head_dim**-0.5
    bias = []
    top = None
    at = 0
    for rows, kind, number, _ in segments:
        amount = flags[number] if kind == "flag" else level_bias[number, head] * LOG2E
        bias.append(amount)
        part = jnp.max(scores[at : at + rows], axis=0, keepdims=True) * (scale * LOG2E) + amount
        top = part if top is None else jnp.maximum(top, part)
        at += rows
    for old in olds:
        top = jnp.maximum(top, old[2][head, 0:1])
    weights_low, product_low = [], []
    at = 0
    for (rows, _, _, _), amount in zip(segments, bias):
        weights = jnp.exp2(scores[at : at + rows] * (scale * LOG2E) + (amount - top))
        weights_low.append(weights.astype(BF16))
        product_low.append((weights * slopes[at : at + rows]).astype(BF16))
        at += rows
    both = jnp.dot(turned, jnp.concatenate(weights_low, axis=0), preferred_element_type=F32)
    extra = jnp.dot(
        turned[:pad_dim], jnp.concatenate(product_low, axis=0), preferred_element_type=F32
    )
    mix = both[:head_dim]
    total = both[head_dim : head_dim + 1]
    row_total = extra[head_dim : head_dim + 1] * scale
    extra = extra[:head_dim] * scale + both[pad_dim : pad_dim + head_dim]
    for old in olds:
        fade = jnp.exp2(old[2][head, 0:1] - top)
        total = total + fade * old[2][head, 1:2]
        row_total = row_total + fade * old[2][head, 2:3]
        mix = mix + fade * old[0][head]
        extra = extra + fade * old[1][head]
    return top, total, row_total, mix, extra


def attend_heads(segments, refs, queries, level_bias, width, olds, keep):
    flags = device_flags()
    stages = [range(first, first + TOGETHER) for first in range(0, HEADS, TOGETHER)]
    make = lambda heads: [head_products(head, segments, refs, queries, width) for head in heads]
    ready = make(stages[0])
    for number, heads in enumerate(stages):
        coming = make(stages[number + 1]) if number + 1 < len(stages) else None
        for head, products in zip(heads, ready):
            keep(head, *head_result(head, segments, level_bias, flags, products, olds, width))
        ready = coming


def keeper(state):
    def keep(head, top, total, row_total, mix, extra):
        state[0][head] = mix
        state[1][head] = extra
        state[2][head, 0:1] = top
        state[2][head, 1:2] = total
        state[2][head, 2:3] = row_total

    return keep


def own_kernel(segments, level_bias, query, qtan, *refs):
    sources, state = refs[: FIELDS + 1], refs[FIELDS + 1 : FIELDS + 4]
    masked, turned = refs[FIELDS + 4 : FIELDS + 6], refs[FIELDS + 6]
    state[2][...] = jnp.zeros(state[2].shape, F32)
    for raw, target in zip((query, qtan), masked):
        turn_queries(raw, turned, target)
    attend_heads(segments, sources, masked, level_bias, query.shape[1], [], keeper(state))


def state_shapes(token_count, width):
    wide = (HEADS, width // HEADS, token_count)
    return (wide, wide, (HEADS, 8, token_count))


def own_cost(token_count, width, key_count):
    return pl.CostEstimate(
        flops=token_count * key_count * HEADS,
        bytes_accessed=token_count * width,
        transcendentals=0,
    )


def attend_own(level_bias, query, qtan, fields, mate, segments):
    token_count, width = query.shape
    states = state_shapes(token_count, width)
    masked = (HEADS, 2 * LANES, token_count)
    operands = (query, qtan, *fields, mate)
    return pl.pallas_call(
        functools.partial(own_kernel, segments),
        out_shape=tuple(jax.ShapeDtypeStruct(s, F32) for s in states)
        + (jax.ShapeDtypeStruct(masked, BF16),) * 2,
        in_specs=[smem_spec()] + [vmem_spec()] * len(operands),
        out_specs=[vmem_spec()] * 5,
        scratch_shapes=[pltpu.VMEM((width, token_count), BF16)],
        compiler_params=pltpu.CompilerParams(vmem_limit_bytes=VMEM_BYTES),
        cost_estimate=own_cost(token_count, width, sum(s[0] for s in segments)),
        name="own",
    )(level_bias, *operands)


def more_kernel(segments, old_count, count, level_bias, *refs):
    queries, refs = refs[:2], refs[2:]
    olds = [refs[3 * i : 3 * i + 3] for i in range(old_count)]
    refs = refs[3 * old_count :]
    sources, state = refs[:count], refs[count:]
    width = state[0].shape[0] * state[0].shape[1]
    state[2][...] = jnp.zeros(state[2].shape, F32)
    attend_heads(segments, sources, queries, level_bias, width, olds, keeper(state))


def attend_more(level_bias, queries, olds, sources, segments, name):
    token_count = queries[0].shape[2]
    width = sources[0].shape[-1]
    operands = (*queries, *[array for old in olds for array in old], *sources)
    return pl.pallas_call(
        functools.partial(more_kernel, segments, len(olds), len(sources)),
        out_shape=tuple(jax.ShapeDtypeStruct(s, F32) for s in state_shapes(token_count, width)),
        in_specs=[smem_spec()] + [vmem_spec()] * len(operands),
        out_specs=[vmem_spec()] * 3,
        compiler_params=pltpu.CompilerParams(vmem_limit_bytes=VMEM_BYTES),
        cost_estimate=own_cost(token_count, width, sum(s[0] for s in segments)),
        name=name,
    )(level_bias, *operands)


def last_kernel(segments, old_count, count, far_count, far_blocks, level_bias, *refs):
    queries, refs = refs[:2], refs[2:]
    olds = [refs[3 * i : 3 * i + 3] for i in range(old_count)]
    refs = refs[3 * old_count :]
    sources, outs = refs[:count], refs[count : count + 2]
    far_keys, mix_acc, tan_acc, turned, sems = refs[count + 2 :]
    width, token_count = outs[0].shape[1], outs[0].shape[0]
    line = lax.broadcasted_iota(jnp.int32, (far_count, FIELDS * far_count), 0)
    lane = lax.broadcasted_iota(jnp.int32, (far_count, FIELDS * far_count), 1)
    far_rows = jnp.concatenate([sources[i][begin:] for i, begin in far_blocks], axis=0)
    for index in range(FIELDS):
        select = (lane == line * FIELDS + index).astype(F32).astype(BF16)
        far_keys[index] = jnp.dot(select, far_rows, preferred_element_type=F32).astype(BF16)
    sources = sources + (far_keys,)

    def keep(head, top, total, row_total, mix, extra):
        inverse = 1.0 / total
        mix = mix * inverse
        mix_acc[head] = mix
        tan_acc[head] = extra * inverse - (row_total * inverse) * mix

    attend_heads(segments, sources, queries, level_bias, width, olds, keep)
    line = lax.broadcasted_iota(jnp.int32, (token_count, token_count), 0)
    lane = lax.broadcasted_iota(jnp.int32, (token_count, token_count), 1)
    unit = (line == lane).astype(F32).astype(BF16)
    sent = []
    for number, acc in enumerate((mix_acc, tan_acc)):
        flat = acc[...].reshape(width, token_count).astype(BF16)
        turned[number] = against(unit, flat).astype(BF16)
        more = chunk_copies(turned.at[number], outs[number], sems, number * FIELDS, FIELDS)
        for copy in more:
            copy.start()
        sent += more
    for copy in sent:
        copy.wait()


def attend_last(level_bias, queries, olds, sources, segments, far_count, far_blocks):
    token_count = queries[0].shape[2]
    width = sources[0].shape[-1]
    states = state_shapes(token_count, width)
    operands = (*queries, *[array for old in olds for array in old], *sources)
    return pl.pallas_call(
        functools.partial(
            last_kernel, segments, len(olds), len(sources), far_count, far_blocks
        ),
        out_shape=(jax.ShapeDtypeStruct((token_count, width), BF16),) * 2,
        in_specs=[smem_spec()] + [vmem_spec()] * len(operands),
        out_specs=[hbm_spec()] * 2,
        scratch_shapes=[
            pltpu.VMEM((FIELDS, far_count, width), BF16),
            pltpu.VMEM(states[0], F32),
            pltpu.VMEM(states[1], F32),
            pltpu.VMEM((2, token_count, width), BF16),
            pltpu.SemaphoreType.DMA((2 * FIELDS,)),
        ],
        compiler_params=pltpu.CompilerParams(vmem_limit_bytes=VMEM_BYTES),
        cost_estimate=own_cost(token_count, width, sum(s[0] for s in segments)),
        name="outer",
    )(level_bias, *operands)


def swap(block, axis, odd):
    count = lax.axis_size(axis)
    route = []
    for low in range(1 if odd else 0, count - 1, 2):
        route += [(low, low + 1), (low + 1, low)]
    return lax.ppermute(block, axis, route)


def part(source, begin, rows):
    return lambda refs, field, window: refs[source][field, begin : begin + rows, window]


def flat_part(source, stride, begin, rows):
    def read(refs, field, window):
        at = field * stride + begin
        return refs[source][at : at + rows, window]

    return read


def forwarded(source, rest, half):
    def read(refs, field, window):
        if field < FIELDS - 1:
            return refs[source][field * half : (field + 1) * half, window]
        return refs[2][rest : rest + half, window]

    return read


def send_to(block, axis, mask):
    return lax.ppermute(block, axis, [(i, i ^ mask) for i in range(lax.axis_size(axis))])


def join(blocks):
    rows = sum(block.shape[0] for block in blocks)
    total, at = None, 0
    for block in blocks:
        count = block.shape[0]
        padded = jnp.pad(block, ((at, rows - at - count), (0, 0)))
        total = padded if total is None else total + padded
        at += count
    return total


def cross_columns(pair):
    count = lax.axis_size("col")
    route = []
    for row in range(lax.axis_size("row")):
        for col in range(count):
            route.append((row * count + col, row * count + (col ^ (2 + row % 2))))
    return lax.ppermute(pair, ("row", "col"), route)


def gather_rows(far):
    count = lax.axis_size("row")
    if count <= 8:
        return [far] + [send_to(far, "row", mask) for mask in range(2, count, 2)]
    for bit in range(1, count.bit_length() - 1):
        far = join([far, send_to(far, "row", 1 << bit)])
    return [far]


def body(
    query_field,
    key_field,
    value_field,
    query_tan,
    key_tan,
    value_tan,
    pool_near,
    pool_far,
    level_bias,
):
    window = query_field.shape[0]
    width = query_field.shape[2]
    cells = window * window
    strip, half = cells // 2, cells // 4
    near_count = cells // (NEAR_POOL * NEAR_POOL)
    row_count, col_count = lax.axis_size("row"), lax.axis_size("col")
    far_count = row_count * col_count
    flat = lambda field: field.reshape(cells, width)
    fields = tuple(flat(f) for f in (key_field, value_field, key_tan, value_tan))

    row_odd, col_even, col_odd, row_even, far = pack(fields, pool_near, pool_far)
    group = strip + near_count
    far = far[:FIELDS]
    got_col_even = swap(col_even, "col", False)
    got_row_odd = swap(row_odd, "row", True)
    got_col_odd = swap(col_odd, "col", True)
    got_row_even = swap(row_even, "row", False)

    *own_state, query, qtan = attend_own(
        level_bias,
        flat(query_field),
        flat(query_tan),
        fields,
        got_row_even,
        [
            (cells, "flag", 0, lambda refs, field, window: refs[field][:, window]),
            (strip, "flag", 0, flat_part(4, group, 0, strip)),
            (near_count, "level", 0, flat_part(4, group, strip, near_count)),
        ],
    )
    queries = (query, qtan)
    far_at = slice(FIELDS * group, FIELDS * group + FIELDS)
    pair = join([far, got_row_even[far_at]])
    far = join([far, got_col_even[far_at], cross_columns(pair)])
    row_state = attend_more(
        level_bias,
        queries,
        [],
        (got_row_odd,),
        [(strip, "flag", 1, part(0, 0, strip))],
        "row_strip",
    )
    got_row_odd, stats = lax.optimization_barrier((got_row_odd, row_state[2]))
    row_state = (row_state[0], row_state[1], stats)
    to_even, to_odd = got_row_odd[:, :half], got_row_odd[:, half:]
    got_outer_even = swap(to_even, "col", False)
    got_outer_odd = swap(to_odd, "col", True)
    got_inner = [swap(block, "row", False) for block in forward(got_col_even, got_col_odd)]
    for bit in range(2, col_count.bit_length() - 1):
        far = join([far, send_to(far, "col", 1 << bit)])
    far = join([far, send_to(far, "row", 1)])

    state = attend_more(
        level_bias,
        queries,
        [row_state],
        (got_col_even, got_col_odd),
        [
            (strip, "flag", 0, flat_part(0, group, 0, strip)),
            (strip, "flag", 2, part(1, 0, strip)),
        ],
        "strips",
    )
    far, stats = lax.optimization_barrier((far, state[2]))
    state = (state[0], state[1], stats)
    far_blocks = gather_rows(far)
    state = attend_more(
        level_bias,
        queries,
        [state],
        (*got_inner, got_col_even, row_even),
        [
            (half, "flag", 0, forwarded(0, 0, half)),
            (half, "flag", 2, forwarded(1, half, half)),
            (near_count, "level", 0, flat_part(2, near_count, strip, near_count)),
            (near_count, "level", 0, flat_part(3, group, strip, near_count)),
            (near_count, "level", 0, flat_part(4, group, strip, near_count)),
        ],
        "inner",
    )
    mixed, mixed_tan = attend_last(
        level_bias,
        queries,
        [state, own_state],
        (got_outer_even, got_outer_odd, *far_blocks),
        [
            (half, "flag", 1, part(0, 0, half)),
            (half, "flag", 3, part(1, 0, half)),
            (far_count, "level", 1, part(2 + len(far_blocks), 0, far_count)),
        ],
        far_count,
        tuple((2 + number, 0) for number in range(len(far_blocks))),
    )
    shape = (window, window, width)
    return (mixed.reshape(shape), mixed_tan.reshape(shape))


def solution(mesh):
    field = P("row", "col", None)
    return jax.shard_map(
        body,
        mesh=mesh,
        in_specs=(field,) * 6 + (P(),) * 3,
        out_specs=(field, field),
        check_vma=False,
    )
```

```python
import functools

import jax
import jax.numpy as jnp
from jax import lax
from jax.experimental import pallas as pl
from jax.experimental.pallas import tpu as pltpu
from jax.sharding import PartitionSpec as P

HEADS = 16
RIM = 8
NEAR_POOL = 4
LOG2E = 1.4426950408889634
OFF = -1e30
PACK_BYTES = 60 * 1024 * 1024
VMEM_BYTES = 28 * 1024 * 1024
LANES = 128
FIELDS = 4
BF16 = jnp.bfloat16
F32 = jnp.float32


def vmem_spec():
    return pl.BlockSpec(memory_space=pltpu.VMEM)


def smem_spec():
    return pl.BlockSpec(memory_space=pltpu.SMEM)


def hbm_spec():
    return pl.BlockSpec(memory_space=pltpu.HBM)


def any_spec():
    return pl.BlockSpec(memory_space=pl.ANY)


def against(left, right):
    return lax.dot_general(left, right, (((1,), (1,)), ((), ())), preferred_element_type=F32)


def chunk_copies(source, target, sems, first, parts):
    rows = source.shape[0]
    step = -(-rows // parts)
    if len(source.shape) == 2:
        step = -(-step // 16) * 16
    copies = []
    for number, begin in enumerate(range(0, rows, step)):
        at = pl.ds(begin, min(step, rows - begin))
        copies.append(pltpu.make_async_copy(source.at[at], target.at[at], sems.at[first + number]))
    return copies


def split3(weights):
    high = weights.astype(BF16)
    rest = weights - high.astype(F32)
    mid = rest.astype(BF16)
    low = (rest - mid.astype(F32)).astype(BF16)
    return jnp.concatenate([high, mid, low], axis=0)


def pool_weights(pool_near, pool_far, cells):
    window = 2 * RIM
    near_side = window // NEAR_POOL
    near_count = near_side * near_side
    lane = lax.broadcasted_iota(jnp.int32, (near_count, cells), 1)
    line = lax.broadcasted_iota(jnp.int32, (near_count, cells), 0)
    row, col = lane // window, lane % window
    near = jnp.zeros((near_count, cells), F32)
    for p in range(NEAR_POOL):
        for q in range(NEAR_POOL):
            hit = (row % NEAR_POOL == p) & (col % NEAR_POOL == q)
            near = jnp.where(hit, pool_near[p, q], near)
    block = (row // NEAR_POOL) * near_side + col // NEAR_POOL
    near = split3(jnp.where(line == block, near, 0.0))
    spread = (line == col).astype(F32).astype(BF16)
    far = jnp.dot(split3(pool_far), spread, preferred_element_type=F32)
    far_line = lax.broadcasted_iota(jnp.int32, far.shape, 0) % window
    far_lane = lax.broadcasted_iota(jnp.int32, far.shape, 1) // window
    far = jnp.where(far_line == far_lane, far, 0.0)
    rows = [
        jnp.sum(far[i * window : (i + 1) * window], axis=0, keepdims=True) for i in range(3)
    ]
    rows.append(jnp.zeros((near_count - 3, cells), F32))
    return jnp.concatenate([near, jnp.concatenate(rows, axis=0).astype(BF16)], axis=0)


def halves(block, width):
    cells = block.shape[0]
    wide = block.astype(F32).reshape(cells // (2 * RIM), 2, RIM, width)
    left = wide[:, 0].reshape(cells // 2, width).astype(BF16)
    right = wide[:, 1].reshape(cells // 2, width).astype(BF16)
    return left, right


def pack_kernel(pool_near, pool_far, *refs):
    sources, outs = refs[:FIELDS], refs[FIELDS : FIELDS + 6]
    held = refs[FIELDS + 6]
    kept, sems, out_sems = refs[FIELDS + 7 : -2], refs[-2], refs[-1]
    cells, width = sources[0].shape
    strip, half = cells // 2, cells // 4
    near_count = cells // (NEAR_POOL * NEAR_POOL)
    row_is_even = lax.axis_index("row") % 2 == 0
    col_is_even = lax.axis_index("col") % 2 == 0
    copies = []
    for index, source in enumerate(sources):
        copies += chunk_copies(source, held.at[index], sems, 2 * index, 2)
    for copy in copies:
        copy.start()
    weights = pool_weights(pool_near, pool_far[...], cells)
    far_rows = []
    sent = []
    for index in range(FIELDS):
        copies[2 * index].wait()
        copies[2 * index + 1].wait()
        block = held[index]
        left, right = halves(block, width)
        even = jnp.where(col_is_even, right, left)
        odd = jnp.where(col_is_even, left, right)
        outer = lambda side: jnp.where(row_is_even, side[:half], side[half:])
        pooled = jnp.dot(weights, block, preferred_element_type=F32)
        near = pooled[:near_count] + (
            pooled[near_count : 2 * near_count] + pooled[2 * near_count : 3 * near_count]
        )
        near = near.astype(BF16)
        far = pooled[3 * near_count :]
        far_rows.append(far[0:1] + (far[1:2] + far[2:3]))
        kept[0][index] = outer(even)
        kept[5][index] = outer(odd)
        at = index * (strip + near_count)
        kept[1][at : at + strip] = even
        kept[1][at + strip : at + strip + near_count] = near
        kept[2][index] = odd
        kept[3][at : at + strip] = jnp.where(row_is_even, block[strip:], block[:strip])
        kept[3][at + strip : at + strip + near_count] = near
        for number in (0, 2, 5):
            copy = pltpu.make_async_copy(
                kept[number].at[index], outs[number].at[index], out_sems.at[6 * index + number]
            )
            copy.start()
            sent.append(copy)
    far_rows.append(jnp.zeros((16 - FIELDS, width), F32))
    kept[4][...] = jnp.concatenate(far_rows, axis=0).astype(BF16)
    for source in (1, 3):
        kept[source][FIELDS * (strip + near_count) :] = kept[4][...]
    for number, source in ((1, 1), (3, 3), (4, 4)):
        copy = pltpu.make_async_copy(kept[source], outs[source], out_sems.at[number])
        copy.start()
        sent.append(copy)
    for copy in sent:
        copy.wait()


def pack(fields, pool_near, pool_far):
    cells, width = fields[0].shape
    strip = cells // 2
    near_count = cells // (NEAR_POOL * NEAR_POOL)
    corner = (FIELDS, strip // 2, width)
    shapes = [
        corner,
        (FIELDS * (strip + near_count) + 16, width),
        (FIELDS, strip, width),
        (FIELDS * (strip + near_count) + 16, width),
        (16, width),
        corner,
    ]
    return pl.pallas_call(
        pack_kernel,
        out_shape=tuple(jax.ShapeDtypeStruct(s, BF16) for s in shapes),
        in_specs=[smem_spec(), vmem_spec()] + [hbm_spec()] * FIELDS,
        out_specs=[hbm_spec()] * len(shapes),
        scratch_shapes=[pltpu.VMEM((FIELDS, cells, width), BF16)]
        + [pltpu.VMEM(s, BF16) for s in shapes]
        + [pltpu.SemaphoreType.DMA((2 * FIELDS,)), pltpu.SemaphoreType.DMA((6 * FIELDS,))],
        compiler_params=pltpu.CompilerParams(vmem_limit_bytes=PACK_BYTES),
        name="pack",
    )(pool_near, pool_far, *fields)


def forward_kernel(col_even, col_odd, first, second, third):
    strip = col_odd.shape[1]
    half = strip // 2
    near_count = (col_even.shape[0] - 16) // FIELDS - strip
    group = strip + near_count
    start = (1 - lax.axis_index("row") % 2) * half
    even = lambda index: col_even[pl.ds(pl.multiple_of(index * group + start, 16), half)]
    odd = lambda index: col_odd[index, pl.ds(pl.multiple_of(start, half), half)]
    for index in range(FIELDS - 1):
        first[index * half : (index + 1) * half] = even(index)
        second[index * half : (index + 1) * half] = odd(index)
    third[:half] = even(FIELDS - 1)
    third[half:strip] = odd(FIELDS - 1)
    for index in range(FIELDS):
        at = strip + index * near_count
        third[at : at + near_count] = col_even[index * group + strip : (index + 1) * group]


def forward(col_even, col_odd):
    _, strip, width = col_odd.shape
    shape = jax.ShapeDtypeStruct(((FIELDS - 1) * strip // 2, width), BF16)
    return pl.pallas_call(
        forward_kernel,
        out_shape=(shape,) * 3,
        in_specs=[vmem_spec()] * 2,
        out_specs=[vmem_spec()] * 3,
        compiler_params=pltpu.CompilerParams(vmem_limit_bytes=VMEM_BYTES),
        name="forward",
    )(col_even, col_odd)


TOGETHER = 2


def masked_start(head, head_dim, width):
    return min(head * head_dim // LANES, (width - 2 * LANES) // LANES) * LANES


def turn_queries(raw, turned, masked):
    width = raw.shape[1]
    head_dim = width // HEADS
    span = 2 * LANES
    line = lax.broadcasted_iota(jnp.int32, (LANES, LANES), 0)
    lane = lax.broadcasted_iota(jnp.int32, (LANES, LANES), 1)
    unit = (line == lane).astype(F32).astype(BF16)
    for at in range(0, width, LANES):
        turned[at : at + LANES] = against(unit, raw[:, at : at + LANES]).astype(BF16)
    channel = lax.broadcasted_iota(jnp.int32, (span, raw.shape[0]), 0)
    for head in range(HEADS):
        start = masked_start(head, head_dim, width)
        low = head * head_dim - start
        keep = ((channel >= low) & (channel < low + head_dim)).astype(F32).astype(BF16)
        masked[head] = turned[start : start + span] * keep


def device_flags():
    row, col = lax.axis_index("row"), lax.axis_index("col")
    row_edge = (row == 0) | (row == lax.axis_size("row") - 1)
    col_edge = (col == 0) | (col == lax.axis_size("col") - 1)
    off = lambda edge: jnp.where(edge, F32(OFF), F32(0.0))
    return (F32(0.0), off(row_edge), off(col_edge), off(row_edge | col_edge))


def head_products(head, segments, refs, queries, width):
    head_dim = width // HEADS
    start = head * head_dim // LANES * LANES
    low = head * head_dim - start
    one_tile = low + head_dim <= LANES
    span = LANES if one_tile else 2 * LANES
    window = slice(start, start + span)
    at = start - masked_start(head, head_dim, width)
    rows_of = lambda field: jnp.concatenate(
        [reader(refs, field, window) for _, _, _, reader in segments], axis=0
    )
    key, value, key_tan, value_tan = (rows_of(field) for field in range(FIELDS))
    query, query_tan = (ref[head, at : at + span] for ref in queries)
    if one_tile:
        scores = jnp.dot(key, query, preferred_element_type=F32)
        slopes = jnp.dot(
            jnp.concatenate([key, key_tan], axis=1),
            jnp.concatenate([query_tan, query], axis=0),
            preferred_element_type=F32,
        )
    else:
        count = key.shape[0]
        both = jnp.dot(
            jnp.concatenate([key, key_tan], axis=0), query, preferred_element_type=F32
        )
        scores = both[:count]
        slopes = jnp.dot(key, query_tan, preferred_element_type=F32) + both[count:]
    line = lax.broadcasted_iota(jnp.int32, (head_dim + 8, span), 0)
    lane = lax.broadcasted_iota(jnp.int32, (head_dim + 8, span), 1)
    pick = ((lane == line + low) & (line < head_dim)).astype(F32).astype(BF16)
    ones_line = lax.broadcasted_iota(jnp.int32, (8, value.shape[0]), 0)
    turned = jnp.concatenate(
        [
            against(pick, value)[:head_dim],
            (ones_line == 0).astype(F32),
            against(pick, value_tan),
        ],
        axis=0,
    )
    return scores, slopes, turned.astype(BF16)


def head_result(head, segments, level_bias, flags, products, olds, width):
    scores, slopes, turned = products
    head_dim = width // HEADS
    pad_dim = head_dim + 8
    scale = head_dim**-0.5
    bias = []
    top = None
    at = 0
    for rows, kind, number, _ in segments:
        amount = flags[number] if kind == "flag" else level_bias[number, head] * LOG2E
        bias.append(amount)
        part = jnp.max(scores[at : at + rows], axis=0, keepdims=True) * (scale * LOG2E) + amount
        top = part if top is None else jnp.maximum(top, part)
        at += rows
    for old in olds:
        top = jnp.maximum(top, old[2][head, 0:1])
    weights_low, product_low = [], []
    at = 0
    for (rows, _, _, _), amount in zip(segments, bias):
        weights = jnp.exp2(scores[at : at + rows] * (scale * LOG2E) + (amount - top))
        weights_low.append(weights.astype(BF16))
        product_low.append((weights * slopes[at : at + rows]).astype(BF16))
        at += rows
    both = jnp.dot(turned, jnp.concatenate(weights_low, axis=0), preferred_element_type=F32)
    extra = jnp.dot(
        turned[:pad_dim], jnp.concatenate(product_low, axis=0), preferred_element_type=F32
    )
    mix = both[:head_dim]
    total = both[head_dim : head_dim + 1]
    row_total = extra[head_dim : head_dim + 1] * scale
    extra = extra[:head_dim] * scale + both[pad_dim : pad_dim + head_dim]
    for old in olds:
        fade = jnp.exp2(old[2][head, 0:1] - top)
        total = total + fade * old[2][head, 1:2]
        row_total = row_total + fade * old[2][head, 2:3]
        mix = mix + fade * old[0][head]
        extra = extra + fade * old[1][head]
    return top, total, row_total, mix, extra


def attend_heads(segments, refs, queries, level_bias, width, olds, keep):
    flags = device_flags()
    stages = [range(first, first + TOGETHER) for first in range(0, HEADS, TOGETHER)]
    make = lambda heads: [head_products(head, segments, refs, queries, width) for head in heads]
    ready = make(stages[0])
    for number, heads in enumerate(stages):
        coming = make(stages[number + 1]) if number + 1 < len(stages) else None
        for head, products in zip(heads, ready):
            keep(head, *head_result(head, segments, level_bias, flags, products, olds, width))
        ready = coming


def keeper(state):
    def keep(head, top, total, row_total, mix, extra):
        state[0][head] = mix
        state[1][head] = extra
        state[2][head, 0:1] = top
        state[2][head, 1:2] = total
        state[2][head, 2:3] = row_total

    return keep


def own_kernel(segments, level_bias, query, qtan, *refs):
    sources, state = refs[: FIELDS + 1], refs[FIELDS + 1 : FIELDS + 4]
    masked, turned = refs[FIELDS + 4 : FIELDS + 6], refs[FIELDS + 6]
    state[2][...] = jnp.zeros(state[2].shape, F32)
    for raw, target in zip((query, qtan), masked):
        turn_queries(raw, turned, target)
    attend_heads(segments, sources, masked, level_bias, query.shape[1], [], keeper(state))


def state_shapes(token_count, width):
    wide = (HEADS, width // HEADS, token_count)
    return (wide, wide, (HEADS, 8, token_count))


def own_cost(token_count, width, key_count):
    return pl.CostEstimate(
        flops=token_count * key_count * HEADS,
        bytes_accessed=token_count * width,
        transcendentals=0,
    )


def attend_own(level_bias, query, qtan, fields, mate, segments):
    token_count, width = query.shape
    states = state_shapes(token_count, width)
    masked = (HEADS, 2 * LANES, token_count)
    operands = (query, qtan, *fields, mate)
    return pl.pallas_call(
        functools.partial(own_kernel, segments),
        out_shape=tuple(jax.ShapeDtypeStruct(s, F32) for s in states)
        + (jax.ShapeDtypeStruct(masked, BF16),) * 2,
        in_specs=[smem_spec()] + [vmem_spec()] * len(operands),
        out_specs=[vmem_spec()] * 5,
        scratch_shapes=[pltpu.VMEM((width, token_count), BF16)],
        compiler_params=pltpu.CompilerParams(vmem_limit_bytes=VMEM_BYTES),
        cost_estimate=own_cost(token_count, width, sum(s[0] for s in segments)),
        name="own",
    )(level_bias, *operands)


def more_kernel(segments, old_count, count, level_bias, *refs):
    queries, refs = refs[:2], refs[2:]
    olds = [refs[3 * i : 3 * i + 3] for i in range(old_count)]
    refs = refs[3 * old_count :]
    sources, state = refs[:count], refs[count:]
    width = state[0].shape[0] * state[0].shape[1]
    state[2][...] = jnp.zeros(state[2].shape, F32)
    attend_heads(segments, sources, queries, level_bias, width, olds, keeper(state))


def attend_more(level_bias, queries, olds, sources, segments, name):
    token_count = queries[0].shape[2]
    width = sources[0].shape[-1]
    operands = (*queries, *[array for old in olds for array in old], *sources)
    return pl.pallas_call(
        functools.partial(more_kernel, segments, len(olds), len(sources)),
        out_shape=tuple(jax.ShapeDtypeStruct(s, F32) for s in state_shapes(token_count, width)),
        in_specs=[smem_spec()] + [vmem_spec()] * len(operands),
        out_specs=[vmem_spec()] * 3,
        compiler_params=pltpu.CompilerParams(vmem_limit_bytes=VMEM_BYTES),
        cost_estimate=own_cost(token_count, width, sum(s[0] for s in segments)),
        name=name,
    )(level_bias, *operands)


def last_kernel(segments, old_count, count, far_count, far_blocks, level_bias, *refs):
    queries, refs = refs[:2], refs[2:]
    olds = [refs[3 * i : 3 * i + 3] for i in range(old_count)]
    refs = refs[3 * old_count :]
    sources, outs = refs[:count], refs[count : count + 2]
    far_keys, mix_acc, tan_acc, turned, sems = refs[count + 2 :]
    width, token_count = outs[0].shape[1], outs[0].shape[0]
    line = lax.broadcasted_iota(jnp.int32, (far_count, FIELDS * far_count), 0)
    lane = lax.broadcasted_iota(jnp.int32, (far_count, FIELDS * far_count), 1)
    far_rows = jnp.concatenate([sources[i][begin:] for i, begin in far_blocks], axis=0)
    for index in range(FIELDS):
        select = (lane == line * FIELDS + index).astype(F32).astype(BF16)
        far_keys[index] = jnp.dot(select, far_rows, preferred_element_type=F32).astype(BF16)
    sources = sources + (far_keys,)

    def keep(head, top, total, row_total, mix, extra):
        inverse = 1.0 / total
        mix = mix * inverse
        mix_acc[head] = mix
        tan_acc[head] = extra * inverse - (row_total * inverse) * mix

    attend_heads(segments, sources, queries, level_bias, width, olds, keep)
    line = lax.broadcasted_iota(jnp.int32, (token_count, token_count), 0)
    lane = lax.broadcasted_iota(jnp.int32, (token_count, token_count), 1)
    unit = (line == lane).astype(F32).astype(BF16)
    sent = []
    for number, acc in enumerate((mix_acc, tan_acc)):
        flat = acc[...].reshape(width, token_count).astype(BF16)
        turned[number] = against(unit, flat).astype(BF16)
        more = chunk_copies(turned.at[number], outs[number], sems, number * FIELDS, FIELDS)
        for copy in more:
            copy.start()
        sent += more
    for copy in sent:
        copy.wait()


def attend_last(level_bias, queries, olds, sources, segments, far_count, far_blocks):
    token_count = queries[0].shape[2]
    width = sources[0].shape[-1]
    states = state_shapes(token_count, width)
    operands = (*queries, *[array for old in olds for array in old], *sources)
    return pl.pallas_call(
        functools.partial(
            last_kernel, segments, len(olds), len(sources), far_count, far_blocks
        ),
        out_shape=(jax.ShapeDtypeStruct((token_count, width), BF16),) * 2,
        in_specs=[smem_spec()] + [vmem_spec()] * len(operands),
        out_specs=[hbm_spec()] * 2,
        scratch_shapes=[
            pltpu.VMEM((FIELDS, far_count, width), BF16),
            pltpu.VMEM(states[0], F32),
            pltpu.VMEM(states[1], F32),
            pltpu.VMEM((2, token_count, width), BF16),
            pltpu.SemaphoreType.DMA((2 * FIELDS,)),
        ],
        compiler_params=pltpu.CompilerParams(vmem_limit_bytes=VMEM_BYTES),
        cost_estimate=own_cost(token_count, width, sum(s[0] for s in segments)),
        name="outer",
    )(level_bias, *operands)


def swap(block, axis, odd):
    count = lax.axis_size(axis)
    route = []
    for low in range(1 if odd else 0, count - 1, 2):
        route += [(low, low + 1), (low + 1, low)]
    return lax.ppermute(block, axis, route)


def part(source, begin, rows):
    return lambda refs, field, window: refs[source][field, begin : begin + rows, window]


def flat_part(source, stride, begin, rows):
    def read(refs, field, window):
        at = field * stride + begin
        return refs[source][at : at + rows, window]

    return read


def forwarded(source, rest, half):
    def read(refs, field, window):
        if field < FIELDS - 1:
            return refs[source][field * half : (field + 1) * half, window]
        return refs[2][rest : rest + half, window]

    return read


def send_to(block, axis, mask):
    return lax.ppermute(block, axis, [(i, i ^ mask) for i in range(lax.axis_size(axis))])


def join(blocks):
    rows = sum(block.shape[0] for block in blocks)
    total, at = None, 0
    for block in blocks:
        count = block.shape[0]
        padded = jnp.pad(block, ((at, rows - at - count), (0, 0)))
        total = padded if total is None else total + padded
        at += count
    return total


def cross_columns(pair):
    count = lax.axis_size("col")
    route = []
    for row in range(lax.axis_size("row")):
        for col in range(count):
            route.append((row * count + col, row * count + (col ^ (2 + row % 2))))
    return lax.ppermute(pair, ("row", "col"), route)


def gather_rows(far):
    count = lax.axis_size("row")
    if count <= 8:
        return [far] + [send_to(far, "row", mask) for mask in range(2, count, 2)]
    for bit in range(1, count.bit_length() - 1):
        far = join([far, send_to(far, "row", 1 << bit)])
    return [far]


def body(
    query_field,
    key_field,
    value_field,
    query_tan,
    key_tan,
    value_tan,
    pool_near,
    pool_far,
    level_bias,
):
    window = query_field.shape[0]
    width = query_field.shape[2]
    cells = window * window
    strip, half = cells // 2, cells // 4
    near_count = cells // (NEAR_POOL * NEAR_POOL)
    row_count, col_count = lax.axis_size("row"), lax.axis_size("col")
    far_count = row_count * col_count
    flat = lambda field: field.reshape(cells, width)
    fields = tuple(flat(f) for f in (key_field, value_field, key_tan, value_tan))

    row_odd_even, col_even, col_odd, row_even, far, row_odd_odd = pack(
        fields, pool_near, pool_far
    )
    group = strip + near_count
    far = far[:FIELDS]
    got_col_even = swap(col_even, "col", False)
    got_row_odd_even = swap(row_odd_even, "row", True)
    got_row_odd_odd = swap(row_odd_odd, "row", True)
    got_col_odd = swap(col_odd, "col", True)
    got_row_even = swap(row_even, "row", False)

    *own_state, query, qtan = attend_own(
        level_bias,
        flat(query_field),
        flat(query_tan),
        fields,
        got_row_even,
        [
            (cells, "flag", 0, lambda refs, field, window: refs[field][:, window]),
            (strip, "flag", 0, flat_part(4, group, 0, strip)),
            (near_count, "level", 0, flat_part(4, group, strip, near_count)),
        ],
    )
    queries = (query, qtan)
    far_at = slice(FIELDS * group, FIELDS * group + FIELDS)
    pair = join([far, got_row_even[far_at]])
    far = join([far, got_col_even[far_at], cross_columns(pair)])
    got_row_odd_even, stats = lax.optimization_barrier((got_row_odd_even, own_state[2]))
    own_state = (own_state[0], own_state[1], stats)
    row_state = attend_more(
        level_bias,
        queries,
        [],
        (got_row_odd_even,),
        [(half, "flag", 1, part(0, 0, half))],
        "row_strip",
    )
    got_row_odd_odd, stats = lax.optimization_barrier((got_row_odd_odd, row_state[2]))
    row_state = (row_state[0], row_state[1], stats)
    got_outer_even = swap(got_row_odd_even, "col", False)
    got_outer_odd = swap(got_row_odd_odd, "col", True)
    got_inner = [swap(block, "row", False) for block in forward(got_col_even, got_col_odd)]
    for bit in range(2, col_count.bit_length() - 1):
        far = join([far, send_to(far, "col", 1 << bit)])
    far = join([far, send_to(far, "row", 1)])

    state = attend_more(
        level_bias,
        queries,
        [row_state],
        (got_col_even, got_col_odd, got_row_odd_odd),
        [
            (strip, "flag", 0, flat_part(0, group, 0, strip)),
            (strip, "flag", 2, part(1, 0, strip)),
            (half, "flag", 1, part(2, 0, half)),
        ],
        "strips",
    )
    far, stats = lax.optimization_barrier((far, state[2]))
    state = (state[0], state[1], stats)
    far_blocks = gather_rows(far)
    state = attend_more(
        level_bias,
        queries,
        [state],
        (*got_inner, got_col_even, row_even),
        [
            (half, "flag", 0, forwarded(0, 0, half)),
            (half, "flag", 2, forwarded(1, half, half)),
            (near_count, "level", 0, flat_part(2, near_count, strip, near_count)),
            (near_count, "level", 0, flat_part(3, group, strip, near_count)),
            (near_count, "level", 0, flat_part(4, group, strip, near_count)),
        ],
        "inner",
    )
    mixed, mixed_tan = attend_last(
        level_bias,
        queries,
        [state, own_state],
        (got_outer_even, got_outer_odd, *far_blocks),
        [
            (half, "flag", 1, part(0, 0, half)),
            (half, "flag", 3, part(1, 0, half)),
            (far_count, "level", 1, part(2 + len(far_blocks), 0, far_count)),
        ],
        far_count,
        tuple((2 + number, 0) for number in range(len(far_blocks))),
    )
    shape = (window, window, width)
    return (mixed.reshape(shape), mixed_tan.reshape(shape))


def solution(mesh):
    field = P("row", "col", None)
    return jax.shard_map(
        body,
        mesh=mesh,
        in_specs=(field,) * 6 + (P(),) * 3,
        out_specs=(field, field),
        check_vma=False,
    )
```

```python
import functools

import jax
import jax.numpy as jnp
from jax import lax
from jax.experimental import pallas as pl
from jax.experimental.pallas import tpu as pltpu
from jax.sharding import PartitionSpec as P

HEADS = 16
RIM = 8
NEAR_POOL = 4
LOG2E = 1.4426950408889634
OFF = -1e30
PACK_BYTES = 60 * 1024 * 1024
VMEM_BYTES = 28 * 1024 * 1024
LANES = 128
FIELDS = 4
BF16 = jnp.bfloat16
F32 = jnp.float32


def vmem_spec():
    return pl.BlockSpec(memory_space=pltpu.VMEM)


def smem_spec():
    return pl.BlockSpec(memory_space=pltpu.SMEM)


def hbm_spec():
    return pl.BlockSpec(memory_space=pltpu.HBM)


def any_spec():
    return pl.BlockSpec(memory_space=pl.ANY)


def against(left, right):
    return lax.dot_general(left, right, (((1,), (1,)), ((), ())), preferred_element_type=F32)


def chunk_copies(source, target, sems, first, parts):
    rows = source.shape[0]
    step = -(-rows // parts)
    if len(source.shape) == 2:
        step = -(-step // 16) * 16
    copies = []
    for number, begin in enumerate(range(0, rows, step)):
        at = pl.ds(begin, min(step, rows - begin))
        copies.append(pltpu.make_async_copy(source.at[at], target.at[at], sems.at[first + number]))
    return copies


def split3(weights):
    high = weights.astype(BF16)
    rest = weights - high.astype(F32)
    mid = rest.astype(BF16)
    low = (rest - mid.astype(F32)).astype(BF16)
    return jnp.concatenate([high, mid, low], axis=0)


def pool_weights(pool_near, pool_far, cells):
    window = 2 * RIM
    near_side = window // NEAR_POOL
    near_count = near_side * near_side
    lane = lax.broadcasted_iota(jnp.int32, (near_count, cells), 1)
    line = lax.broadcasted_iota(jnp.int32, (near_count, cells), 0)
    row, col = lane // window, lane % window
    near = jnp.zeros((near_count, cells), F32)
    for p in range(NEAR_POOL):
        for q in range(NEAR_POOL):
            hit = (row % NEAR_POOL == p) & (col % NEAR_POOL == q)
            near = jnp.where(hit, pool_near[p, q], near)
    block = (row // NEAR_POOL) * near_side + col // NEAR_POOL
    near = split3(jnp.where(line == block, near, 0.0))
    spread = (line == col).astype(F32).astype(BF16)
    far = jnp.dot(split3(pool_far), spread, preferred_element_type=F32)
    far_line = lax.broadcasted_iota(jnp.int32, far.shape, 0) % window
    far_lane = lax.broadcasted_iota(jnp.int32, far.shape, 1) // window
    far = jnp.where(far_line == far_lane, far, 0.0)
    rows = [
        jnp.sum(far[i * window : (i + 1) * window], axis=0, keepdims=True) for i in range(3)
    ]
    rows.append(jnp.zeros((near_count - 3, cells), F32))
    return jnp.concatenate([near, jnp.concatenate(rows, axis=0).astype(BF16)], axis=0)


def halves(block, width):
    cells = block.shape[0]
    wide = block.astype(F32).reshape(cells // (2 * RIM), 2, RIM, width)
    left = wide[:, 0].reshape(cells // 2, width).astype(BF16)
    right = wide[:, 1].reshape(cells // 2, width).astype(BF16)
    return left, right


def pack_kernel(pool_near, pool_far, *refs):
    sources, outs = refs[:FIELDS], refs[FIELDS : FIELDS + 6]
    held = refs[FIELDS + 6]
    kept, sems, out_sems = refs[FIELDS + 7 : -2], refs[-2], refs[-1]
    cells, width = sources[0].shape
    strip, half = cells // 2, cells // 4
    near_count = cells // (NEAR_POOL * NEAR_POOL)
    row_is_even = lax.axis_index("row") % 2 == 0
    col_is_even = lax.axis_index("col") % 2 == 0
    copies = []
    for index, source in enumerate(sources):
        copies += chunk_copies(source, held.at[index], sems, 2 * index, 2)
    for copy in copies:
        copy.start()
    weights = pool_weights(pool_near, pool_far[...], cells)
    far_rows = []
    sent = []
    for index in range(FIELDS):
        copies[2 * index].wait()
        copies[2 * index + 1].wait()
        block = held[index]
        left, right = halves(block, width)
        even = jnp.where(col_is_even, right, left)
        odd = jnp.where(col_is_even, left, right)
        outer = lambda side: jnp.where(row_is_even, side[:half], side[half:])
        pooled = jnp.dot(weights, block, preferred_element_type=F32)
        near = pooled[:near_count] + (
            pooled[near_count : 2 * near_count] + pooled[2 * near_count : 3 * near_count]
        )
        near = near.astype(BF16)
        far = pooled[3 * near_count :]
        far_rows.append(far[0:1] + (far[1:2] + far[2:3]))
        kept[0][index] = outer(even)
        kept[5][index] = outer(odd)
        at = index * (strip + near_count)
        kept[1][at : at + strip] = even
        kept[1][at + strip : at + strip + near_count] = near
        kept[2][index] = odd
        kept[3][at : at + strip] = jnp.where(row_is_even, block[strip:], block[:strip])
        kept[3][at + strip : at + strip + near_count] = near
        for number in (0, 2, 5):
            copy = pltpu.make_async_copy(
                kept[number].at[index], outs[number].at[index], out_sems.at[6 * index + number]
            )
            copy.start()
            sent.append(copy)
    far_rows.append(jnp.zeros((16 - FIELDS, width), F32))
    kept[4][...] = jnp.concatenate(far_rows, axis=0).astype(BF16)
    for source in (1, 3):
        kept[source][FIELDS * (strip + near_count) :] = kept[4][...]
    for number, source in ((1, 1), (3, 3), (4, 4)):
        copy = pltpu.make_async_copy(kept[source], outs[source], out_sems.at[number])
        copy.start()
        sent.append(copy)
    for copy in sent:
        copy.wait()


def pack(fields, pool_near, pool_far):
    cells, width = fields[0].shape
    strip = cells // 2
    near_count = cells // (NEAR_POOL * NEAR_POOL)
    corner = (FIELDS, strip // 2, width)
    shapes = [
        corner,
        (FIELDS * (strip + near_count) + 16, width),
        (FIELDS, strip, width),
        (FIELDS * (strip + near_count) + 16, width),
        (16, width),
        corner,
    ]
    return pl.pallas_call(
        pack_kernel,
        out_shape=tuple(jax.ShapeDtypeStruct(s, BF16) for s in shapes),
        in_specs=[smem_spec(), vmem_spec()] + [hbm_spec()] * FIELDS,
        out_specs=[hbm_spec()] * len(shapes),
        scratch_shapes=[pltpu.VMEM((FIELDS, cells, width), BF16)]
        + [pltpu.VMEM(s, BF16) for s in shapes]
        + [pltpu.SemaphoreType.DMA((2 * FIELDS,)), pltpu.SemaphoreType.DMA((6 * FIELDS,))],
        compiler_params=pltpu.CompilerParams(vmem_limit_bytes=PACK_BYTES),
        name="pack",
    )(pool_near, pool_far, *fields)


def forward_kernel(col_even, col_odd, first, second, third):
    strip = col_odd.shape[1]
    half = strip // 2
    near_count = (col_even.shape[0] - 16) // FIELDS - strip
    group = strip + near_count
    start = (1 - lax.axis_index("row") % 2) * half
    even = lambda index: col_even[pl.ds(pl.multiple_of(index * group + start, 16), half)]
    odd = lambda index: col_odd[index, pl.ds(pl.multiple_of(start, half), half)]
    for index in range(FIELDS - 1):
        first[index * half : (index + 1) * half] = even(index)
        second[index * half : (index + 1) * half] = odd(index)
    third[:half] = even(FIELDS - 1)
    third[half:strip] = odd(FIELDS - 1)
    for index in range(FIELDS):
        at = strip + index * near_count
        third[at : at + near_count] = col_even[index * group + strip : (index + 1) * group]


def forward(col_even, col_odd):
    _, strip, width = col_odd.shape
    shape = jax.ShapeDtypeStruct(((FIELDS - 1) * strip // 2, width), BF16)
    return pl.pallas_call(
        forward_kernel,
        out_shape=(shape,) * 3,
        in_specs=[vmem_spec()] * 2,
        out_specs=[vmem_spec()] * 3,
        compiler_params=pltpu.CompilerParams(vmem_limit_bytes=VMEM_BYTES),
        name="forward",
    )(col_even, col_odd)


TOGETHER = 2


def masked_start(head, head_dim, width):
    return min(head * head_dim // LANES, (width - 2 * LANES) // LANES) * LANES


def turn_queries(raw, turned, masked):
    width = raw.shape[1]
    head_dim = width // HEADS
    span = 2 * LANES
    line = lax.broadcasted_iota(jnp.int32, (LANES, LANES), 0)
    lane = lax.broadcasted_iota(jnp.int32, (LANES, LANES), 1)
    unit = (line == lane).astype(F32).astype(BF16)
    for at in range(0, width, LANES):
        turned[at : at + LANES] = against(unit, raw[:, at : at + LANES]).astype(BF16)
    channel = lax.broadcasted_iota(jnp.int32, (span, raw.shape[0]), 0)
    for head in range(HEADS):
        start = masked_start(head, head_dim, width)
        low = head * head_dim - start
        keep = ((channel >= low) & (channel < low + head_dim)).astype(F32).astype(BF16)
        masked[head] = turned[start : start + span] * keep


def device_flags():
    row, col = lax.axis_index("row"), lax.axis_index("col")
    row_edge = (row == 0) | (row == lax.axis_size("row") - 1)
    col_edge = (col == 0) | (col == lax.axis_size("col") - 1)
    off = lambda edge: jnp.where(edge, F32(OFF), F32(0.0))
    return (F32(0.0), off(row_edge), off(col_edge), off(row_edge | col_edge))


def head_products(head, segments, refs, queries, width):
    head_dim = width // HEADS
    start = head * head_dim // LANES * LANES
    low = head * head_dim - start
    one_tile = low + head_dim <= LANES
    span = LANES if one_tile else 2 * LANES
    window = slice(start, start + span)
    at = start - masked_start(head, head_dim, width)
    rows_of = lambda field: jnp.concatenate(
        [reader(refs, field, window) for _, _, _, reader in segments], axis=0
    )
    key, value, key_tan, value_tan = (rows_of(field) for field in range(FIELDS))
    query, query_tan = (ref[head, at : at + span] for ref in queries)
    if one_tile:
        scores = jnp.dot(key, query, preferred_element_type=F32)
        slopes = jnp.dot(
            jnp.concatenate([key, key_tan], axis=1),
            jnp.concatenate([query_tan, query], axis=0),
            preferred_element_type=F32,
        )
    else:
        count = key.shape[0]
        both = jnp.dot(
            jnp.concatenate([key, key_tan], axis=0), query, preferred_element_type=F32
        )
        scores = both[:count]
        slopes = jnp.dot(key, query_tan, preferred_element_type=F32) + both[count:]
    line = lax.broadcasted_iota(jnp.int32, (head_dim + 8, span), 0)
    lane = lax.broadcasted_iota(jnp.int32, (head_dim + 8, span), 1)
    pick = ((lane == line + low) & (line < head_dim)).astype(F32).astype(BF16)
    ones_line = lax.broadcasted_iota(jnp.int32, (8, value.shape[0]), 0)
    turned = jnp.concatenate(
        [
            against(pick, value)[:head_dim],
            (ones_line == 0).astype(F32),
            against(pick, value_tan),
        ],
        axis=0,
    )
    return scores, slopes, turned.astype(BF16)


def head_result(head, segments, level_bias, flags, products, olds, width):
    scores, slopes, turned = products
    head_dim = width // HEADS
    pad_dim = head_dim + 8
    scale = head_dim**-0.5
    bias = []
    top = None
    at = 0
    for rows, kind, number, _ in segments:
        amount = flags[number] if kind == "flag" else level_bias[number, head] * LOG2E
        bias.append(amount)
        part = jnp.max(scores[at : at + rows], axis=0, keepdims=True) * (scale * LOG2E) + amount
        top = part if top is None else jnp.maximum(top, part)
        at += rows
    for old in olds:
        top = jnp.maximum(top, old[2][head, 0:1])
    weights_low, product_low = [], []
    at = 0
    for (rows, _, _, _), amount in zip(segments, bias):
        weights = jnp.exp2(scores[at : at + rows] * (scale * LOG2E) + (amount - top))
        weights_low.append(weights.astype(BF16))
        product_low.append((weights * slopes[at : at + rows]).astype(BF16))
        at += rows
    both = jnp.dot(turned, jnp.concatenate(weights_low, axis=0), preferred_element_type=F32)
    extra = jnp.dot(
        turned[:pad_dim], jnp.concatenate(product_low, axis=0), preferred_element_type=F32
    )
    mix = both[:head_dim]
    total = both[head_dim : head_dim + 1]
    row_total = extra[head_dim : head_dim + 1] * scale
    extra = extra[:head_dim] * scale + both[pad_dim : pad_dim + head_dim]
    for old in olds:
        fade = jnp.exp2(old[2][head, 0:1] - top)
        total = total + fade * old[2][head, 1:2]
        row_total = row_total + fade * old[2][head, 2:3]
        mix = mix + fade * old[0][head]
        extra = extra + fade * old[1][head]
    return top, total, row_total, mix, extra


def attend_heads(segments, refs, queries, level_bias, width, olds, keep):
    flags = device_flags()
    stages = [range(first, first + TOGETHER) for first in range(0, HEADS, TOGETHER)]
    make = lambda heads: [head_products(head, segments, refs, queries, width) for head in heads]
    ready = make(stages[0])
    for number, heads in enumerate(stages):
        coming = make(stages[number + 1]) if number + 1 < len(stages) else None
        for head, products in zip(heads, ready):
            keep(head, *head_result(head, segments, level_bias, flags, products, olds, width))
        ready = coming


def keeper(state):
    def keep(head, top, total, row_total, mix, extra):
        state[0][head] = mix
        state[1][head] = extra
        state[2][head, 0:1] = top
        state[2][head, 1:2] = total
        state[2][head, 2:3] = row_total

    return keep


def own_kernel(segments, level_bias, query, qtan, *refs):
    sources, state = refs[: FIELDS + 1], refs[FIELDS + 1 : FIELDS + 4]
    masked, turned = refs[FIELDS + 4 : FIELDS + 6], refs[FIELDS + 6]
    state[2][...] = jnp.zeros(state[2].shape, F32)
    for raw, target in zip((query, qtan), masked):
        turn_queries(raw, turned, target)
    attend_heads(segments, sources, masked, level_bias, query.shape[1], [], keeper(state))


def state_shapes(token_count, width):
    wide = (HEADS, width // HEADS, token_count)
    return (wide, wide, (HEADS, 8, token_count))


def own_cost(token_count, width, key_count):
    return pl.CostEstimate(
        flops=token_count * key_count * HEADS,
        bytes_accessed=token_count * width,
        transcendentals=0,
    )


def attend_own(level_bias, query, qtan, fields, mate, segments):
    token_count, width = query.shape
    states = state_shapes(token_count, width)
    masked = (HEADS, 2 * LANES, token_count)
    operands = (query, qtan, *fields, mate)
    return pl.pallas_call(
        functools.partial(own_kernel, segments),
        out_shape=tuple(jax.ShapeDtypeStruct(s, F32) for s in states)
        + (jax.ShapeDtypeStruct(masked, BF16),) * 2,
        in_specs=[smem_spec()] + [vmem_spec()] * len(operands),
        out_specs=[vmem_spec()] * 5,
        scratch_shapes=[pltpu.VMEM((width, token_count), BF16)],
        compiler_params=pltpu.CompilerParams(vmem_limit_bytes=VMEM_BYTES),
        cost_estimate=own_cost(token_count, width, sum(s[0] for s in segments)),
        name="own",
    )(level_bias, *operands)


def more_kernel(segments, old_count, count, level_bias, *refs):
    queries, refs = refs[:2], refs[2:]
    olds = [refs[3 * i : 3 * i + 3] for i in range(old_count)]
    refs = refs[3 * old_count :]
    sources, state = refs[:count], refs[count:]
    width = state[0].shape[0] * state[0].shape[1]
    state[2][...] = jnp.zeros(state[2].shape, F32)
    attend_heads(segments, sources, queries, level_bias, width, olds, keeper(state))


def attend_more(level_bias, queries, olds, sources, segments, name):
    token_count = queries[0].shape[2]
    width = sources[0].shape[-1]
    operands = (*queries, *[array for old in olds for array in old], *sources)
    return pl.pallas_call(
        functools.partial(more_kernel, segments, len(olds), len(sources)),
        out_shape=tuple(jax.ShapeDtypeStruct(s, F32) for s in state_shapes(token_count, width)),
        in_specs=[smem_spec()] + [vmem_spec()] * len(operands),
        out_specs=[vmem_spec()] * 3,
        compiler_params=pltpu.CompilerParams(vmem_limit_bytes=VMEM_BYTES),
        cost_estimate=own_cost(token_count, width, sum(s[0] for s in segments)),
        name=name,
    )(level_bias, *operands)


def last_kernel(segments, old_count, count, far_count, far_blocks, level_bias, *refs):
    queries, refs = refs[:2], refs[2:]
    olds = [refs[3 * i : 3 * i + 3] for i in range(old_count)]
    refs = refs[3 * old_count :]
    sources, outs = refs[:count], refs[count : count + 2]
    far_keys, mix_acc, tan_acc, turned, sems = refs[count + 2 :]
    width, token_count = outs[0].shape[1], outs[0].shape[0]
    line = lax.broadcasted_iota(jnp.int32, (far_count, FIELDS * far_count), 0)
    lane = lax.broadcasted_iota(jnp.int32, (far_count, FIELDS * far_count), 1)
    far_rows = jnp.concatenate([sources[i][begin:] for i, begin in far_blocks], axis=0)
    for index in range(FIELDS):
        select = (lane == line * FIELDS + index).astype(F32).astype(BF16)
        far_keys[index] = jnp.dot(select, far_rows, preferred_element_type=F32).astype(BF16)
    sources = sources + (far_keys,)

    def keep(head, top, total, row_total, mix, extra):
        inverse = 1.0 / total
        mix = mix * inverse
        mix_acc[head] = mix
        tan_acc[head] = extra * inverse - (row_total * inverse) * mix

    attend_heads(segments, sources, queries, level_bias, width, olds, keep)
    line = lax.broadcasted_iota(jnp.int32, (token_count, token_count), 0)
    lane = lax.broadcasted_iota(jnp.int32, (token_count, token_count), 1)
    unit = (line == lane).astype(F32).astype(BF16)
    sent = []
    for number, acc in enumerate((mix_acc, tan_acc)):
        flat = acc[...].reshape(width, token_count).astype(BF16)
        turned[number] = against(unit, flat).astype(BF16)
        more = chunk_copies(turned.at[number], outs[number], sems, number * FIELDS, FIELDS)
        for copy in more:
            copy.start()
        sent += more
    for copy in sent:
        copy.wait()


def attend_last(level_bias, queries, olds, sources, segments, far_count, far_blocks):
    token_count = queries[0].shape[2]
    width = sources[0].shape[-1]
    states = state_shapes(token_count, width)
    operands = (*queries, *[array for old in olds for array in old], *sources)
    return pl.pallas_call(
        functools.partial(
            last_kernel, segments, len(olds), len(sources), far_count, far_blocks
        ),
        out_shape=(jax.ShapeDtypeStruct((token_count, width), BF16),) * 2,
        in_specs=[smem_spec()] + [vmem_spec()] * len(operands),
        out_specs=[hbm_spec()] * 2,
        scratch_shapes=[
            pltpu.VMEM((FIELDS, far_count, width), BF16),
            pltpu.VMEM(states[0], F32),
            pltpu.VMEM(states[1], F32),
            pltpu.VMEM((2, token_count, width), BF16),
            pltpu.SemaphoreType.DMA((2 * FIELDS,)),
        ],
        compiler_params=pltpu.CompilerParams(vmem_limit_bytes=VMEM_BYTES),
        cost_estimate=own_cost(token_count, width, sum(s[0] for s in segments)),
        name="outer",
    )(level_bias, *operands)


def swap(block, axis, odd):
    count = lax.axis_size(axis)
    route = []
    for low in range(1 if odd else 0, count - 1, 2):
        route += [(low, low + 1), (low + 1, low)]
    return lax.ppermute(block, axis, route)


def part(source, begin, rows):
    return lambda refs, field, window: refs[source][field, begin : begin + rows, window]


def flat_part(source, stride, begin, rows):
    def read(refs, field, window):
        at = field * stride + begin
        return refs[source][at : at + rows, window]

    return read


def forwarded(source, rest, half):
    def read(refs, field, window):
        if field < FIELDS - 1:
            return refs[source][field * half : (field + 1) * half, window]
        return refs[2][rest : rest + half, window]

    return read


def send_to(block, axis, mask):
    return lax.ppermute(block, axis, [(i, i ^ mask) for i in range(lax.axis_size(axis))])


def join(blocks):
    rows = sum(block.shape[0] for block in blocks)
    total, at = None, 0
    for block in blocks:
        count = block.shape[0]
        padded = jnp.pad(block, ((at, rows - at - count), (0, 0)))
        total = padded if total is None else total + padded
        at += count
    return total


def cross_columns(pair):
    count = lax.axis_size("col")
    route = []
    for row in range(lax.axis_size("row")):
        for col in range(count):
            route.append((row * count + col, row * count + (col ^ (2 + row % 2))))
    return lax.ppermute(pair, ("row", "col"), route)


def gather_rows(far):
    count = lax.axis_size("row")
    if count <= 8:
        return [far] + [send_to(far, "row", mask) for mask in range(2, count, 2)]
    for bit in range(1, count.bit_length() - 1):
        far = join([far, send_to(far, "row", 1 << bit)])
    return [far]


def body(
    query_field,
    key_field,
    value_field,
    query_tan,
    key_tan,
    value_tan,
    pool_near,
    pool_far,
    level_bias,
):
    window = query_field.shape[0]
    width = query_field.shape[2]
    cells = window * window
    strip, half = cells // 2, cells // 4
    near_count = cells // (NEAR_POOL * NEAR_POOL)
    row_count, col_count = lax.axis_size("row"), lax.axis_size("col")
    far_count = row_count * col_count
    flat = lambda field: field.reshape(cells, width)
    fields = tuple(flat(f) for f in (key_field, value_field, key_tan, value_tan))

    row_odd_even, col_even, col_odd, row_even, far, row_odd_odd = pack(
        fields, pool_near, pool_far
    )
    group = strip + near_count
    far = far[:FIELDS]
    got_col_even = swap(col_even, "col", False)
    got_row_odd_even = swap(row_odd_even, "row", True)
    got_row_odd_odd = swap(row_odd_odd, "row", True)
    got_col_odd = swap(col_odd, "col", True)
    got_row_even = swap(row_even, "row", False)

    *own_state, query, qtan = attend_own(
        level_bias,
        flat(query_field),
        flat(query_tan),
        fields,
        got_row_even,
        [
            (cells, "flag", 0, lambda refs, field, window: refs[field][:, window]),
            (strip, "flag", 0, flat_part(4, group, 0, strip)),
            (near_count, "level", 0, flat_part(4, group, strip, near_count)),
        ],
    )
    queries = (query, qtan)
    far_at = slice(FIELDS * group, FIELDS * group + FIELDS)
    pair = join([far, got_row_even[far_at]])
    far = join([far, got_col_even[far_at], cross_columns(pair)])
    got_row_odd_even, stats = lax.optimization_barrier((got_row_odd_even, own_state[2]))
    own_state = (own_state[0], own_state[1], stats)
    row_state = attend_more(
        level_bias,
        queries,
        [],
        (got_row_odd_even,),
        [(half, "flag", 1, part(0, 0, half))],
        "row_strip",
    )
    got_row_odd_odd, stats = lax.optimization_barrier((got_row_odd_odd, row_state[2]))
    row_state = (row_state[0], row_state[1], stats)
    got_outer_even = swap(got_row_odd_even, "col", False)
    got_outer_odd = swap(got_row_odd_odd, "col", True)
    got_inner = [swap(block, "row", False) for block in forward(got_col_even, got_col_odd)]
    for bit in range(2, col_count.bit_length() - 1):
        far = join([far, send_to(far, "col", 1 << bit)])
    far = join([far, send_to(far, "row", 1)])

    state = attend_more(
        level_bias,
        queries,
        [row_state],
        (got_col_even, got_col_odd),
        [
            (strip, "flag", 0, flat_part(0, group, 0, strip)),
            (strip, "flag", 2, part(1, 0, strip)),
        ],
        "strips",
    )
    far, stats = lax.optimization_barrier((far, state[2]))
    state = (state[0], state[1], stats)
    far_blocks = gather_rows(far)
    state = attend_more(
        level_bias,
        queries,
        [state],
        (*got_inner, got_col_even, row_even, got_row_odd_odd),
        [
            (half, "flag", 1, part(5, 0, half)),
            (half, "flag", 0, forwarded(0, 0, half)),
            (half, "flag", 2, forwarded(1, half, half)),
            (near_count, "level", 0, flat_part(2, near_count, strip, near_count)),
            (near_count, "level", 0, flat_part(3, group, strip, near_count)),
            (near_count, "level", 0, flat_part(4, group, strip, near_count)),
        ],
        "inner",
    )
    mixed, mixed_tan = attend_last(
        level_bias,
        queries,
        [state, own_state],
        (got_outer_even, got_outer_odd, *far_blocks),
        [
            (half, "flag", 1, part(0, 0, half)),
            (half, "flag", 3, part(1, 0, half)),
            (far_count, "level", 1, part(2 + len(far_blocks), 0, far_count)),
        ],
        far_count,
        tuple((2 + number, 0) for number in range(len(far_blocks))),
    )
    shape = (window, window, width)
    return (mixed.reshape(shape), mixed_tan.reshape(shape))


def solution(mesh):
    field = P("row", "col", None)
    return jax.shard_map(
        body,
        mesh=mesh,
        in_specs=(field,) * 6 + (P(),) * 3,
        out_specs=(field, field),
        check_vma=False,
    )
```

```python
import functools

import jax
import jax.numpy as jnp
from jax import lax
from jax.experimental import pallas as pl
from jax.experimental.pallas import tpu as pltpu
from jax.sharding import PartitionSpec as P

HEADS = 16
RIM = 8
NEAR_POOL = 4
LOG2E = 1.4426950408889634
OFF = -1e30
PACK_BYTES = 60 * 1024 * 1024
VMEM_BYTES = 28 * 1024 * 1024
LANES = 128
FIELDS = 4
BF16 = jnp.bfloat16
F32 = jnp.float32


def vmem_spec():
    return pl.BlockSpec(memory_space=pltpu.VMEM)


def smem_spec():
    return pl.BlockSpec(memory_space=pltpu.SMEM)


def hbm_spec():
    return pl.BlockSpec(memory_space=pltpu.HBM)


def any_spec():
    return pl.BlockSpec(memory_space=pl.ANY)


def against(left, right):
    return lax.dot_general(left, right, (((1,), (1,)), ((), ())), preferred_element_type=F32)


def chunk_copies(source, target, sems, first, parts):
    rows = source.shape[0]
    step = -(-rows // parts)
    if len(source.shape) == 2:
        step = -(-step // 16) * 16
    copies = []
    for number, begin in enumerate(range(0, rows, step)):
        at = pl.ds(begin, min(step, rows - begin))
        copies.append(pltpu.make_async_copy(source.at[at], target.at[at], sems.at[first + number]))
    return copies


def split3(weights):
    high = weights.astype(BF16)
    rest = weights - high.astype(F32)
    mid = rest.astype(BF16)
    low = (rest - mid.astype(F32)).astype(BF16)
    return jnp.concatenate([high, mid, low], axis=0)


def pool_weights(pool_near, pool_far, cells):
    window = 2 * RIM
    near_side = window // NEAR_POOL
    near_count = near_side * near_side
    lane = lax.broadcasted_iota(jnp.int32, (near_count, cells), 1)
    line = lax.broadcasted_iota(jnp.int32, (near_count, cells), 0)
    row, col = lane // window, lane % window
    near = jnp.zeros((near_count, cells), F32)
    for p in range(NEAR_POOL):
        for q in range(NEAR_POOL):
            hit = (row % NEAR_POOL == p) & (col % NEAR_POOL == q)
            near = jnp.where(hit, pool_near[p, q], near)
    block = (row // NEAR_POOL) * near_side + col // NEAR_POOL
    near = split3(jnp.where(line == block, near, 0.0))
    spread = (line == col).astype(F32).astype(BF16)
    far = jnp.dot(split3(pool_far), spread, preferred_element_type=F32)
    far_line = lax.broadcasted_iota(jnp.int32, far.shape, 0) % window
    far_lane = lax.broadcasted_iota(jnp.int32, far.shape, 1) // window
    far = jnp.where(far_line == far_lane, far, 0.0)
    rows = [
        jnp.sum(far[i * window : (i + 1) * window], axis=0, keepdims=True) for i in range(3)
    ]
    rows.append(jnp.zeros((near_count - 3, cells), F32))
    return jnp.concatenate([near, jnp.concatenate(rows, axis=0).astype(BF16)], axis=0)


def halves(block, width):
    cells = block.shape[0]
    wide = block.astype(F32).reshape(cells // (2 * RIM), 2, RIM, width)
    left = wide[:, 0].reshape(cells // 2, width).astype(BF16)
    right = wide[:, 1].reshape(cells // 2, width).astype(BF16)
    return left, right


def pack_kernel(pool_near, pool_far, *refs):
    sources, outs = refs[:FIELDS], refs[FIELDS : FIELDS + 6]
    held = refs[FIELDS + 6]
    kept, sems, out_sems = refs[FIELDS + 7 : -2], refs[-2], refs[-1]
    cells, width = sources[0].shape
    strip, half = cells // 2, cells // 4
    near_count = cells // (NEAR_POOL * NEAR_POOL)
    row_is_even = lax.axis_index("row") % 2 == 0
    col_is_even = lax.axis_index("col") % 2 == 0
    copies = []
    for index, source in enumerate(sources):
        copies += chunk_copies(source, held.at[index], sems, 2 * index, 2)
    for copy in copies:
        copy.start()
    weights = pool_weights(pool_near, pool_far[...], cells)
    far_rows = []
    sent = []
    for index in range(FIELDS):
        copies[2 * index].wait()
        copies[2 * index + 1].wait()
        block = held[index]
        left, right = halves(block, width)
        even = jnp.where(col_is_even, right, left)
        odd = jnp.where(col_is_even, left, right)
        outer = lambda side: jnp.where(row_is_even, side[:half], side[half:])
        pooled = jnp.dot(weights, block, preferred_element_type=F32)
        near = pooled[:near_count] + (
            pooled[near_count : 2 * near_count] + pooled[2 * near_count : 3 * near_count]
        )
        near = near.astype(BF16)
        far = pooled[3 * near_count :]
        far_rows.append(far[0:1] + (far[1:2] + far[2:3]))
        kept[0][index] = outer(even)
        kept[5][index] = outer(odd)
        at = index * (strip + near_count)
        kept[1][at : at + strip] = even
        kept[1][at + strip : at + strip + near_count] = near
        kept[2][index] = odd
        kept[3][at : at + strip] = jnp.where(row_is_even, block[strip:], block[:strip])
        kept[3][at + strip : at + strip + near_count] = near
        field = pl.ds(at, strip + near_count)
        for number in (0, 1, 2, 3, 5):
            place = field if number in (1, 3) else index
            copy = pltpu.make_async_copy(
                kept[number].at[place], outs[number].at[place], out_sems.at[6 * index + number]
            )
            copy.start()
            sent.append(copy)
    far_rows.append(jnp.zeros((16 - FIELDS, width), F32))
    kept[4][...] = jnp.concatenate(far_rows, axis=0).astype(BF16)
    rest = pl.ds(FIELDS * (strip + near_count), 16)
    for number, (target, place) in enumerate(((1, rest), (3, rest), (4, pl.ds(0, 16)))):
        copy = pltpu.make_async_copy(
            kept[4], outs[target].at[place], out_sems.at[6 * FIELDS + number]
        )
        copy.start()
        sent.append(copy)
    for copy in sent:
        copy.wait()


def pack(fields, pool_near, pool_far):
    cells, width = fields[0].shape
    strip = cells // 2
    near_count = cells // (NEAR_POOL * NEAR_POOL)
    corner = (FIELDS, strip // 2, width)
    shapes = [
        corner,
        (FIELDS * (strip + near_count) + 16, width),
        (FIELDS, strip, width),
        (FIELDS * (strip + near_count) + 16, width),
        (16, width),
        corner,
    ]
    return pl.pallas_call(
        pack_kernel,
        out_shape=tuple(jax.ShapeDtypeStruct(s, BF16) for s in shapes),
        in_specs=[smem_spec(), vmem_spec()] + [hbm_spec()] * FIELDS,
        out_specs=[hbm_spec()] * len(shapes),
        scratch_shapes=[pltpu.VMEM((FIELDS, cells, width), BF16)]
        + [pltpu.VMEM(s, BF16) for s in shapes]
        + [pltpu.SemaphoreType.DMA((2 * FIELDS,)), pltpu.SemaphoreType.DMA((6 * FIELDS + 3,))],
        compiler_params=pltpu.CompilerParams(vmem_limit_bytes=PACK_BYTES),
        name="pack",
    )(pool_near, pool_far, *fields)


def forward_kernel(col_even, col_odd, first, second, third):
    strip = col_odd.shape[1]
    half = strip // 2
    near_count = (col_even.shape[0] - 16) // FIELDS - strip
    group = strip + near_count
    start = (1 - lax.axis_index("row") % 2) * half
    even = lambda index: col_even[pl.ds(pl.multiple_of(index * group + start, 16), half)]
    odd = lambda index: col_odd[index, pl.ds(pl.multiple_of(start, half), half)]
    for index in range(FIELDS - 1):
        first[index * half : (index + 1) * half] = even(index)
        second[index * half : (index + 1) * half] = odd(index)
    third[:half] = even(FIELDS - 1)
    third[half:strip] = odd(FIELDS - 1)
    for index in range(FIELDS):
        at = strip + index * near_count
        third[at : at + near_count] = col_even[index * group + strip : (index + 1) * group]


def forward(col_even, col_odd):
    _, strip, width = col_odd.shape
    shape = jax.ShapeDtypeStruct(((FIELDS - 1) * strip // 2, width), BF16)
    return pl.pallas_call(
        forward_kernel,
        out_shape=(shape,) * 3,
        in_specs=[vmem_spec()] * 2,
        out_specs=[vmem_spec()] * 3,
        compiler_params=pltpu.CompilerParams(vmem_limit_bytes=VMEM_BYTES),
        name="forward",
    )(col_even, col_odd)


TOGETHER = 4


def masked_start(head, head_dim, width):
    return min(head * head_dim // LANES, (width - 2 * LANES) // LANES) * LANES


def turn_queries(raw, turned, masked):
    width = raw.shape[1]
    head_dim = width // HEADS
    span = 2 * LANES
    line = lax.broadcasted_iota(jnp.int32, (LANES, LANES), 0)
    lane = lax.broadcasted_iota(jnp.int32, (LANES, LANES), 1)
    unit = (line == lane).astype(F32).astype(BF16)
    for at in range(0, width, LANES):
        turned[at : at + LANES] = against(unit, raw[:, at : at + LANES]).astype(BF16)
    channel = lax.broadcasted_iota(jnp.int32, (span, raw.shape[0]), 0)
    for head in range(HEADS):
        start = masked_start(head, head_dim, width)
        low = head * head_dim - start
        keep = ((channel >= low) & (channel < low + head_dim)).astype(F32).astype(BF16)
        masked[head] = turned[start : start + span] * keep


def device_flags():
    row, col = lax.axis_index("row"), lax.axis_index("col")
    row_edge = (row == 0) | (row == lax.axis_size("row") - 1)
    col_edge = (col == 0) | (col == lax.axis_size("col") - 1)
    off = lambda edge: jnp.where(edge, F32(OFF), F32(0.0))
    return (F32(0.0), off(row_edge), off(col_edge), off(row_edge | col_edge))


def head_products(head, segments, refs, queries, width):
    head_dim = width // HEADS
    start = head * head_dim // LANES * LANES
    low = head * head_dim - start
    one_tile = low + head_dim <= LANES
    span = LANES if one_tile else 2 * LANES
    window = slice(start, start + span)
    at = start - masked_start(head, head_dim, width)
    rows_of = lambda field: jnp.concatenate(
        [reader(refs, field, window) for _, _, _, reader in segments], axis=0
    )
    key, value, key_tan, value_tan = (rows_of(field) for field in range(FIELDS))
    query, query_tan = (ref[head, at : at + span] for ref in queries)
    if one_tile:
        scores = jnp.dot(key, query, preferred_element_type=F32)
        slopes = jnp.dot(
            jnp.concatenate([key, key_tan], axis=1),
            jnp.concatenate([query_tan, query], axis=0),
            preferred_element_type=F32,
        )
    else:
        count = key.shape[0]
        both = jnp.dot(
            jnp.concatenate([key, key_tan], axis=0), query, preferred_element_type=F32
        )
        scores = both[:count]
        slopes = jnp.dot(key, query_tan, preferred_element_type=F32) + both[count:]
    line = lax.broadcasted_iota(jnp.int32, (head_dim + 8, span), 0)
    lane = lax.broadcasted_iota(jnp.int32, (head_dim + 8, span), 1)
    pick = ((lane == line + low) & (line < head_dim)).astype(F32).astype(BF16)
    ones_line = lax.broadcasted_iota(jnp.int32, (8, value.shape[0]), 0)
    turned = jnp.concatenate(
        [
            against(pick, value)[:head_dim],
            (ones_line == 0).astype(F32),
            against(pick, value_tan),
        ],
        axis=0,
    )
    return scores, slopes, turned.astype(BF16)


def head_result(head, segments, level_bias, flags, products, olds, width):
    scores, slopes, turned = products
    head_dim = width // HEADS
    pad_dim = head_dim + 8
    scale = head_dim**-0.5
    bias = []
    top = None
    at = 0
    for rows, kind, number, _ in segments:
        amount = flags[number] if kind == "flag" else level_bias[number, head] * LOG2E
        bias.append(amount)
        part = jnp.max(scores[at : at + rows], axis=0, keepdims=True) * (scale * LOG2E) + amount
        top = part if top is None else jnp.maximum(top, part)
        at += rows
    for old in olds:
        top = jnp.maximum(top, old[2][head, 0:1])
    weights_low, product_low = [], []
    at = 0
    for (rows, _, _, _), amount in zip(segments, bias):
        weights = jnp.exp2(scores[at : at + rows] * (scale * LOG2E) + (amount - top))
        weights_low.append(weights.astype(BF16))
        product_low.append((weights * slopes[at : at + rows]).astype(BF16))
        at += rows
    both = jnp.dot(turned, jnp.concatenate(weights_low, axis=0), preferred_element_type=F32)
    extra = jnp.dot(
        turned[:pad_dim], jnp.concatenate(product_low, axis=0), preferred_element_type=F32
    )
    mix = both[:head_dim]
    total = both[head_dim : head_dim + 1]
    row_total = extra[head_dim : head_dim + 1] * scale
    extra = extra[:head_dim] * scale + both[pad_dim : pad_dim + head_dim]
    for old in olds:
        fade = jnp.exp2(old[2][head, 0:1] - top)
        total = total + fade * old[2][head, 1:2]
        row_total = row_total + fade * old[2][head, 2:3]
        mix = mix + fade * old[0][head]
        extra = extra + fade * old[1][head]
    return top, total, row_total, mix, extra


def attend_heads(segments, refs, queries, level_bias, width, olds, keep):
    flags = device_flags()
    stages = [range(first, first + TOGETHER) for first in range(0, HEADS, TOGETHER)]
    make = lambda heads: [head_products(head, segments, refs, queries, width) for head in heads]
    ready = make(stages[0])
    for number, heads in enumerate(stages):
        coming = make(stages[number + 1]) if number + 1 < len(stages) else None
        for head, products in zip(heads, ready):
            keep(head, *head_result(head, segments, level_bias, flags, products, olds, width))
        ready = coming


def keeper(state):
    def keep(head, top, total, row_total, mix, extra):
        state[0][head] = mix
        state[1][head] = extra
        state[2][head, 0:1] = top
        state[2][head, 1:2] = total
        state[2][head, 2:3] = row_total

    return keep


def own_kernel(segments, level_bias, query, qtan, *refs):
    sources, state = refs[: FIELDS + 1], refs[FIELDS + 1 : FIELDS + 4]
    masked, turned = refs[FIELDS + 4 : FIELDS + 6], refs[FIELDS + 6]
    state[2][...] = jnp.zeros(state[2].shape, F32)
    for raw, target in zip((query, qtan), masked):
        turn_queries(raw, turned, target)
    attend_heads(segments, sources, masked, level_bias, query.shape[1], [], keeper(state))


def state_shapes(token_count, width):
    wide = (HEADS, width // HEADS, token_count)
    return (wide, wide, (HEADS, 8, token_count))


def own_cost(token_count, width, key_count):
    return pl.CostEstimate(
        flops=token_count * key_count * HEADS,
        bytes_accessed=token_count * width,
        transcendentals=0,
    )


def attend_own(level_bias, query, qtan, fields, mate, segments):
    token_count, width = query.shape
    states = state_shapes(token_count, width)
    masked = (HEADS, 2 * LANES, token_count)
    operands = (query, qtan, *fields, mate)
    return pl.pallas_call(
        functools.partial(own_kernel, segments),
        out_shape=tuple(jax.ShapeDtypeStruct(s, F32) for s in states)
        + (jax.ShapeDtypeStruct(masked, BF16),) * 2,
        in_specs=[smem_spec()] + [vmem_spec()] * len(operands),
        out_specs=[vmem_spec()] * 5,
        scratch_shapes=[pltpu.VMEM((width, token_count), BF16)],
        compiler_params=pltpu.CompilerParams(vmem_limit_bytes=VMEM_BYTES),
        cost_estimate=own_cost(token_count, width, sum(s[0] for s in segments)),
        name="own",
    )(level_bias, *operands)


def more_kernel(segments, old_count, count, level_bias, *refs):
    queries, refs = refs[:2], refs[2:]
    olds = [refs[3 * i : 3 * i + 3] for i in range(old_count)]
    refs = refs[3 * old_count :]
    sources, state = refs[:count], refs[count:]
    width = state[0].shape[0] * state[0].shape[1]
    state[2][...] = jnp.zeros(state[2].shape, F32)
    attend_heads(segments, sources, queries, level_bias, width, olds, keeper(state))


def attend_more(level_bias, queries, olds, sources, segments, name):
    token_count = queries[0].shape[2]
    width = sources[0].shape[-1]
    operands = (*queries, *[array for old in olds for array in old], *sources)
    return pl.pallas_call(
        functools.partial(more_kernel, segments, len(olds), len(sources)),
        out_shape=tuple(jax.ShapeDtypeStruct(s, F32) for s in state_shapes(token_count, width)),
        in_specs=[smem_spec()] + [vmem_spec()] * len(operands),
        out_specs=[vmem_spec()] * 3,
        compiler_params=pltpu.CompilerParams(vmem_limit_bytes=VMEM_BYTES),
        cost_estimate=own_cost(token_count, width, sum(s[0] for s in segments)),
        name=name,
    )(level_bias, *operands)


def last_kernel(segments, old_count, count, far_count, far_blocks, level_bias, *refs):
    queries, refs = refs[:2], refs[2:]
    olds = [refs[3 * i : 3 * i + 3] for i in range(old_count)]
    refs = refs[3 * old_count :]
    sources, outs = refs[:count], refs[count : count + 2]
    far_keys, mix_acc, tan_acc, turned, sems = refs[count + 2 :]
    width, token_count = outs[0].shape[1], outs[0].shape[0]
    line = lax.broadcasted_iota(jnp.int32, (far_count, FIELDS * far_count), 0)
    lane = lax.broadcasted_iota(jnp.int32, (far_count, FIELDS * far_count), 1)
    far_rows = jnp.concatenate([sources[i][begin:] for i, begin in far_blocks], axis=0)
    for index in range(FIELDS):
        select = (lane == line * FIELDS + index).astype(F32).astype(BF16)
        far_keys[index] = jnp.dot(select, far_rows, preferred_element_type=F32).astype(BF16)
    sources = sources + (far_keys,)

    def keep(head, top, total, row_total, mix, extra):
        inverse = 1.0 / total
        mix = mix * inverse
        mix_acc[head] = mix
        tan_acc[head] = extra * inverse - (row_total * inverse) * mix

    attend_heads(segments, sources, queries, level_bias, width, olds, keep)
    line = lax.broadcasted_iota(jnp.int32, (token_count, token_count), 0)
    lane = lax.broadcasted_iota(jnp.int32, (token_count, token_count), 1)
    unit = (line == lane).astype(F32).astype(BF16)
    sent = []
    for number, acc in enumerate((mix_acc, tan_acc)):
        flat = acc[...].reshape(width, token_count).astype(BF16)
        turned[number] = against(unit, flat).astype(BF16)
        more = chunk_copies(turned.at[number], outs[number], sems, number * FIELDS, FIELDS)
        for copy in more:
            copy.start()
        sent += more
    for copy in sent:
        copy.wait()


def attend_last(level_bias, queries, olds, sources, segments, far_count, far_blocks):
    token_count = queries[0].shape[2]
    width = sources[0].shape[-1]
    states = state_shapes(token_count, width)
    operands = (*queries, *[array for old in olds for array in old], *sources)
    return pl.pallas_call(
        functools.partial(
            last_kernel, segments, len(olds), len(sources), far_count, far_blocks
        ),
        out_shape=(jax.ShapeDtypeStruct((token_count, width), BF16),) * 2,
        in_specs=[smem_spec()] + [vmem_spec()] * len(operands),
        out_specs=[hbm_spec()] * 2,
        scratch_shapes=[
            pltpu.VMEM((FIELDS, far_count, width), BF16),
            pltpu.VMEM(states[0], F32),
            pltpu.VMEM(states[1], F32),
            pltpu.VMEM((2, token_count, width), BF16),
            pltpu.SemaphoreType.DMA((2 * FIELDS,)),
        ],
        compiler_params=pltpu.CompilerParams(vmem_limit_bytes=VMEM_BYTES),
        cost_estimate=own_cost(token_count, width, sum(s[0] for s in segments)),
        name="outer",
    )(level_bias, *operands)


def swap(block, axis, odd):
    count = lax.axis_size(axis)
    route = []
    for low in range(1 if odd else 0, count - 1, 2):
        route += [(low, low + 1), (low + 1, low)]
    return lax.ppermute(block, axis, route)


def part(source, begin, rows):
    return lambda refs, field, window: refs[source][field, begin : begin + rows, window]


def flat_part(source, stride, begin, rows):
    def read(refs, field, window):
        at = field * stride + begin
        return refs[source][at : at + rows, window]

    return read


def forwarded(source, rest, half):
    def read(refs, field, window):
        if field < FIELDS - 1:
            return refs[source][field * half : (field + 1) * half, window]
        return refs[2][rest : rest + half, window]

    return read


def send_to(block, axis, mask):
    return lax.ppermute(block, axis, [(i, i ^ mask) for i in range(lax.axis_size(axis))])


def join(blocks):
    rows = sum(block.shape[0] for block in blocks)
    total, at = None, 0
    for block in blocks:
        count = block.shape[0]
        padded = jnp.pad(block, ((at, rows - at - count), (0, 0)))
        total = padded if total is None else total + padded
        at += count
    return total


def cross_columns(pair):
    count = lax.axis_size("col")
    route = []
    for row in range(lax.axis_size("row")):
        for col in range(count):
            route.append((row * count + col, row * count + (col ^ (2 + row % 2))))
    return lax.ppermute(pair, ("row", "col"), route)


def gather_rows(far):
    count = lax.axis_size("row")
    if count <= 8:
        return [far] + [send_to(far, "row", mask) for mask in range(2, count, 2)]
    for bit in range(1, count.bit_length() - 1):
        far = join([far, send_to(far, "row", 1 << bit)])
    return [far]


def body(
    query_field,
    key_field,
    value_field,
    query_tan,
    key_tan,
    value_tan,
    pool_near,
    pool_far,
    level_bias,
):
    window = query_field.shape[0]
    width = query_field.shape[2]
    cells = window * window
    strip, half = cells // 2, cells // 4
    near_count = cells // (NEAR_POOL * NEAR_POOL)
    row_count, col_count = lax.axis_size("row"), lax.axis_size("col")
    far_count = row_count * col_count
    flat = lambda field: field.reshape(cells, width)
    fields = tuple(flat(f) for f in (key_field, value_field, key_tan, value_tan))

    row_odd_even, col_even, col_odd, row_even, far, row_odd_odd = pack(
        fields, pool_near, pool_far
    )
    group = strip + near_count
    far = far[:FIELDS]
    got_col_even = swap(col_even, "col", False)
    got_row_odd_even = swap(row_odd_even, "row", True)
    got_row_odd_odd = swap(row_odd_odd, "row", True)
    got_col_odd = swap(col_odd, "col", True)
    got_row_even = swap(row_even, "row", False)

    *own_state, query, qtan = attend_own(
        level_bias,
        flat(query_field),
        flat(query_tan),
        fields,
        got_row_even,
        [
            (cells, "flag", 0, lambda refs, field, window: refs[field][:, window]),
            (strip, "flag", 0, flat_part(4, group, 0, strip)),
            (near_count, "level", 0, flat_part(4, group, strip, near_count)),
        ],
    )
    queries = (query, qtan)
    far_at = slice(FIELDS * group, FIELDS * group + FIELDS)
    pair = join([far, got_row_even[far_at]])
    far = join([far, got_col_even[far_at], cross_columns(pair)])
    got_row_odd_even, stats = lax.optimization_barrier((got_row_odd_even, own_state[2]))
    own_state = (own_state[0], own_state[1], stats)
    row_state = attend_more(
        level_bias,
        queries,
        [],
        (got_row_odd_even,),
        [(half, "flag", 1, part(0, 0, half))],
        "row_strip",
    )
    got_row_odd_odd, stats = lax.optimization_barrier((got_row_odd_odd, row_state[2]))
    row_state = (row_state[0], row_state[1], stats)
    got_outer_even = swap(got_row_odd_even, "col", False)
    got_outer_odd = swap(got_row_odd_odd, "col", True)
    got_inner = [swap(block, "row", False) for block in forward(got_col_even, got_col_odd)]
    for bit in range(2, col_count.bit_length() - 1):
        far = join([far, send_to(far, "col", 1 << bit)])
    far = join([far, send_to(far, "row", 1)])

    state = attend_more(
        level_bias,
        queries,
        [row_state],
        (got_col_even, got_col_odd),
        [
            (strip, "flag", 0, flat_part(0, group, 0, strip)),
            (strip, "flag", 2, part(1, 0, strip)),
        ],
        "strips",
    )
    far, stats = lax.optimization_barrier((far, state[2]))
    state = (state[0], state[1], stats)
    far_blocks = gather_rows(far)
    state = attend_more(
        level_bias,
        queries,
        [state],
        (*got_inner, got_col_even, row_even, got_row_odd_odd),
        [
            (half, "flag", 1, part(5, 0, half)),
            (half, "flag", 0, forwarded(0, 0, half)),
            (half, "flag", 2, forwarded(1, half, half)),
            (near_count, "level", 0, flat_part(2, near_count, strip, near_count)),
            (near_count, "level", 0, flat_part(3, group, strip, near_count)),
            (near_count, "level", 0, flat_part(4, group, strip, near_count)),
        ],
        "inner",
    )
    mixed, mixed_tan = attend_last(
        level_bias,
        queries,
        [state, own_state],
        (got_outer_even, got_outer_odd, *far_blocks),
        [
            (half, "flag", 1, part(0, 0, half)),
            (half, "flag", 3, part(1, 0, half)),
            (far_count, "level", 1, part(2 + len(far_blocks), 0, far_count)),
        ],
        far_count,
        tuple((2 + number, 0) for number in range(len(far_blocks))),
    )
    shape = (window, window, width)
    return (mixed.reshape(shape), mixed_tan.reshape(shape))


def solution(mesh):
    field = P("row", "col", None)
    return jax.shard_map(
        body,
        mesh=mesh,
        in_specs=(field,) * 6 + (P(),) * 3,
        out_specs=(field, field),
        check_vma=False,
    )
```

```python
import functools

import jax
import jax.numpy as jnp
from jax import lax
from jax.experimental import pallas as pl
from jax.experimental.pallas import tpu as pltpu
from jax.sharding import PartitionSpec as P

HEADS = 16
RIM = 8
NEAR_POOL = 4
LOG2E = 1.4426950408889634
OFF = -1e30
PACK_BYTES = 60 * 1024 * 1024
VMEM_BYTES = 28 * 1024 * 1024
LANES = 128
FIELDS = 4
BF16 = jnp.bfloat16
F32 = jnp.float32


def vmem_spec():
    return pl.BlockSpec(memory_space=pltpu.VMEM)


def smem_spec():
    return pl.BlockSpec(memory_space=pltpu.SMEM)


def hbm_spec():
    return pl.BlockSpec(memory_space=pltpu.HBM)


def any_spec():
    return pl.BlockSpec(memory_space=pl.ANY)


def against(left, right):
    return lax.dot_general(left, right, (((1,), (1,)), ((), ())), preferred_element_type=F32)


def chunk_copies(source, target, sems, first, parts):
    rows = source.shape[0]
    step = -(-rows // parts)
    if len(source.shape) == 2:
        step = -(-step // 16) * 16
    copies = []
    for number, begin in enumerate(range(0, rows, step)):
        at = pl.ds(begin, min(step, rows - begin))
        copies.append(pltpu.make_async_copy(source.at[at], target.at[at], sems.at[first + number]))
    return copies


def split3(weights):
    high = weights.astype(BF16)
    rest = weights - high.astype(F32)
    mid = rest.astype(BF16)
    low = (rest - mid.astype(F32)).astype(BF16)
    return jnp.concatenate([high, mid, low], axis=0)


def pool_weights(pool_near, pool_far, cells):
    window = 2 * RIM
    near_side = window // NEAR_POOL
    near_count = near_side * near_side
    lane = lax.broadcasted_iota(jnp.int32, (near_count, cells), 1)
    line = lax.broadcasted_iota(jnp.int32, (near_count, cells), 0)
    row, col = lane // window, lane % window
    near = jnp.zeros((near_count, cells), F32)
    for p in range(NEAR_POOL):
        for q in range(NEAR_POOL):
            hit = (row % NEAR_POOL == p) & (col % NEAR_POOL == q)
            near = jnp.where(hit, pool_near[p, q], near)
    block = (row // NEAR_POOL) * near_side + col // NEAR_POOL
    near = split3(jnp.where(line == block, near, 0.0))
    spread = (line == col).astype(F32).astype(BF16)
    far = jnp.dot(split3(pool_far), spread, preferred_element_type=F32)
    far_line = lax.broadcasted_iota(jnp.int32, far.shape, 0) % window
    far_lane = lax.broadcasted_iota(jnp.int32, far.shape, 1) // window
    far = jnp.where(far_line == far_lane, far, 0.0)
    rows = [
        jnp.sum(far[i * window : (i + 1) * window], axis=0, keepdims=True) for i in range(3)
    ]
    rows.append(jnp.zeros((near_count - 3, cells), F32))
    return jnp.concatenate([near, jnp.concatenate(rows, axis=0).astype(BF16)], axis=0)


def halves(block, width):
    cells = block.shape[0]
    wide = block.astype(F32).reshape(cells // (2 * RIM), 2, RIM, width)
    left = wide[:, 0].reshape(cells // 2, width).astype(BF16)
    right = wide[:, 1].reshape(cells // 2, width).astype(BF16)
    return left, right


def pack_kernel(pool_near, pool_far, *refs):
    sources, outs = refs[:FIELDS], refs[FIELDS : FIELDS + 6]
    held = refs[FIELDS + 6]
    kept, sems, out_sems = refs[FIELDS + 7 : -2], refs[-2], refs[-1]
    cells, width = sources[0].shape
    strip, half = cells // 2, cells // 4
    near_count = cells // (NEAR_POOL * NEAR_POOL)
    row_is_even = lax.axis_index("row") % 2 == 0
    col_is_even = lax.axis_index("col") % 2 == 0
    copies = []
    for index, source in enumerate(sources):
        copies += chunk_copies(source, held.at[index], sems, 2 * index, 2)
    for copy in copies:
        copy.start()
    weights = pool_weights(pool_near, pool_far[...], cells)
    far_rows = []
    sent = []
    for index in range(FIELDS):
        copies[2 * index].wait()
        copies[2 * index + 1].wait()
        block = held[index]
        left, right = halves(block, width)
        even = jnp.where(col_is_even, right, left)
        odd = jnp.where(col_is_even, left, right)
        outer = lambda side: jnp.where(row_is_even, side[:half], side[half:])
        pooled = jnp.dot(weights, block, preferred_element_type=F32)
        near = pooled[:near_count] + (
            pooled[near_count : 2 * near_count] + pooled[2 * near_count : 3 * near_count]
        )
        near = near.astype(BF16)
        far = pooled[3 * near_count :]
        far_rows.append(far[0:1] + (far[1:2] + far[2:3]))
        kept[0][index] = outer(even)
        kept[5][index] = outer(odd)
        at = index * (strip + near_count)
        kept[1][at : at + strip] = even
        kept[1][at + strip : at + strip + near_count] = near
        kept[2][index] = odd
        kept[3][at : at + strip] = jnp.where(row_is_even, block[strip:], block[:strip])
        kept[3][at + strip : at + strip + near_count] = near
        field = pl.ds(at, strip + near_count)
        for number in (0, 1, 2, 3, 5):
            place = field if number in (1, 3) else index
            copy = pltpu.make_async_copy(
                kept[number].at[place], outs[number].at[place], out_sems.at[6 * index + number]
            )
            copy.start()
            sent.append(copy)
    far_rows.append(jnp.zeros((16 - FIELDS, width), F32))
    kept[4][...] = jnp.concatenate(far_rows, axis=0).astype(BF16)
    rest = pl.ds(FIELDS * (strip + near_count), 16)
    for number, (target, place) in enumerate(((1, rest), (3, rest), (4, pl.ds(0, 16)))):
        copy = pltpu.make_async_copy(
            kept[4], outs[target].at[place], out_sems.at[6 * FIELDS + number]
        )
        copy.start()
        sent.append(copy)
    for copy in sent:
        copy.wait()


def pack(fields, pool_near, pool_far):
    cells, width = fields[0].shape
    strip = cells // 2
    near_count = cells // (NEAR_POOL * NEAR_POOL)
    corner = (FIELDS, strip // 2, width)
    shapes = [
        corner,
        (FIELDS * (strip + near_count) + 16, width),
        (FIELDS, strip, width),
        (FIELDS * (strip + near_count) + 16, width),
        (16, width),
        corner,
    ]
    return pl.pallas_call(
        pack_kernel,
        out_shape=tuple(jax.ShapeDtypeStruct(s, BF16) for s in shapes),
        in_specs=[smem_spec(), vmem_spec()] + [hbm_spec()] * FIELDS,
        out_specs=[hbm_spec()] * len(shapes),
        scratch_shapes=[pltpu.VMEM((FIELDS, cells, width), BF16)]
        + [pltpu.VMEM(s, BF16) for s in shapes]
        + [pltpu.SemaphoreType.DMA((2 * FIELDS,)), pltpu.SemaphoreType.DMA((6 * FIELDS + 3,))],
        compiler_params=pltpu.CompilerParams(vmem_limit_bytes=PACK_BYTES),
        name="pack",
    )(pool_near, pool_far, *fields)


def forward_kernel(col_even, col_odd, first, second, third):
    strip = col_odd.shape[1]
    half = strip // 2
    near_count = (col_even.shape[0] - 16) // FIELDS - strip
    group = strip + near_count
    start = (1 - lax.axis_index("row") % 2) * half
    even = lambda index: col_even[pl.ds(pl.multiple_of(index * group + start, 16), half)]
    odd = lambda index: col_odd[index, pl.ds(pl.multiple_of(start, half), half)]
    for index in range(FIELDS - 1):
        first[index * half : (index + 1) * half] = even(index)
        second[index * half : (index + 1) * half] = odd(index)
    third[:half] = even(FIELDS - 1)
    third[half:strip] = odd(FIELDS - 1)
    for index in range(FIELDS):
        at = strip + index * near_count
        third[at : at + near_count] = col_even[index * group + strip : (index + 1) * group]


def forward(col_even, col_odd):
    _, strip, width = col_odd.shape
    shape = jax.ShapeDtypeStruct(((FIELDS - 1) * strip // 2, width), BF16)
    return pl.pallas_call(
        forward_kernel,
        out_shape=(shape,) * 3,
        in_specs=[vmem_spec()] * 2,
        out_specs=[vmem_spec()] * 3,
        compiler_params=pltpu.CompilerParams(vmem_limit_bytes=VMEM_BYTES),
        name="forward",
    )(col_even, col_odd)


TOGETHER = 2


def masked_start(head, head_dim, width):
    return min(head * head_dim // LANES, (width - 2 * LANES) // LANES) * LANES


def turn_queries(raw, turned, masked):
    width = raw.shape[1]
    head_dim = width // HEADS
    span = 2 * LANES
    line = lax.broadcasted_iota(jnp.int32, (LANES, LANES), 0)
    lane = lax.broadcasted_iota(jnp.int32, (LANES, LANES), 1)
    unit = (line == lane).astype(F32).astype(BF16)
    for at in range(0, width, LANES):
        turned[at : at + LANES] = against(unit, raw[:, at : at + LANES]).astype(BF16)
    channel = lax.broadcasted_iota(jnp.int32, (span, raw.shape[0]), 0)
    for head in range(HEADS):
        start = masked_start(head, head_dim, width)
        low = head * head_dim - start
        keep = ((channel >= low) & (channel < low + head_dim)).astype(F32).astype(BF16)
        masked[head] = turned[start : start + span] * keep


def device_flags():
    row, col = lax.axis_index("row"), lax.axis_index("col")
    row_edge = (row == 0) | (row == lax.axis_size("row") - 1)
    col_edge = (col == 0) | (col == lax.axis_size("col") - 1)
    off = lambda edge: jnp.where(edge, F32(OFF), F32(0.0))
    return (F32(0.0), off(row_edge), off(col_edge), off(row_edge | col_edge))


def head_products(head, segments, refs, queries, width):
    head_dim = width // HEADS
    start = head * head_dim // LANES * LANES
    low = head * head_dim - start
    one_tile = low + head_dim <= LANES
    span = LANES if one_tile else 2 * LANES
    window = slice(start, start + span)
    at = start - masked_start(head, head_dim, width)
    rows_of = lambda field: jnp.concatenate(
        [reader(refs, field, window) for _, _, _, reader in segments], axis=0
    )
    key, value, key_tan, value_tan = (rows_of(field) for field in range(FIELDS))
    query, query_tan = (ref[head, at : at + span] for ref in queries)
    if one_tile:
        scores = jnp.dot(key, query, preferred_element_type=F32)
        slopes = jnp.dot(
            jnp.concatenate([key, key_tan], axis=1),
            jnp.concatenate([query_tan, query], axis=0),
            preferred_element_type=F32,
        )
    else:
        count = key.shape[0]
        both = jnp.dot(
            jnp.concatenate([key, key_tan], axis=0), query, preferred_element_type=F32
        )
        scores = both[:count]
        slopes = jnp.dot(key, query_tan, preferred_element_type=F32) + both[count:]
    line = lax.broadcasted_iota(jnp.int32, (head_dim + 8, span), 0)
    lane = lax.broadcasted_iota(jnp.int32, (head_dim + 8, span), 1)
    pick = ((lane == line + low) & (line < head_dim)).astype(F32).astype(BF16)
    ones_line = lax.broadcasted_iota(jnp.int32, (8, value.shape[0]), 0)
    turned = jnp.concatenate(
        [
            against(pick, value)[:head_dim],
            (ones_line == 0).astype(F32),
            against(pick, value_tan),
        ],
        axis=0,
    )
    return scores, slopes, turned.astype(BF16)


def head_result(head, segments, level_bias, flags, products, olds, width):
    scores, slopes, turned = products
    head_dim = width // HEADS
    pad_dim = head_dim + 8
    scale = head_dim**-0.5
    bias = []
    top = None
    at = 0
    for rows, kind, number, _ in segments:
        amount = flags[number] if kind == "flag" else level_bias[number, head] * LOG2E
        bias.append(amount)
        part = jnp.max(scores[at : at + rows], axis=0, keepdims=True) * (scale * LOG2E) + amount
        top = part if top is None else jnp.maximum(top, part)
        at += rows
    for old in olds:
        top = jnp.maximum(top, old[2][head, 0:1])
    weights_low, product_low = [], []
    at = 0
    for (rows, _, _, _), amount in zip(segments, bias):
        weights = jnp.exp2(scores[at : at + rows] * (scale * LOG2E) + (amount - top))
        weights_low.append(weights.astype(BF16))
        product_low.append((weights * slopes[at : at + rows]).astype(BF16))
        at += rows
    both = jnp.dot(turned, jnp.concatenate(weights_low, axis=0), preferred_element_type=F32)
    extra = jnp.dot(
        turned[:pad_dim], jnp.concatenate(product_low, axis=0), preferred_element_type=F32
    )
    mix = both[:head_dim]
    total = both[head_dim : head_dim + 1]
    row_total = extra[head_dim : head_dim + 1] * scale
    extra = extra[:head_dim] * scale + both[pad_dim : pad_dim + head_dim]
    for old in olds:
        fade = jnp.exp2(old[2][head, 0:1] - top)
        total = total + fade * old[2][head, 1:2]
        row_total = row_total + fade * old[2][head, 2:3]
        mix = mix + fade * old[0][head]
        extra = extra + fade * old[1][head]
    return top, total, row_total, mix, extra


def attend_heads(segments, refs, queries, level_bias, width, olds, keep):
    flags = device_flags()
    stages = [range(first, first + TOGETHER) for first in range(0, HEADS, TOGETHER)]
    make = lambda heads: [head_products(head, segments, refs, queries, width) for head in heads]
    ready = make(stages[0])
    for number, heads in enumerate(stages):
        coming = make(stages[number + 1]) if number + 1 < len(stages) else None
        for head, products in zip(heads, ready):
            keep(head, *head_result(head, segments, level_bias, flags, products, olds, width))
        ready = coming


def keeper(state):
    def keep(head, top, total, row_total, mix, extra):
        state[0][head] = mix
        state[1][head] = extra
        state[2][head, 0:1] = top
        state[2][head, 1:2] = total
        state[2][head, 2:3] = row_total

    return keep


def own_kernel(segments, level_bias, query, qtan, *refs):
    sources, state = refs[: FIELDS + 2], refs[FIELDS + 2 : FIELDS + 5]
    masked, turned = refs[FIELDS + 5 : FIELDS + 7], refs[FIELDS + 7]
    state[2][...] = jnp.zeros(state[2].shape, F32)
    for raw, target in zip((query, qtan), masked):
        turn_queries(raw, turned, target)
    attend_heads(segments, sources, masked, level_bias, query.shape[1], [], keeper(state))


def state_shapes(token_count, width):
    wide = (HEADS, width // HEADS, token_count)
    return (wide, wide, (HEADS, 8, token_count))


def own_cost(token_count, width, key_count):
    return pl.CostEstimate(
        flops=token_count * key_count * HEADS,
        bytes_accessed=token_count * width,
        transcendentals=0,
    )


def attend_own(level_bias, query, qtan, fields, more, segments):
    token_count, width = query.shape
    states = state_shapes(token_count, width)
    masked = (HEADS, 2 * LANES, token_count)
    operands = (query, qtan, *fields, *more)
    return pl.pallas_call(
        functools.partial(own_kernel, segments),
        out_shape=tuple(jax.ShapeDtypeStruct(s, F32) for s in states)
        + (jax.ShapeDtypeStruct(masked, BF16),) * 2,
        in_specs=[smem_spec()] + [vmem_spec()] * len(operands),
        out_specs=[vmem_spec()] * 5,
        scratch_shapes=[pltpu.VMEM((width, token_count), BF16)],
        compiler_params=pltpu.CompilerParams(vmem_limit_bytes=VMEM_BYTES),
        cost_estimate=own_cost(token_count, width, sum(s[0] for s in segments)),
        name="own",
    )(level_bias, *operands)


def more_kernel(segments, old_count, count, level_bias, *refs):
    queries, refs = refs[:2], refs[2:]
    olds = [refs[3 * i : 3 * i + 3] for i in range(old_count)]
    refs = refs[3 * old_count :]
    sources, state = refs[:count], refs[count:]
    width = state[0].shape[0] * state[0].shape[1]
    state[2][...] = jnp.zeros(state[2].shape, F32)
    attend_heads(segments, sources, queries, level_bias, width, olds, keeper(state))


def attend_more(level_bias, queries, olds, sources, segments, name):
    token_count = queries[0].shape[2]
    width = sources[0].shape[-1]
    operands = (*queries, *[array for old in olds for array in old], *sources)
    return pl.pallas_call(
        functools.partial(more_kernel, segments, len(olds), len(sources)),
        out_shape=tuple(jax.ShapeDtypeStruct(s, F32) for s in state_shapes(token_count, width)),
        in_specs=[smem_spec()] + [vmem_spec()] * len(operands),
        out_specs=[vmem_spec()] * 3,
        compiler_params=pltpu.CompilerParams(vmem_limit_bytes=VMEM_BYTES),
        cost_estimate=own_cost(token_count, width, sum(s[0] for s in segments)),
        name=name,
    )(level_bias, *operands)


def last_kernel(segments, old_count, count, far_count, far_blocks, level_bias, *refs):
    queries, refs = refs[:2], refs[2:]
    olds = [refs[3 * i : 3 * i + 3] for i in range(old_count)]
    refs = refs[3 * old_count :]
    sources, outs = refs[:count], refs[count : count + 2]
    far_keys, mix_acc, tan_acc, turned, sems = refs[count + 2 :]
    width, token_count = outs[0].shape[1], outs[0].shape[0]
    line = lax.broadcasted_iota(jnp.int32, (far_count, FIELDS * far_count), 0)
    lane = lax.broadcasted_iota(jnp.int32, (far_count, FIELDS * far_count), 1)
    far_rows = jnp.concatenate([sources[i][begin:] for i, begin in far_blocks], axis=0)
    for index in range(FIELDS):
        select = (lane == line * FIELDS + index).astype(F32).astype(BF16)
        far_keys[index] = jnp.dot(select, far_rows, preferred_element_type=F32).astype(BF16)
    sources = sources + (far_keys,)

    def keep(head, top, total, row_total, mix, extra):
        inverse = 1.0 / total
        mix = mix * inverse
        mix_acc[head] = mix
        tan_acc[head] = extra * inverse - (row_total * inverse) * mix

    attend_heads(segments, sources, queries, level_bias, width, olds, keep)
    line = lax.broadcasted_iota(jnp.int32, (token_count, token_count), 0)
    lane = lax.broadcasted_iota(jnp.int32, (token_count, token_count), 1)
    unit = (line == lane).astype(F32).astype(BF16)
    sent = []
    for number, acc in enumerate((mix_acc, tan_acc)):
        flat = acc[...].reshape(width, token_count).astype(BF16)
        turned[number] = against(unit, flat).astype(BF16)
        more = chunk_copies(turned.at[number], outs[number], sems, number * FIELDS, FIELDS)
        for copy in more:
            copy.start()
        sent += more
    for copy in sent:
        copy.wait()


def attend_last(level_bias, queries, olds, sources, segments, far_count, far_blocks):
    token_count = queries[0].shape[2]
    width = sources[0].shape[-1]
    states = state_shapes(token_count, width)
    operands = (*queries, *[array for old in olds for array in old], *sources)
    return pl.pallas_call(
        functools.partial(
            last_kernel, segments, len(olds), len(sources), far_count, far_blocks
        ),
        out_shape=(jax.ShapeDtypeStruct((token_count, width), BF16),) * 2,
        in_specs=[smem_spec()] + [vmem_spec()] * len(operands),
        out_specs=[hbm_spec()] * 2,
        scratch_shapes=[
            pltpu.VMEM((FIELDS, far_count, width), BF16),
            pltpu.VMEM(states[0], F32),
            pltpu.VMEM(states[1], F32),
            pltpu.VMEM((2, token_count, width), BF16),
            pltpu.SemaphoreType.DMA((2 * FIELDS,)),
        ],
        compiler_params=pltpu.CompilerParams(vmem_limit_bytes=VMEM_BYTES),
        cost_estimate=own_cost(token_count, width, sum(s[0] for s in segments)),
        name="outer",
    )(level_bias, *operands)


def swap(block, axis, odd):
    count = lax.axis_size(axis)
    route = []
    for low in range(1 if odd else 0, count - 1, 2):
        route += [(low, low + 1), (low + 1, low)]
    return lax.ppermute(block, axis, route)


def part(source, begin, rows):
    return lambda refs, field, window: refs[source][field, begin : begin + rows, window]


def flat_part(source, stride, begin, rows):
    def read(refs, field, window):
        at = field * stride + begin
        return refs[source][at : at + rows, window]

    return read


def forwarded(source, rest, half):
    def read(refs, field, window):
        if field < FIELDS - 1:
            return refs[source][field * half : (field + 1) * half, window]
        return refs[2][rest : rest + half, window]

    return read


def send_to(block, axis, mask):
    return lax.ppermute(block, axis, [(i, i ^ mask) for i in range(lax.axis_size(axis))])


def join(blocks):
    rows = sum(block.shape[0] for block in blocks)
    total, at = None, 0
    for block in blocks:
        count = block.shape[0]
        padded = jnp.pad(block, ((at, rows - at - count), (0, 0)))
        total = padded if total is None else total + padded
        at += count
    return total


def cross_columns(pair):
    count = lax.axis_size("col")
    route = []
    for row in range(lax.axis_size("row")):
        for col in range(count):
            route.append((row * count + col, row * count + (col ^ (2 + row % 2))))
    return lax.ppermute(pair, ("row", "col"), route)


def gather_rows(far):
    count = lax.axis_size("row")
    if count <= 8:
        return [far] + [send_to(far, "row", mask) for mask in range(2, count, 2)]
    for bit in range(1, count.bit_length() - 1):
        far = join([far, send_to(far, "row", 1 << bit)])
    return [far]


def body(
    query_field,
    key_field,
    value_field,
    query_tan,
    key_tan,
    value_tan,
    pool_near,
    pool_far,
    level_bias,
):
    window = query_field.shape[0]
    width = query_field.shape[2]
    cells = window * window
    strip, half = cells // 2, cells // 4
    near_count = cells // (NEAR_POOL * NEAR_POOL)
    row_count, col_count = lax.axis_size("row"), lax.axis_size("col")
    far_count = row_count * col_count
    flat = lambda field: field.reshape(cells, width)
    fields = tuple(flat(f) for f in (key_field, value_field, key_tan, value_tan))

    row_odd_even, col_even, col_odd, row_even, far, row_odd_odd = pack(
        fields, pool_near, pool_far
    )
    group = strip + near_count
    far = far[:FIELDS]
    got_col_even = swap(col_even, "col", False)
    got_row_odd_even = swap(row_odd_even, "row", True)
    got_row_odd_odd = swap(row_odd_odd, "row", True)
    got_col_odd = swap(col_odd, "col", True)
    got_row_even = swap(row_even, "row", False)

    *own_state, query, qtan = attend_own(
        level_bias,
        flat(query_field),
        flat(query_tan),
        fields,
        (got_row_even, row_even),
        [
            (cells, "flag", 0, lambda refs, field, window: refs[field][:, window]),
            (strip, "flag", 0, flat_part(4, group, 0, strip)),
            (near_count, "level", 0, flat_part(4, group, strip, near_count)),
            (near_count, "level", 0, flat_part(5, group, strip, near_count)),
        ],
    )
    queries = (query, qtan)
    far_at = slice(FIELDS * group, FIELDS * group + FIELDS)
    pair = join([far, got_row_even[far_at]])
    far = join([far, got_col_even[far_at], cross_columns(pair)])
    got_row_odd_even, stats = lax.optimization_barrier((got_row_odd_even, own_state[2]))
    own_state = (own_state[0], own_state[1], stats)
    row_state = attend_more(
        level_bias,
        queries,
        [],
        (got_row_odd_even,),
        [(half, "flag", 1, part(0, 0, half))],
        "row_strip",
    )
    got_row_odd_odd, stats = lax.optimization_barrier((got_row_odd_odd, row_state[2]))
    row_state = (row_state[0], row_state[1], stats)
    got_outer_even = swap(got_row_odd_even, "col", False)
    got_outer_odd = swap(got_row_odd_odd, "col", True)
    got_inner = [swap(block, "row", False) for block in forward(got_col_even, got_col_odd)]
    for bit in range(2, col_count.bit_length() - 1):
        far = join([far, send_to(far, "col", 1 << bit)])
    far = join([far, send_to(far, "row", 1)])

    state = attend_more(
        level_bias,
        queries,
        [row_state],
        (got_col_even, got_col_odd),
        [
            (strip, "flag", 0, flat_part(0, group, 0, strip)),
            (strip, "flag", 2, part(1, 0, strip)),
        ],
        "strips",
    )
    far, stats = lax.optimization_barrier((far, state[2]))
    state = (state[0], state[1], stats)
    far_blocks = gather_rows(far)
    state = attend_more(
        level_bias,
        queries,
        [state],
        (*got_inner, got_col_even, got_row_odd_odd),
        [
            (half, "flag", 1, part(4, 0, half)),
            (half, "flag", 0, forwarded(0, 0, half)),
            (half, "flag", 2, forwarded(1, half, half)),
            (near_count, "level", 0, flat_part(2, near_count, strip, near_count)),
            (near_count, "level", 0, flat_part(3, group, strip, near_count)),
        ],
        "inner",
    )
    mixed, mixed_tan = attend_last(
        level_bias,
        queries,
        [state, own_state],
        (got_outer_even, got_outer_odd, *far_blocks),
        [
            (half, "flag", 1, part(0, 0, half)),
            (half, "flag", 3, part(1, 0, half)),
            (far_count, "level", 1, part(2 + len(far_blocks), 0, far_count)),
        ],
        far_count,
        tuple((2 + number, 0) for number in range(len(far_blocks))),
    )
    shape = (window, window, width)
    return (mixed.reshape(shape), mixed_tan.reshape(shape))


def solution(mesh):
    field = P("row", "col", None)
    return jax.shard_map(
        body,
        mesh=mesh,
        in_specs=(field,) * 6 + (P(),) * 3,
        out_specs=(field, field),
        check_vma=False,
    )
```
